128 devices in a mesh: dp: 16 (over x, z_hi, core), tensor: 8 (over y, z_lo).
Axes of the slice: x: 4, y: 4, z: 4 (z_hi: 2, z_lo: 2; z = z_hi * 2 + z_lo), core: 2. Of those that a mesh axis runs over, the one named last changes fastest.
Arguments:
- tokens: bfloat16 [32768, 1024], P(('dp', 'tensor')), may hold values from -6 to 6
- cotangent: bfloat16 [32768, 1024], P(('dp', 'tensor')), may hold values from -6 to 6
- destination: int32 [32768], P(('dp', 'tensor')), may hold values from 0 to 32767, as said below
- variate_ids: int32 [32768], P(('dp', 'tensor')), may hold values from 0 to 7
- time_ids: int32 [32768], P(('dp', 'tensor')), may hold values from 0 to 511
- seq_lengths: int32 [16, 4], P('dp'), may hold values from 1 to 2048, as said below
- qkv_weight: bfloat16 [3, 1024, 1024], P(None, 'dp', 'tensor'), may hold values from -0.1875 to 0.1875
- out_weight: bfloat16 [1024, 1024], P('tensor', 'dp'), may hold values from -4 to 4
- gate_up_weight: bfloat16 [2, 1024, 4096], P(None, 'dp', 'tensor'), may hold values from -0.1875 to 0.1875
- down_weight: bfloat16 [4096, 1024], P('tensor', 'dp'), may hold values from -0.09375 to 0.09375
- norm_gains: bfloat16 [2, 1024], P(None, 'dp'), may hold values from 0.5 to 1.5
- qk_gains: float32 [2, 64], replicated, may hold values from 0.5 to 1.5
- variate_bias: float32 [2, 16], P(None, 'tensor'), may hold values from -3 to 3
Outputs:
- mixed: bfloat16 [32768, 1024], P(('dp', 'tensor'))
- input_grad: bfloat16 [32768, 1024], P(('dp', 'tensor'))
- qkv_grad: float32 [3, 1024, 1024], P(None, 'dp', 'tensor')
- out_grad: float32 [1024, 1024], P('tensor', 'dp')
- gate_up_grad: float32 [2, 1024, 4096], P(None, 'dp', 'tensor')
- down_grad: float32 [4096, 1024], P('tensor', 'dp')
- gains_grad: float32 [2, 1024], P(None, 'dp')
- qk_gains_grad: float32 [2, 64], replicated
- bias_grad: float32 [2, 16], P(None, 'tensor')
The draws below stay inside these ranges and needn't reach their ends.
Inputs may be any that keep to these rules, and one draw needn't show every extreme that they name: `destination`: a permutation of the 32768 rows; among the 256 input rows of each device exactly 2 go to each aligned block of 256 rows of the group order. `seq_lengths`: each row sums to 2048; in each group one sequence, at a place drawn from the seed, holds more than 1792 tokens.
All inputs are finite; a program needn't handle non-finite values.
Results may differ from the reference program's by a relative error of at most 0.028.
Values may be sent and summed in bfloat16 or wider, within the bound.
No kernel may reach another device: no remote copies, remote signals or barrier semaphores. Data moves between devices by JAX's collectives and lax.ppermute only.
A program may use at most 128 MiB of HBM per device.

```python
import jax
import jax.numpy as jnp
from jax import lax

D = 1024
HEADS = 16
HEAD_DIM = 64
FF = 4096
GROUP_TOK = 2048
SEQS = 4
VARIATES = 8
MAX_TIME = 512
QBLOCK = 512
TOK_DEV = 256
TOKENS = 32768


def draw_destination(key, part):
    key = jax.random.fold_in(key, 11)
    device_count = TOKENS // TOK_DEV
    each_rows = TOK_DEV // device_count
    deal_key, shuffle_key = jax.random.split(key)

    def shuffled(sub_key):
        return jax.random.permutation(sub_key, TOK_DEV)
    within = jax.vmap(shuffled)(jax.random.split(deal_key, device_count))
    within = within + (jnp.arange(device_count) * TOK_DEV)[:, None]
    dealt_rows = within.reshape(device_count, device_count, each_rows).transpose(1, 0, 2).reshape(device_count, TOK_DEV)

    def mix_row(sub_key, row_values):
        return row_values[jax.random.permutation(sub_key, TOK_DEV)]
    mixed_rows = jax.vmap(mix_row)(jax.random.split(shuffle_key, device_count), dealt_rows)
    return mixed_rows.reshape(TOKENS).astype(jnp.int32)


def draw_seq_lengths(key, part):
    key = jax.random.fold_in(key, 23)
    groups_count = TOKENS // GROUP_TOK
    pick_key, size_key = jax.random.split(key)
    short_lengths = jax.random.randint(size_key, (groups_count, SEQS), 1, TOK_DEV // SEQS + 1)
    long_index = jax.random.randint(pick_key, (groups_count,), 0, SEQS)
    is_long = jnp.arange(SEQS)[None, :] == long_index[:, None]
    short_lengths = jnp.where(is_long, 0, short_lengths)
    long_length = GROUP_TOK - jnp.sum(short_lengths, axis=1, keepdims=True)
    return jnp.where(is_long, long_length, short_lengths).astype(jnp.int32)


def touch_ends(drawn, key, low, top_value):
    shape = drawn.shape
    index_at = [jax.random.randint(jax.random.fold_in(key, axis), (), 0, shape[axis]) for axis in range(len(shape))]
    drawn = drawn.at[tuple(index_at)].set(low)
    longest = shape.index(max(shape))
    index_at[longest] = (index_at[longest] + 1) % shape[longest]
    return drawn.at[tuple(index_at)].set(top_value)


def block_levels(stream_key, dims, pieces, smallest, top_value):
    factor_of, own = 1.0, jax.random.fold_in(stream_key, 6)
    for axis_at, parts in pieces:
        draws = jnp.exp(jax.random.uniform(jax.random.fold_in(own, axis_at), (parts,), jnp.float32, smallest / len(pieces), top_value / len(pieces)))
        factor_of = factor_of * jnp.repeat(draws, dims[axis_at] // parts).reshape([-1 if axis == axis_at else 1 for axis in range(len(dims))])
    return factor_of


def gaussian(key, dims, scale, limit, shards=(), kind=jnp.bfloat16):
    values = scale * jax.random.normal(key, dims, jnp.float32)
    if shards:
        values = values * block_levels(key, dims, shards, -0.22, 0.18)
    return jnp.clip(values, -limit, limit).astype(kind)


def setup_inputs(seed: int = 0) -> dict:
    seeds = jax.random.split(jax.random.key(seed), 14)
    tokens = gaussian(seeds[0], (TOKENS, D), 1.0, 6.0, ((0, 128),))
    cotangent = gaussian(seeds[1], (TOKENS, D), 1.0, 6.0, ((0, 128),))
    destination = draw_destination(jax.random.fold_in(seeds[13], 71), 0)
    variate_ids = touch_ends(jax.random.randint(seeds[3], (TOKENS,), 0, VARIATES), jax.random.fold_in(seeds[3], 1), 0, VARIATES - 1).astype(jnp.int32)
    time_ids = touch_ends(jax.random.randint(seeds[4], (TOKENS,), 0, MAX_TIME), jax.random.fold_in(seeds[4], 1), 0, MAX_TIME - 1).astype(jnp.int32)
    seq_lengths = draw_seq_lengths(jax.random.fold_in(seeds[13], 71), 0)
    qkv_weight = gaussian(seeds[6], (3, D, D), D ** -0.5, 0.1875, ((1, 16), (2, 8)))
    out_weight = gaussian(seeds[7], (D, D), (max(1, 4 * D // GROUP_TOK)) ** -0.5, 4.0, ((0, 8), (1, 16)))
    gate_up_weight = gaussian(seeds[8], (2, D, FF), D ** -0.5, 0.1875, ((1, 16), (2, 8)))
    down_weight = gaussian(seeds[9], (FF, D), FF ** -0.5, 0.09375, ((0, 8), (1, 16)))
    norm_gains = jnp.clip(1.0 + 0.1 * jax.random.normal(seeds[10], (2, D), jnp.float32), 0.5, 1.5).astype(jnp.bfloat16)
    qk_gains = jnp.clip(1.0 + 0.1 * jax.random.normal(seeds[11], (2, HEAD_DIM), jnp.float32), 0.5, 1.5)
    variate_bias = gaussian(seeds[12], (2, HEADS), 1.0, 3.0, ((1, 8),), jnp.float32)
    return {"tokens": tokens, "cotangent": cotangent, "destination": destination, "variate_ids": variate_ids, "time_ids": time_ids, "seq_lengths": seq_lengths, "qkv_weight": qkv_weight, "out_weight": out_weight, "gate_up_weight": gate_up_weight, "down_weight": down_weight, "norm_gains": norm_gains, "qk_gains": qk_gains, "variate_bias": variate_bias}


EPS = 1e-06
THETA = 10000.0
MASKED = -1e+30

@jax.custom_vjp
def low(v):
    return lax.optimization_barrier(v.astype(jnp.bfloat16)).astype(jnp.float32)

@jax.custom_vjp
def low_back(v):
    return v

def low_keep(v):
    return (low(v), None)

def low_pass(kept, grad):
    return (grad,)

def back_keep(v):
    return (v, None)

def back_low(kept, grad):
    return (low(grad),)
low.defvjp(low_keep, low_pass)
low_back.defvjp(back_keep, back_low)

def product(left, right):
    return jnp.dot(left, right, preferred_element_type=jnp.float32, precision=lax.Precision.HIGHEST)

def root_norm(values, gain):
    return values * lax.rsqrt(lax.optimization_barrier(jnp.mean(values * values, axis=-1, keepdims=True)) + EPS) * gain

def rotary(time_rows):
    half_dim = HEAD_DIM // 2
    steps_up = jnp.arange(half_dim).astype(jnp.float32)
    inverse = THETA ** (-2.0 * steps_up / HEAD_DIM)
    angles = time_rows.astype(jnp.float32)[:, None] * inverse[None, :]
    return (jnp.cos(angles)[:, None, :], jnp.sin(angles)[:, None, :])

def turn(values, cosine, sine):
    half_dim = values.shape[-1] // 2
    first_half = values[..., :half_dim]
    second_half = values[..., half_dim:]
    return jnp.concatenate([first_half * cosine - second_half * sine, first_half * sine + second_half * cosine], axis=-1)

def attend_block(query_rows, seg_rows, var_rows, key_rows, value_rows, segments, variates, bias_pair):
    raw_scores = low_back(jnp.einsum('bhd,khd->hbk', query_rows, key_rows, precision=lax.Precision.HIGHEST))
    same_var = var_rows[:, None] == variates[None, :]
    scores = raw_scores + jnp.where(same_var[None], bias_pair[0][:, None, None], bias_pair[1][:, None, None])
    inside = (seg_rows[:, None] == segments[None, :])[None]
    scores = jnp.where(inside, scores, MASKED)
    row_top = lax.optimization_barrier(jnp.max(scores, axis=-1, keepdims=True))
    exp_scores = jnp.exp(scores - row_top)
    probs = exp_scores / lax.optimization_barrier(jnp.sum(exp_scores, axis=-1, keepdims=True))
    return jnp.einsum('hbk,khd->bhd', low(probs), value_rows, precision=lax.Precision.HIGHEST)

def layer_rows(params, stream, segments, variates, time_rows):
    qkv_w, out_w, gate_up_w, down_w, norm_gain, qk_gain, var_bias = params
    length_now = stream.shape[0]
    normed = low(root_norm(stream, norm_gain[0]))
    query = low_back(product(normed, qkv_w[0])).reshape(length_now, HEADS, HEAD_DIM)
    keys_raw = low_back(product(normed, qkv_w[1])).reshape(length_now, HEADS, HEAD_DIM)
    values_raw = low_back(product(normed, qkv_w[2])).reshape(length_now, HEADS, HEAD_DIM)
    cosine, sine = rotary(time_rows)
    query_rot = low(turn(root_norm(query, qk_gain[0]), cosine, sine) * HEAD_DIM ** (-0.5))
    key_rot = low(turn(root_norm(keys_raw, qk_gain[1]), cosine, sine))
    value_rot = low(values_raw)
    block_count = length_now // QBLOCK

    def one_block(pieces_now):
        return attend_block(pieces_now[0], pieces_now[1], pieces_now[2], key_rot, value_rot, segments, variates, var_bias)
    attended = lax.map(jax.checkpoint(one_block), (query_rot.reshape(block_count, QBLOCK, HEADS, HEAD_DIM), segments.reshape(block_count, QBLOCK), variates.reshape(block_count, QBLOCK)))
    attn_rows = low_back(low(attended.reshape(length_now, D)))
    hidden_one = stream + low_back(product(attn_rows, out_w))
    ffn_in = low(root_norm(hidden_one, norm_gain[1]))
    gate_rows = low_back(product(ffn_in, gate_up_w[0]))
    up_rows = low_back(product(ffn_in, gate_up_w[1]))
    hidden = low(jax.nn.silu(gate_rows) * up_rows)
    return hidden_one + low_back(product(hidden, down_w))

def reference(tokens, cotangent, destination, variate_ids, time_ids, seq_lengths, qkv_weight, out_weight, gate_up_weight, down_weight, norm_gains, qk_gains, variate_bias):
    groups_count = TOKENS // GROUP_TOK

    def to_groups(values):
        placed = jnp.zeros((TOKENS,) + values.shape[1:], values.dtype).at[destination].set(values)
        return placed.reshape((groups_count, GROUP_TOK) + values.shape[1:])
    stream = to_groups(tokens.astype(jnp.float32))
    grad_groups = to_groups(cotangent.astype(jnp.float32))
    variates = to_groups(variate_ids)
    time_rows = to_groups(time_ids)
    ends = jnp.cumsum(seq_lengths, axis=1)
    positions = jnp.arange(GROUP_TOK).astype(jnp.int32)
    segments = lax.optimization_barrier(jnp.sum((positions[None, :, None] >= ends[:, None, :]).astype(jnp.int32), axis=2))
    params = (qkv_weight.astype(jnp.float32), out_weight.astype(jnp.float32), gate_up_weight.astype(jnp.float32), down_weight.astype(jnp.float32), norm_gains.astype(jnp.float32), qk_gains.astype(jnp.float32), variate_bias.astype(jnp.float32))

    def whole_layer(params_now, stream_now):

        def group_step(unused, pieces_now):
            return (unused, jax.checkpoint(layer_rows)(params_now, pieces_now[0], pieces_now[1], pieces_now[2], pieces_now[3]))
        _, results = lax.scan(group_step, None, (stream_now, segments, variates, time_rows))
        return results
    outputs, pullback = jax.vjp(whole_layer, params, stream)
    param_grads, stream_grads = pullback(grad_groups)
    mixed = outputs.reshape(TOKENS, D)[destination].astype(jnp.bfloat16)
    input_grad = stream_grads.reshape(TOKENS, D)[destination].astype(jnp.bfloat16)
    return (mixed, input_grad, param_grads[0], param_grads[1], param_grads[2], param_grads[3], param_grads[4], param_grads[5], param_grads[6])
```

```python
import functools

import jax
import jax.numpy as jnp
from jax import lax
from jax.experimental import pallas as pl
from jax.experimental.pallas import tpu as pltpu
from jax.sharding import Mesh
from jax.sharding import PartitionSpec as P

HEADS = 16
HEAD_DIM = 64
HALF = HEAD_DIM // 2
D = 1024
FF = 4096
ROWS = 256
RING = 4
PLANE = ROWS * RING
GROUP = 2 * PLANE
DEVICES = 128
VARIATES = 8
SEQS = 4
WIDE = 128
EPS = 1e-06
THETA = 10000.0
LOG2E = 1.4426950408889634
FAR = -16384.0
F32 = jnp.float32
BF16 = jnp.bfloat16

ALL = ("x", "zh", "core", "y", "zl")
FLAT = ("x", "zh", "zl")
NT = (((1,), (1,)), ((), ()))
TN = (((0,), (0,)), ((), ()))


def mm(left, right, dims=(((1,), (0,)), ((), ()))):
    return lax.dot_general(left, right, dims, preferred_element_type=F32)


def root_stats(values):
    return lax.rsqrt(jnp.mean(values * values, axis=-1, keepdims=True) + EPS)


def norm_back(grad_in, normed, scale_inv):
    return scale_inv * (grad_in - normed * jnp.mean(grad_in * normed, axis=-1, keepdims=True))


def pieces(values, count):
    out = []
    for _ in range(count):
        part = lax.reduce_precision(values, 8, 7)
        out.append(part.astype(BF16))
        values = values - part
    return out


def ring(values, step):
    return lax.ppermute(values, "y", [(i, (i + step) % RING) for i in range(RING)])


def swap_core(values):
    return lax.ppermute(values, "core", [(0, 1), (1, 0)])


def gather_ring(values):
    ahead = ring(values, -1)
    behind = ring(values, 1)
    half = values.shape[0] // 2
    far_top = ring(ahead[:half], -1)
    far_low = ring(behind[half:], 1)
    return [values, ahead, jnp.concatenate([far_top, far_low], 0), behind]


def reduce_ring(parts):
    far = ring(parts[2], 2)
    near = ring(parts[1], 1)
    back = ring(parts[3], -1)
    return (
        parts[0].astype(F32) + near.astype(F32) + back.astype(F32) + far.astype(F32)
    )


def flat_gather(shard):
    many = jnp.broadcast_to(shard[None], (16,) + shard.shape)
    mine = lax.all_to_all(many, FLAT, 0, 0, tiled=True)
    other = swap_core(mine)
    low = lax.axis_index("core") == 0
    both = jnp.stack([jnp.where(low, mine, other), jnp.where(low, other, mine)])
    return both.reshape((2, 4, 2, 2) + shard.shape)


def weights_of(shard):
    kinds, depth, width = shard.shape
    full = flat_gather(shard)
    return full.transpose(4, 1, 2, 0, 5, 3, 6).reshape(kinds, 16 * depth, 2 * width)


def grads_home(full, kinds, depth, width):
    core = lax.axis_index("core")
    split = full.reshape(kinds, 4, 2, 2, depth, 2, width)
    keep = lax.dynamic_index_in_dim(split, core, 3, keepdims=False)
    send = lax.dynamic_index_in_dim(split, 1 - core, 3, keepdims=False)
    got = swap_core(send)
    total = (keep.astype(F32) + got.astype(F32)).astype(BF16)
    total = total.transpose(1, 2, 4, 0, 3, 5).reshape(16, kinds, depth, width)
    arrived = lax.all_to_all(total, FLAT, 0, 0, tiled=True)
    return jnp.sum(arrived.astype(F32), axis=0)


def attend_kernel(q_ref, k_ref, v_ref, o_ref, *, chunks):
    size = k_ref.shape[1] // chunks
    query = q_ref[0]
    total = None
    for c in range(chunks):
        rows = pl.ds(c * size, size)
        score = mm(query, k_ref[0, rows, :], NT)
        prob = jnp.exp2(score).astype(BF16)
        part = mm(prob, v_ref[0, rows, :])
        total = part if total is None else total + part
    row_sum = total[:, HEAD_DIM : HEAD_DIM + 1]
    lane = lax.broadcasted_iota(jnp.int32, total.shape, 1)
    o_ref[0] = jnp.where(lane < HEAD_DIM, total / row_sum, jnp.log2(row_sum))


def attend(q_aug, k_aug, v_aug):
    heads, rows, wide = q_aug.shape
    block = 512
    return pl.pallas_call(
        functools.partial(attend_kernel, chunks=4),
        grid=(heads, rows // block),
        in_specs=[
            pl.BlockSpec((1, block, wide), lambda h, i: (h, i, 0)),
            pl.BlockSpec((1, rows, wide), lambda h, i: (h, 0, 0)),
            pl.BlockSpec((1, rows, wide), lambda h, i: (h, 0, 0)),
        ],
        out_specs=pl.BlockSpec((1, block, wide), lambda h, i: (h, i, 0)),
        out_shape=jax.ShapeDtypeStruct((heads, rows, wide), F32),
        compiler_params=pltpu.CompilerParams(vmem_limit_bytes=48 * 2**20),
        cost_estimate=pl.CostEstimate(
            flops=heads * rows * rows * wide * 8, bytes_accessed=heads * rows * wide * 10,
            transcendentals=heads * rows * rows,
        ),
    )(q_aug, k_aug, v_aug)


def attend_back_kernel(q_ref, k_ref, v_ref, g_ref, dq_ref, dk_ref, dv_ref, *, chunks):
    size = k_ref.shape[1] // chunks
    query = q_ref[0]
    grad = g_ref[0]

    @pl.when(pl.program_id(1) == 0)
    def _():
        dk_ref[...] = jnp.zeros_like(dk_ref)
        dv_ref[...] = jnp.zeros_like(dv_ref)

    total = None
    for c in range(chunks):
        rows = pl.ds(c * size, size)
        keys = k_ref[0, rows, :]
        prob = jnp.exp2(mm(keys, query, NT))
        slope = mm(v_ref[0, rows, :], grad, NT)
        d_score = (prob * slope).astype(BF16)
        dv_ref[0, rows, :] += mm(prob.astype(BF16), grad)
        dk_ref[0, rows, :] += mm(d_score, query)
        part = mm(d_score, keys, TN)
        total = part if total is None else total + part
    dq_ref[0] = total


def attend_back(q_aug, k_aug, v_aug, g_aug):
    heads, rows, wide = q_aug.shape
    block = 512
    moving = pl.BlockSpec((1, block, wide), lambda h, i: (h, i, 0))
    fixed = pl.BlockSpec((1, rows, wide), lambda h, i: (h, 0, 0))
    shape = jax.ShapeDtypeStruct((heads, rows, wide), F32)
    return pl.pallas_call(
        functools.partial(attend_back_kernel, chunks=4),
        grid=(heads, rows // block),
        in_specs=[moving, fixed, fixed, moving],
        out_specs=[moving, fixed, fixed],
        out_shape=[shape] * 3,
        compiler_params=pltpu.CompilerParams(vmem_limit_bytes=48 * 2**20),
        cost_estimate=pl.CostEstimate(
            flops=heads * rows * rows * wide * 20, bytes_accessed=heads * rows * wide * 20,
            transcendentals=heads * rows * rows,
        ),
    )(q_aug, k_aug, v_aug, g_aug)


def feed_kernel(b_ref, g_ref, w_ref, y_ref, db_ref, hid_ref, dg_ref, du_ref, y_sum, db_sum):
    step = pl.program_id(0)
    rows = b_ref[...]
    gate_w, up_w, down_w = w_ref[0], w_ref[1], w_ref[2]
    gate = mm(rows, gate_w)
    up = mm(rows, up_w)
    d_hidden = mm(g_ref[...], down_w)
    sig = 1.0 / (1.0 + jnp.exp(-gate))
    silu = gate * sig
    hidden = (silu * up).astype(BF16)
    d_gate = (d_hidden * up * (sig * (1.0 + gate * (1.0 - sig)))).astype(BF16)
    d_up = (d_hidden * silu).astype(BF16)
    hid_ref[...] = hidden
    dg_ref[...] = d_gate
    du_ref[...] = d_up
    y_part = mm(hidden, down_w, NT)
    db_part = mm(d_gate, gate_w, NT) + mm(d_up, up_w, NT)

    @pl.when(step == 0)
    def _():
        y_sum[...] = y_part
        db_sum[...] = db_part

    @pl.when(step > 0)
    def _():
        y_sum[...] += y_part
        db_sum[...] += db_part

    @pl.when(step == pl.num_programs(0) - 1)
    def _():
        y_ref[...] = y_sum[...].astype(BF16)
        db_ref[...] = db_sum[...].astype(BF16)


def feed(rows_b, rows_g, weights):
    rows = rows_b.shape[0]
    width = weights.shape[2]
    block = 256
    whole = pl.BlockSpec((rows, D), lambda f: (0, 0))
    part = pl.BlockSpec((rows, block), lambda f: (0, f))
    low_d = jax.ShapeDtypeStruct((rows, D), BF16)
    low_f = jax.ShapeDtypeStruct((rows, width), BF16)
    return pl.pallas_call(
        feed_kernel,
        grid=(width // block,),
        in_specs=[whole, whole, pl.BlockSpec((3, D, block), lambda f: (0, 0, f))],
        out_specs=[whole, whole, part, part, part],
        out_shape=[low_d, low_d, low_f, low_f, low_f],
        scratch_shapes=[pltpu.VMEM((rows, D), F32)] * 2,
        compiler_params=pltpu.CompilerParams(vmem_limit_bytes=48 * 2**20),
        cost_estimate=pl.CostEstimate(
            flops=12 * rows * D * width, bytes_accessed=6 * D * width + rows * D * 8 + rows * width * 6,
            transcendentals=rows * width,
        ),
    )(rows_b, rows_g, weights)


def turn(values, cosine, sine):
    first, second = values[..., :HALF], values[..., HALF:]
    return jnp.concatenate(
        [first * cosine - second * sine, first * sine + second * cosine], axis=-1
    )


def turn_back(grads, cosine, sine):
    upper, lower = grads[..., :HALF], grads[..., HALF:]
    return jnp.concatenate(
        [upper * cosine + lower * sine, lower * cosine - upper * sine], axis=-1
    )


def body(
    tokens,
    cotangent,
    destination,
    variate_ids,
    time_ids,
    seq_lengths,
    qkv_weight,
    out_weight,
    gate_up_weight,
    down_weight,
    norm_gains,
    qk_gains,
    variate_bias,
):
    core = lax.axis_index("core")
    low_core = core == 0
    y_at = lax.axis_index("y")
    zl_at = lax.axis_index("zl")

    def mine_other(pair):
        return (
            jnp.where(low_core, pair[..., :WIDE], pair[..., WIDE:]),
            jnp.where(low_core, pair[..., WIDE:], pair[..., :WIDE]),
        )

    def side_by_side(mine, other):
        return jnp.concatenate(
            [jnp.where(low_core, mine, other), jnp.where(low_core, other, mine)], axis=-1
        )

    slot = destination % ROWS
    group_at = destination // GROUP
    block_at = (destination % GROUP) // ROWS
    device_at = ((group_at // 2) * 2 + block_at // 4) * 8 + (block_at % 4) * 2 + group_at % 2
    key = device_at * ROWS + slot
    rank = jnp.sum((key[None, :] < key[:, None]).astype(jnp.int32), axis=1)
    deal = (jnp.arange(ROWS)[:, None] == rank[None, :]).astype(BF16)
    facts = jnp.stack([slot, variate_ids, time_ids // 32, time_ids % 32], axis=1).astype(BF16)
    facts = jnp.concatenate([facts, jnp.zeros((ROWS, WIDE - 4), BF16)], axis=1)
    gains_row = jnp.broadcast_to(norm_gains.reshape(1, WIDE), (ROWS, WIDE))
    outgoing = jnp.concatenate([tokens, cotangent, facts, gains_row], axis=1)
    span = outgoing.shape[1]
    outgoing = mm(deal, outgoing).astype(BF16).reshape(DEVICES, 2, span)
    arrived = lax.all_to_all(outgoing, ALL, 0, 0, tiled=True)

    attn_shard = jnp.concatenate([qkv_weight, out_weight.T[None]], 0)
    feed_shard = jnp.concatenate([gate_up_weight, down_weight.T[None]], 0)
    attn_shard, arrived = lax.optimization_barrier((attn_shard, arrived))
    attn_w = weights_of(attn_shard)
    feed_shard, attn_w = lax.optimization_barrier((feed_shard, attn_w))
    feed_w = weights_of(feed_shard)

    lengths_other = swap_core(seq_lengths)
    lengths = jnp.where(zl_at == core, seq_lengths, lengths_other)[0]
    bias_other = lax.ppermute(variate_bias, "zl", [(0, 1), (1, 0)])
    bias_pair = jnp.where(zl_at == core, variate_bias, bias_other)

    all_gains = arrived[:, 0, span - WIDE :].reshape(16, 8, 2, 64)[:, 0]
    all_gains = all_gains.transpose(1, 0, 2).reshape(2, D).astype(F32)
    gain_one, gain_two = all_gains[0], all_gains[1]
    slots = arrived[:, :, 2 * D].reshape(2 * DEVICES)
    place = (jnp.arange(ROWS).astype(BF16)[:, None] == slots[None, :]).astype(BF16)
    placed = mm(place, arrived.reshape(2 * DEVICES, span))
    inputs = placed[:, :D]
    grad_rows = placed[:, D : 2 * D].astype(BF16)
    facts_here = placed[:, 2 * D : 2 * D + WIDE].astype(BF16)

    scale_one = root_stats(inputs)
    normed_one = inputs * scale_one
    attn_in = (normed_one * gain_one).astype(BF16)
    attn_all = gather_ring(jnp.concatenate([attn_in, facts_here], axis=1))
    attn_all = jnp.concatenate(attn_all, 0)
    facts_all = attn_all[:, D:].astype(F32)
    attn_all = attn_all[:, :D]
    grad_all = gather_ring(grad_rows)

    variates_own = facts_all[:, 1].astype(jnp.int32)
    times = facts_all[:, 2] * 32.0 + facts_all[:, 3]
    variates = jnp.concatenate([variates_own, swap_core(variates_own)])
    blocks_y = (y_at + jnp.arange(RING)) % RING
    blocks = jnp.concatenate([core * RING + blocks_y, (1 - core) * RING + blocks_y])
    positions = (blocks[:, None] * ROWS + jnp.arange(ROWS)[None, :]).reshape(GROUP)
    segments = jnp.sum((positions[:, None] >= jnp.cumsum(lengths)[None, :]).astype(jnp.int32), 1)

    projected = jnp.einsum("gd,kde->kge", attn_all, attn_w[:3], preferred_element_type=F32)
    heads_here = 4
    query_raw = projected[0].reshape(PLANE, heads_here, HEAD_DIM)
    key_raw = projected[1].reshape(PLANE, heads_here, HEAD_DIM)
    query_inv = root_stats(query_raw)
    query_unit = query_raw * query_inv
    key_inv = root_stats(key_raw)
    key_unit = key_raw * key_inv
    inverse = THETA ** (-2.0 * jnp.arange(HALF).astype(F32) / HEAD_DIM)
    angles = times[:, None] * inverse[None, :]
    cosine, sine = jnp.cos(angles)[:, None, :], jnp.sin(angles)[:, None, :]
    query_rot = turn(query_unit * qk_gains[0], cosine, sine) * (HEAD_DIM ** (-0.5) * LOG2E)
    key_rot = turn(key_unit * qk_gains[1], cosine, sine)
    qkv_low = jnp.stack(
        [
            query_rot.reshape(PLANE, 2 * WIDE).astype(BF16),
            key_rot.reshape(PLANE, 2 * WIDE).astype(BF16),
            projected[2].astype(BF16),
        ]
    )
    qkv_mine, qkv_send = mine_other(qkv_low)
    qkv_got = swap_core(qkv_send)
    qkv_mine = jnp.concatenate([qkv_mine, qkv_got], axis=1)
    qkv_mine = qkv_mine.reshape(3, GROUP, 2, HEAD_DIM).transpose(0, 2, 1, 3)

    var_hot = (variates[:, None] == jnp.arange(VARIATES)[None, :]).astype(F32)
    seg_hot = (segments[:, None] == jnp.arange(SEQS)[None, :]).astype(F32)
    bias_parts = pieces(bias_pair * LOG2E, 3)
    query_tail = jnp.concatenate([var_hot] * 3 + [seg_hot], axis=1).astype(BF16)
    key_bias = [
        jnp.where(
            (var_hot > 0)[None], part[0][:, None, None].astype(F32), part[1][:, None, None].astype(F32)
        )
        for part in bias_parts
    ]
    seg_far = jnp.broadcast_to(((1.0 - seg_hot) * FAR)[None], (2, GROUP, SEQS))
    key_tail = jnp.concatenate(key_bias + [seg_far, jnp.ones((2, GROUP, 3), F32)], axis=2).astype(BF16)
    tail = 3 * VARIATES + SEQS
    spare = WIDE - HEAD_DIM
    query_tail = jnp.broadcast_to(query_tail[None], (2, GROUP, tail))
    zeros = jnp.zeros((2, GROUP, spare), BF16)
    query_aug = jnp.concatenate([qkv_mine[0], query_tail, zeros[..., tail:]], axis=2)
    key_aug = jnp.concatenate([qkv_mine[1], key_tail, zeros[..., tail + 3 :]], axis=2)
    value_aug = jnp.concatenate(
        [qkv_mine[2], jnp.ones((2, GROUP, 3), BF16), zeros[..., 3:]], axis=2
    )
    attended = attend(query_aug, key_aug, value_aug)
    log_total = attended[:, :, HEAD_DIM : HEAD_DIM + 1]
    attended = attended[:, :, :HEAD_DIM]
    att_low = attended.transpose(1, 0, 2).reshape(GROUP, WIDE).astype(BF16)
    att_plane = side_by_side(att_low[:PLANE], swap_core(att_low[PLANE:]))
    out_part = mm(att_plane, attn_w[3], NT).astype(BF16).reshape(RING, ROWS, D)
    hidden_one = inputs + reduce_ring([out_part[r] for r in range(RING)])

    scale_two = root_stats(hidden_one)
    normed_two = hidden_one * scale_two
    feed_in = (normed_two * gain_two).astype(BF16)
    feed_all = gather_ring(feed_in)
    fed = [feed(feed_all[r], grad_all[r], feed_w) for r in range(RING)]
    grad_normed_two = reduce_ring([f[1] for f in fed])
    mixed = (hidden_one + reduce_ring([f[0] for f in fed])).astype(BF16)

    feed_rows = jnp.concatenate(feed_all, 0)
    hidden_all = jnp.concatenate([f[2] for f in fed], 0)
    d_pair = jnp.stack(
        [jnp.concatenate([f[3] for f in fed], 0), jnp.concatenate([f[4] for f in fed], 0)]
    )
    grad_cat = jnp.concatenate(grad_all, 0)
    gate_up_full = jnp.einsum("gd,kgf->kdf", feed_rows, d_pair, preferred_element_type=F32).astype(BF16)
    down_full = mm(grad_cat, hidden_all, TN).astype(BF16)
    feed_grad = grads_home(jnp.concatenate([gate_up_full, down_full[None]], 0), 3, 64, 512)

    gain_two_grad = jnp.sum(grad_normed_two * normed_two, axis=0)
    grad_one = grad_rows.astype(F32) + norm_back(grad_normed_two * gain_two, normed_two, scale_two)

    grad_one_all = jnp.concatenate(gather_ring(grad_one.astype(BF16)), 0)
    grad_att = mm(grad_one_all, attn_w[3]).astype(BF16)
    grad_mine, grad_send = mine_other(grad_att)
    grad_mine = jnp.concatenate([grad_mine, swap_core(grad_send)], 0)
    grad_mine = grad_mine.reshape(GROUP, 2, HEAD_DIM).transpose(1, 0, 2)
    dots = jnp.sum(grad_mine.astype(F32) * attended, axis=-1, keepdims=True)
    grad_aug = jnp.concatenate([grad_mine] + pieces(-dots, 3) + [zeros[..., 3:]], axis=2)
    query_back = jnp.concatenate(
        [qkv_mine[0], query_tail] + pieces(-log_total, 3) + [zeros[..., tail + 3 :]], axis=2
    )
    d_query, d_key, d_value = attend_back(query_back, key_aug, value_aug, grad_aug)
    by_variate = jnp.sum(d_key[:, :, HEAD_DIM : HEAD_DIM + VARIATES] * var_hot[None], axis=(1, 2))
    by_all = jnp.sum(d_key[:, :, HEAD_DIM : HEAD_DIM + VARIATES], axis=(1, 2))
    bias_part = jnp.stack([by_variate, by_all - by_variate])
    d_all = jnp.stack([d_query, d_key * (1.0 / LOG2E), d_value])[..., :HEAD_DIM].astype(BF16)
    d_all = d_all.transpose(0, 2, 1, 3).reshape(3, GROUP, WIDE)
    d_plane = side_by_side(d_all[:, :PLANE], swap_core(d_all[:, PLANE:]))
    d_query_rows = d_plane[0].astype(F32).reshape(PLANE, heads_here, HEAD_DIM)
    d_key_rows = d_plane[1].astype(F32).reshape(PLANE, heads_here, HEAD_DIM)
    grad_q_unit = turn_back(d_query_rows * HEAD_DIM ** (-0.5), cosine, sine)
    grad_k_unit = turn_back(d_key_rows, cosine, sine)
    query_gain_grad = jnp.sum(grad_q_unit * query_unit, axis=(0, 1))
    key_gain_grad = jnp.sum(grad_k_unit * key_unit, axis=(0, 1))
    grad_q_raw = norm_back(grad_q_unit * qk_gains[0], query_unit, query_inv)
    grad_k_raw = norm_back(grad_k_unit * qk_gains[1], key_unit, key_inv)
    grad_proj = jnp.stack(
        [
            grad_q_raw.reshape(PLANE, 2 * WIDE).astype(BF16),
            grad_k_raw.reshape(PLANE, 2 * WIDE).astype(BF16),
            d_plane[2],
        ]
    )
    in_part = jnp.einsum("kge,kde->gd", grad_proj, attn_w[:3], preferred_element_type=F32)
    in_part = in_part.astype(BF16).reshape(RING, ROWS, D)
    grad_normed_one = reduce_ring([in_part[r] for r in range(RING)])
    qkv_full = jnp.einsum("gd,kge->kde", attn_all, grad_proj, preferred_element_type=F32).astype(BF16)
    out_full = mm(grad_one_all, att_plane, TN).astype(BF16)
    attn_grad = grads_home(jnp.concatenate([qkv_full, out_full[None]], 0), 4, 64, 128)

    gain_one_grad = jnp.sum(grad_normed_one * normed_one, axis=0)
    input_grad = grad_one + norm_back(grad_normed_one * gain_one, normed_one, scale_one)

    back_mixed = mm(place, mixed, TN).astype(BF16).reshape(DEVICES, 2, D)
    home_mixed = lax.all_to_all(back_mixed, ALL, 0, 0, tiled=True)
    new_tokens = mm(deal, home_mixed.reshape(ROWS, D), TN).astype(BF16)

    gain_sums = jnp.stack([gain_one_grad, gain_two_grad]).reshape(2, 16, 64).transpose(1, 0, 2)
    gain_sums = jnp.broadcast_to(gain_sums.reshape(16, 1, WIDE), (16, 8, WIDE))
    qk_row = jnp.concatenate([query_gain_grad, key_gain_grad])
    qk_row = jnp.broadcast_to(qk_row[None, None], (16, 8, WIDE))
    here = (jnp.arange(8) == y_at * 2 + core)[None, :, None]
    bias_row = jnp.where(here, bias_part.reshape(1, 1, 4), 0.0)
    bias_row = jnp.broadcast_to(bias_row, (16, 8, 4))
    smalls = jnp.concatenate([gain_sums, qk_row, bias_row, jnp.zeros((16, 8, WIDE - 4), F32)], axis=2)
    smalls = jnp.stack(pieces(smalls.reshape(DEVICES, 3 * WIDE), 2), axis=1)
    back_grads = mm(place, input_grad.astype(BF16), TN).astype(BF16).reshape(DEVICES, 2, D)
    home = lax.all_to_all(jnp.concatenate([back_grads, smalls], axis=2), ALL, 0, 0, tiled=True)
    token_grads = mm(deal, home[:, :, :D].reshape(ROWS, D), TN).astype(BF16)
    sums = jnp.sum(home[:, :, D:].astype(F32), axis=(0, 1))
    gains_grad = sums[:WIDE].reshape(2, 64)
    qk_grad = sums[WIDE : 2 * WIDE].reshape(2, 64)
    bias_grad = sums[2 * WIDE : 2 * WIDE + 4].reshape(2, 2)

    return (
        new_tokens,
        token_grads,
        attn_grad[:3],
        attn_grad[3].T,
        feed_grad[:2],
        feed_grad[2].T,
        gains_grad,
        qk_grad,
        bias_grad,
    )


def solution(mesh):
    fine = Mesh(mesh.devices.reshape(4, 2, 2, 4, 2), ALL)
    dp = ("x", "zh", "core")
    tensor = ("y", "zl")
    in_specs = (
        P(ALL, None),
        P(ALL, None),
        P(ALL),
        P(ALL),
        P(ALL),
        P(dp, None),
        P(None, dp, tensor),
        P(tensor, dp),
        P(None, dp, tensor),
        P(tensor, dp),
        P(None, dp),
        P(),
        P(None, tensor),
    )
    out_specs = (
        P(ALL, None),
        P(ALL, None),
        P(None, dp, tensor),
        P(tensor, dp),
        P(None, dp, tensor),
        P(tensor, dp),
        P(None, dp),
        P(),
        P(None, tensor),
    )
    return jax.shard_map(body, mesh=fine, in_specs=in_specs, out_specs=out_specs, check_vma=False)
```

```python
import functools

import jax
import jax.numpy as jnp
from jax import lax
from jax.experimental import pallas as pl
from jax.experimental.pallas import tpu as pltpu
from jax.sharding import Mesh
from jax.sharding import PartitionSpec as P

HEADS = 16
HEAD_DIM = 64
HALF = HEAD_DIM // 2
D = 1024
FF = 4096
ROWS = 256
RING = 4
PLANE = ROWS * RING
GROUP = 2 * PLANE
DEVICES = 128
VARIATES = 8
SEQS = 4
WIDE = 128
EPS = 1e-06
THETA = 10000.0
LOG2E = 1.4426950408889634
FAR = -16384.0
F32 = jnp.float32
BF16 = jnp.bfloat16

ALL = ("x", "zh", "core", "y", "zl")
FLAT = ("x", "zh", "zl")
NT = (((1,), (1,)), ((), ()))
TN = (((0,), (0,)), ((), ()))


def mm(left, right, dims=(((1,), (0,)), ((), ()))):
    return lax.dot_general(left, right, dims, preferred_element_type=F32)


def root_stats(values):
    return lax.rsqrt(jnp.mean(values * values, axis=-1, keepdims=True) + EPS)


def norm_back(grad_in, normed, scale_inv):
    return scale_inv * (grad_in - normed * jnp.mean(grad_in * normed, axis=-1, keepdims=True))


def pieces(values, count):
    out = []
    for _ in range(count):
        part = lax.reduce_precision(values, 8, 7)
        out.append(part.astype(BF16))
        values = values - part
    return out


def ring(values, step):
    return lax.ppermute(values, "y", [(i, (i + step) % RING) for i in range(RING)])


def swap_core(values):
    return lax.ppermute(values, "core", [(0, 1), (1, 0)])


def gather_ring(values):
    ahead = ring(values, -1)
    behind = ring(values, 1)
    half = values.shape[0] // 2
    far_top = ring(ahead[:half], -1)
    far_low = ring(behind[half:], 1)
    return [values, ahead, jnp.concatenate([far_top, far_low], 0), behind]


def reduce_ring(parts):
    far = ring(parts[2], 2)
    near = ring(parts[1], 1)
    back = ring(parts[3], -1)
    return (
        parts[0].astype(F32) + near.astype(F32) + back.astype(F32) + far.astype(F32)
    )


def flat_gather(shard):
    many = jnp.broadcast_to(shard[None], (16,) + shard.shape)
    mine = lax.all_to_all(many, FLAT, 0, 0, tiled=True)
    return mine, swap_core(mine)


def assemble_kernel(core_ref, mine_ref, other_ref, out_ref, sems, *, depth, width):
    core = core_ref[0]
    copies = []
    for side, ref in enumerate((mine_ref, other_ref)):
        at = core if side == 0 else 1 - core
        for i in range(16):
            rows = pl.multiple_of((i // 2) * 2 * depth + at * depth, depth)
            target = out_ref.at[:, pl.ds(rows, depth), pl.ds((i % 2) * width, width)]
            copies.append(pltpu.make_async_copy(ref.at[i], target, sems.at[side, i]))
    for copy in copies:
        copy.start()
    for copy in copies:
        copy.wait()


def assemble(core, mine, other):
    _, kinds, depth, width = mine.shape
    anywhere = pl.BlockSpec(memory_space=pl.ANY)
    return pl.pallas_call(
        functools.partial(assemble_kernel, depth=depth, width=width),
        in_specs=[pl.BlockSpec(memory_space=pltpu.SMEM), anywhere, anywhere],
        out_specs=anywhere,
        out_shape=jax.ShapeDtypeStruct((kinds, 16 * depth, 2 * width), BF16),
        scratch_shapes=[pltpu.SemaphoreType.DMA((2, 16))],
        cost_estimate=pl.CostEstimate(
            flops=0, bytes_accessed=kinds * 128 * depth * width, transcendentals=0
        ),
    )(core, mine, other)


def grads_home(split):
    total = (split[0].astype(F32) + swap_core(split[1]).astype(F32)).astype(BF16)
    arrived = lax.all_to_all(total, FLAT, 0, 0, tiled=True)
    return jnp.sum(arrived.astype(F32), axis=0)


def weight_grad_kernel(core_ref, *refs, parts, switch):
    lefts, others, rights = refs[:parts], refs[parts : 2 * parts], refs[2 * parts : 3 * parts]
    out_ref = refs[3 * parts]
    core = core_ref[0]
    kind = pl.program_id(0)

    def work(sides):
        total = None
        for side, right in zip(sides, rights):
            part = mm(side[...], right[0], TN)
            total = part if total is None else total + part
        total = total.astype(BF16)
        depth = total.shape[0] // 16
        for p in range(8):
            for c in range(2):
                at = (2 * p + c) * depth
                out_ref[jnp.bitwise_xor(core, c), p, 0, 0] = total[at : at + depth]

    @pl.when(kind < switch)
    def _():
        work(lefts)

    @pl.when(kind >= switch)
    def _():
        work(others)


def weight_grads(core, lefts, others, rights, switch):
    parts = len(lefts)
    kinds, _, width = rights[0].shape
    half = width // 2
    sides = [pl.BlockSpec((v.shape[0], D), lambda k, z: (0, 0)) for v in list(lefts) + list(others)]
    moving = [pl.BlockSpec((1, v.shape[1], half), lambda k, z: (k, 0, z)) for v in rights]
    rows = sum(v.shape[1] for v in rights)
    out = pl.pallas_call(
        functools.partial(weight_grad_kernel, parts=parts, switch=switch),
        grid=(kinds, 2),
        in_specs=[pl.BlockSpec(memory_space=pltpu.SMEM)] + sides + moving,
        out_specs=pl.BlockSpec((2, 8, 1, 1, 64, half), lambda k, z: (0, 0, z, k, 0, 0)),
        out_shape=jax.ShapeDtypeStruct((2, 8, 2, kinds, 64, half), BF16),
        compiler_params=pltpu.CompilerParams(vmem_limit_bytes=48 * 2**20),
        cost_estimate=pl.CostEstimate(
            flops=2 * kinds * rows * D * width,
            bytes_accessed=2 * kinds * D * width + 4 * rows * D + 2 * kinds * rows * width,
            transcendentals=0,
        ),
    )(core, *lefts, *others, *rights)
    return out.reshape(2, 16, kinds, 64, half)


def lanes_of(shape):
    return lax.broadcasted_iota(jnp.int32, shape, 1)


def head_sums(values):
    wide = values.shape[1]
    row = lax.broadcasted_iota(jnp.int32, (wide, wide), 0) // HEAD_DIM
    same = (row == lanes_of((wide, wide)) // HEAD_DIM).astype(BF16)
    high = values.astype(BF16)
    low = (values - high.astype(F32)).astype(BF16)
    return mm(high, same) + mm(low, same)


def partner(values):
    wide = values.shape[1]
    first = lanes_of(values.shape) % HEAD_DIM < HALF
    return jnp.where(first, pltpu.roll(values, wide - HALF, 1), pltpu.roll(values, HALF, 1))


def angles_of(facts, freq_ref):
    facts = facts.astype(F32)
    times = facts[:, 2:3] * 32.0 + facts[:, 3:4]
    angle = times * freq_ref[0:1, :WIDE]
    first = lanes_of(angle.shape) % HEAD_DIM < HALF
    cosine = jnp.cos(angle)
    sine = jnp.sin(angle)
    sine = jnp.where(first, -sine, sine)
    return jnp.concatenate([cosine, cosine], 1), jnp.concatenate([sine, sine], 1)


def project_kernel(core_ref, a_ref, w_ref, freq_ref, mine_ref, send_ref, raw_ref):
    low = core_ref[0] == 0
    rows = a_ref[:, :D]
    cosine, sine = angles_of(a_ref[:, D:], freq_ref)

    def emit(kind, value):
        left, right = value[:, :WIDE], value[:, WIDE:]
        mine_ref[kind] = jnp.where(low, left, right).astype(BF16)
        send_ref[kind] = jnp.where(low, right, left).astype(BF16)

    for kind in range(2):
        raw = mm(rows, w_ref[kind])
        raw_ref[kind] = raw
        unit = raw * lax.rsqrt(head_sums(raw * raw) * (1.0 / HEAD_DIM) + EPS)
        value = unit * freq_ref[1 + kind : 2 + kind, :]
        value = value * cosine + partner(value) * sine
        if kind == 0:
            value = value * (HEAD_DIM ** (-0.5) * LOG2E)
        emit(kind, value)
    emit(2, mm(rows, w_ref[2]))


def project(core, rows_all, attn_w, freq):
    block = 512
    both = pl.BlockSpec((3, block, WIDE), lambda i: (0, i, 0))
    low = jax.ShapeDtypeStruct((3, PLANE, WIDE), BF16)
    return pl.pallas_call(
        project_kernel,
        grid=(PLANE // block,),
        in_specs=[
            pl.BlockSpec(memory_space=pltpu.SMEM),
            pl.BlockSpec((block, D + WIDE), lambda i: (i, 0)),
            pl.BlockSpec((3, D, 2 * WIDE), lambda i: (0, 0, 0)),
            pl.BlockSpec((8, 2 * WIDE), lambda i: (0, 0)),
        ],
        out_specs=[both, both, pl.BlockSpec((2, block, 2 * WIDE), lambda i: (0, i, 0))],
        out_shape=[low, low, jax.ShapeDtypeStruct((2, PLANE, 2 * WIDE), F32)],
        compiler_params=pltpu.CompilerParams(vmem_limit_bytes=48 * 2**20),
        cost_estimate=pl.CostEstimate(
            flops=8 * PLANE * D * 2 * WIDE, bytes_accessed=PLANE * D * 8, transcendentals=PLANE * 1024
        ),
    )(core, rows_all, attn_w, freq)


def unproject_kernel(
    core_ref, mine_ref, got_ref, raw_ref, facts_ref, w_ref, freq_ref, dp_ref, part_ref, gain_ref
):
    low = core_ref[0] == 0
    cosine, sine = angles_of(facts_ref[...], freq_ref)

    @pl.when(pl.program_id(0) == 0)
    def _():
        gain_ref[...] = jnp.zeros_like(gain_ref)

    total = None
    for kind in range(3):
        mine, got = mine_ref[kind], got_ref[kind]
        grad = jnp.concatenate([jnp.where(low, mine, got), jnp.where(low, got, mine)], 1)
        if kind < 2:
            grad = grad.astype(F32)
            if kind == 0:
                grad = grad * (HEAD_DIM ** (-0.5))
            raw = raw_ref[kind]
            inv = lax.rsqrt(head_sums(raw * raw) * (1.0 / HEAD_DIM) + EPS)
            unit = raw * inv
            grad = grad * cosine - partner(grad) * sine
            gain_ref[kind : kind + 1, :] += jnp.sum(grad * unit, axis=0, keepdims=True)
            scaled = grad * freq_ref[1 + kind : 2 + kind, :]
            mean = head_sums(scaled * unit) * (1.0 / HEAD_DIM)
            grad = (inv * (scaled - unit * mean)).astype(BF16)
        dp_ref[kind] = grad
        part = mm(grad, w_ref[kind], NT)
        total = part if total is None else total + part
    part_ref[...] = total.astype(BF16)


def unproject(core, mine, got, raw, rows_all, attn_w, freq):
    block = 512
    both = pl.BlockSpec((3, block, WIDE), lambda i: (0, i, 0))
    return pl.pallas_call(
        unproject_kernel,
        grid=(PLANE // block,),
        in_specs=[
            pl.BlockSpec(memory_space=pltpu.SMEM),
            both,
            both,
            pl.BlockSpec((2, block, 2 * WIDE), lambda i: (0, i, 0)),
            pl.BlockSpec((block, WIDE), lambda i: (i, D // WIDE)),
            pl.BlockSpec((3, D, 2 * WIDE), lambda i: (0, 0, 0)),
            pl.BlockSpec((8, 2 * WIDE), lambda i: (0, 0)),
        ],
        out_specs=[
            pl.BlockSpec((3, block, 2 * WIDE), lambda i: (0, i, 0)),
            pl.BlockSpec((block, D), lambda i: (i, 0)),
            pl.BlockSpec((8, 2 * WIDE), lambda i: (0, 0)),
        ],
        out_shape=[
            jax.ShapeDtypeStruct((3, PLANE, 2 * WIDE), BF16),
            jax.ShapeDtypeStruct((PLANE, D), BF16),
            jax.ShapeDtypeStruct((8, 2 * WIDE), F32),
        ],
        compiler_params=pltpu.CompilerParams(vmem_limit_bytes=48 * 2**20),
        cost_estimate=pl.CostEstimate(
            flops=8 * PLANE * D * 2 * WIDE, bytes_accessed=PLANE * D * 8, transcendentals=PLANE * 1024
        ),
    )(core, mine, got, raw, rows_all, attn_w, freq)


LOG_LANE = 3 * VARIATES + SEQS


def with_pieces(base, values, first_lane, lanes):
    for i in range(3):
        part = values.astype(BF16).astype(F32)
        base = jnp.where(lanes == first_lane + i, part, base)
        values = values - part
    return base


def attend_kernel(qkv_ref, all_ref, qt_ref, kt_ref, vt_ref, att_ref, low_ref, tail_ref, *, chunks):
    size = all_ref.shape[1] // chunks
    query = jnp.concatenate([qkv_ref[0], qt_ref[...]], 1)
    zero = jnp.zeros_like(query)
    head_of = (lanes_of(query.shape) // HEAD_DIM) % 2
    lanes = lanes_of((query.shape[0], WIDE))
    out = None
    tail = qt_ref[...].astype(F32)
    for head in range(2):
        masked = jnp.where(head_of == head, query, zero)
        total = None
        for c in range(chunks):
            rows = pl.ds(c * size, size)
            keys = jnp.concatenate([all_ref[1, rows, :], kt_ref[rows, :]], 1)
            values = jnp.concatenate([all_ref[2, rows, :], vt_ref[rows, :]], 1)
            prob = jnp.exp2(mm(masked, keys, NT)).astype(BF16)
            part = mm(prob, values)
            total = part if total is None else total + part
        row_sum = total[:, WIDE : WIDE + 1]
        here = total[:, :WIDE] / row_sum
        out = here if head == 0 else jnp.where(lanes < HEAD_DIM, out, here)
        tail = with_pieces(tail, -jnp.log2(row_sum), head * HEAD_DIM + LOG_LANE, lanes)
    att_ref[...] = out
    low_ref[...] = out.astype(BF16)
    tail_ref[...] = tail.astype(BF16)


def attend(qkv, query_tail, key_tail, value_tail):
    block = 512
    rows = qkv.shape[1]
    moving = pl.BlockSpec((block, WIDE), lambda i: (i, 0))
    fixed = pl.BlockSpec((rows, WIDE), lambda i: (0, 0))
    low = jax.ShapeDtypeStruct((rows, WIDE), BF16)
    return pl.pallas_call(
        functools.partial(attend_kernel, chunks=4),
        grid=(rows // block,),
        in_specs=[
            pl.BlockSpec((1, block, WIDE), lambda i: (0, i, 0)),
            pl.BlockSpec((3, rows, WIDE), lambda i: (0, 0, 0)),
            moving,
            fixed,
            fixed,
        ],
        out_specs=[moving, moving, moving],
        out_shape=[jax.ShapeDtypeStruct((rows, WIDE), F32), low, low],
        compiler_params=pltpu.CompilerParams(vmem_limit_bytes=48 * 2**20),
        cost_estimate=pl.CostEstimate(
            flops=16 * rows * rows * WIDE, bytes_accessed=rows * WIDE * 24, transcendentals=2 * rows * rows
        ),
    )(qkv, qkv, query_tail, key_tail, value_tail)


def attend_back_kernel(
    qkv_ref, all_ref, qt_ref, kt_ref, vt_ref, hot_ref, grad_ref, att_ref,
    dq_ref, dk_ref, dv_ref, bias_ref, dk_sum, dv_sum, *, chunks
):
    size = all_ref.shape[1] // chunks
    step = pl.program_id(0)
    query = jnp.concatenate([qkv_ref[0], qt_ref[...]], 1)
    grad = grad_ref[...]
    zero = jnp.zeros_like(query)
    head_of = (lanes_of(query.shape) // HEAD_DIM) % 2
    lanes = lanes_of((query.shape[0], WIDE))
    overlap = grad.astype(F32) * att_ref[...]

    @pl.when(step == 0)
    def _():
        dk_sum[...] = jnp.zeros_like(dk_sum)
        dv_sum[...] = jnp.zeros_like(dv_sum)

    out = None
    for head in range(2):
        mine = head_of[:, :WIDE] == head
        masked = jnp.where(head_of == head, query, zero)
        grad_here = jnp.where(mine, grad, zero[:, :WIDE])
        dots = jnp.sum(jnp.where(mine, overlap, 0.0), axis=1, keepdims=True)
        extra = with_pieces(jnp.zeros(lanes.shape, F32), -dots, 0, lanes).astype(BF16)
        grad_wide = jnp.concatenate([grad_here, extra], 1)
        total = None
        for c in range(chunks):
            rows = pl.ds(c * size, size)
            keys = all_ref[1, rows, :]
            prob = jnp.exp2(mm(jnp.concatenate([keys, kt_ref[rows, :]], 1), masked, NT))
            slope = mm(jnp.concatenate([all_ref[2, rows, :], vt_ref[rows, :]], 1), grad_wide, NT)
            d_score = (prob * slope).astype(BF16)
            dv_sum[rows, :] += mm(prob.astype(BF16), grad_here)
            dk_sum[rows, :] += mm(d_score, masked)
            part = mm(d_score, keys, TN)
            total = part if total is None else total + part
        out = total if head == 0 else jnp.where(lanes < HEAD_DIM, out, total)
    dq_ref[...] = out.astype(BF16)

    @pl.when(step == pl.num_programs(0) - 1)
    def _():
        dk_ref[...] = (dk_sum[:, :WIDE] * (1.0 / LOG2E)).astype(BF16)
        dv_ref[...] = dv_sum[...].astype(BF16)
        counts = dk_sum[:, WIDE:]
        bias_ref[...] = jnp.zeros_like(bias_ref)
        bias_ref[0:1, :] = jnp.sum(counts * hot_ref[...].astype(F32), axis=0, keepdims=True)
        bias_ref[1:2, :] = jnp.sum(counts, axis=0, keepdims=True)


def attend_back(qkv, query_tail, key_tail, value_tail, query_hot, grad, attended):
    block = 512
    rows = qkv.shape[1]
    moving = pl.BlockSpec((block, WIDE), lambda i: (i, 0))
    fixed = pl.BlockSpec((rows, WIDE), lambda i: (0, 0))
    low = jax.ShapeDtypeStruct((rows, WIDE), BF16)
    return pl.pallas_call(
        functools.partial(attend_back_kernel, chunks=4),
        grid=(rows // block,),
        in_specs=[
            pl.BlockSpec((1, block, WIDE), lambda i: (0, i, 0)),
            pl.BlockSpec((3, rows, WIDE), lambda i: (0, 0, 0)),
            moving,
            fixed,
            fixed,
            fixed,
            moving,
            moving,
        ],
        out_specs=[moving, fixed, fixed, pl.BlockSpec((8, WIDE), lambda i: (0, 0))],
        out_shape=[low, low, low, jax.ShapeDtypeStruct((8, WIDE), F32)],
        scratch_shapes=[pltpu.VMEM((rows, 2 * WIDE), F32), pltpu.VMEM((rows, WIDE), F32)],
        compiler_params=pltpu.CompilerParams(vmem_limit_bytes=48 * 2**20),
        cost_estimate=pl.CostEstimate(
            flops=40 * rows * rows * WIDE, bytes_accessed=rows * WIDE * 24, transcendentals=2 * rows * rows
        ),
    )(qkv, qkv, query_tail, key_tail, value_tail, query_hot, grad, attended)


def feed_kernel(b_ref, g_ref, w_ref, y_ref, db_ref, act_ref, y_sum, db_sum):
    step = pl.program_id(0)
    rows = b_ref[...]
    gate_w, up_w, down_w = w_ref[0], w_ref[1], w_ref[2]
    gate = mm(rows, gate_w)
    up = mm(rows, up_w)
    d_hidden = mm(g_ref[...], down_w)
    sig = 1.0 / (1.0 + jnp.exp(-gate))
    silu = gate * sig
    hidden = (silu * up).astype(BF16)
    d_gate = (d_hidden * up * (sig * (1.0 + gate * (1.0 - sig)))).astype(BF16)
    d_up = (d_hidden * silu).astype(BF16)
    act_ref[0] = d_gate
    act_ref[1] = d_up
    act_ref[2] = hidden
    y_part = mm(hidden, down_w, NT)
    db_part = mm(d_gate, gate_w, NT) + mm(d_up, up_w, NT)

    @pl.when(step == 0)
    def _():
        y_sum[...] = y_part
        db_sum[...] = db_part

    @pl.when(step > 0)
    def _():
        y_sum[...] += y_part
        db_sum[...] += db_part

    @pl.when(step == pl.num_programs(0) - 1)
    def _():
        y_ref[...] = y_sum[...].astype(BF16)
        db_ref[...] = db_sum[...].astype(BF16)


def feed(rows_b, rows_g, weights):
    rows = rows_b.shape[0]
    width = weights.shape[2]
    block = 256
    whole = pl.BlockSpec((rows, D), lambda f: (0, 0))
    part = pl.BlockSpec((3, rows, block), lambda f: (0, 0, f))
    low_d = jax.ShapeDtypeStruct((rows, D), BF16)
    low_f = jax.ShapeDtypeStruct((3, rows, width), BF16)
    return pl.pallas_call(
        feed_kernel,
        grid=(width // block,),
        in_specs=[whole, whole, pl.BlockSpec((3, D, block), lambda f: (0, 0, f))],
        out_specs=[whole, whole, part],
        out_shape=[low_d, low_d, low_f],
        scratch_shapes=[pltpu.VMEM((rows, D), F32)] * 2,
        compiler_params=pltpu.CompilerParams(vmem_limit_bytes=48 * 2**20),
        cost_estimate=pl.CostEstimate(
            flops=12 * rows * D * width, bytes_accessed=6 * D * width + rows * D * 8 + rows * width * 6,
            transcendentals=rows * width,
        ),
    )(rows_b, rows_g, weights)


def body(
    tokens,
    cotangent,
    destination,
    variate_ids,
    time_ids,
    seq_lengths,
    qkv_weight,
    out_weight,
    gate_up_weight,
    down_weight,
    norm_gains,
    qk_gains,
    variate_bias,
):
    core = lax.axis_index("core")
    low_core = core == 0
    y_at = lax.axis_index("y")
    zl_at = lax.axis_index("zl")

    core_scalar = core.reshape(1).astype(jnp.int32)

    def side_by_side(mine, other):
        return jnp.concatenate(
            [jnp.where(low_core, mine, other), jnp.where(low_core, other, mine)], axis=-1
        )

    slot = destination % ROWS
    group_at = destination // GROUP
    block_at = (destination % GROUP) // ROWS
    device_at = ((group_at // 2) * 2 + block_at // 4) * 8 + (block_at % 4) * 2 + group_at % 2
    key = device_at * ROWS + slot
    rank = jnp.sum((key[None, :] < key[:, None]).astype(jnp.int32), axis=1)
    deal = (jnp.arange(ROWS)[:, None] == rank[None, :]).astype(BF16)
    facts = jnp.stack([slot, variate_ids, time_ids // 32, time_ids % 32], axis=1).astype(BF16)
    facts = jnp.concatenate([facts, jnp.zeros((ROWS, WIDE - 4), BF16)], axis=1)
    gains_row = jnp.broadcast_to(norm_gains.reshape(1, WIDE), (ROWS, WIDE))
    outgoing = jnp.concatenate([tokens, cotangent, facts, gains_row], axis=1)
    span = outgoing.shape[1]
    outgoing = mm(deal, outgoing).astype(BF16).reshape(DEVICES, 2, span)
    arrived = lax.all_to_all(outgoing, ALL, 0, 0, tiled=True)

    attn_shard = jnp.concatenate([qkv_weight, out_weight.T[None]], 0)
    feed_shard = jnp.concatenate([gate_up_weight, down_weight.T[None]], 0)
    attn_shard, arrived = lax.optimization_barrier((attn_shard, arrived))
    attn_mine, attn_other = flat_gather(attn_shard)
    attn_w = assemble(core_scalar, attn_mine, attn_other)
    feed_shard, attn_other = lax.optimization_barrier((feed_shard, attn_other))
    feed_mine, feed_other = flat_gather(feed_shard)
    feed_w = assemble(core_scalar, feed_mine, feed_other)

    lengths_other = swap_core(seq_lengths)
    lengths = jnp.where(zl_at == core, seq_lengths, lengths_other)[0]
    bias_other = lax.ppermute(variate_bias, "zl", [(0, 1), (1, 0)])
    bias_pair = jnp.where(zl_at == core, variate_bias, bias_other)

    all_gains = arrived[:, 0, span - WIDE :].reshape(16, 8, 2, 64)[:, 0]
    all_gains = all_gains.transpose(1, 0, 2).reshape(2, D).astype(F32)
    gain_one, gain_two = all_gains[0], all_gains[1]
    slots = arrived[:, :, 2 * D].reshape(2 * DEVICES)
    place = (jnp.arange(ROWS).astype(BF16)[:, None] == slots[None, :]).astype(BF16)
    placed = mm(place, arrived.reshape(2 * DEVICES, span))
    inputs = placed[:, :D]
    grad_rows = placed[:, D : 2 * D].astype(BF16)
    facts_here = placed[:, 2 * D : 2 * D + WIDE].astype(BF16)

    scale_one = root_stats(inputs)
    normed_one = inputs * scale_one
    attn_in = (normed_one * gain_one).astype(BF16)
    attn_all = gather_ring(jnp.concatenate([attn_in, facts_here], axis=1))
    attn_all = jnp.concatenate(attn_all, 0)
    grad_all = gather_ring(grad_rows)

    variates_own = attn_all[:, D + 1].astype(jnp.int32)
    variates = jnp.concatenate([variates_own, swap_core(variates_own)])
    blocks_y = (y_at + jnp.arange(RING)) % RING
    blocks = jnp.concatenate([core * RING + blocks_y, (1 - core) * RING + blocks_y])
    positions = (blocks[:, None] * ROWS + jnp.arange(ROWS)[None, :]).reshape(GROUP)
    segments = jnp.sum((positions[:, None] >= jnp.cumsum(lengths)[None, :]).astype(jnp.int32), 1)

    inverse = THETA ** (-2.0 * jnp.arange(HALF).astype(F32) / HEAD_DIM)
    freq = jnp.concatenate(
        [
            jnp.tile(inverse, 8)[None],
            jnp.tile(qk_gains, (1, 4)),
            jnp.zeros((5, 2 * WIDE), F32),
        ]
    )
    qkv_mine, qkv_send, raw = project(core_scalar, attn_all, attn_w, freq)
    qkv = jnp.concatenate([qkv_mine, swap_core(qkv_send)], axis=1)

    lane = jnp.arange(WIDE)[None, :]
    tail_lane = lane % HEAD_DIM
    bias_lane = tail_lane < 3 * VARIATES
    seg_lane = (tail_lane >= 3 * VARIATES) & (tail_lane < LOG_LANE)
    one_lane = (tail_lane >= LOG_LANE) & (tail_lane < LOG_LANE + 3)
    equal = bias_lane & (tail_lane % VARIATES == variates[:, None])
    inside = seg_lane & (tail_lane - 3 * VARIATES == segments[:, None])
    query_tail = (equal | inside).astype(BF16)
    bias_parts = jnp.stack(pieces(bias_pair * LOG2E, 3)).astype(F32)
    bias_rows = jnp.repeat(bias_parts, VARIATES, axis=0).transpose(1, 2, 0)
    bias_rows = jnp.pad(bias_rows, ((0, 0), (0, 0), (0, HEAD_DIM - 3 * VARIATES))).reshape(2, WIDE)
    key_tail = jnp.where(equal, bias_rows[0:1], bias_rows[1:2])
    key_tail = jnp.where(seg_lane, jnp.where(inside, 0.0, FAR), key_tail)
    key_tail = jnp.where(one_lane, 1.0, key_tail).astype(BF16)
    value_tail = jnp.broadcast_to((lane < 3).astype(BF16), (GROUP, WIDE))
    attended, att_low, query_back = attend(qkv, query_tail, key_tail, value_tail)
    att_plane = side_by_side(att_low[:PLANE], swap_core(att_low[PLANE:]))
    out_part = mm(att_plane, attn_w[3], NT).astype(BF16).reshape(RING, ROWS, D)
    hidden_one = inputs + reduce_ring([out_part[r] for r in range(RING)])

    scale_two = root_stats(hidden_one)
    normed_two = hidden_one * scale_two
    feed_in = (normed_two * gain_two).astype(BF16)
    feed_all = gather_ring(feed_in)
    fed = [feed(feed_all[r], grad_all[r], feed_w) for r in range(RING)]
    grad_normed_two = reduce_ring([f[1] for f in fed])
    mixed = (hidden_one + reduce_ring([f[0] for f in fed])).astype(BF16)

    feed_grad = grads_home(
        weight_grads(core_scalar, feed_all, grad_all, [f[2] for f in fed], 2)
    )

    gain_two_grad = jnp.sum(grad_normed_two * normed_two, axis=0)
    grad_one = grad_rows.astype(F32) + norm_back(grad_normed_two * gain_two, normed_two, scale_two)

    grad_one_all = jnp.concatenate(gather_ring(grad_one.astype(BF16)), 0)
    grad_att = mm(grad_one_all, attn_w[3]).astype(BF16)
    grad_left, grad_right = grad_att[:, :WIDE], grad_att[:, WIDE:]
    grad_send = jnp.where(low_core, grad_right, grad_left)
    grad_mine = jnp.where(low_core, grad_left, grad_right)
    grad_mine = jnp.concatenate([grad_mine, swap_core(grad_send)], 0)
    d_query, d_key, d_value, bias_sums = attend_back(
        qkv, query_back, key_tail, value_tail, query_tail, grad_mine, attended
    )
    first_part = (jnp.arange(HEAD_DIM) < VARIATES)[None, None]
    bias_sums = jnp.where(first_part, bias_sums[:2].reshape(2, 2, HEAD_DIM), 0.0)
    bias_sums = jnp.sum(bias_sums, axis=2)
    bias_part = jnp.stack([bias_sums[0], bias_sums[1] - bias_sums[0]])
    back_mixed = mm(place, mixed, TN).astype(BF16).reshape(DEVICES, 2, D)
    home_mixed = lax.all_to_all(back_mixed, ALL, 0, 0, tiled=True)
    d_mine = jnp.stack([d_query[:PLANE], d_key[:PLANE], d_value[:PLANE]])
    d_got = swap_core(jnp.stack([d_query[PLANE:], d_key[PLANE:], d_value[PLANE:]]))
    d_got, home_mixed = lax.optimization_barrier((d_got, home_mixed))
    grad_proj, in_part, qk_sums = unproject(
        core_scalar, d_mine, d_got, raw, attn_all, attn_w, freq
    )
    in_part = in_part.reshape(RING, ROWS, D)
    grad_normed_one = reduce_ring([in_part[r] for r in range(RING)])
    attn_grad = grads_home(
        weight_grads(
            core_scalar,
            [attn_all],
            [grad_one_all],
            [jnp.concatenate([grad_proj, att_plane[None]], 0)],
            3,
        )
    )
    qk_sums = jnp.sum(qk_sums[:2].reshape(2, 4, HEAD_DIM), axis=1)

    gain_one_grad = jnp.sum(grad_normed_one * normed_one, axis=0)
    input_grad = grad_one + norm_back(grad_normed_one * gain_one, normed_one, scale_one)

    new_tokens = mm(deal, home_mixed.reshape(ROWS, D), TN).astype(BF16)

    gain_sums = jnp.stack([gain_one_grad, gain_two_grad]).reshape(2, 16, 64).transpose(1, 0, 2)
    gain_sums = jnp.broadcast_to(gain_sums.reshape(16, 1, WIDE), (16, 8, WIDE))
    qk_row = qk_sums.reshape(WIDE)
    qk_row = jnp.broadcast_to(qk_row[None, None], (16, 8, WIDE))
    here = (jnp.arange(8) == y_at * 2 + core)[None, :, None]
    bias_row = jnp.where(here, bias_part.reshape(1, 1, 4), 0.0)
    bias_row = jnp.broadcast_to(bias_row, (16, 8, 4))
    smalls = jnp.concatenate([gain_sums, qk_row, bias_row, jnp.zeros((16, 8, WIDE - 4), F32)], axis=2)
    smalls = jnp.stack(pieces(smalls.reshape(DEVICES, 3 * WIDE), 2), axis=1)
    back_grads = mm(place, input_grad.astype(BF16), TN).astype(BF16).reshape(DEVICES, 2, D)
    home = lax.all_to_all(jnp.concatenate([back_grads, smalls], axis=2), ALL, 0, 0, tiled=True)
    token_grads = mm(deal, home[:, :, :D].reshape(ROWS, D), TN).astype(BF16)
    sums = jnp.sum(home[:, :, D:].astype(F32), axis=(0, 1))
    gains_grad = sums[:WIDE].reshape(2, 64)
    qk_grad = sums[WIDE : 2 * WIDE].reshape(2, 64)
    bias_grad = sums[2 * WIDE : 2 * WIDE + 4].reshape(2, 2)

    return (
        new_tokens,
        token_grads,
        attn_grad[:3],
        attn_grad[3].T,
        feed_grad[:2],
        feed_grad[2].T,
        gains_grad,
        qk_grad,
        bias_grad,
    )


def solution(mesh):
    fine = Mesh(mesh.devices.reshape(4, 2, 2, 4, 2), ALL)
    dp = ("x", "zh", "core")
    tensor = ("y", "zl")
    in_specs = (
        P(ALL, None),
        P(ALL, None),
        P(ALL),
        P(ALL),
        P(ALL),
        P(dp, None),
        P(None, dp, tensor),
        P(tensor, dp),
        P(None, dp, tensor),
        P(tensor, dp),
        P(None, dp),
        P(),
        P(None, tensor),
    )
    out_specs = (
        P(ALL, None),
        P(ALL, None),
        P(None, dp, tensor),
        P(tensor, dp),
        P(None, dp, tensor),
        P(tensor, dp),
        P(None, dp),
        P(),
        P(None, tensor),
    )
    return jax.shard_map(body, mesh=fine, in_specs=in_specs, out_specs=out_specs, check_vma=False)
```

```python
import functools

import jax
import jax.numpy as jnp
from jax import lax
from jax.experimental import pallas as pl
from jax.experimental.pallas import tpu as pltpu
from jax.sharding import Mesh
from jax.sharding import PartitionSpec as P

HEADS = 16
HEAD_DIM = 64
HALF = HEAD_DIM // 2
D = 1024
FF = 4096
ROWS = 256
RING = 4
PLANE = ROWS * RING
GROUP = 2 * PLANE
DEVICES = 128
VARIATES = 8
SEQS = 4
WIDE = 128
EPS = 1e-06
THETA = 10000.0
LOG2E = 1.4426950408889634
FAR = -16384.0
F32 = jnp.float32
BF16 = jnp.bfloat16

ALL = ("x", "zh", "core", "y", "zl")
FLAT = ("x", "zh", "zl")
NT = (((1,), (1,)), ((), ()))
TN = (((0,), (0,)), ((), ()))


def mm(left, right, dims=(((1,), (0,)), ((), ()))):
    return lax.dot_general(left, right, dims, preferred_element_type=F32)


def root_stats(values):
    return lax.rsqrt(jnp.mean(values * values, axis=-1, keepdims=True) + EPS)


def norm_back(grad_in, normed, scale_inv):
    return scale_inv * (grad_in - normed * jnp.mean(grad_in * normed, axis=-1, keepdims=True))


def pieces(values, count):
    out = []
    for _ in range(count):
        part = lax.reduce_precision(values, 8, 7)
        out.append(part.astype(BF16))
        values = values - part
    return out


def ring(values, step):
    return lax.ppermute(values, "y", [(i, (i + step) % RING) for i in range(RING)])


def swap_core(values):
    return lax.ppermute(values, "core", [(0, 1), (1, 0)])


def gather_ring(values):
    ahead = ring(values, -1)
    behind = ring(values, 1)
    half = values.shape[0] // 2
    far_top = ring(ahead[:half], -1)
    far_low = ring(behind[half:], 1)
    return [values, ahead, jnp.concatenate([far_top, far_low], 0), behind]


def reduce_ring(parts):
    far = ring(parts[2], 2)
    near = ring(parts[1], 1)
    back = ring(parts[3], -1)
    return (
        parts[0].astype(F32) + near.astype(F32) + back.astype(F32) + far.astype(F32)
    )


def flat_gather(shard):
    many = jnp.broadcast_to(shard[None], (16,) + shard.shape)
    return lax.all_to_all(many, FLAT, 0, 0, tiled=True)


def assemble_kernel(core_ref, mine_ref, other_ref, out_ref):
    core = core_ref[0]
    _, _, depth, width = mine_ref.shape
    for ref, at in ((mine_ref, core), (other_ref, 1 - core)):
        rows = pl.ds(pl.multiple_of(at * depth, depth), depth)
        for z in range(2):
            out_ref[:, rows, z * width : (z + 1) * width] = ref[z]


def assemble(core, mine, other):
    _, kinds, depth, width = mine.shape
    pair = pl.BlockSpec((2, kinds, depth, width), lambda p: (p, 0, 0, 0))
    return pl.pallas_call(
        assemble_kernel,
        grid=(8,),
        in_specs=[pl.BlockSpec(memory_space=pltpu.SMEM), pair, pair],
        out_specs=pl.BlockSpec((kinds, 2 * depth, 2 * width), lambda p: (0, p, 0)),
        out_shape=jax.ShapeDtypeStruct((kinds, 16 * depth, 2 * width), BF16),
        cost_estimate=pl.CostEstimate(
            flops=0, bytes_accessed=kinds * 128 * depth * width, transcendentals=0
        ),
    )(core, mine, other)


def grads_home(split):
    total = (split[0].astype(F32) + swap_core(split[1]).astype(F32)).astype(BF16)
    arrived = lax.all_to_all(total, FLAT, 0, 0, tiled=True)
    return jnp.sum(arrived.astype(F32), axis=0)


def weight_grad_kernel(core_ref, *refs, parts, switch):
    lefts, others, rights = refs[:parts], refs[parts : 2 * parts], refs[2 * parts : 3 * parts]
    out_ref = refs[3 * parts]
    core = core_ref[0]
    kind = pl.program_id(0)

    def work(sides):
        total = None
        for side, right in zip(sides, rights):
            part = mm(side[...], right[0], TN)
            total = part if total is None else total + part
        total = total.astype(BF16)
        depth = total.shape[0] // 16
        for p in range(8):
            for c in range(2):
                at = (2 * p + c) * depth
                out_ref[jnp.bitwise_xor(core, c), p, 0, 0] = total[at : at + depth]

    @pl.when(kind < switch)
    def _():
        work(lefts)

    @pl.when(kind >= switch)
    def _():
        work(others)


def weight_grads(core, lefts, others, rights, switch):
    parts = len(lefts)
    kinds, _, width = rights[0].shape
    half = width // 2
    sides = [pl.BlockSpec((v.shape[0], D), lambda k, z: (0, 0)) for v in list(lefts) + list(others)]
    moving = [pl.BlockSpec((1, v.shape[1], half), lambda k, z: (k, 0, z)) for v in rights]
    rows = sum(v.shape[1] for v in rights)
    out = pl.pallas_call(
        functools.partial(weight_grad_kernel, parts=parts, switch=switch),
        grid=(kinds, 2),
        in_specs=[pl.BlockSpec(memory_space=pltpu.SMEM)] + sides + moving,
        out_specs=pl.BlockSpec((2, 8, 1, 1, 64, half), lambda k, z: (0, 0, z, k, 0, 0)),
        out_shape=jax.ShapeDtypeStruct((2, 8, 2, kinds, 64, half), BF16),
        compiler_params=pltpu.CompilerParams(vmem_limit_bytes=48 * 2**20),
        cost_estimate=pl.CostEstimate(
            flops=2 * kinds * rows * D * width,
            bytes_accessed=2 * kinds * D * width + 4 * rows * D + 2 * kinds * rows * width,
            transcendentals=0,
        ),
    )(core, *lefts, *others, *rights)
    return out.reshape(2, 16, kinds, 64, half)


def lanes_of(shape):
    return lax.broadcasted_iota(jnp.int32, shape, 1)


def head_sums(values):
    wide = values.shape[1]
    row = lax.broadcasted_iota(jnp.int32, (wide, wide), 0) // HEAD_DIM
    same = (row == lanes_of((wide, wide)) // HEAD_DIM).astype(BF16)
    high = values.astype(BF16)
    low = (values - high.astype(F32)).astype(BF16)
    return mm(high, same) + mm(low, same)


def partner(values):
    wide = values.shape[1]
    first = lanes_of(values.shape) % HEAD_DIM < HALF
    return jnp.where(first, pltpu.roll(values, wide - HALF, 1), pltpu.roll(values, HALF, 1))


def angles_of(facts, freq_ref):
    facts = facts.astype(F32)
    times = facts[:, 2:3] * 32.0 + facts[:, 3:4]
    angle = times * freq_ref[0:1, :WIDE]
    first = lanes_of(angle.shape) % HEAD_DIM < HALF
    cosine = jnp.cos(angle)
    sine = jnp.sin(angle)
    sine = jnp.where(first, -sine, sine)
    return jnp.concatenate([cosine, cosine], 1), jnp.concatenate([sine, sine], 1)


def project_kernel(core_ref, a_ref, w_ref, freq_ref, mine_ref, send_ref, raw_ref):
    low = core_ref[0] == 0
    rows = a_ref[:, :D]
    cosine, sine = angles_of(a_ref[:, D:], freq_ref)

    def emit(kind, value):
        left, right = value[:, :WIDE], value[:, WIDE:]
        mine_ref[kind] = jnp.where(low, left, right).astype(BF16)
        send_ref[kind] = jnp.where(low, right, left).astype(BF16)

    for kind in range(2):
        raw = mm(rows, w_ref[kind])
        raw_ref[kind] = raw
        unit = raw * lax.rsqrt(head_sums(raw * raw) * (1.0 / HEAD_DIM) + EPS)
        value = unit * freq_ref[1 + kind : 2 + kind, :]
        value = value * cosine + partner(value) * sine
        if kind == 0:
            value = value * (HEAD_DIM ** (-0.5) * LOG2E)
        emit(kind, value)
    emit(2, mm(rows, w_ref[2]))


def project(core, rows_all, attn_w, freq):
    block = 512
    both = pl.BlockSpec((3, block, WIDE), lambda i: (0, i, 0))
    low = jax.ShapeDtypeStruct((3, PLANE, WIDE), BF16)
    return pl.pallas_call(
        project_kernel,
        grid=(PLANE // block,),
        in_specs=[
            pl.BlockSpec(memory_space=pltpu.SMEM),
            pl.BlockSpec((block, D + WIDE), lambda i: (i, 0)),
            pl.BlockSpec((3, D, 2 * WIDE), lambda i: (0, 0, 0)),
            pl.BlockSpec((8, 2 * WIDE), lambda i: (0, 0)),
        ],
        out_specs=[both, both, pl.BlockSpec((2, block, 2 * WIDE), lambda i: (0, i, 0))],
        out_shape=[low, low, jax.ShapeDtypeStruct((2, PLANE, 2 * WIDE), F32)],
        compiler_params=pltpu.CompilerParams(vmem_limit_bytes=48 * 2**20),
        cost_estimate=pl.CostEstimate(
            flops=8 * PLANE * D * 2 * WIDE, bytes_accessed=PLANE * D * 8, transcendentals=PLANE * 1024
        ),
    )(core, rows_all, attn_w, freq)


def unproject_kernel(
    core_ref, mine_ref, got_ref, raw_ref, facts_ref, w_ref, freq_ref, dp_ref, part_ref, gain_ref
):
    low = core_ref[0] == 0
    cosine, sine = angles_of(facts_ref[...], freq_ref)

    @pl.when(pl.program_id(0) == 0)
    def _():
        gain_ref[...] = jnp.zeros_like(gain_ref)

    total = None
    for kind in range(3):
        mine, got = mine_ref[kind], got_ref[kind]
        grad = jnp.concatenate([jnp.where(low, mine, got), jnp.where(low, got, mine)], 1)
        if kind < 2:
            grad = grad.astype(F32)
            if kind == 0:
                grad = grad * (HEAD_DIM ** (-0.5))
            raw = raw_ref[kind]
            inv = lax.rsqrt(head_sums(raw * raw) * (1.0 / HEAD_DIM) + EPS)
            unit = raw * inv
            grad = grad * cosine - partner(grad) * sine
            gain_ref[kind : kind + 1, :] += jnp.sum(grad * unit, axis=0, keepdims=True)
            scaled = grad * freq_ref[1 + kind : 2 + kind, :]
            mean = head_sums(scaled * unit) * (1.0 / HEAD_DIM)
            grad = (inv * (scaled - unit * mean)).astype(BF16)
        dp_ref[kind] = grad
        part = mm(grad, w_ref[kind], NT)
        total = part if total is None else total + part
    part_ref[...] = total.astype(BF16)


def unproject(core, mine, got, raw, rows_all, attn_w, freq):
    block = 512
    both = pl.BlockSpec((3, block, WIDE), lambda i: (0, i, 0))
    return pl.pallas_call(
        unproject_kernel,
        grid=(PLANE // block,),
        in_specs=[
            pl.BlockSpec(memory_space=pltpu.SMEM),
            both,
            both,
            pl.BlockSpec((2, block, 2 * WIDE), lambda i: (0, i, 0)),
            pl.BlockSpec((block, WIDE), lambda i: (i, D // WIDE)),
            pl.BlockSpec((3, D, 2 * WIDE), lambda i: (0, 0, 0)),
            pl.BlockSpec((8, 2 * WIDE), lambda i: (0, 0)),
        ],
        out_specs=[
            pl.BlockSpec((3, block, 2 * WIDE), lambda i: (0, i, 0)),
            pl.BlockSpec((block, D), lambda i: (i, 0)),
            pl.BlockSpec((8, 2 * WIDE), lambda i: (0, 0)),
        ],
        out_shape=[
            jax.ShapeDtypeStruct((3, PLANE, 2 * WIDE), BF16),
            jax.ShapeDtypeStruct((PLANE, D), BF16),
            jax.ShapeDtypeStruct((8, 2 * WIDE), F32),
        ],
        compiler_params=pltpu.CompilerParams(vmem_limit_bytes=48 * 2**20),
        cost_estimate=pl.CostEstimate(
            flops=8 * PLANE * D * 2 * WIDE, bytes_accessed=PLANE * D * 8, transcendentals=PLANE * 1024
        ),
    )(core, mine, got, raw, rows_all, attn_w, freq)


LOG_LANE = 3 * VARIATES + SEQS


def with_pieces(base, values, first_lane, lanes):
    for i in range(3):
        part = values.astype(BF16).astype(F32)
        base = jnp.where(lanes == first_lane + i, part, base)
        values = values - part
    return base


def attend_kernel(qkv_ref, all_ref, qt_ref, kt_ref, vt_ref, att_ref, low_ref, tail_ref, *, chunks):
    size = all_ref.shape[1] // chunks
    query = jnp.concatenate([qkv_ref[0], qt_ref[...]], 1)
    zero = jnp.zeros_like(query)
    head_of = (lanes_of(query.shape) // HEAD_DIM) % 2
    lanes = lanes_of((query.shape[0], WIDE))
    out = None
    tail = qt_ref[...].astype(F32)
    for head in range(2):
        masked = jnp.where(head_of == head, query, zero)
        total = None
        for c in range(chunks):
            rows = pl.ds(c * size, size)
            keys = jnp.concatenate([all_ref[1, rows, :], kt_ref[rows, :]], 1)
            values = jnp.concatenate([all_ref[2, rows, :], vt_ref[rows, :]], 1)
            prob = jnp.exp2(mm(masked, keys, NT)).astype(BF16)
            part = mm(prob, values)
            total = part if total is None else total + part
        row_sum = total[:, WIDE : WIDE + 1]
        here = total[:, :WIDE] / row_sum
        out = here if head == 0 else jnp.where(lanes < HEAD_DIM, out, here)
        tail = with_pieces(tail, -jnp.log2(row_sum), head * HEAD_DIM + LOG_LANE, lanes)
    att_ref[...] = out
    low_ref[...] = out.astype(BF16)
    tail_ref[...] = tail.astype(BF16)


def attend(qkv, query_tail, key_tail, value_tail):
    block = 512
    rows = qkv.shape[1]
    moving = pl.BlockSpec((block, WIDE), lambda i: (i, 0))
    fixed = pl.BlockSpec((rows, WIDE), lambda i: (0, 0))
    low = jax.ShapeDtypeStruct((rows, WIDE), BF16)
    return pl.pallas_call(
        functools.partial(attend_kernel, chunks=4),
        grid=(rows // block,),
        in_specs=[
            pl.BlockSpec((1, block, WIDE), lambda i: (0, i, 0)),
            pl.BlockSpec((3, rows, WIDE), lambda i: (0, 0, 0)),
            moving,
            fixed,
            fixed,
        ],
        out_specs=[moving, moving, moving],
        out_shape=[jax.ShapeDtypeStruct((rows, WIDE), F32), low, low],
        compiler_params=pltpu.CompilerParams(vmem_limit_bytes=48 * 2**20),
        cost_estimate=pl.CostEstimate(
            flops=16 * rows * rows * WIDE, bytes_accessed=rows * WIDE * 24, transcendentals=2 * rows * rows
        ),
    )(qkv, qkv, query_tail, key_tail, value_tail)


def attend_back_kernel(
    qkv_ref, all_ref, qt_ref, kt_ref, vt_ref, hot_ref, grad_ref, att_ref,
    dq_ref, dk_ref, dv_ref, bias_ref, dk_sum, dv_sum, *, chunks
):
    size = all_ref.shape[1] // chunks
    step = pl.program_id(0)
    query = jnp.concatenate([qkv_ref[0], qt_ref[...]], 1)
    grad = grad_ref[...]
    zero = jnp.zeros_like(query)
    head_of = (lanes_of(query.shape) // HEAD_DIM) % 2
    lanes = lanes_of((query.shape[0], WIDE))
    overlap = grad.astype(F32) * att_ref[...]

    @pl.when(step == 0)
    def _():
        dk_sum[...] = jnp.zeros_like(dk_sum)
        dv_sum[...] = jnp.zeros_like(dv_sum)

    out = None
    for head in range(2):
        mine = head_of[:, :WIDE] == head
        masked = jnp.where(head_of == head, query, zero)
        grad_here = jnp.where(mine, grad, zero[:, :WIDE])
        dots = jnp.sum(jnp.where(mine, overlap, 0.0), axis=1, keepdims=True)
        extra = with_pieces(jnp.zeros(lanes.shape, F32), -dots, 0, lanes).astype(BF16)
        grad_wide = jnp.concatenate([grad_here, extra], 1)
        total = None
        for c in range(chunks):
            rows = pl.ds(c * size, size)
            keys = all_ref[1, rows, :]
            prob = jnp.exp2(mm(jnp.concatenate([keys, kt_ref[rows, :]], 1), masked, NT))
            slope = mm(jnp.concatenate([all_ref[2, rows, :], vt_ref[rows, :]], 1), grad_wide, NT)
            d_score = (prob * slope).astype(BF16)
            dv_sum[rows, :] += mm(prob.astype(BF16), grad_here)
            dk_sum[rows, :] += mm(d_score, masked)
            part = mm(d_score, keys, TN)
            total = part if total is None else total + part
        out = total if head == 0 else jnp.where(lanes < HEAD_DIM, out, total)
    dq_ref[...] = out.astype(BF16)

    @pl.when(step == pl.num_programs(0) - 1)
    def _():
        dk_ref[...] = (dk_sum[:, :WIDE] * (1.0 / LOG2E)).astype(BF16)
        dv_ref[...] = dv_sum[...].astype(BF16)
        counts = dk_sum[:, WIDE:]
        bias_ref[...] = jnp.zeros_like(bias_ref)
        bias_ref[0:1, :] = jnp.sum(counts * hot_ref[...].astype(F32), axis=0, keepdims=True)
        bias_ref[1:2, :] = jnp.sum(counts, axis=0, keepdims=True)


def attend_back(qkv, query_tail, key_tail, value_tail, query_hot, grad, attended):
    block = 512
    rows = qkv.shape[1]
    moving = pl.BlockSpec((block, WIDE), lambda i: (i, 0))
    fixed = pl.BlockSpec((rows, WIDE), lambda i: (0, 0))
    low = jax.ShapeDtypeStruct((rows, WIDE), BF16)
    return pl.pallas_call(
        functools.partial(attend_back_kernel, chunks=4),
        grid=(rows // block,),
        in_specs=[
            pl.BlockSpec((1, block, WIDE), lambda i: (0, i, 0)),
            pl.BlockSpec((3, rows, WIDE), lambda i: (0, 0, 0)),
            moving,
            fixed,
            fixed,
            fixed,
            moving,
            moving,
        ],
        out_specs=[moving, fixed, fixed, pl.BlockSpec((8, WIDE), lambda i: (0, 0))],
        out_shape=[low, low, low, jax.ShapeDtypeStruct((8, WIDE), F32)],
        scratch_shapes=[pltpu.VMEM((rows, 2 * WIDE), F32), pltpu.VMEM((rows, WIDE), F32)],
        compiler_params=pltpu.CompilerParams(vmem_limit_bytes=48 * 2**20),
        cost_estimate=pl.CostEstimate(
            flops=40 * rows * rows * WIDE, bytes_accessed=rows * WIDE * 24, transcendentals=2 * rows * rows
        ),
    )(qkv, qkv, query_tail, key_tail, value_tail, query_hot, grad, attended)


def feed_kernel(b_ref, g_ref, w_ref, y_ref, db_ref, act_ref, y_sum, db_sum):
    step = pl.program_id(0)
    rows = b_ref[...]
    gate_w, up_w, down_w = w_ref[0], w_ref[1], w_ref[2]
    gate = mm(rows, gate_w)
    up = mm(rows, up_w)
    d_hidden = mm(g_ref[...], down_w)
    sig = 1.0 / (1.0 + jnp.exp(-gate))
    silu = gate * sig
    hidden = (silu * up).astype(BF16)
    d_gate = (d_hidden * up * (sig * (1.0 + gate * (1.0 - sig)))).astype(BF16)
    d_up = (d_hidden * silu).astype(BF16)
    act_ref[0] = d_gate
    act_ref[1] = d_up
    act_ref[2] = hidden
    y_part = mm(hidden, down_w, NT)
    db_part = mm(d_gate, gate_w, NT) + mm(d_up, up_w, NT)

    @pl.when(step == 0)
    def _():
        y_sum[...] = y_part
        db_sum[...] = db_part

    @pl.when(step > 0)
    def _():
        y_sum[...] += y_part
        db_sum[...] += db_part

    @pl.when(step == pl.num_programs(0) - 1)
    def _():
        y_ref[...] = y_sum[...].astype(BF16)
        db_ref[...] = db_sum[...].astype(BF16)


def feed(rows_b, rows_g, weights):
    rows = rows_b.shape[0]
    width = weights.shape[2]
    block = 256
    whole = pl.BlockSpec((rows, D), lambda f: (0, 0))
    part = pl.BlockSpec((3, rows, block), lambda f: (0, 0, f))
    low_d = jax.ShapeDtypeStruct((rows, D), BF16)
    low_f = jax.ShapeDtypeStruct((3, rows, width), BF16)
    return pl.pallas_call(
        feed_kernel,
        grid=(width // block,),
        in_specs=[whole, whole, pl.BlockSpec((3, D, block), lambda f: (0, 0, f))],
        out_specs=[whole, whole, part],
        out_shape=[low_d, low_d, low_f],
        scratch_shapes=[pltpu.VMEM((rows, D), F32)] * 2,
        compiler_params=pltpu.CompilerParams(vmem_limit_bytes=48 * 2**20),
        cost_estimate=pl.CostEstimate(
            flops=12 * rows * D * width, bytes_accessed=6 * D * width + rows * D * 8 + rows * width * 6,
            transcendentals=rows * width,
        ),
    )(rows_b, rows_g, weights)


def body(
    tokens,
    cotangent,
    destination,
    variate_ids,
    time_ids,
    seq_lengths,
    qkv_weight,
    out_weight,
    gate_up_weight,
    down_weight,
    norm_gains,
    qk_gains,
    variate_bias,
):
    core = lax.axis_index("core")
    low_core = core == 0
    y_at = lax.axis_index("y")
    zl_at = lax.axis_index("zl")

    core_scalar = core.reshape(1).astype(jnp.int32)

    def side_by_side(mine, other):
        return jnp.concatenate(
            [jnp.where(low_core, mine, other), jnp.where(low_core, other, mine)], axis=-1
        )

    attn_shard = jnp.concatenate([qkv_weight, out_weight.T[None]], 0)
    feed_shard = jnp.concatenate([gate_up_weight, down_weight.T[None]], 0)
    attn_mine = flat_gather(attn_shard)

    slot = destination % ROWS
    group_at = destination // GROUP
    block_at = (destination % GROUP) // ROWS
    device_at = ((group_at // 2) * 2 + block_at // 4) * 8 + (block_at % 4) * 2 + group_at % 2
    key = device_at * ROWS + slot
    rank = jnp.sum((key[None, :] < key[:, None]).astype(jnp.int32), axis=1)
    deal = (jnp.arange(ROWS)[:, None] == rank[None, :]).astype(BF16)
    facts = jnp.stack([slot, variate_ids, time_ids // 32, time_ids % 32], axis=1).astype(BF16)
    facts = jnp.concatenate([facts, jnp.zeros((ROWS, WIDE - 4), BF16)], axis=1)
    gains_row = jnp.broadcast_to(norm_gains.reshape(1, WIDE), (ROWS, WIDE))
    outgoing = jnp.concatenate([tokens, cotangent, facts, gains_row], axis=1)
    span = outgoing.shape[1]
    outgoing = mm(deal, outgoing).astype(BF16).reshape(DEVICES, 2, span)
    outgoing, attn_mine = lax.optimization_barrier((outgoing, attn_mine))
    arrived = lax.all_to_all(outgoing, ALL, 0, 0, tiled=True)

    attn_w = assemble(core_scalar, attn_mine, swap_core(attn_mine))
    feed_shard, arrived = lax.optimization_barrier((feed_shard, arrived))
    feed_mine = flat_gather(feed_shard)
    feed_w = assemble(core_scalar, feed_mine, swap_core(feed_mine))

    lengths_other = swap_core(seq_lengths)
    lengths = jnp.where(zl_at == core, seq_lengths, lengths_other)[0]
    bias_other = lax.ppermute(variate_bias, "zl", [(0, 1), (1, 0)])
    bias_pair = jnp.where(zl_at == core, variate_bias, bias_other)

    all_gains = arrived[:, 0, span - WIDE :].reshape(16, 8, 2, 64)[:, 0]
    all_gains = all_gains.transpose(1, 0, 2).reshape(2, D).astype(F32)
    gain_one, gain_two = all_gains[0], all_gains[1]
    slots = arrived[:, :, 2 * D].reshape(2 * DEVICES)
    place = (jnp.arange(ROWS).astype(BF16)[:, None] == slots[None, :]).astype(BF16)
    placed = mm(place, arrived.reshape(2 * DEVICES, span))
    inputs = placed[:, :D]
    grad_rows = placed[:, D : 2 * D].astype(BF16)
    facts_here = placed[:, 2 * D : 2 * D + WIDE].astype(BF16)

    scale_one = root_stats(inputs)
    normed_one = inputs * scale_one
    attn_in = (normed_one * gain_one).astype(BF16)
    attn_all = gather_ring(jnp.concatenate([attn_in, facts_here], axis=1))
    attn_all = jnp.concatenate(attn_all, 0)
    grad_all = gather_ring(grad_rows)

    variates_own = attn_all[:, D + 1].astype(jnp.int32)
    variates = jnp.concatenate([variates_own, swap_core(variates_own)])
    blocks_y = (y_at + jnp.arange(RING)) % RING
    blocks = jnp.concatenate([core * RING + blocks_y, (1 - core) * RING + blocks_y])
    positions = (blocks[:, None] * ROWS + jnp.arange(ROWS)[None, :]).reshape(GROUP)
    segments = jnp.sum((positions[:, None] >= jnp.cumsum(lengths)[None, :]).astype(jnp.int32), 1)

    inverse = THETA ** (-2.0 * jnp.arange(HALF).astype(F32) / HEAD_DIM)
    freq = jnp.concatenate(
        [
            jnp.tile(inverse, 8)[None],
            jnp.tile(qk_gains, (1, 4)),
            jnp.zeros((5, 2 * WIDE), F32),
        ]
    )
    qkv_mine, qkv_send, raw = project(core_scalar, attn_all, attn_w, freq)
    qkv = jnp.concatenate([qkv_mine, swap_core(qkv_send)], axis=1)

    lane = jnp.arange(WIDE)[None, :]
    tail_lane = lane % HEAD_DIM
    bias_lane = tail_lane < 3 * VARIATES
    seg_lane = (tail_lane >= 3 * VARIATES) & (tail_lane < LOG_LANE)
    one_lane = (tail_lane >= LOG_LANE) & (tail_lane < LOG_LANE + 3)
    equal = bias_lane & (tail_lane % VARIATES == variates[:, None])
    inside = seg_lane & (tail_lane - 3 * VARIATES == segments[:, None])
    query_tail = (equal | inside).astype(BF16)
    bias_parts = jnp.stack(pieces(bias_pair * LOG2E, 3)).astype(F32)
    bias_rows = jnp.repeat(bias_parts, VARIATES, axis=0).transpose(1, 2, 0)
    bias_rows = jnp.pad(bias_rows, ((0, 0), (0, 0), (0, HEAD_DIM - 3 * VARIATES))).reshape(2, WIDE)
    key_tail = jnp.where(equal, bias_rows[0:1], bias_rows[1:2])
    key_tail = jnp.where(seg_lane, jnp.where(inside, 0.0, FAR), key_tail)
    key_tail = jnp.where(one_lane, 1.0, key_tail).astype(BF16)
    value_tail = jnp.broadcast_to((lane < 3).astype(BF16), (GROUP, WIDE))
    attended, att_low, query_back = attend(qkv, query_tail, key_tail, value_tail)
    att_low, grad_all = lax.optimization_barrier((att_low, grad_all))
    att_plane = side_by_side(att_low[:PLANE], swap_core(att_low[PLANE:]))
    out_part = mm(att_plane, attn_w[3], NT).astype(BF16).reshape(RING, ROWS, D)
    hidden_one = inputs + reduce_ring([out_part[r] for r in range(RING)])

    scale_two = root_stats(hidden_one)
    normed_two = hidden_one * scale_two
    feed_in = (normed_two * gain_two).astype(BF16)
    feed_all = gather_ring(feed_in)
    fed = [feed(feed_all[r], grad_all[r], feed_w) for r in range(RING)]
    grad_normed_two = reduce_ring([f[1] for f in fed])

    feed_grad = grads_home(
        weight_grads(core_scalar, feed_all, grad_all, [f[2] for f in fed], 2)
    )

    gain_two_grad = jnp.sum(grad_normed_two * normed_two, axis=0)
    grad_one = grad_rows.astype(F32) + norm_back(grad_normed_two * gain_two, normed_two, scale_two)

    grad_one_all = jnp.concatenate(gather_ring(grad_one.astype(BF16)), 0)
    y_parts, grad_one_all = lax.optimization_barrier(([f[0] for f in fed], grad_one_all))
    mixed = (hidden_one + reduce_ring(y_parts)).astype(BF16)
    grad_att = mm(grad_one_all, attn_w[3]).astype(BF16)
    grad_left, grad_right = grad_att[:, :WIDE], grad_att[:, WIDE:]
    grad_send = jnp.where(low_core, grad_right, grad_left)
    grad_mine = jnp.where(low_core, grad_left, grad_right)
    grad_mine = jnp.concatenate([grad_mine, swap_core(grad_send)], 0)
    d_query, d_key, d_value, bias_sums = attend_back(
        qkv, query_back, key_tail, value_tail, query_tail, grad_mine, attended
    )
    first_part = (jnp.arange(HEAD_DIM) < VARIATES)[None, None]
    bias_sums = jnp.where(first_part, bias_sums[:2].reshape(2, 2, HEAD_DIM), 0.0)
    bias_sums = jnp.sum(bias_sums, axis=2)
    bias_part = jnp.stack([bias_sums[0], bias_sums[1] - bias_sums[0]])
    mixed, feed_grad = lax.optimization_barrier((mixed, feed_grad))
    back_mixed = mm(place, mixed, TN).astype(BF16).reshape(DEVICES, 2, D)
    home_mixed = lax.all_to_all(back_mixed, ALL, 0, 0, tiled=True)
    d_mine = jnp.stack([d_query[:PLANE], d_key[:PLANE], d_value[:PLANE]])
    d_got = swap_core(jnp.stack([d_query[PLANE:], d_key[PLANE:], d_value[PLANE:]]))
    d_got, home_mixed = lax.optimization_barrier((d_got, home_mixed))
    grad_proj, in_part, qk_sums = unproject(
        core_scalar, d_mine, d_got, raw, attn_all, attn_w, freq
    )
    in_part = in_part.reshape(RING, ROWS, D)
    grad_normed_one = reduce_ring([in_part[r] for r in range(RING)])
    attn_grad = grads_home(
        weight_grads(
            core_scalar,
            [attn_all],
            [grad_one_all],
            [jnp.concatenate([grad_proj, att_plane[None]], 0)],
            3,
        )
    )
    qk_sums = jnp.sum(qk_sums[:2].reshape(2, 4, HEAD_DIM), axis=1)

    gain_one_grad = jnp.sum(grad_normed_one * normed_one, axis=0)
    input_grad = grad_one + norm_back(grad_normed_one * gain_one, normed_one, scale_one)

    new_tokens = mm(deal, home_mixed.reshape(ROWS, D), TN).astype(BF16)

    gain_sums = jnp.stack([gain_one_grad, gain_two_grad]).reshape(2, 16, 64).transpose(1, 0, 2)
    gain_sums = jnp.broadcast_to(gain_sums.reshape(16, 1, WIDE), (16, 8, WIDE))
    qk_row = qk_sums.reshape(WIDE)
    qk_row = jnp.broadcast_to(qk_row[None, None], (16, 8, WIDE))
    here = (jnp.arange(8) == y_at * 2 + core)[None, :, None]
    bias_row = jnp.where(here, bias_part.reshape(1, 1, 4), 0.0)
    bias_row = jnp.broadcast_to(bias_row, (16, 8, 4))
    smalls = jnp.concatenate([gain_sums, qk_row, bias_row, jnp.zeros((16, 8, WIDE - 4), F32)], axis=2)
    smalls = jnp.stack(pieces(smalls.reshape(DEVICES, 3 * WIDE), 2), axis=1)
    back_grads = mm(place, input_grad.astype(BF16), TN).astype(BF16).reshape(DEVICES, 2, D)
    last = jnp.concatenate([back_grads, smalls], axis=2)
    last, new_tokens, attn_grad, feed_grad = lax.optimization_barrier(
        (last, new_tokens, attn_grad, feed_grad)
    )
    home = lax.all_to_all(last, ALL, 0, 0, tiled=True)
    token_grads = mm(deal, home[:, :, :D].reshape(ROWS, D), TN).astype(BF16)
    sums = jnp.sum(home[:, :, D:].astype(F32), axis=(0, 1))
    gains_grad = sums[:WIDE].reshape(2, 64)
    qk_grad = sums[WIDE : 2 * WIDE].reshape(2, 64)
    bias_grad = sums[2 * WIDE : 2 * WIDE + 4].reshape(2, 2)

    return (
        new_tokens,
        token_grads,
        attn_grad[:3],
        attn_grad[3].T,
        feed_grad[:2],
        feed_grad[2].T,
        gains_grad,
        qk_grad,
        bias_grad,
    )


def solution(mesh):
    fine = Mesh(mesh.devices.reshape(4, 2, 2, 4, 2), ALL)
    dp = ("x", "zh", "core")
    tensor = ("y", "zl")
    in_specs = (
        P(ALL, None),
        P(ALL, None),
        P(ALL),
        P(ALL),
        P(ALL),
        P(dp, None),
        P(None, dp, tensor),
        P(tensor, dp),
        P(None, dp, tensor),
        P(tensor, dp),
        P(None, dp),
        P(),
        P(None, tensor),
    )
    out_specs = (
        P(ALL, None),
        P(ALL, None),
        P(None, dp, tensor),
        P(tensor, dp),
        P(None, dp, tensor),
        P(tensor, dp),
        P(None, dp),
        P(),
        P(None, tensor),
    )
    return jax.shard_map(body, mesh=fine, in_specs=in_specs, out_specs=out_specs, check_vma=False)
```

```python
import functools

import jax
import jax.numpy as jnp
from jax import lax
from jax.experimental import pallas as pl
from jax.experimental.pallas import tpu as pltpu
from jax.sharding import Mesh
from jax.sharding import PartitionSpec as P

HEADS = 16
HEAD_DIM = 64
HALF = HEAD_DIM // 2
D = 1024
FF = 4096
ROWS = 256
RING = 4
PLANE = ROWS * RING
GROUP = 2 * PLANE
DEVICES = 128
VARIATES = 8
SEQS = 4
WIDE = 128
EPS = 1e-06
THETA = 10000.0
LOG2E = 1.4426950408889634
FAR = -16384.0
F32 = jnp.float32
BF16 = jnp.bfloat16

ALL = ("x", "zh", "core", "y", "zl")
FLAT = ("x", "zh", "zl")
NT = (((1,), (1,)), ((), ()))
TN = (((0,), (0,)), ((), ()))


def mm(left, right, dims=(((1,), (0,)), ((), ()))):
    return lax.dot_general(left, right, dims, preferred_element_type=F32)


def root_stats(values):
    return lax.rsqrt(jnp.mean(values * values, axis=-1, keepdims=True) + EPS)


def norm_back(grad_in, normed, scale_inv):
    return scale_inv * (grad_in - normed * jnp.mean(grad_in * normed, axis=-1, keepdims=True))


def pieces(values, count):
    out = []
    for _ in range(count):
        part = lax.reduce_precision(values, 8, 7)
        out.append(part.astype(BF16))
        values = values - part
    return out


def ring(values, step):
    return lax.ppermute(values, "y", [(i, (i + step) % RING) for i in range(RING)])


def swap_core(values):
    return lax.ppermute(values, "core", [(0, 1), (1, 0)])


def gather_ring(values):
    ahead = ring(values, -1)
    behind = ring(values, 1)
    half = values.shape[0] // 2
    far_top = ring(ahead[:half], -1)
    far_low = ring(behind[half:], 1)
    return [values, ahead, jnp.concatenate([far_top, far_low], 0), behind]


def gather_direct(values):
    return [values, ring(values, -1), ring(values, 2), ring(values, 1)]


def send_ring(parts):
    half = parts[2].shape[0] // 2
    return [
        ring(parts[1], 1),
        ring(parts[3], -1),
        ring(parts[2][:half], 2),
        ring(parts[2][half:], 2),
    ]


def add_ring(own, got):
    far = jnp.concatenate([got[2], got[3]], 0)
    return own.astype(F32) + got[0].astype(F32) + got[1].astype(F32) + far.astype(F32)


def reduce_ring(parts):
    return add_ring(parts[0], send_ring(parts))


def flat_gather(shard):
    many = jnp.broadcast_to(shard[None], (16,) + shard.shape)
    return lax.all_to_all(many, FLAT, 0, 0, tiled=True)


def assemble_kernel(core_ref, mine_ref, other_ref, out_ref):
    core = core_ref[0]
    _, _, depth, width = mine_ref.shape
    for ref, at in ((mine_ref, core), (other_ref, 1 - core)):
        rows = pl.ds(pl.multiple_of(at * depth, depth), depth)
        for z in range(2):
            out_ref[:, rows, z * width : (z + 1) * width] = ref[z]


def assemble(core, mine, other):
    _, kinds, depth, width = mine.shape
    pair = pl.BlockSpec((2, kinds, depth, width), lambda p: (p, 0, 0, 0))
    return pl.pallas_call(
        assemble_kernel,
        grid=(8,),
        in_specs=[pl.BlockSpec(memory_space=pltpu.SMEM), pair, pair],
        out_specs=pl.BlockSpec((kinds, 2 * depth, 2 * width), lambda p: (0, p, 0)),
        out_shape=jax.ShapeDtypeStruct((kinds, 16 * depth, 2 * width), BF16),
        cost_estimate=pl.CostEstimate(
            flops=0, bytes_accessed=kinds * 128 * depth * width, transcendentals=0
        ),
    )(core, mine, other)


def chip_total(split):
    return (split[0].astype(F32) + swap_core(split[1]).astype(F32)).astype(BF16)


def plane_total(total):
    return lax.all_to_all(total, FLAT, 0, 0, tiled=True)


def weight_grad_kernel(core_ref, *refs, parts, switch):
    lefts, others, rights = refs[:parts], refs[parts : 2 * parts], refs[2 * parts : 3 * parts]
    keep_ref, send_ref = refs[3 * parts :]
    low = core_ref[0] == 0
    kind = pl.program_id(0)

    def work(sides):
        total = None
        for side, right in zip(sides, rights):
            part = mm(side[...], right[0], TN)
            total = part if total is None else total + part
        total = total.astype(BF16)
        depth = total.shape[0] // 16
        for p in range(8):
            at = 2 * p * depth
            even, odd = total[at : at + depth], total[at + depth : at + 2 * depth]
            keep_ref[p, 0, 0] = jnp.where(low, even, odd)
            send_ref[p, 0, 0] = jnp.where(low, odd, even)

    @pl.when(kind < switch)
    def _():
        work(lefts)

    @pl.when(kind >= switch)
    def _():
        work(others)


def weight_grads(core, lefts, others, rights, switch):
    parts = len(lefts)
    kinds, _, width = rights[0].shape
    half = width // 2
    sides = [pl.BlockSpec((v.shape[0], D), lambda k, z: (0, 0)) for v in list(lefts) + list(others)]
    moving = [pl.BlockSpec((1, v.shape[1], half), lambda k, z: (k, 0, z)) for v in rights]
    rows = sum(v.shape[1] for v in rights)
    out = pl.pallas_call(
        functools.partial(weight_grad_kernel, parts=parts, switch=switch),
        grid=(kinds, 2),
        in_specs=[pl.BlockSpec(memory_space=pltpu.SMEM)] + sides + moving,
        out_specs=[pl.BlockSpec((8, 1, 1, 64, half), lambda k, z: (0, z, k, 0, 0))] * 2,
        out_shape=[jax.ShapeDtypeStruct((8, 2, kinds, 64, half), BF16)] * 2,
        compiler_params=pltpu.CompilerParams(vmem_limit_bytes=48 * 2**20),
        cost_estimate=pl.CostEstimate(
            flops=2 * kinds * rows * D * width,
            bytes_accessed=2 * kinds * D * width + 4 * rows * D + 2 * kinds * rows * width,
            transcendentals=0,
        ),
    )(core, *lefts, *others, *rights)
    return [v.reshape(16, kinds, 64, half) for v in out]


def lanes_of(shape):
    return lax.broadcasted_iota(jnp.int32, shape, 1)


def head_sums(values):
    wide = values.shape[1]
    row = lax.broadcasted_iota(jnp.int32, (wide, wide), 0) // HEAD_DIM
    same = (row == lanes_of((wide, wide)) // HEAD_DIM).astype(BF16)
    high = values.astype(BF16)
    low = (values - high.astype(F32)).astype(BF16)
    return mm(high, same) + mm(low, same)


def partner(values):
    wide = values.shape[1]
    first = lanes_of(values.shape) % HEAD_DIM < HALF
    return jnp.where(first, pltpu.roll(values, wide - HALF, 1), pltpu.roll(values, HALF, 1))


def angles_of(facts, freq_ref):
    facts = facts.astype(F32)
    times = facts[:, 2:3] * 32.0 + facts[:, 3:4]
    angle = times * freq_ref[0:1, :WIDE]
    first = lanes_of(angle.shape) % HEAD_DIM < HALF
    cosine = jnp.cos(angle)
    sine = jnp.sin(angle)
    sine = jnp.where(first, -sine, sine)
    return jnp.concatenate([cosine, cosine], 1), jnp.concatenate([sine, sine], 1)


def project_kernel(core_ref, a_ref, w_ref, freq_ref, mine_ref, send_ref, raw_ref):
    low = core_ref[0] == 0
    rows = a_ref[:, :D]
    cosine, sine = angles_of(a_ref[:, D:], freq_ref)

    def emit(kind, value):
        left, right = value[:, :WIDE], value[:, WIDE:]
        mine_ref[kind] = jnp.where(low, left, right).astype(BF16)
        send_ref[kind] = jnp.where(low, right, left).astype(BF16)

    for kind in range(2):
        raw = mm(rows, w_ref[kind])
        raw_ref[kind] = raw
        unit = raw * lax.rsqrt(head_sums(raw * raw) * (1.0 / HEAD_DIM) + EPS)
        value = unit * freq_ref[1 + kind : 2 + kind, :]
        value = value * cosine + partner(value) * sine
        if kind == 0:
            value = value * (HEAD_DIM ** (-0.5) * LOG2E)
        emit(kind, value)
    emit(2, mm(rows, w_ref[2]))


def project(core, rows_all, attn_w, freq):
    block = 512
    both = pl.BlockSpec((3, block, WIDE), lambda i: (0, i, 0))
    low = jax.ShapeDtypeStruct((3, PLANE, WIDE), BF16)
    return pl.pallas_call(
        project_kernel,
        grid=(PLANE // block,),
        in_specs=[
            pl.BlockSpec(memory_space=pltpu.SMEM),
            pl.BlockSpec((block, D + WIDE), lambda i: (i, 0)),
            pl.BlockSpec((3, D, 2 * WIDE), lambda i: (0, 0, 0)),
            pl.BlockSpec((8, 2 * WIDE), lambda i: (0, 0)),
        ],
        out_specs=[both, both, pl.BlockSpec((2, block, 2 * WIDE), lambda i: (0, i, 0))],
        out_shape=[low, low, jax.ShapeDtypeStruct((2, PLANE, 2 * WIDE), F32)],
        compiler_params=pltpu.CompilerParams(vmem_limit_bytes=48 * 2**20),
        cost_estimate=pl.CostEstimate(
            flops=8 * PLANE * D * 2 * WIDE, bytes_accessed=PLANE * D * 8, transcendentals=PLANE * 1024
        ),
    )(core, rows_all, attn_w, freq)


def unproject_kernel(
    core_ref, mine_ref, got_ref, raw_ref, facts_ref, w_ref, freq_ref, dp_ref, part_ref, gain_ref
):
    low = core_ref[0] == 0
    cosine, sine = angles_of(facts_ref[...], freq_ref)

    @pl.when(pl.program_id(0) == 0)
    def _():
        gain_ref[...] = jnp.zeros_like(gain_ref)

    total = None
    for kind in range(3):
        mine, got = mine_ref[kind], got_ref[kind]
        grad = jnp.concatenate([jnp.where(low, mine, got), jnp.where(low, got, mine)], 1)
        if kind < 2:
            grad = grad.astype(F32)
            if kind == 0:
                grad = grad * (HEAD_DIM ** (-0.5))
            raw = raw_ref[kind]
            inv = lax.rsqrt(head_sums(raw * raw) * (1.0 / HEAD_DIM) + EPS)
            unit = raw * inv
            grad = grad * cosine - partner(grad) * sine
            gain_ref[kind : kind + 1, :] += jnp.sum(grad * unit, axis=0, keepdims=True)
            scaled = grad * freq_ref[1 + kind : 2 + kind, :]
            mean = head_sums(scaled * unit) * (1.0 / HEAD_DIM)
            grad = (inv * (scaled - unit * mean)).astype(BF16)
        dp_ref[kind] = grad
        part = mm(grad, w_ref[kind], NT)
        total = part if total is None else total + part
    part_ref[...] = total.astype(BF16)


def unproject(core, mine, got, raw, rows_all, attn_w, freq):
    block = 512
    both = pl.BlockSpec((3, block, WIDE), lambda i: (0, i, 0))
    return pl.pallas_call(
        unproject_kernel,
        grid=(PLANE // block,),
        in_specs=[
            pl.BlockSpec(memory_space=pltpu.SMEM),
            both,
            both,
            pl.BlockSpec((2, block, 2 * WIDE), lambda i: (0, i, 0)),
            pl.BlockSpec((block, WIDE), lambda i: (i, D // WIDE)),
            pl.BlockSpec((3, D, 2 * WIDE), lambda i: (0, 0, 0)),
            pl.BlockSpec((8, 2 * WIDE), lambda i: (0, 0)),
        ],
        out_specs=[
            pl.BlockSpec((3, block, 2 * WIDE), lambda i: (0, i, 0)),
            pl.BlockSpec((block, D), lambda i: (i, 0)),
            pl.BlockSpec((8, 2 * WIDE), lambda i: (0, 0)),
        ],
        out_shape=[
            jax.ShapeDtypeStruct((3, PLANE, 2 * WIDE), BF16),
            jax.ShapeDtypeStruct((PLANE, D), BF16),
            jax.ShapeDtypeStruct((8, 2 * WIDE), F32),
        ],
        compiler_params=pltpu.CompilerParams(vmem_limit_bytes=48 * 2**20),
        cost_estimate=pl.CostEstimate(
            flops=8 * PLANE * D * 2 * WIDE, bytes_accessed=PLANE * D * 8, transcendentals=PLANE * 1024
        ),
    )(core, mine, got, raw, rows_all, attn_w, freq)


LOG_LANE = 3 * VARIATES + SEQS


def with_pieces(base, values, first_lane, lanes):
    for i in range(3):
        part = values.astype(BF16).astype(F32)
        base = jnp.where(lanes == first_lane + i, part, base)
        values = values - part
    return base


def attend_kernel(qkv_ref, all_ref, qt_ref, kt_ref, vt_ref, att_ref, low_ref, tail_ref, *, chunks):
    size = all_ref.shape[1] // chunks
    query = jnp.concatenate([qkv_ref[0], qt_ref[...]], 1)
    zero = jnp.zeros_like(query)
    head_of = (lanes_of(query.shape) // HEAD_DIM) % 2
    lanes = lanes_of((query.shape[0], WIDE))
    out = None
    tail = qt_ref[...].astype(F32)
    for head in range(2):
        masked = jnp.where(head_of == head, query, zero)
        total = None
        for c in range(chunks):
            rows = pl.ds(c * size, size)
            keys = jnp.concatenate([all_ref[1, rows, :], kt_ref[rows, :]], 1)
            values = jnp.concatenate([all_ref[2, rows, :], vt_ref[rows, :]], 1)
            prob = jnp.exp2(mm(masked, keys, NT)).astype(BF16)
            part = mm(prob, values)
            total = part if total is None else total + part
        row_sum = total[:, WIDE : WIDE + 1]
        here = total[:, :WIDE] / row_sum
        out = here if head == 0 else jnp.where(lanes < HEAD_DIM, out, here)
        tail = with_pieces(tail, -jnp.log2(row_sum), head * HEAD_DIM + LOG_LANE, lanes)
    att_ref[...] = out
    low_ref[...] = out.astype(BF16)
    tail_ref[...] = tail.astype(BF16)


def attend(qkv, query_tail, key_tail, value_tail):
    block = 512
    rows = qkv.shape[1]
    moving = pl.BlockSpec((block, WIDE), lambda i: (i, 0))
    fixed = pl.BlockSpec((rows, WIDE), lambda i: (0, 0))
    low = jax.ShapeDtypeStruct((rows, WIDE), BF16)
    return pl.pallas_call(
        functools.partial(attend_kernel, chunks=4),
        grid=(rows // block,),
        in_specs=[
            pl.BlockSpec((1, block, WIDE), lambda i: (0, i, 0)),
            pl.BlockSpec((3, rows, WIDE), lambda i: (0, 0, 0)),
            moving,
            fixed,
            fixed,
        ],
        out_specs=[moving, moving, moving],
        out_shape=[jax.ShapeDtypeStruct((rows, WIDE), F32), low, low],
        compiler_params=pltpu.CompilerParams(vmem_limit_bytes=48 * 2**20),
        cost_estimate=pl.CostEstimate(
            flops=16 * rows * rows * WIDE, bytes_accessed=rows * WIDE * 24, transcendentals=2 * rows * rows
        ),
    )(qkv, qkv, query_tail, key_tail, value_tail)


def attend_back_kernel(
    qkv_ref, all_ref, qt_ref, kt_ref, vt_ref, hot_ref, grad_ref, att_ref,
    dq_ref, dk_ref, dv_ref, bias_ref, dk_sum, dv_sum, *, chunks
):
    size = all_ref.shape[1] // chunks
    step = pl.program_id(0)
    query = jnp.concatenate([qkv_ref[0], qt_ref[...]], 1)
    grad = grad_ref[...]
    zero = jnp.zeros_like(query)
    head_of = (lanes_of(query.shape) // HEAD_DIM) % 2
    lanes = lanes_of((query.shape[0], WIDE))
    overlap = grad.astype(F32) * att_ref[...]

    @pl.when(step == 0)
    def _():
        dk_sum[...] = jnp.zeros_like(dk_sum)
        dv_sum[...] = jnp.zeros_like(dv_sum)

    out = None
    for head in range(2):
        mine = head_of[:, :WIDE] == head
        masked = jnp.where(head_of == head, query, zero)
        grad_here = jnp.where(mine, grad, zero[:, :WIDE])
        dots = jnp.sum(jnp.where(mine, overlap, 0.0), axis=1, keepdims=True)
        extra = with_pieces(jnp.zeros(lanes.shape, F32), -dots, 0, lanes).astype(BF16)
        grad_wide = jnp.concatenate([grad_here, extra], 1)
        total = None
        for c in range(chunks):
            rows = pl.ds(c * size, size)
            keys = all_ref[1, rows, :]
            prob = jnp.exp2(mm(jnp.concatenate([keys, kt_ref[rows, :]], 1), masked, NT))
            slope = mm(jnp.concatenate([all_ref[2, rows, :], vt_ref[rows, :]], 1), grad_wide, NT)
            d_score = (prob * slope).astype(BF16)
            dv_sum[rows, :] += mm(prob.astype(BF16), grad_here)
            dk_sum[rows, :] += mm(d_score, masked)
            part = mm(d_score, keys, TN)
            total = part if total is None else total + part
        out = total if head == 0 else jnp.where(lanes < HEAD_DIM, out, total)
    dq_ref[...] = out.astype(BF16)

    @pl.when(step == pl.num_programs(0) - 1)
    def _():
        dk_ref[...] = (dk_sum[:, :WIDE] * (1.0 / LOG2E)).astype(BF16)
        dv_ref[...] = dv_sum[...].astype(BF16)
        counts = dk_sum[:, WIDE:]
        bias_ref[...] = jnp.zeros_like(bias_ref)
        bias_ref[0:1, :] = jnp.sum(counts * hot_ref[...].astype(F32), axis=0, keepdims=True)
        bias_ref[1:2, :] = jnp.sum(counts, axis=0, keepdims=True)


def attend_back(qkv, query_tail, key_tail, value_tail, query_hot, grad, attended):
    block = 512
    rows = qkv.shape[1]
    moving = pl.BlockSpec((block, WIDE), lambda i: (i, 0))
    fixed = pl.BlockSpec((rows, WIDE), lambda i: (0, 0))
    low = jax.ShapeDtypeStruct((rows, WIDE), BF16)
    return pl.pallas_call(
        functools.partial(attend_back_kernel, chunks=4),
        grid=(rows // block,),
        in_specs=[
            pl.BlockSpec((1, block, WIDE), lambda i: (0, i, 0)),
            pl.BlockSpec((3, rows, WIDE), lambda i: (0, 0, 0)),
            moving,
            fixed,
            fixed,
            fixed,
            moving,
            moving,
        ],
        out_specs=[moving, fixed, fixed, pl.BlockSpec((8, WIDE), lambda i: (0, 0))],
        out_shape=[low, low, low, jax.ShapeDtypeStruct((8, WIDE), F32)],
        scratch_shapes=[pltpu.VMEM((rows, 2 * WIDE), F32), pltpu.VMEM((rows, WIDE), F32)],
        compiler_params=pltpu.CompilerParams(vmem_limit_bytes=48 * 2**20),
        cost_estimate=pl.CostEstimate(
            flops=40 * rows * rows * WIDE, bytes_accessed=rows * WIDE * 24, transcendentals=2 * rows * rows
        ),
    )(qkv, qkv, query_tail, key_tail, value_tail, query_hot, grad, attended)


def feed_kernel(b_ref, g_ref, w_ref, y_ref, db_ref, act_ref, y_sum, db_sum):
    step = pl.program_id(0)
    rows = b_ref[...]
    gate_w, up_w, down_w = w_ref[0], w_ref[1], w_ref[2]
    gate = mm(rows, gate_w)
    up = mm(rows, up_w)
    d_hidden = mm(g_ref[...], down_w)
    sig = 1.0 / (1.0 + jnp.exp(-gate))
    silu = gate * sig
    hidden = (silu * up).astype(BF16)
    d_gate = (d_hidden * up * (sig * (1.0 + gate * (1.0 - sig)))).astype(BF16)
    d_up = (d_hidden * silu).astype(BF16)
    act_ref[0] = d_gate
    act_ref[1] = d_up
    act_ref[2] = hidden
    y_part = mm(hidden, down_w, NT)
    db_part = mm(d_gate, gate_w, NT) + mm(d_up, up_w, NT)

    @pl.when(step == 0)
    def _():
        y_sum[...] = y_part
        db_sum[...] = db_part

    @pl.when(step > 0)
    def _():
        y_sum[...] += y_part
        db_sum[...] += db_part

    @pl.when(step == pl.num_programs(0) - 1)
    def _():
        y_ref[...] = y_sum[...].astype(BF16)
        db_ref[...] = db_sum[...].astype(BF16)


def feed(rows_b, rows_g, weights):
    rows = rows_b.shape[0]
    width = weights.shape[2]
    block = 256
    whole = pl.BlockSpec((rows, D), lambda f: (0, 0))
    part = pl.BlockSpec((3, rows, block), lambda f: (0, 0, f))
    low_d = jax.ShapeDtypeStruct((rows, D), BF16)
    low_f = jax.ShapeDtypeStruct((3, rows, width), BF16)
    return pl.pallas_call(
        feed_kernel,
        grid=(width // block,),
        in_specs=[whole, whole, pl.BlockSpec((3, D, block), lambda f: (0, 0, f))],
        out_specs=[whole, whole, part],
        out_shape=[low_d, low_d, low_f],
        scratch_shapes=[pltpu.VMEM((rows, D), F32)] * 2,
        compiler_params=pltpu.CompilerParams(vmem_limit_bytes=48 * 2**20),
        cost_estimate=pl.CostEstimate(
            flops=12 * rows * D * width, bytes_accessed=6 * D * width + rows * D * 8 + rows * width * 6,
            transcendentals=rows * width,
        ),
    )(rows_b, rows_g, weights)


def body(
    tokens,
    cotangent,
    destination,
    variate_ids,
    time_ids,
    seq_lengths,
    qkv_weight,
    out_weight,
    gate_up_weight,
    down_weight,
    norm_gains,
    qk_gains,
    variate_bias,
):
    core = lax.axis_index("core")
    low_core = core == 0
    y_at = lax.axis_index("y")
    zl_at = lax.axis_index("zl")

    core_scalar = core.reshape(1).astype(jnp.int32)

    def side_by_side(mine, other):
        return jnp.concatenate(
            [jnp.where(low_core, mine, other), jnp.where(low_core, other, mine)], axis=-1
        )

    attn_shard = jnp.concatenate([qkv_weight, out_weight.T[None]], 0)
    feed_shard = jnp.concatenate([gate_up_weight, down_weight.T[None]], 0)
    slot = destination % ROWS
    group_at = destination // GROUP
    block_at = (destination % GROUP) // ROWS
    device_at = ((group_at // 2) * 2 + block_at // 4) * 8 + (block_at % 4) * 2 + group_at % 2
    key = device_at * ROWS + slot
    rank = jnp.sum((key[None, :] < key[:, None]).astype(jnp.int32), axis=1)
    deal = (jnp.arange(ROWS)[:, None] == rank[None, :]).astype(BF16)
    facts = jnp.stack([slot, variate_ids, time_ids // 32, time_ids % 32], axis=1).astype(BF16)
    facts = jnp.concatenate([facts, jnp.zeros((ROWS, WIDE - 4), BF16)], axis=1)
    gains_row = jnp.broadcast_to(norm_gains.reshape(1, WIDE), (ROWS, WIDE))
    outgoing = jnp.concatenate([tokens, cotangent, facts, gains_row], axis=1)
    span = outgoing.shape[1]
    outgoing = mm(deal, outgoing).astype(BF16).reshape(DEVICES, 2, span)
    arrived = lax.all_to_all(outgoing, ALL, 0, 0, tiled=True)

    lengths_other = swap_core(seq_lengths)
    lengths = jnp.where(zl_at == core, seq_lengths, lengths_other)[0]
    bias_other = lax.ppermute(variate_bias, "zl", [(0, 1), (1, 0)])
    bias_pair = jnp.where(zl_at == core, variate_bias, bias_other)

    all_gains = arrived[:, 0, span - WIDE :].reshape(16, 8, 2, 64)[:, 0]
    all_gains = all_gains.transpose(1, 0, 2).reshape(2, D).astype(F32)
    gain_one, gain_two = all_gains[0], all_gains[1]
    slots = arrived[:, :, 2 * D].reshape(2 * DEVICES)
    place = (jnp.arange(ROWS).astype(BF16)[:, None] == slots[None, :]).astype(BF16)
    placed = mm(place, arrived.reshape(2 * DEVICES, span))
    inputs = placed[:, :D]
    grad_rows = placed[:, D : 2 * D].astype(BF16)
    facts_here = placed[:, 2 * D : 2 * D + WIDE].astype(BF16)

    scale_one = root_stats(inputs)
    normed_one = inputs * scale_one
    attn_in = (normed_one * gain_one).astype(BF16)
    attn_in = jnp.concatenate([attn_in, facts_here], axis=1)
    attn_shard, attn_in = lax.optimization_barrier((attn_shard, attn_in))
    attn_mine = flat_gather(attn_shard)
    attn_w = assemble(core_scalar, attn_mine, swap_core(attn_mine))
    attn_all = gather_direct(attn_in)
    attn_all = jnp.concatenate(attn_all, 0)
    grad_rows, attn_all = lax.optimization_barrier((grad_rows, attn_all))
    feed_shard, attn_mine = lax.optimization_barrier((feed_shard, attn_mine))
    grad_all = gather_direct(grad_rows)
    feed_mine = flat_gather(feed_shard)

    variates_own = attn_all[:, D + 1].astype(jnp.int32)
    variates = jnp.concatenate([variates_own, swap_core(variates_own)])
    blocks_y = (y_at + jnp.arange(RING)) % RING
    blocks = jnp.concatenate([core * RING + blocks_y, (1 - core) * RING + blocks_y])
    positions = (blocks[:, None] * ROWS + jnp.arange(ROWS)[None, :]).reshape(GROUP)
    segments = jnp.sum((positions[:, None] >= jnp.cumsum(lengths)[None, :]).astype(jnp.int32), 1)

    inverse = THETA ** (-2.0 * jnp.arange(HALF).astype(F32) / HEAD_DIM)
    freq = jnp.concatenate(
        [
            jnp.tile(inverse, 8)[None],
            jnp.tile(qk_gains, (1, 4)),
            jnp.zeros((5, 2 * WIDE), F32),
        ]
    )
    qkv_mine, qkv_send, raw = project(core_scalar, attn_all, attn_w, freq)
    qkv = jnp.concatenate([qkv_mine, swap_core(qkv_send)], axis=1)

    lane = jnp.arange(WIDE)[None, :]
    tail_lane = lane % HEAD_DIM
    bias_lane = tail_lane < 3 * VARIATES
    seg_lane = (tail_lane >= 3 * VARIATES) & (tail_lane < LOG_LANE)
    one_lane = (tail_lane >= LOG_LANE) & (tail_lane < LOG_LANE + 3)
    equal = bias_lane & (tail_lane % VARIATES == variates[:, None])
    inside = seg_lane & (tail_lane - 3 * VARIATES == segments[:, None])
    query_tail = (equal | inside).astype(BF16)
    bias_parts = jnp.stack(pieces(bias_pair * LOG2E, 3)).astype(F32)
    bias_rows = jnp.repeat(bias_parts, VARIATES, axis=0).transpose(1, 2, 0)
    bias_rows = jnp.pad(bias_rows, ((0, 0), (0, 0), (0, HEAD_DIM - 3 * VARIATES))).reshape(2, WIDE)
    key_tail = jnp.where(equal, bias_rows[0:1], bias_rows[1:2])
    key_tail = jnp.where(seg_lane, jnp.where(inside, 0.0, FAR), key_tail)
    key_tail = jnp.where(one_lane, 1.0, key_tail).astype(BF16)
    value_tail = jnp.broadcast_to((lane < 3).astype(BF16), (GROUP, WIDE))
    attended, att_low, query_back = attend(qkv, query_tail, key_tail, value_tail)
    att_low, grad_all, feed_mine = lax.optimization_barrier((att_low, grad_all, feed_mine))
    feed_w = assemble(core_scalar, feed_mine, swap_core(feed_mine))
    att_plane = side_by_side(att_low[:PLANE], swap_core(att_low[PLANE:]))
    out_part = mm(att_plane, attn_w[3], NT).astype(BF16).reshape(RING, ROWS, D)
    got = send_ring([out_part[r] for r in range(RING)])
    got[0], feed_w = lax.optimization_barrier((got[0], feed_w))
    hidden_one = inputs + add_ring(out_part[0], got)

    scale_two = root_stats(hidden_one)
    normed_two = hidden_one * scale_two
    feed_in = (normed_two * gain_two).astype(BF16)
    ahead, behind = ring(feed_in, -1), ring(feed_in, 1)
    fed_own = feed(feed_in, grad_all[0], feed_w)
    ahead, behind, fed_own = lax.optimization_barrier((ahead, behind, fed_own))
    far_top, far_low = ring(ahead[: ROWS // 2], -1), ring(behind[ROWS // 2 :], 1)
    fed_ahead = feed(ahead, grad_all[1], feed_w)
    fed_behind = feed(behind, grad_all[3], feed_w)
    far_top, far_low, fed_ahead, fed_behind = lax.optimization_barrier(
        (far_top, far_low, fed_ahead, fed_behind)
    )
    far = jnp.concatenate([far_top, far_low], 0)
    fed_far = feed(far, grad_all[2], feed_w)
    feed_all = [feed_in, ahead, far, behind]
    fed = [fed_own, fed_ahead, fed_far, fed_behind]
    feed_split = weight_grads(core_scalar, feed_all, grad_all, [f[2] for f in fed], 2)
    db_got = send_ring([f[1] for f in fed])
    db_got, feed_split = lax.optimization_barrier((db_got, feed_split))
    grad_normed_two = add_ring(fed_own[1], db_got)

    gain_two_grad = jnp.sum(grad_normed_two * normed_two, axis=0)
    grad_one = grad_rows.astype(F32) + norm_back(grad_normed_two * gain_two, normed_two, scale_two)

    grad_one_all = gather_direct(grad_one.astype(BF16))
    feed_total = chip_total(feed_split)
    feed_arrived = plane_total(feed_total)
    grad_one_all, feed_total = lax.optimization_barrier((grad_one_all, feed_total))
    grad_one_all = jnp.concatenate(grad_one_all, 0)
    y_parts, grad_one_all = lax.optimization_barrier(([f[0] for f in fed], grad_one_all))
    y_got = send_ring(y_parts)
    grad_att = mm(grad_one_all, attn_w[3]).astype(BF16)
    grad_left, grad_right = grad_att[:, :WIDE], grad_att[:, WIDE:]
    grad_send = jnp.where(low_core, grad_right, grad_left)
    grad_mine = jnp.where(low_core, grad_left, grad_right)
    grad_mine = jnp.concatenate([grad_mine, swap_core(grad_send)], 0)
    d_query, d_key, d_value, bias_sums = attend_back(
        qkv, query_back, key_tail, value_tail, query_tail, grad_mine, attended
    )
    first_part = (jnp.arange(HEAD_DIM) < VARIATES)[None, None]
    bias_sums = jnp.where(first_part, bias_sums[:2].reshape(2, 2, HEAD_DIM), 0.0)
    bias_sums = jnp.sum(bias_sums, axis=2)
    bias_part = jnp.stack([bias_sums[0], bias_sums[1] - bias_sums[0]])
    d_query, y_got, feed_arrived = lax.optimization_barrier((d_query, y_got, feed_arrived))
    mixed = (hidden_one + add_ring(y_parts[0], y_got)).astype(BF16)
    d_mine = jnp.stack([d_query[:PLANE], d_key[:PLANE], d_value[:PLANE]])
    d_got = swap_core(jnp.stack([d_query[PLANE:], d_key[PLANE:], d_value[PLANE:]]))
    grad_proj, in_part, qk_sums = unproject(
        core_scalar, d_mine, d_got, raw, attn_all, attn_w, freq
    )
    in_part = in_part.reshape(RING, ROWS, D)
    in_got = send_ring([in_part[r] for r in range(RING)])
    attn_split = weight_grads(
        core_scalar,
        [attn_all],
        [grad_one_all],
        [jnp.concatenate([grad_proj, att_plane[None]], 0)],
        3,
    )
    attn_total = chip_total(attn_split)
    attn_arrived = plane_total(attn_total)
    in_got, attn_total = lax.optimization_barrier((in_got, attn_total))
    grad_normed_one = add_ring(in_part[0], in_got)
    feed_grad = jnp.sum(feed_arrived.astype(F32), axis=0)
    attn_grad = jnp.sum(attn_arrived.astype(F32), axis=0)
    qk_sums = jnp.sum(qk_sums[:2].reshape(2, 4, HEAD_DIM), axis=1)

    gain_one_grad = jnp.sum(grad_normed_one * normed_one, axis=0)
    input_grad = grad_one + norm_back(grad_normed_one * gain_one, normed_one, scale_one)

    gain_sums = jnp.stack([gain_one_grad, gain_two_grad]).reshape(2, 16, 64).transpose(1, 0, 2)
    gain_sums = jnp.broadcast_to(gain_sums.reshape(16, 1, WIDE), (16, 8, WIDE))
    qk_row = qk_sums.reshape(WIDE)
    qk_row = jnp.broadcast_to(qk_row[None, None], (16, 8, WIDE))
    here = (jnp.arange(8) == y_at * 2 + core)[None, :, None]
    bias_row = jnp.where(here, bias_part.reshape(1, 1, 4), 0.0)
    bias_row = jnp.broadcast_to(bias_row, (16, 8, 4))
    smalls = jnp.concatenate([gain_sums, qk_row, bias_row, jnp.zeros((16, 8, WIDE - 4), F32)], axis=2)
    smalls = jnp.stack(pieces(smalls.reshape(DEVICES, 3 * WIDE), 2), axis=1)
    rows_back = jnp.concatenate([mixed, input_grad.astype(BF16)], axis=1)
    rows_back = mm(place, rows_back, TN).astype(BF16).reshape(DEVICES, 2, 2 * D)
    last = jnp.concatenate([rows_back, smalls], axis=2)
    last, attn_grad, feed_grad = lax.optimization_barrier((last, attn_grad, feed_grad))
    home = lax.all_to_all(last, ALL, 0, 0, tiled=True)
    rows_home = mm(deal, home[:, :, : 2 * D].reshape(ROWS, 2 * D), TN).astype(BF16)
    new_tokens, token_grads = rows_home[:, :D], rows_home[:, D:]
    sums = jnp.sum(home[:, :, 2 * D :].astype(F32), axis=(0, 1))
    gains_grad = sums[:WIDE].reshape(2, 64)
    qk_grad = sums[WIDE : 2 * WIDE].reshape(2, 64)
    bias_grad = sums[2 * WIDE : 2 * WIDE + 4].reshape(2, 2)

    return (
        new_tokens,
        token_grads,
        attn_grad[:3],
        attn_grad[3].T,
        feed_grad[:2],
        feed_grad[2].T,
        gains_grad,
        qk_grad,
        bias_grad,
    )


def solution(mesh):
    fine = Mesh(mesh.devices.reshape(4, 2, 2, 4, 2), ALL)
    dp = ("x", "zh", "core")
    tensor = ("y", "zl")
    in_specs = (
        P(ALL, None),
        P(ALL, None),
        P(ALL),
        P(ALL),
        P(ALL),
        P(dp, None),
        P(None, dp, tensor),
        P(tensor, dp),
        P(None, dp, tensor),
        P(tensor, dp),
        P(None, dp),
        P(),
        P(None, tensor),
    )
    out_specs = (
        P(ALL, None),
        P(ALL, None),
        P(None, dp, tensor),
        P(tensor, dp),
        P(None, dp, tensor),
        P(tensor, dp),
        P(None, dp),
        P(),
        P(None, tensor),
    )
    return jax.shard_map(body, mesh=fine, in_specs=in_specs, out_specs=out_specs, check_vma=False)
```

```python
import functools

import jax
import jax.numpy as jnp
from jax import lax
from jax.experimental import pallas as pl
from jax.experimental.pallas import tpu as pltpu
from jax.sharding import Mesh
from jax.sharding import PartitionSpec as P

HEADS = 16
HEAD_DIM = 64
HALF = HEAD_DIM // 2
D = 1024
FF = 4096
ROWS = 256
RING = 4
PLANE = ROWS * RING
GROUP = 2 * PLANE
DEVICES = 128
VARIATES = 8
SEQS = 4
WIDE = 128
EPS = 1e-06
THETA = 10000.0
LOG2E = 1.4426950408889634
FAR = -16384.0
F32 = jnp.float32
BF16 = jnp.bfloat16

ALL = ("x", "zh", "core", "y", "zl")
FLAT = ("x", "zh", "zl")
NT = (((1,), (1,)), ((), ()))
TN = (((0,), (0,)), ((), ()))


def mm(left, right, dims=(((1,), (0,)), ((), ()))):
    return lax.dot_general(left, right, dims, preferred_element_type=F32)


def root_stats(values):
    return lax.rsqrt(jnp.mean(values * values, axis=-1, keepdims=True) + EPS)


def norm_back(grad_in, normed, scale_inv):
    return scale_inv * (grad_in - normed * jnp.mean(grad_in * normed, axis=-1, keepdims=True))


def pieces(values, count):
    out = []
    for _ in range(count):
        part = lax.reduce_precision(values, 8, 7)
        out.append(part.astype(BF16))
        values = values - part
    return out


def ring(values, step):
    return lax.ppermute(values, "y", [(i, (i + step) % RING) for i in range(RING)])


def swap_core(values):
    return lax.ppermute(values, "core", [(0, 1), (1, 0)])


def gather_ring(values):
    ahead = ring(values, -1)
    behind = ring(values, 1)
    half = values.shape[0] // 2
    far_top = ring(ahead[:half], -1)
    far_low = ring(behind[half:], 1)
    return [values, ahead, jnp.concatenate([far_top, far_low], 0), behind]


def gather_direct(values):
    return [values, ring(values, -1), ring(values, 2), ring(values, 1)]


def send_ring(parts):
    half = parts[2].shape[0] // 2
    return [
        ring(parts[1], 1),
        ring(parts[3], -1),
        ring(parts[2][:half], 2),
        ring(parts[2][half:], 2),
    ]


def add_ring(own, got):
    far = jnp.concatenate([got[2], got[3]], 0)
    return own.astype(F32) + got[0].astype(F32) + got[1].astype(F32) + far.astype(F32)


def reduce_ring(parts):
    return add_ring(parts[0], send_ring(parts))


def flat_gather(shard):
    many = jnp.broadcast_to(shard[None], (16,) + shard.shape)
    return lax.all_to_all(many, FLAT, 0, 0, tiled=True)


def assemble_kernel(core_ref, mine_ref, other_ref, out_ref):
    core = core_ref[0]
    count, _, depth, width = mine_ref.shape
    for ref, side in ((mine_ref, core), (other_ref, 1 - core)):
        for i in range(count):
            at = (i // 2) * 2 * depth + side * depth
            rows = pl.ds(pl.multiple_of(at, depth), depth)
            out_ref[:, rows, (i % 2) * width : (i % 2 + 1) * width] = ref[i]


def assemble(core, mine, other, steps):
    _, kinds, depth, width = mine.shape
    pair = pl.BlockSpec((16 // steps, kinds, depth, width), lambda p: (p, 0, 0, 0))
    return pl.pallas_call(
        assemble_kernel,
        grid=(steps,),
        in_specs=[pl.BlockSpec(memory_space=pltpu.SMEM), pair, pair],
        out_specs=pl.BlockSpec((kinds, 16 // steps * depth, 2 * width), lambda p: (0, p, 0)),
        out_shape=jax.ShapeDtypeStruct((kinds, 16 * depth, 2 * width), BF16),
        compiler_params=pltpu.CompilerParams(vmem_limit_bytes=48 * 2**20),
        cost_estimate=pl.CostEstimate(
            flops=0, bytes_accessed=kinds * 128 * depth * width, transcendentals=0
        ),
    )(core, mine, other)


def chip_total(split):
    return (split[0].astype(F32) + swap_core(split[1]).astype(F32)).astype(BF16)


def plane_total(total):
    return lax.all_to_all(total, FLAT, 0, 0, tiled=True)


def plane_rounds(total, beside):
    def round_of(values, axes, at):
        parts = [
            lax.dynamic_index_in_dim(values, (at + r) % RING, 0, keepdims=False) for r in range(RING)
        ]
        moves = [[(i, (i + r) % RING) for i in range(RING)] for r in range(RING)]
        return parts[0], [lax.ppermute(parts[r], axes, moves[r]) for r in (1, 3, 2)]

    def added(own, got):
        return sum((v.astype(F32) for v in got), own.astype(F32))

    values = total.reshape((RING, RING) + total.shape[1:])
    own, got = round_of(values, "x", lax.axis_index("x"))
    values = added(own, got).astype(BF16)
    own, got = round_of(values, ("zh", "zl"), lax.axis_index("zh") * 2 + lax.axis_index("zl"))
    got, beside = lax.optimization_barrier((got, beside))
    return added(own, got), beside


def lanes_of(shape):
    return lax.broadcasted_iota(jnp.int32, shape, 1)


def receive_kernel(rows_ref, gains_ref, x_ref, g_ref, a_ref, place_ref, gain_ref):
    facts = rows_ref[:, 2 * D : 2 * D + WIDE]
    slots = jnp.transpose(facts.astype(F32))[0:1, :]
    at = lax.broadcasted_iota(jnp.int32, (ROWS, ROWS), 0).astype(F32)
    place = (at == slots).astype(BF16)
    place_ref[...] = place
    gains = gains_ref[...].astype(F32)
    turned = pltpu.roll(gains, HEAD_DIM, 1)
    left = lanes_of((1, WIDE)) < HEAD_DIM
    one, two = [], []
    for c in range(D // WIDE):
        even, odd = slice(2 * c, 2 * c + 1), slice(2 * c + 1, 2 * c + 2)
        one.append(jnp.where(left, gains[even], turned[odd]))
        two.append(jnp.where(left, turned[even], gains[odd]))
    gain_one = jnp.concatenate(one, 1)
    gain_ref[...] = jnp.zeros_like(gain_ref)
    gain_ref[0:1, :] = gain_one
    gain_ref[1:2, :] = jnp.concatenate(two, 1)
    rows = mm(place, rows_ref[:, :D])
    x_ref[...] = rows
    a_ref[:, :D] = (rows * root_stats(rows) * gain_one).astype(BF16)
    a_ref[:, D:] = mm(place, facts).astype(BF16)
    g_ref[...] = mm(place, rows_ref[:, D : 2 * D]).astype(BF16)


def receive(rows, gains):
    return pl.pallas_call(
        receive_kernel,
        out_shape=[
            jax.ShapeDtypeStruct((ROWS, D), F32),
            jax.ShapeDtypeStruct((ROWS, D), BF16),
            jax.ShapeDtypeStruct((ROWS, D + WIDE), BF16),
            jax.ShapeDtypeStruct((ROWS, ROWS), BF16),
            jax.ShapeDtypeStruct((8, D), F32),
        ],
        cost_estimate=pl.CostEstimate(
            flops=2 * ROWS * ROWS * 2304, bytes_accessed=ROWS * D * 12, transcendentals=0
        ),
    )(rows, gains)


def finish_kernel(
    own_ref, near_ref, back_ref, top_ref, low_ref, x_ref, grad_ref, mixed_ref, place_ref,
    gain_ref, two_ref, small_ref, at_ref, out_ref,
):
    rows = x_ref[...]
    scale = root_stats(rows)
    normed = rows * scale
    far = jnp.concatenate([top_ref[...], low_ref[...]], 0).astype(F32)
    grad = own_ref[...].astype(F32) + near_ref[...].astype(F32) + back_ref[...].astype(F32) + far
    one = jnp.sum(grad * normed, axis=0, keepdims=True)
    two = two_ref[...]
    scaled = grad * gain_ref[0:1, :]
    back = scale * (scaled - normed * jnp.mean(scaled * normed, axis=1, keepdims=True))
    result = (grad_ref[...] + back).astype(BF16)
    place = place_ref[...]
    out_ref[:, :D] = mm(place, mixed_ref[...], TN).astype(BF16)
    out_ref[:, D : 2 * D] = mm(place, result, TN).astype(BF16)
    left = lanes_of((1, WIDE)) < HEAD_DIM
    tiles = []
    for c in range(D // WIDE):
        cols = slice(c * WIDE, (c + 1) * WIDE)
        a, b = one[:, cols], two[:, cols]
        even = jnp.where(left, a, pltpu.roll(jnp.broadcast_to(b, (8, WIDE)), HEAD_DIM, 1)[0:1])
        odd = jnp.where(left, pltpu.roll(jnp.broadcast_to(a, (8, WIDE)), HEAD_DIM, 1)[0:1], b)
        tiles += [jnp.broadcast_to(even, (16, WIDE)), jnp.broadcast_to(odd, (16, WIDE))]
    gains = jnp.concatenate(tiles, 0)
    row = lax.broadcasted_iota(jnp.int32, (ROWS, WIDE), 0)
    heads = jnp.broadcast_to(small_ref[0:1, :], (ROWS, WIDE))
    bias = jnp.where((row // 2) % 8 == at_ref[0], small_ref[1:2, :], 0.0)
    for i, value in enumerate((gains, heads, bias)):
        high = value.astype(BF16).astype(F32)
        value = jnp.where(row % 2 == 0, high, value - high).astype(BF16)
        out_ref[:, 2 * D + i * WIDE : 2 * D + (i + 1) * WIDE] = value


def finish(own, got, rows, grad, mixed, place, gains, two, small, at):
    specs = [pl.BlockSpec(memory_space=pltpu.VMEM)] * 12
    return pl.pallas_call(
        finish_kernel,
        in_specs=specs + [pl.BlockSpec(memory_space=pltpu.SMEM)],
        out_shape=jax.ShapeDtypeStruct((ROWS, 2 * D + 3 * WIDE), BF16),
        cost_estimate=pl.CostEstimate(
            flops=4 * ROWS * ROWS * D, bytes_accessed=ROWS * D * 20, transcendentals=0
        ),
    )(own, *got, rows, grad, mixed, place, gains, two, small, at)


def weight_grad_kernel(core_ref, *refs, parts, switch):
    lefts, others, rights = refs[:parts], refs[parts : 2 * parts], refs[2 * parts : 3 * parts]
    keep_ref, send_ref = refs[3 * parts :]
    low = core_ref[0] == 0
    kind = pl.program_id(0)

    def work(sides):
        total = None
        for side, right in zip(sides, rights):
            part = mm(side[...], right[0], TN)
            total = part if total is None else total + part
        total = total.astype(BF16)
        depth = total.shape[0] // 16
        for p in range(8):
            at = 2 * p * depth
            even, odd = total[at : at + depth], total[at + depth : at + 2 * depth]
            keep_ref[p, 0, 0] = jnp.where(low, even, odd)
            send_ref[p, 0, 0] = jnp.where(low, odd, even)

    @pl.when(kind < switch)
    def _():
        work(lefts)

    @pl.when(kind >= switch)
    def _():
        work(others)


def weight_grads(core, lefts, others, rights, switch):
    parts = len(lefts)
    kinds, _, width = rights[0].shape
    half = width // 2
    sides = [pl.BlockSpec((v.shape[0], D), lambda k, z: (0, 0)) for v in list(lefts) + list(others)]
    moving = [pl.BlockSpec((1, v.shape[1], half), lambda k, z: (k, 0, z)) for v in rights]
    rows = sum(v.shape[1] for v in rights)
    out = pl.pallas_call(
        functools.partial(weight_grad_kernel, parts=parts, switch=switch),
        grid=(kinds, 2),
        in_specs=[pl.BlockSpec(memory_space=pltpu.SMEM)] + sides + moving,
        out_specs=[pl.BlockSpec((8, 1, 1, 64, half), lambda k, z: (0, z, k, 0, 0))] * 2,
        out_shape=[jax.ShapeDtypeStruct((8, 2, kinds, 64, half), BF16)] * 2,
        compiler_params=pltpu.CompilerParams(vmem_limit_bytes=48 * 2**20),
        cost_estimate=pl.CostEstimate(
            flops=2 * kinds * rows * D * width,
            bytes_accessed=2 * kinds * D * width + 4 * rows * D + 2 * kinds * rows * width,
            transcendentals=0,
        ),
    )(core, *lefts, *others, *rights)
    return [v.reshape(16, kinds, 64, half) for v in out]


def head_sums(values):
    wide = values.shape[1]
    row = lax.broadcasted_iota(jnp.int32, (wide, wide), 0) // HEAD_DIM
    same = (row == lanes_of((wide, wide)) // HEAD_DIM).astype(BF16)
    high = values.astype(BF16)
    low = (values - high.astype(F32)).astype(BF16)
    return mm(high, same) + mm(low, same)


def partner(values):
    wide = values.shape[1]
    first = lanes_of(values.shape) % HEAD_DIM < HALF
    return jnp.where(first, pltpu.roll(values, wide - HALF, 1), pltpu.roll(values, HALF, 1))


def angles_of(facts, freq_ref):
    facts = facts.astype(F32)
    times = facts[:, 2:3] * 32.0 + facts[:, 3:4]
    angle = times * freq_ref[0:1, :WIDE]
    first = lanes_of(angle.shape) % HEAD_DIM < HALF
    cosine = jnp.cos(angle)
    sine = jnp.sin(angle)
    sine = jnp.where(first, -sine, sine)
    return jnp.concatenate([cosine, cosine], 1), jnp.concatenate([sine, sine], 1)


def project_kernel(core_ref, a_ref, w_ref, freq_ref, mine_ref, send_ref, raw_ref):
    low = core_ref[0] == 0
    rows = a_ref[:, :D]
    cosine, sine = angles_of(a_ref[:, D:], freq_ref)

    def emit(kind, value):
        left, right = value[:, :WIDE], value[:, WIDE:]
        mine_ref[kind] = jnp.where(low, left, right).astype(BF16)
        send_ref[kind] = jnp.where(low, right, left).astype(BF16)

    for kind in range(2):
        raw = mm(rows, w_ref[kind])
        raw_ref[kind] = raw
        unit = raw * lax.rsqrt(head_sums(raw * raw) * (1.0 / HEAD_DIM) + EPS)
        value = unit * freq_ref[1 + kind : 2 + kind, :]
        value = value * cosine + partner(value) * sine
        if kind == 0:
            value = value * (HEAD_DIM ** (-0.5) * LOG2E)
        emit(kind, value)
    emit(2, mm(rows, w_ref[2]))


def project(core, rows_all, attn_w, freq):
    block = 512
    both = pl.BlockSpec((3, block, WIDE), lambda i: (0, i, 0))
    low = jax.ShapeDtypeStruct((3, PLANE, WIDE), BF16)
    return pl.pallas_call(
        project_kernel,
        grid=(PLANE // block,),
        in_specs=[
            pl.BlockSpec(memory_space=pltpu.SMEM),
            pl.BlockSpec((block, D + WIDE), lambda i: (i, 0)),
            pl.BlockSpec((3, D, 2 * WIDE), lambda i: (0, 0, 0)),
            pl.BlockSpec((8, 2 * WIDE), lambda i: (0, 0)),
        ],
        out_specs=[both, both, pl.BlockSpec((2, block, 2 * WIDE), lambda i: (0, i, 0))],
        out_shape=[low, low, jax.ShapeDtypeStruct((2, PLANE, 2 * WIDE), F32)],
        compiler_params=pltpu.CompilerParams(vmem_limit_bytes=48 * 2**20),
        cost_estimate=pl.CostEstimate(
            flops=8 * PLANE * D * 2 * WIDE, bytes_accessed=PLANE * D * 8, transcendentals=PLANE * 1024
        ),
    )(core, rows_all, attn_w, freq)


def unproject_kernel(
    core_ref, mine_ref, got_ref, raw_ref, facts_ref, w_ref, freq_ref, dp_ref, part_ref, gain_ref
):
    low = core_ref[0] == 0
    cosine, sine = angles_of(facts_ref[...], freq_ref)

    @pl.when(pl.program_id(0) == 0)
    def _():
        gain_ref[...] = jnp.zeros_like(gain_ref)

    total = None
    for kind in range(3):
        mine, got = mine_ref[kind], got_ref[kind]
        grad = jnp.concatenate([jnp.where(low, mine, got), jnp.where(low, got, mine)], 1)
        if kind < 2:
            grad = grad.astype(F32)
            if kind == 0:
                grad = grad * (HEAD_DIM ** (-0.5))
            raw = raw_ref[kind]
            inv = lax.rsqrt(head_sums(raw * raw) * (1.0 / HEAD_DIM) + EPS)
            unit = raw * inv
            grad = grad * cosine - partner(grad) * sine
            gain_ref[kind : kind + 1, :] += jnp.sum(grad * unit, axis=0, keepdims=True)
            scaled = grad * freq_ref[1 + kind : 2 + kind, :]
            mean = head_sums(scaled * unit) * (1.0 / HEAD_DIM)
            grad = (inv * (scaled - unit * mean)).astype(BF16)
        dp_ref[kind] = grad
        part = mm(grad, w_ref[kind], NT)
        total = part if total is None else total + part
    part_ref[...] = total.astype(BF16)


def unproject(core, mine, got, raw, rows_all, attn_w, freq):
    block = 512
    both = pl.BlockSpec((3, block, WIDE), lambda i: (0, i, 0))
    return pl.pallas_call(
        unproject_kernel,
        grid=(PLANE // block,),
        in_specs=[
            pl.BlockSpec(memory_space=pltpu.SMEM),
            both,
            both,
            pl.BlockSpec((2, block, 2 * WIDE), lambda i: (0, i, 0)),
            pl.BlockSpec((block, WIDE), lambda i: (i, D // WIDE)),
            pl.BlockSpec((3, D, 2 * WIDE), lambda i: (0, 0, 0)),
            pl.BlockSpec((8, 2 * WIDE), lambda i: (0, 0)),
        ],
        out_specs=[
            pl.BlockSpec((3, block, 2 * WIDE), lambda i: (0, i, 0)),
            pl.BlockSpec((block, D), lambda i: (i, 0)),
            pl.BlockSpec((8, 2 * WIDE), lambda i: (0, 0)),
        ],
        out_shape=[
            jax.ShapeDtypeStruct((3, PLANE, 2 * WIDE), BF16),
            jax.ShapeDtypeStruct((PLANE, D), BF16),
            jax.ShapeDtypeStruct((8, 2 * WIDE), F32),
        ],
        compiler_params=pltpu.CompilerParams(vmem_limit_bytes=48 * 2**20),
        cost_estimate=pl.CostEstimate(
            flops=8 * PLANE * D * 2 * WIDE, bytes_accessed=PLANE * D * 8, transcendentals=PLANE * 1024
        ),
    )(core, mine, got, raw, rows_all, attn_w, freq)


LOG_LANE = 3 * VARIATES + SEQS


def with_pieces(base, values, first_lane, lanes):
    for i in range(3):
        part = values.astype(BF16).astype(F32)
        base = jnp.where(lanes == first_lane + i, part, base)
        values = values - part
    return base


def attend_kernel(qkv_ref, all_ref, qt_ref, kt_ref, vt_ref, att_ref, low_ref, tail_ref, *, chunks):
    size = all_ref.shape[1] // chunks
    query = jnp.concatenate([qkv_ref[0], qt_ref[...]], 1)
    zero = jnp.zeros_like(query)
    head_of = (lanes_of(query.shape) // HEAD_DIM) % 2
    lanes = lanes_of((query.shape[0], WIDE))
    out = None
    tail = qt_ref[...].astype(F32)
    for head in range(2):
        masked = jnp.where(head_of == head, query, zero)
        total = None
        for c in range(chunks):
            rows = pl.ds(c * size, size)
            keys = jnp.concatenate([all_ref[1, rows, :], kt_ref[rows, :]], 1)
            values = jnp.concatenate([all_ref[2, rows, :], vt_ref[rows, :]], 1)
            prob = jnp.exp2(mm(masked, keys, NT)).astype(BF16)
            part = mm(prob, values)
            total = part if total is None else total + part
        row_sum = total[:, WIDE : WIDE + 1]
        here = total[:, :WIDE] / row_sum
        out = here if head == 0 else jnp.where(lanes < HEAD_DIM, out, here)
        tail = with_pieces(tail, -jnp.log2(row_sum), head * HEAD_DIM + LOG_LANE, lanes)
    att_ref[...] = out
    low_ref[...] = out.astype(BF16)
    tail_ref[...] = tail.astype(BF16)


def attend(qkv, query_tail, key_tail, value_tail):
    block = 512
    rows = qkv.shape[1]
    moving = pl.BlockSpec((block, WIDE), lambda i: (i, 0))
    fixed = pl.BlockSpec((rows, WIDE), lambda i: (0, 0))
    low = jax.ShapeDtypeStruct((rows, WIDE), BF16)
    return pl.pallas_call(
        functools.partial(attend_kernel, chunks=4),
        grid=(rows // block,),
        in_specs=[
            pl.BlockSpec((1, block, WIDE), lambda i: (0, i, 0)),
            pl.BlockSpec((3, rows, WIDE), lambda i: (0, 0, 0)),
            moving,
            fixed,
            fixed,
        ],
        out_specs=[moving, moving, moving],
        out_shape=[jax.ShapeDtypeStruct((rows, WIDE), F32), low, low],
        compiler_params=pltpu.CompilerParams(vmem_limit_bytes=48 * 2**20),
        cost_estimate=pl.CostEstimate(
            flops=16 * rows * rows * WIDE, bytes_accessed=rows * WIDE * 24, transcendentals=2 * rows * rows
        ),
    )(qkv, qkv, query_tail, key_tail, value_tail)


def attend_back_kernel(
    qkv_ref, all_ref, qt_ref, kt_ref, vt_ref, hot_ref, grad_ref, att_ref,
    dq_ref, dk_ref, dv_ref, bias_ref, dk_sum, dv_sum, *, chunks
):
    size = all_ref.shape[1] // chunks
    step = pl.program_id(0)
    query = jnp.concatenate([qkv_ref[0], qt_ref[...]], 1)
    grad = grad_ref[...]
    zero = jnp.zeros_like(query)
    head_of = (lanes_of(query.shape) // HEAD_DIM) % 2
    lanes = lanes_of((query.shape[0], WIDE))
    overlap = grad.astype(F32) * att_ref[...]

    @pl.when(step == 0)
    def _():
        dk_sum[...] = jnp.zeros_like(dk_sum)
        dv_sum[...] = jnp.zeros_like(dv_sum)

    out = None
    for head in range(2):
        mine = head_of[:, :WIDE] == head
        masked = jnp.where(head_of == head, query, zero)
        grad_here = jnp.where(mine, grad, zero[:, :WIDE])
        dots = jnp.sum(jnp.where(mine, overlap, 0.0), axis=1, keepdims=True)
        extra = with_pieces(jnp.zeros(lanes.shape, F32), -dots, 0, lanes).astype(BF16)
        grad_wide = jnp.concatenate([grad_here, extra], 1)
        total = None
        for c in range(chunks):
            rows = pl.ds(c * size, size)
            keys = all_ref[1, rows, :]
            prob = jnp.exp2(mm(jnp.concatenate([keys, kt_ref[rows, :]], 1), masked, NT))
            slope = mm(jnp.concatenate([all_ref[2, rows, :], vt_ref[rows, :]], 1), grad_wide, NT)
            d_score = (prob * slope).astype(BF16)
            dv_sum[rows, :] += mm(prob.astype(BF16), grad_here)
            dk_sum[rows, :] += mm(d_score, masked)
            part = mm(d_score, keys, TN)
            total = part if total is None else total + part
        out = total if head == 0 else jnp.where(lanes < HEAD_DIM, out, total)
    dq_ref[...] = out.astype(BF16)

    @pl.when(step == pl.num_programs(0) - 1)
    def _():
        dk_ref[...] = (dk_sum[:, :WIDE] * (1.0 / LOG2E)).astype(BF16)
        dv_ref[...] = dv_sum[...].astype(BF16)
        counts = dk_sum[:, WIDE:]
        bias_ref[...] = jnp.zeros_like(bias_ref)
        bias_ref[0:1, :] = jnp.sum(counts * hot_ref[...].astype(F32), axis=0, keepdims=True)
        bias_ref[1:2, :] = jnp.sum(counts, axis=0, keepdims=True)


def attend_back(qkv, query_tail, key_tail, value_tail, query_hot, grad, attended):
    block = 512
    rows = qkv.shape[1]
    moving = pl.BlockSpec((block, WIDE), lambda i: (i, 0))
    fixed = pl.BlockSpec((rows, WIDE), lambda i: (0, 0))
    low = jax.ShapeDtypeStruct((rows, WIDE), BF16)
    return pl.pallas_call(
        functools.partial(attend_back_kernel, chunks=4),
        grid=(rows // block,),
        in_specs=[
            pl.BlockSpec((1, block, WIDE), lambda i: (0, i, 0)),
            pl.BlockSpec((3, rows, WIDE), lambda i: (0, 0, 0)),
            moving,
            fixed,
            fixed,
            fixed,
            moving,
            moving,
        ],
        out_specs=[moving, fixed, fixed, pl.BlockSpec((8, WIDE), lambda i: (0, 0))],
        out_shape=[low, low, low, jax.ShapeDtypeStruct((8, WIDE), F32)],
        scratch_shapes=[pltpu.VMEM((rows, 2 * WIDE), F32), pltpu.VMEM((rows, WIDE), F32)],
        compiler_params=pltpu.CompilerParams(vmem_limit_bytes=48 * 2**20),
        cost_estimate=pl.CostEstimate(
            flops=40 * rows * rows * WIDE, bytes_accessed=rows * WIDE * 24, transcendentals=2 * rows * rows
        ),
    )(qkv, qkv, query_tail, key_tail, value_tail, query_hot, grad, attended)


def feed_kernel(b_ref, g_ref, w_ref, y_ref, db_ref, act_ref, y_sum, db_sum):
    step = pl.program_id(0)
    rows = b_ref[...]
    gate_w, up_w, down_w = w_ref[0], w_ref[1], w_ref[2]
    gate = mm(rows, gate_w)
    up = mm(rows, up_w)
    d_hidden = mm(g_ref[...], down_w)
    sig = 1.0 / (1.0 + jnp.exp(-gate))
    silu = gate * sig
    hidden = (silu * up).astype(BF16)
    d_gate = (d_hidden * up * (sig * (1.0 + gate * (1.0 - sig)))).astype(BF16)
    d_up = (d_hidden * silu).astype(BF16)
    act_ref[0] = d_gate
    act_ref[1] = d_up
    act_ref[2] = hidden
    y_part = mm(hidden, down_w, NT)
    db_part = mm(d_gate, gate_w, NT) + mm(d_up, up_w, NT)

    @pl.when(step == 0)
    def _():
        y_sum[...] = y_part
        db_sum[...] = db_part

    @pl.when(step > 0)
    def _():
        y_sum[...] += y_part
        db_sum[...] += db_part

    @pl.when(step == pl.num_programs(0) - 1)
    def _():
        y_ref[...] = y_sum[...].astype(BF16)
        db_ref[...] = db_sum[...].astype(BF16)


def feed(rows_b, rows_g, weights):
    rows = rows_b.shape[0]
    width = weights.shape[2]
    block = 256
    whole = pl.BlockSpec((rows, D), lambda f: (0, 0))
    part = pl.BlockSpec((3, rows, block), lambda f: (0, 0, f))
    low_d = jax.ShapeDtypeStruct((rows, D), BF16)
    low_f = jax.ShapeDtypeStruct((3, rows, width), BF16)
    return pl.pallas_call(
        feed_kernel,
        grid=(width // block,),
        in_specs=[whole, whole, pl.BlockSpec((3, D, block), lambda f: (0, 0, f))],
        out_specs=[whole, whole, part],
        out_shape=[low_d, low_d, low_f],
        scratch_shapes=[pltpu.VMEM((rows, D), F32)] * 2,
        compiler_params=pltpu.CompilerParams(vmem_limit_bytes=48 * 2**20),
        cost_estimate=pl.CostEstimate(
            flops=12 * rows * D * width, bytes_accessed=6 * D * width + rows * D * 8 + rows * width * 6,
            transcendentals=rows * width,
        ),
    )(rows_b, rows_g, weights)


def body(
    tokens,
    cotangent,
    destination,
    variate_ids,
    time_ids,
    seq_lengths,
    qkv_weight,
    out_weight,
    gate_up_weight,
    down_weight,
    norm_gains,
    qk_gains,
    variate_bias,
):
    core = lax.axis_index("core")
    low_core = core == 0
    y_at = lax.axis_index("y")
    zl_at = lax.axis_index("zl")

    core_scalar = core.reshape(1).astype(jnp.int32)

    def side_by_side(mine, other):
        return jnp.concatenate(
            [jnp.where(low_core, mine, other), jnp.where(low_core, other, mine)], axis=-1
        )

    attn_shard = jnp.concatenate([qkv_weight, out_weight.T[None]], 0)
    feed_shard = jnp.concatenate([gate_up_weight, down_weight.T[None]], 0)
    slot = destination % ROWS
    group_at = destination // GROUP
    block_at = (destination % GROUP) // ROWS
    device_at = ((group_at // 2) * 2 + block_at // 4) * 8 + (block_at % 4) * 2 + group_at % 2
    key = device_at * ROWS + slot
    rank = jnp.sum((key[None, :] < key[:, None]).astype(jnp.int32), axis=1)
    deal = (jnp.arange(ROWS)[:, None] == rank[None, :]).astype(BF16)
    facts = jnp.stack([slot, variate_ids, time_ids // 32, time_ids % 32], axis=1).astype(BF16)
    facts = jnp.concatenate([facts, jnp.zeros((ROWS, WIDE - 4), BF16)], axis=1)
    gains_row = jnp.broadcast_to(norm_gains.reshape(1, WIDE), (ROWS, WIDE))
    outgoing = jnp.concatenate([tokens, cotangent, facts, gains_row], axis=1)
    span = outgoing.shape[1]
    outgoing = mm(deal, outgoing).astype(BF16).reshape(DEVICES, 2, span)
    arrived = lax.all_to_all(outgoing, ALL, 0, 0, tiled=True)

    lengths_other = swap_core(seq_lengths)
    lengths = jnp.where(zl_at == core, seq_lengths, lengths_other)[0]
    bias_other = lax.ppermute(variate_bias, "zl", [(0, 1), (1, 0)])
    bias_pair = jnp.where(zl_at == core, variate_bias, bias_other)

    all_gains = arrived[:, 0, span - WIDE :].reshape(16, 8, WIDE)[:, 0]
    inputs, grad_rows, attn_in, place, gains = receive(arrived.reshape(2 * DEVICES, span), all_gains)
    gain_two = gains[1]
    attn_shard, attn_in = lax.optimization_barrier((attn_shard, attn_in))
    attn_mine = flat_gather(attn_shard)
    attn_w = assemble(core_scalar, attn_mine, swap_core(attn_mine), 2)
    attn_all = gather_direct(attn_in)
    grad_rows, attn_all = lax.optimization_barrier((grad_rows, attn_all))
    attn_all = jnp.concatenate(attn_all, 0)
    feed_shard, attn_mine = lax.optimization_barrier((feed_shard, attn_mine))
    grad_all = gather_direct(grad_rows)
    feed_mine = flat_gather(feed_shard)

    variates_own = attn_all[:, D + 1].astype(jnp.int32)
    variates = jnp.concatenate([variates_own, swap_core(variates_own)])
    blocks_y = (y_at + jnp.arange(RING)) % RING
    blocks = jnp.concatenate([core * RING + blocks_y, (1 - core) * RING + blocks_y])
    positions = (blocks[:, None] * ROWS + jnp.arange(ROWS)[None, :]).reshape(GROUP)
    segments = jnp.sum((positions[:, None] >= jnp.cumsum(lengths)[None, :]).astype(jnp.int32), 1)

    inverse = THETA ** (-2.0 * jnp.arange(HALF).astype(F32) / HEAD_DIM)
    freq = jnp.concatenate(
        [
            jnp.tile(inverse, 8)[None],
            jnp.tile(qk_gains, (1, 4)),
            jnp.zeros((5, 2 * WIDE), F32),
        ]
    )
    qkv_mine, qkv_send, raw = project(core_scalar, attn_all, attn_w, freq)
    qkv = jnp.concatenate([qkv_mine, swap_core(qkv_send)], axis=1)

    lane = jnp.arange(WIDE)[None, :]
    tail_lane = lane % HEAD_DIM
    bias_lane = tail_lane < 3 * VARIATES
    seg_lane = (tail_lane >= 3 * VARIATES) & (tail_lane < LOG_LANE)
    one_lane = (tail_lane >= LOG_LANE) & (tail_lane < LOG_LANE + 3)
    equal = bias_lane & (tail_lane % VARIATES == variates[:, None])
    inside = seg_lane & (tail_lane - 3 * VARIATES == segments[:, None])
    query_tail = (equal | inside).astype(BF16)
    bias_parts = jnp.stack(pieces(bias_pair * LOG2E, 3)).astype(F32)
    bias_rows = jnp.repeat(bias_parts, VARIATES, axis=0).transpose(1, 2, 0)
    bias_rows = jnp.pad(bias_rows, ((0, 0), (0, 0), (0, HEAD_DIM - 3 * VARIATES))).reshape(2, WIDE)
    key_tail = jnp.where(equal, bias_rows[0:1], bias_rows[1:2])
    key_tail = jnp.where(seg_lane, jnp.where(inside, 0.0, FAR), key_tail)
    key_tail = jnp.where(one_lane, 1.0, key_tail).astype(BF16)
    value_tail = jnp.broadcast_to((lane < 3).astype(BF16), (GROUP, WIDE))
    attended, att_low, query_back = attend(qkv, query_tail, key_tail, value_tail)
    att_low, grad_all = lax.optimization_barrier((att_low, grad_all))
    att_other = swap_core(att_low[PLANE:])
    att_other, feed_mine = lax.optimization_barrier((att_other, feed_mine))
    feed_w = assemble(core_scalar, feed_mine, swap_core(feed_mine), 4)
    att_plane = side_by_side(att_low[:PLANE], att_other)
    out_part = mm(att_plane, attn_w[3], NT).astype(BF16).reshape(RING, ROWS, D)
    got = send_ring([out_part[r] for r in range(RING)])
    got[0], feed_w = lax.optimization_barrier((got[0], feed_w))
    hidden_one = inputs + add_ring(out_part[0], got)

    scale_two = root_stats(hidden_one)
    normed_two = hidden_one * scale_two
    feed_in = (normed_two * gain_two).astype(BF16)
    ahead, behind = ring(feed_in, -1), ring(feed_in, 1)
    fed_own = feed(feed_in, grad_all[0], feed_w)
    ahead, behind, fed_own = lax.optimization_barrier((ahead, behind, fed_own))
    far_top, far_low = ring(ahead[: ROWS // 2], -1), ring(behind[ROWS // 2 :], 1)
    fed_ahead = feed(ahead, grad_all[1], feed_w)
    fed_behind = feed(behind, grad_all[3], feed_w)
    far_top, far_low, fed_ahead, fed_behind = lax.optimization_barrier(
        (far_top, far_low, fed_ahead, fed_behind)
    )
    far = jnp.concatenate([far_top, far_low], 0)
    fed_far = feed(far, grad_all[2], feed_w)
    feed_all = [feed_in, ahead, far, behind]
    fed = [fed_own, fed_ahead, fed_far, fed_behind]
    feed_split = weight_grads(core_scalar, feed_all, grad_all, [f[2] for f in fed], 2)
    db_got = send_ring([f[1] for f in fed])
    db_got, feed_split = lax.optimization_barrier((db_got, feed_split))
    grad_normed_two = add_ring(fed_own[1], db_got)

    gain_two_grad = jnp.sum(grad_normed_two * normed_two, axis=0)
    grad_one = grad_rows.astype(F32) + norm_back(grad_normed_two * gain_two, normed_two, scale_two)

    grad_one_all = gather_direct(grad_one.astype(BF16))
    feed_total = chip_total(feed_split)
    feed_arrived = plane_total(feed_total)
    grad_one_all, feed_total = lax.optimization_barrier((grad_one_all, feed_total))
    grad_one_all = jnp.concatenate(grad_one_all, 0)
    y_parts, grad_one_all = lax.optimization_barrier(([f[0] for f in fed], grad_one_all))
    y_got = send_ring(y_parts)
    grad_att = mm(grad_one_all, attn_w[3]).astype(BF16)
    grad_left, grad_right = grad_att[:, :WIDE], grad_att[:, WIDE:]
    grad_send = jnp.where(low_core, grad_right, grad_left)
    grad_mine = jnp.where(low_core, grad_left, grad_right)
    grad_mine = jnp.concatenate([grad_mine, swap_core(grad_send)], 0)
    d_query, d_key, d_value, bias_sums = attend_back(
        qkv, query_back, key_tail, value_tail, query_tail, grad_mine, attended
    )
    first_part = (jnp.arange(HEAD_DIM) < VARIATES)[None, None]
    bias_sums = jnp.where(first_part, bias_sums[:2].reshape(2, 2, HEAD_DIM), 0.0)
    bias_sums = jnp.sum(bias_sums, axis=2)
    bias_part = jnp.stack([bias_sums[0], bias_sums[1] - bias_sums[0]])
    d_query, y_got, feed_arrived = lax.optimization_barrier((d_query, y_got, feed_arrived))
    mixed = (hidden_one + add_ring(y_parts[0], y_got)).astype(BF16)
    d_mine = jnp.stack([d_query[:PLANE], d_key[:PLANE], d_value[:PLANE]])
    d_got = swap_core(jnp.stack([d_query[PLANE:], d_key[PLANE:], d_value[PLANE:]]))
    grad_proj, in_part, qk_sums = unproject(
        core_scalar, d_mine, d_got, raw, attn_all, attn_w, freq
    )
    in_part = in_part.reshape(RING, ROWS, D)
    in_got = send_ring([in_part[r] for r in range(RING)])
    attn_split = weight_grads(
        core_scalar,
        [attn_all],
        [grad_one_all],
        [jnp.concatenate([grad_proj, att_plane[None]], 0)],
        3,
    )
    in_got, attn_split = lax.optimization_barrier((in_got, attn_split))
    attn_total = chip_total(attn_split)
    feed_grad = jnp.sum(feed_arrived.astype(F32), axis=0)
    qk_sums = jnp.sum(qk_sums[:2].reshape(2, 4, HEAD_DIM), axis=1)

    small = jnp.zeros((8, WIDE), F32).at[0].set(qk_sums.reshape(WIDE))
    small = small.at[1, :4].set(bias_part.reshape(4))
    tensor_at = (y_at * 2 + core).reshape(1).astype(jnp.int32)
    last = finish(
        in_part[0], in_got, inputs, grad_one, mixed, place, gains, gain_two_grad[None], small, tensor_at
    )
    span = last.shape[1]
    last = last.reshape(DEVICES, 2, span)
    home = lax.all_to_all(last, ALL, 0, 0, tiled=True)
    attn_grad, home = plane_rounds(attn_total, home)
    rows_home = mm(deal, home[:, :, : 2 * D].reshape(ROWS, 2 * D), TN).astype(BF16)
    new_tokens, token_grads = rows_home[:, :D], rows_home[:, D:]
    sums = jnp.sum(home[:, :, 2 * D :].astype(F32), axis=(0, 1))
    gains_grad = sums[:WIDE].reshape(2, 64)
    qk_grad = sums[WIDE : 2 * WIDE].reshape(2, 64)
    bias_grad = sums[2 * WIDE : 2 * WIDE + 4].reshape(2, 2)

    return (
        new_tokens,
        token_grads,
        attn_grad[:3],
        attn_grad[3].T,
        feed_grad[:2],
        feed_grad[2].T,
        gains_grad,
        qk_grad,
        bias_grad,
    )


def solution(mesh):
    fine = Mesh(mesh.devices.reshape(4, 2, 2, 4, 2), ALL)
    dp = ("x", "zh", "core")
    tensor = ("y", "zl")
    in_specs = (
        P(ALL, None),
        P(ALL, None),
        P(ALL),
        P(ALL),
        P(ALL),
        P(dp, None),
        P(None, dp, tensor),
        P(tensor, dp),
        P(None, dp, tensor),
        P(tensor, dp),
        P(None, dp),
        P(),
        P(None, tensor),
    )
    out_specs = (
        P(ALL, None),
        P(ALL, None),
        P(None, dp, tensor),
        P(tensor, dp),
        P(None, dp, tensor),
        P(tensor, dp),
        P(None, dp),
        P(),
        P(None, tensor),
    )
    return jax.shard_map(body, mesh=fine, in_specs=in_specs, out_specs=out_specs, check_vma=False)
```

```python
import functools

import jax
import jax.numpy as jnp
from jax import lax
from jax.experimental import pallas as pl
from jax.experimental.pallas import tpu as pltpu
from jax.sharding import Mesh
from jax.sharding import PartitionSpec as P

HEADS = 16
HEAD_DIM = 64
HALF = HEAD_DIM // 2
D = 1024
FF = 4096
ROWS = 256
RING = 4
PLANE = ROWS * RING
GROUP = 2 * PLANE
DEVICES = 128
VARIATES = 8
SEQS = 4
WIDE = 128
EPS = 1e-06
THETA = 10000.0
LOG2E = 1.4426950408889634
FAR = -16384.0
F32 = jnp.float32
BF16 = jnp.bfloat16

ALL = ("x", "zh", "core", "y", "zl")
FLAT = ("x", "zh", "zl")
NT = (((1,), (1,)), ((), ()))
TN = (((0,), (0,)), ((), ()))


def mm(left, right, dims=(((1,), (0,)), ((), ()))):
    return lax.dot_general(left, right, dims, preferred_element_type=F32)


def root_stats(values):
    return lax.rsqrt(jnp.mean(values * values, axis=-1, keepdims=True) + EPS)


def norm_back(grad_in, normed, scale_inv):
    return scale_inv * (grad_in - normed * jnp.mean(grad_in * normed, axis=-1, keepdims=True))


def pieces(values, count):
    out = []
    for _ in range(count):
        part = lax.reduce_precision(values, 8, 7)
        out.append(part.astype(BF16))
        values = values - part
    return out


def ring(values, step):
    return lax.ppermute(values, "y", [(i, (i + step) % RING) for i in range(RING)])


def swap_core(values):
    return lax.ppermute(values, "core", [(0, 1), (1, 0)])


def gather_ring(values):
    ahead = ring(values, -1)
    behind = ring(values, 1)
    half = values.shape[0] // 2
    far_top = ring(ahead[:half], -1)
    far_low = ring(behind[half:], 1)
    return [values, ahead, jnp.concatenate([far_top, far_low], 0), behind]


def gather_direct(values):
    return [values, ring(values, -1), ring(values, 2), ring(values, 1)]


def send_ring(parts):
    half = parts[2].shape[0] // 2
    return [
        ring(parts[1], 1),
        ring(parts[3], -1),
        ring(parts[2][:half], 2),
        ring(parts[2][half:], 2),
    ]


def add_ring(own, got):
    far = jnp.concatenate([got[2], got[3]], 0)
    return own.astype(F32) + got[0].astype(F32) + got[1].astype(F32) + far.astype(F32)


def reduce_ring(parts):
    return add_ring(parts[0], send_ring(parts))


def gather_round(values, axes, at):
    moves = [[((i + r) % RING, i) for i in range(RING)] for r in range(RING)]
    rows = [values] + [lax.ppermute(values, axes, moves[r]) for r in range(1, RING)]
    return jnp.roll(jnp.stack(rows), at, axis=0)


def flat_gather(shard):
    many = jnp.broadcast_to(shard[None], (16,) + shard.shape)
    return lax.all_to_all(many, FLAT, 0, 0, tiled=True)


def assemble_kernel(core_ref, mine_ref, other_ref, out_ref):
    core = core_ref[0]
    count, _, depth, width = mine_ref.shape
    for ref, side in ((mine_ref, core), (other_ref, 1 - core)):
        for i in range(count):
            at = (i // 2) * 2 * depth + side * depth
            rows = pl.ds(pl.multiple_of(at, depth), depth)
            out_ref[:, rows, (i % 2) * width : (i % 2 + 1) * width] = ref[i]


def assemble(core, mine, other, steps):
    _, kinds, depth, width = mine.shape
    pair = pl.BlockSpec((16 // steps, kinds, depth, width), lambda p: (p, 0, 0, 0))
    return pl.pallas_call(
        assemble_kernel,
        grid=(steps,),
        in_specs=[pl.BlockSpec(memory_space=pltpu.SMEM), pair, pair],
        out_specs=pl.BlockSpec((kinds, 16 // steps * depth, 2 * width), lambda p: (0, p, 0)),
        out_shape=jax.ShapeDtypeStruct((kinds, 16 * depth, 2 * width), BF16),
        compiler_params=pltpu.CompilerParams(vmem_limit_bytes=48 * 2**20),
        cost_estimate=pl.CostEstimate(
            flops=0, bytes_accessed=kinds * 128 * depth * width, transcendentals=0
        ),
    )(core, mine, other)


def chip_total(split):
    return (split[0].astype(F32) + swap_core(split[1]).astype(F32)).astype(BF16)


def plane_total(total):
    return lax.all_to_all(total, FLAT, 0, 0, tiled=True)


def plane_rounds(total, last, exchange):
    def round_of(values, axes, at):
        parts = [
            lax.dynamic_index_in_dim(values, (at + r) % RING, 0, keepdims=False) for r in range(RING)
        ]
        moves = [[(i, (i + r) % RING) for i in range(RING)] for r in range(RING)]
        return parts[0], [lax.ppermute(parts[r], axes, moves[r]) for r in (1, 3, 2)]

    def added(own, got):
        return sum((v.astype(F32) for v in got), own.astype(F32))

    values = total.reshape((RING, RING) + total.shape[1:])
    own, got = round_of(values, "x", lax.axis_index("x"))
    got, last = lax.optimization_barrier((got, last))
    values = added(own, got).astype(BF16)
    beside = exchange(last)
    own, got = round_of(values, ("zh", "zl"), lax.axis_index("zh") * 2 + lax.axis_index("zl"))
    got, beside = lax.optimization_barrier((got, beside))
    return added(own, got), beside


def lanes_of(shape):
    return lax.broadcasted_iota(jnp.int32, shape, 1)


QUARTER = D // RING
SPAN = D + WIDE + QUARTER
GAIN_LANE = 16


def deal_kernel(tok_ref, cot_ref, facts_ref, gains_ref, out_ref, deal_ref):
    wide = jnp.concatenate([facts_ref[...], jnp.zeros((WIDE - 8, ROWS), F32)], 0)
    facts = jnp.transpose(wide)
    keys = facts_ref[0:1, :]
    rank = jnp.sum((facts[:, 0:1] < keys).astype(F32), axis=0, keepdims=True)
    at = lax.broadcasted_iota(jnp.int32, (ROWS, ROWS), 0).astype(F32)
    deal_ref[...] = (at == rank).astype(BF16)
    low = jnp.where(lanes_of(facts.shape) == 0, 0.0, facts).astype(BF16)
    row = lax.broadcasted_iota(jnp.int32, (4 * ROWS, 1), 0)
    device, step, odd = row // 8, (row // 2) % RING, row % 2
    ahead = (device // 8) * 8 + ((device // 2 + step) % RING) * 2 + device % 2
    spread = ((2 * ahead + odd).astype(F32) == rank).astype(BF16)
    out_ref[:, :D] = mm(spread, tok_ref[...]).astype(BF16)
    tail = mm(spread, low)
    lane = lanes_of(tail.shape)
    gains = jnp.broadcast_to(gains_ref[...][None], (DEVICES, 8, WIDE)).reshape(tail.shape)
    tail = jnp.where((lane >= GAIN_LANE) & (lane < GAIN_LANE + 16), gains, tail)
    out_ref[:, D : D + WIDE] = tail.astype(BF16)
    own = ((2 * device + (row % 8) // RING).astype(F32) == rank).astype(BF16)
    part = None
    for m in range(RING):
        here = mm(own, cot_ref[:, m * QUARTER : (m + 1) * QUARTER])
        part = here if m == 0 else jnp.where(row % RING == m, here, part)
    out_ref[:, D + WIDE :] = part.astype(BF16)


def deal_rows(tokens, cotangent, facts, gains):
    return pl.pallas_call(
        deal_kernel,
        out_shape=[
            jax.ShapeDtypeStruct((4 * ROWS, SPAN), BF16),
            jax.ShapeDtypeStruct((ROWS, ROWS), BF16),
        ],
        compiler_params=pltpu.CompilerParams(vmem_limit_bytes=48 * 2**20),
        cost_estimate=pl.CostEstimate(
            flops=8 * ROWS * ROWS * 2304, bytes_accessed=ROWS * D * 16, transcendentals=0
        ),
    )(tokens, cotangent, facts, gains)


def receive_kernel(rows_ref, gains_ref, x_ref, g_ref, a_ref, place_ref, gain_ref):
    count = 4 * ROWS
    facts = rows_ref[:, D : D + WIDE]
    slots = jnp.transpose(facts.astype(F32))[1:2, :]
    at = lax.broadcasted_iota(jnp.int32, (ROWS, count), 0)
    arrival = lanes_of((ROWS, count))
    here = at.astype(F32) == slots
    gains = gains_ref[...].astype(F32)
    turned = pltpu.roll(gains, HEAD_DIM, 1)
    left = lanes_of((1, WIDE)) < HEAD_DIM
    one, two = [], []
    for c in range(D // WIDE):
        even, odd = slice(2 * c, 2 * c + 1), slice(2 * c + 1, 2 * c + 2)
        one.append(jnp.where(left, gains[even], turned[odd]))
        two.append(jnp.where(left, turned[even], gains[odd]))
    gain_one = jnp.concatenate(one, 1)
    gain_ref[...] = jnp.zeros_like(gain_ref)
    gain_ref[0:1, :] = gain_one
    gain_ref[1:2, :] = jnp.concatenate(two, 1)
    for r in range(RING):
        place = (here & ((arrival // 2) % RING == r)).astype(BF16)
        rows = mm(place, rows_ref[:, :D])
        block = slice(r * ROWS, (r + 1) * ROWS)
        a_ref[block, :D] = (rows * root_stats(rows) * gain_one).astype(BF16)
        a_ref[block, D:] = mm(place, facts).astype(BF16)
        if r == 0:
            x_ref[...] = rows
            first = place
    pick = ((at // 2) * 8 + at % 2 == arrival).astype(BF16)
    place = mm(first, pick, NT).astype(BF16)
    place_ref[...] = place
    for m in range(RING):
        pick = ((at // 2) * 8 + (at % 2) * RING + m == arrival).astype(BF16)
        quarter = mm(place, pick).astype(BF16)
        g_ref[:, m * QUARTER : (m + 1) * QUARTER] = mm(quarter, rows_ref[:, D + WIDE :]).astype(BF16)


def receive(rows, gains):
    return pl.pallas_call(
        receive_kernel,
        out_shape=[
            jax.ShapeDtypeStruct((ROWS, D), F32),
            jax.ShapeDtypeStruct((ROWS, D), BF16),
            jax.ShapeDtypeStruct((PLANE, D + WIDE), BF16),
            jax.ShapeDtypeStruct((ROWS, ROWS), BF16),
            jax.ShapeDtypeStruct((8, D), F32),
        ],
        compiler_params=pltpu.CompilerParams(vmem_limit_bytes=48 * 2**20),
        cost_estimate=pl.CostEstimate(
            flops=32 * ROWS * ROWS * D, bytes_accessed=ROWS * D * 24, transcendentals=0
        ),
    )(rows, gains)


def finish_kernel(
    own_ref, near_ref, back_ref, top_ref, low_ref, x_ref, grad_ref, mixed_ref, place_ref,
    gain_ref, two_ref, small_ref, at_ref, out_ref,
):
    rows = x_ref[...]
    scale = root_stats(rows)
    normed = rows * scale
    far = jnp.concatenate([top_ref[...], low_ref[...]], 0).astype(F32)
    grad = own_ref[...].astype(F32) + near_ref[...].astype(F32) + back_ref[...].astype(F32) + far
    one = jnp.sum(grad * normed, axis=0, keepdims=True)
    two = two_ref[...]
    scaled = grad * gain_ref[0:1, :]
    back = scale * (scaled - normed * jnp.mean(scaled * normed, axis=1, keepdims=True))
    result = (grad_ref[...] + back).astype(BF16)
    place = place_ref[...]
    out_ref[:, :D] = mm(place, mixed_ref[...], TN).astype(BF16)
    out_ref[:, D : 2 * D] = mm(place, result, TN).astype(BF16)
    left = lanes_of((1, WIDE)) < HEAD_DIM
    tiles = []
    for c in range(D // WIDE):
        cols = slice(c * WIDE, (c + 1) * WIDE)
        a, b = one[:, cols], two[:, cols]
        even = jnp.where(left, a, pltpu.roll(jnp.broadcast_to(b, (8, WIDE)), HEAD_DIM, 1)[0:1])
        odd = jnp.where(left, pltpu.roll(jnp.broadcast_to(a, (8, WIDE)), HEAD_DIM, 1)[0:1], b)
        tiles += [jnp.broadcast_to(even, (16, WIDE)), jnp.broadcast_to(odd, (16, WIDE))]
    gains = jnp.concatenate(tiles, 0)
    row = lax.broadcasted_iota(jnp.int32, (ROWS, WIDE), 0)
    heads = jnp.broadcast_to(small_ref[0:1, :], (ROWS, WIDE))
    bias = jnp.where((row // 2) % 8 == at_ref[0], small_ref[1:2, :], 0.0)
    for i, value in enumerate((gains, heads, bias)):
        high = value.astype(BF16).astype(F32)
        value = jnp.where(row % 2 == 0, high, value - high).astype(BF16)
        out_ref[:, 2 * D + i * WIDE : 2 * D + (i + 1) * WIDE] = value


def finish(own, got, rows, grad, mixed, place, gains, two, small, at):
    specs = [pl.BlockSpec(memory_space=pltpu.VMEM)] * 12
    return pl.pallas_call(
        finish_kernel,
        in_specs=specs + [pl.BlockSpec(memory_space=pltpu.SMEM)],
        out_shape=jax.ShapeDtypeStruct((ROWS, 2 * D + 3 * WIDE), BF16),
        cost_estimate=pl.CostEstimate(
            flops=4 * ROWS * ROWS * D, bytes_accessed=ROWS * D * 20, transcendentals=0
        ),
    )(own, *got, rows, grad, mixed, place, gains, two, small, at)


def weight_grad_kernel(core_ref, *refs, parts, switch, steps):
    lefts, others, rights = refs[:parts], refs[parts : 2 * parts], refs[2 * parts : 3 * parts]
    keep_ref, send_ref, turned_ref = refs[3 * parts :]
    low = core_ref[0] == 0
    step = pl.program_id(0)

    def load(sides):
        at = 0
        for side in sides:
            rows = side.shape[0]
            turned_ref[:, at : at + rows] = side[...].T
            at += rows

    @pl.when(step == 0)
    def _():
        load(lefts)

    @pl.when(step == switch * steps)
    def _():
        load(others)

    right = jnp.concatenate([ref[0] for ref in rights], 0)
    total = mm(turned_ref[...], right).astype(BF16)
    depth = total.shape[0] // 16
    width = keep_ref.shape[-1]
    for z in range(total.shape[1] // width):
        cols = slice(z * width, (z + 1) * width)
        for p in range(8):
            at = 2 * p * depth
            even, odd = total[at : at + depth, cols], total[at + depth : at + 2 * depth, cols]
            keep_ref[p, z, 0] = jnp.where(low, even, odd)
            send_ref[p, z, 0] = jnp.where(low, odd, even)


def weight_grads(core, lefts, others, rights, switch, steps):
    parts = len(lefts)
    kinds, _, width = rights[0].shape
    block, half = width // steps, width // 2
    sides = [pl.BlockSpec((v.shape[0], D), lambda s: (0, 0)) for v in list(lefts) + list(others)]
    moving = [
        pl.BlockSpec((1, v.shape[1], block), lambda s: (s // steps, 0, s % steps)) for v in rights
    ]
    rows = sum(v.shape[1] for v in rights)
    out = pl.pallas_call(
        functools.partial(weight_grad_kernel, parts=parts, switch=switch, steps=steps),
        grid=(kinds * steps,),
        in_specs=[pl.BlockSpec(memory_space=pltpu.SMEM)] + sides + moving,
        out_specs=[
            pl.BlockSpec((8, 2 // steps, 1, 64, half), lambda s: (0, s % steps, s // steps, 0, 0))
        ]
        * 2,
        out_shape=[jax.ShapeDtypeStruct((8, 2, kinds, 64, half), BF16)] * 2,
        scratch_shapes=[pltpu.VMEM((D, rows), BF16)],
        compiler_params=pltpu.CompilerParams(vmem_limit_bytes=48 * 2**20),
        cost_estimate=pl.CostEstimate(
            flops=2 * kinds * rows * D * width,
            bytes_accessed=2 * kinds * D * width + 4 * rows * D + 2 * kinds * rows * width,
            transcendentals=0,
        ),
    )(core, *lefts, *others, *rights)
    return [v.reshape(16, kinds, 64, half) for v in out]


def head_sums(values):
    wide = values.shape[1]
    row = lax.broadcasted_iota(jnp.int32, (wide, wide), 0) // HEAD_DIM
    same = (row == lanes_of((wide, wide)) // HEAD_DIM).astype(BF16)
    high = values.astype(BF16)
    low = (values - high.astype(F32)).astype(BF16)
    return mm(high, same) + mm(low, same)


def partner(values):
    wide = values.shape[1]
    first = lanes_of(values.shape) % HEAD_DIM < HALF
    return jnp.where(first, pltpu.roll(values, wide - HALF, 1), pltpu.roll(values, HALF, 1))


def angles_of(facts, freq_ref):
    facts = facts.astype(F32)
    times = facts[:, 3:4] * 32.0 + facts[:, 4:5]
    angle = times * freq_ref[0:1, :WIDE]
    first = lanes_of(angle.shape) % HEAD_DIM < HALF
    cosine = jnp.cos(angle)
    sine = jnp.sin(angle)
    sine = jnp.where(first, -sine, sine)
    return jnp.concatenate([cosine, cosine], 1), jnp.concatenate([sine, sine], 1)


def project_kernel(core_ref, a_ref, w_ref, freq_ref, mine_ref, send_ref, raw_ref):
    low = core_ref[0] == 0
    rows = a_ref[:, :D]
    cosine, sine = angles_of(a_ref[:, D:], freq_ref)

    def emit(kind, value):
        left, right = value[:, :WIDE], value[:, WIDE:]
        mine_ref[kind] = jnp.where(low, left, right).astype(BF16)
        send_ref[kind] = jnp.where(low, right, left).astype(BF16)

    for kind in range(2):
        raw = mm(rows, w_ref[kind])
        raw_ref[kind] = raw
        unit = raw * lax.rsqrt(head_sums(raw * raw) * (1.0 / HEAD_DIM) + EPS)
        value = unit * freq_ref[1 + kind : 2 + kind, :]
        value = value * cosine + partner(value) * sine
        if kind == 0:
            value = value * (HEAD_DIM ** (-0.5) * LOG2E)
        emit(kind, value)
    emit(2, mm(rows, w_ref[2]))


def project(core, rows_all, attn_w, freq):
    block = 512
    both = pl.BlockSpec((3, block, WIDE), lambda i: (0, i, 0))
    low = jax.ShapeDtypeStruct((3, PLANE, WIDE), BF16)
    return pl.pallas_call(
        project_kernel,
        grid=(PLANE // block,),
        in_specs=[
            pl.BlockSpec(memory_space=pltpu.SMEM),
            pl.BlockSpec((block, D + WIDE), lambda i: (i, 0)),
            pl.BlockSpec((3, D, 2 * WIDE), lambda i: (0, 0, 0)),
            pl.BlockSpec((8, 2 * WIDE), lambda i: (0, 0)),
        ],
        out_specs=[both, both, pl.BlockSpec((2, block, 2 * WIDE), lambda i: (0, i, 0))],
        out_shape=[low, low, jax.ShapeDtypeStruct((2, PLANE, 2 * WIDE), F32)],
        compiler_params=pltpu.CompilerParams(vmem_limit_bytes=48 * 2**20),
        cost_estimate=pl.CostEstimate(
            flops=8 * PLANE * D * 2 * WIDE, bytes_accessed=PLANE * D * 8, transcendentals=PLANE * 1024
        ),
    )(core, rows_all, attn_w, freq)


def unproject_kernel(
    core_ref, mine_ref, got_ref, raw_ref, facts_ref, w_ref, freq_ref, dp_ref, part_ref, gain_ref
):
    low = core_ref[0] == 0
    cosine, sine = angles_of(facts_ref[...], freq_ref)

    @pl.when(pl.program_id(0) == 0)
    def _():
        gain_ref[...] = jnp.zeros_like(gain_ref)

    total = None
    for kind in range(3):
        mine, got = mine_ref[kind], got_ref[kind]
        grad = jnp.concatenate([jnp.where(low, mine, got), jnp.where(low, got, mine)], 1)
        if kind < 2:
            grad = grad.astype(F32)
            if kind == 0:
                grad = grad * (HEAD_DIM ** (-0.5))
            raw = raw_ref[kind]
            inv = lax.rsqrt(head_sums(raw * raw) * (1.0 / HEAD_DIM) + EPS)
            unit = raw * inv
            grad = grad * cosine - partner(grad) * sine
            gain_ref[kind : kind + 1, :] += jnp.sum(grad * unit, axis=0, keepdims=True)
            scaled = grad * freq_ref[1 + kind : 2 + kind, :]
            mean = head_sums(scaled * unit) * (1.0 / HEAD_DIM)
            grad = (inv * (scaled - unit * mean)).astype(BF16)
        dp_ref[kind] = grad
        part = mm(grad, w_ref[kind], NT)
        total = part if total is None else total + part
    part_ref[...] = total.astype(BF16)


def unproject(core, mine, got, raw, rows_all, attn_w, freq):
    block = 512
    both = pl.BlockSpec((3, block, WIDE), lambda i: (0, i, 0))
    return pl.pallas_call(
        unproject_kernel,
        grid=(PLANE // block,),
        in_specs=[
            pl.BlockSpec(memory_space=pltpu.SMEM),
            both,
            both,
            pl.BlockSpec((2, block, 2 * WIDE), lambda i: (0, i, 0)),
            pl.BlockSpec((block, WIDE), lambda i: (i, D // WIDE)),
            pl.BlockSpec((3, D, 2 * WIDE), lambda i: (0, 0, 0)),
            pl.BlockSpec((8, 2 * WIDE), lambda i: (0, 0)),
        ],
        out_specs=[
            pl.BlockSpec((3, block, 2 * WIDE), lambda i: (0, i, 0)),
            pl.BlockSpec((block, D), lambda i: (i, 0)),
            pl.BlockSpec((8, 2 * WIDE), lambda i: (0, 0)),
        ],
        out_shape=[
            jax.ShapeDtypeStruct((3, PLANE, 2 * WIDE), BF16),
            jax.ShapeDtypeStruct((PLANE, D), BF16),
            jax.ShapeDtypeStruct((8, 2 * WIDE), F32),
        ],
        compiler_params=pltpu.CompilerParams(vmem_limit_bytes=48 * 2**20),
        cost_estimate=pl.CostEstimate(
            flops=8 * PLANE * D * 2 * WIDE, bytes_accessed=PLANE * D * 8, transcendentals=PLANE * 1024
        ),
    )(core, mine, got, raw, rows_all, attn_w, freq)


LOG_LANE = 3 * VARIATES + SEQS


def with_pieces(base, values, first_lane, lanes):
    for i in range(3):
        part = values.astype(BF16).astype(F32)
        base = jnp.where(lanes == first_lane + i, part, base)
        values = values - part
    return base


def attend_kernel(qkv_ref, all_ref, qt_ref, kt_ref, vt_ref, att_ref, low_ref, tail_ref, *, chunks):
    size = all_ref.shape[1] // chunks
    query = jnp.concatenate([qkv_ref[0], qt_ref[...]], 1)
    zero = jnp.zeros_like(query)
    head_of = (lanes_of(query.shape) // HEAD_DIM) % 2
    lanes = lanes_of((query.shape[0], WIDE))
    out = None
    tail = qt_ref[...].astype(F32)
    for head in range(2):
        masked = jnp.where(head_of == head, query, zero)
        total = None
        for c in range(chunks):
            rows = pl.ds(c * size, size)
            keys = jnp.concatenate([all_ref[1, rows, :], kt_ref[rows, :]], 1)
            values = jnp.concatenate([all_ref[2, rows, :], vt_ref[rows, :]], 1)
            prob = jnp.exp2(mm(masked, keys, NT)).astype(BF16)
            part = mm(prob, values)
            total = part if total is None else total + part
        row_sum = total[:, WIDE : WIDE + 1]
        here = total[:, :WIDE] / row_sum
        out = here if head == 0 else jnp.where(lanes < HEAD_DIM, out, here)
        tail = with_pieces(tail, -jnp.log2(row_sum), head * HEAD_DIM + LOG_LANE, lanes)
    att_ref[...] = out
    low_ref[...] = out.astype(BF16)
    tail_ref[...] = tail.astype(BF16)


def attend(qkv, query_tail, key_tail, value_tail):
    block = 512
    rows = qkv.shape[1]
    moving = pl.BlockSpec((block, WIDE), lambda i: (i, 0))
    fixed = pl.BlockSpec((rows, WIDE), lambda i: (0, 0))
    low = jax.ShapeDtypeStruct((rows, WIDE), BF16)
    return pl.pallas_call(
        functools.partial(attend_kernel, chunks=4),
        grid=(rows // block,),
        in_specs=[
            pl.BlockSpec((1, block, WIDE), lambda i: (0, i, 0)),
            pl.BlockSpec((3, rows, WIDE), lambda i: (0, 0, 0)),
            moving,
            fixed,
            fixed,
        ],
        out_specs=[moving, moving, moving],
        out_shape=[jax.ShapeDtypeStruct((rows, WIDE), F32), low, low],
        compiler_params=pltpu.CompilerParams(vmem_limit_bytes=48 * 2**20),
        cost_estimate=pl.CostEstimate(
            flops=16 * rows * rows * WIDE, bytes_accessed=rows * WIDE * 24, transcendentals=2 * rows * rows
        ),
    )(qkv, qkv, query_tail, key_tail, value_tail)


def attend_back_kernel(
    qkv_ref, all_ref, qt_ref, kt_ref, vt_ref, hot_ref, grad_ref, att_ref,
    dq_ref, dk_ref, dv_ref, bias_ref, dk_sum, dv_sum, *, chunks
):
    size = all_ref.shape[1] // chunks
    step = pl.program_id(0)
    query = jnp.concatenate([qkv_ref[0], qt_ref[...]], 1)
    grad = grad_ref[...]
    zero = jnp.zeros_like(query)
    head_of = (lanes_of(query.shape) // HEAD_DIM) % 2
    lanes = lanes_of((query.shape[0], WIDE))
    overlap = grad.astype(F32) * att_ref[...]

    @pl.when(step == 0)
    def _():
        dk_sum[...] = jnp.zeros_like(dk_sum)
        dv_sum[...] = jnp.zeros_like(dv_sum)

    out = None
    for head in range(2):
        mine = head_of[:, :WIDE] == head
        masked = jnp.where(head_of == head, query, zero)
        grad_here = jnp.where(mine, grad, zero[:, :WIDE])
        dots = jnp.sum(jnp.where(mine, overlap, 0.0), axis=1, keepdims=True)
        extra = with_pieces(jnp.zeros(lanes.shape, F32), -dots, 0, lanes).astype(BF16)
        grad_wide = jnp.concatenate([grad_here, extra], 1)
        total = None
        for c in range(chunks):
            rows = pl.ds(c * size, size)
            keys = all_ref[1, rows, :]
            prob = jnp.exp2(mm(jnp.concatenate([keys, kt_ref[rows, :]], 1), masked, NT))
            slope = mm(jnp.concatenate([all_ref[2, rows, :], vt_ref[rows, :]], 1), grad_wide, NT)
            d_score = (prob * slope).astype(BF16)
            dv_sum[rows, :] += mm(prob.astype(BF16), grad_here)
            dk_sum[rows, :] += mm(d_score, masked)
            part = mm(d_score, keys, TN)
            total = part if total is None else total + part
        out = total if head == 0 else jnp.where(lanes < HEAD_DIM, out, total)
    dq_ref[...] = out.astype(BF16)

    @pl.when(step == pl.num_programs(0) - 1)
    def _():
        dk_ref[...] = (dk_sum[:, :WIDE] * (1.0 / LOG2E)).astype(BF16)
        dv_ref[...] = dv_sum[...].astype(BF16)
        counts = dk_sum[:, WIDE:]
        bias_ref[...] = jnp.zeros_like(bias_ref)
        bias_ref[0:1, :] = jnp.sum(counts * hot_ref[...].astype(F32), axis=0, keepdims=True)
        bias_ref[1:2, :] = jnp.sum(counts, axis=0, keepdims=True)


def attend_back(qkv, query_tail, key_tail, value_tail, query_hot, grad, attended):
    block = 512
    rows = qkv.shape[1]
    moving = pl.BlockSpec((block, WIDE), lambda i: (i, 0))
    fixed = pl.BlockSpec((rows, WIDE), lambda i: (0, 0))
    low = jax.ShapeDtypeStruct((rows, WIDE), BF16)
    return pl.pallas_call(
        functools.partial(attend_back_kernel, chunks=4),
        grid=(rows // block,),
        in_specs=[
            pl.BlockSpec((1, block, WIDE), lambda i: (0, i, 0)),
            pl.BlockSpec((3, rows, WIDE), lambda i: (0, 0, 0)),
            moving,
            fixed,
            fixed,
            fixed,
            moving,
            moving,
        ],
        out_specs=[moving, fixed, fixed, pl.BlockSpec((8, WIDE), lambda i: (0, 0))],
        out_shape=[low, low, low, jax.ShapeDtypeStruct((8, WIDE), F32)],
        scratch_shapes=[pltpu.VMEM((rows, 2 * WIDE), F32), pltpu.VMEM((rows, WIDE), F32)],
        compiler_params=pltpu.CompilerParams(vmem_limit_bytes=48 * 2**20),
        cost_estimate=pl.CostEstimate(
            flops=40 * rows * rows * WIDE, bytes_accessed=rows * WIDE * 24, transcendentals=2 * rows * rows
        ),
    )(qkv, qkv, query_tail, key_tail, value_tail, query_hot, grad, attended)


def feed_kernel(b_ref, g_ref, w_ref, y_ref, db_ref, act_ref, y_sum, db_sum):
    step = pl.program_id(0)
    rows = b_ref[...]
    gate_w, up_w, down_w = w_ref[0], w_ref[1], w_ref[2]
    gate = mm(rows, gate_w)
    up = mm(rows, up_w)
    d_hidden = mm(g_ref[...], down_w)
    sig = 1.0 / (1.0 + jnp.exp(-gate))
    silu = gate * sig
    hidden = (silu * up).astype(BF16)
    d_gate = (d_hidden * up * (sig * (1.0 + gate * (1.0 - sig)))).astype(BF16)
    d_up = (d_hidden * silu).astype(BF16)
    act_ref[0] = d_gate
    act_ref[1] = d_up
    act_ref[2] = hidden
    y_part = mm(hidden, down_w, NT)
    db_part = mm(d_gate, gate_w, NT) + mm(d_up, up_w, NT)

    @pl.when(step == 0)
    def _():
        y_sum[...] = y_part
        db_sum[...] = db_part

    @pl.when(step > 0)
    def _():
        y_sum[...] += y_part
        db_sum[...] += db_part

    @pl.when(step == pl.num_programs(0) - 1)
    def _():
        y_ref[...] = y_sum[...].astype(BF16)
        db_ref[...] = db_sum[...].astype(BF16)


def feed(rows_b, rows_g, weights):
    rows = rows_b.shape[0]
    width = weights.shape[2]
    block = 256
    whole = pl.BlockSpec((rows, D), lambda f: (0, 0))
    part = pl.BlockSpec((3, rows, block), lambda f: (0, 0, f))
    low_d = jax.ShapeDtypeStruct((rows, D), BF16)
    low_f = jax.ShapeDtypeStruct((3, rows, width), BF16)
    return pl.pallas_call(
        feed_kernel,
        grid=(width // block,),
        in_specs=[whole, whole, pl.BlockSpec((3, D, block), lambda f: (0, 0, f))],
        out_specs=[whole, whole, part],
        out_shape=[low_d, low_d, low_f],
        scratch_shapes=[pltpu.VMEM((rows, D), F32)] * 2,
        compiler_params=pltpu.CompilerParams(vmem_limit_bytes=48 * 2**20),
        cost_estimate=pl.CostEstimate(
            flops=12 * rows * D * width, bytes_accessed=6 * D * width + rows * D * 8 + rows * width * 6,
            transcendentals=rows * width,
        ),
    )(rows_b, rows_g, weights)


def body(
    tokens,
    cotangent,
    destination,
    variate_ids,
    time_ids,
    seq_lengths,
    qkv_weight,
    out_weight,
    gate_up_weight,
    down_weight,
    norm_gains,
    qk_gains,
    variate_bias,
):
    core = lax.axis_index("core")
    low_core = core == 0
    y_at = lax.axis_index("y")
    zl_at = lax.axis_index("zl")

    core_scalar = core.reshape(1).astype(jnp.int32)

    def side_by_side(mine, other):
        return jnp.concatenate(
            [jnp.where(low_core, mine, other), jnp.where(low_core, other, mine)], axis=-1
        )

    attn_shard = jnp.concatenate([qkv_weight, out_weight.T[None]], 0)
    feed_shard = jnp.concatenate([gate_up_weight, down_weight.T[None]], 0)
    attn_mine = gather_round(attn_shard, ("zh", "zl"), lax.axis_index("zh") * 2 + zl_at)
    attn_mine = gather_round(attn_mine, "x", lax.axis_index("x")).reshape((16,) + attn_shard.shape)
    attn_w = assemble(core_scalar, attn_mine, swap_core(attn_mine), 2)

    slot = destination % ROWS
    group_at = destination // GROUP
    block_at = (destination % GROUP) // ROWS
    device_at = ((group_at // 2) * 2 + block_at // 4) * 8 + (block_at % 4) * 2 + group_at % 2
    key = device_at * ROWS + slot
    zero = jnp.zeros_like(slot)
    facts = jnp.stack([key, slot, variate_ids, time_ids // 32, time_ids % 32, zero, zero, zero])
    gains_row = jnp.pad(
        norm_gains.reshape(8, 16), ((0, 0), (GAIN_LANE, WIDE - GAIN_LANE - 16))
    ).astype(F32)
    outgoing, deal = deal_rows(tokens, cotangent, facts.astype(F32), gains_row)
    arrived = lax.all_to_all(outgoing.reshape(DEVICES, 8, SPAN), ALL, 0, 0, tiled=True)
    arrived, attn_w = lax.optimization_barrier((arrived, attn_w))

    lengths_other = swap_core(seq_lengths)
    lengths = jnp.where(zl_at == core, seq_lengths, lengths_other)[0]
    bias_other = lax.ppermute(variate_bias, "zl", [(0, 1), (1, 0)])
    bias_pair = jnp.where(zl_at == core, variate_bias, bias_other)

    all_gains = arrived.reshape(16, 8, 8, SPAN)[:, 0, :, D + GAIN_LANE : D + GAIN_LANE + 16]
    inputs, grad_rows, attn_all, place, gains = receive(
        arrived.reshape(4 * ROWS, SPAN), all_gains.reshape(16, WIDE)
    )
    gain_two = gains[1]
    feed_shard, attn_all = lax.optimization_barrier((feed_shard, attn_all))
    feed_mine = flat_gather(feed_shard)
    grad_all = gather_direct(grad_rows)

    variates_own = attn_all[:, D + 2].astype(jnp.int32)
    variates = jnp.concatenate([variates_own, swap_core(variates_own)])
    blocks_y = (y_at + jnp.arange(RING)) % RING
    blocks = jnp.concatenate([core * RING + blocks_y, (1 - core) * RING + blocks_y])
    positions = (blocks[:, None] * ROWS + jnp.arange(ROWS)[None, :]).reshape(GROUP)
    segments = jnp.sum((positions[:, None] >= jnp.cumsum(lengths)[None, :]).astype(jnp.int32), 1)

    inverse = THETA ** (-2.0 * jnp.arange(HALF).astype(F32) / HEAD_DIM)
    freq = jnp.concatenate(
        [
            jnp.tile(inverse, 8)[None],
            jnp.tile(qk_gains, (1, 4)),
            jnp.zeros((5, 2 * WIDE), F32),
        ]
    )
    qkv_mine, qkv_send, raw = project(core_scalar, attn_all, attn_w, freq)
    qkv = jnp.concatenate([qkv_mine, swap_core(qkv_send)], axis=1)

    lane = jnp.arange(WIDE)[None, :]
    tail_lane = lane % HEAD_DIM
    bias_lane = tail_lane < 3 * VARIATES
    seg_lane = (tail_lane >= 3 * VARIATES) & (tail_lane < LOG_LANE)
    one_lane = (tail_lane >= LOG_LANE) & (tail_lane < LOG_LANE + 3)
    equal = bias_lane & (tail_lane % VARIATES == variates[:, None])
    inside = seg_lane & (tail_lane - 3 * VARIATES == segments[:, None])
    query_tail = (equal | inside).astype(BF16)
    bias_parts = jnp.stack(pieces(bias_pair * LOG2E, 3)).astype(F32)
    bias_rows = jnp.repeat(bias_parts, VARIATES, axis=0).transpose(1, 2, 0)
    bias_rows = jnp.pad(bias_rows, ((0, 0), (0, 0), (0, HEAD_DIM - 3 * VARIATES))).reshape(2, WIDE)
    key_tail = jnp.where(equal, bias_rows[0:1], bias_rows[1:2])
    key_tail = jnp.where(seg_lane, jnp.where(inside, 0.0, FAR), key_tail)
    key_tail = jnp.where(one_lane, 1.0, key_tail).astype(BF16)
    value_tail = jnp.broadcast_to((lane < 3).astype(BF16), (GROUP, WIDE))
    attended, att_low, query_back = attend(qkv, query_tail, key_tail, value_tail)
    att_low, grad_all = lax.optimization_barrier((att_low, grad_all))
    att_other = swap_core(att_low[PLANE:])
    att_other, feed_mine = lax.optimization_barrier((att_other, feed_mine))
    feed_w = assemble(core_scalar, feed_mine, swap_core(feed_mine), 4)
    att_plane = side_by_side(att_low[:PLANE], att_other)
    out_part = mm(att_plane, attn_w[3], NT).astype(BF16).reshape(RING, ROWS, D)
    got = send_ring([out_part[r] for r in range(RING)])
    got[0], feed_w = lax.optimization_barrier((got[0], feed_w))
    hidden_one = inputs + add_ring(out_part[0], got)

    scale_two = root_stats(hidden_one)
    normed_two = hidden_one * scale_two
    feed_in = (normed_two * gain_two).astype(BF16)
    ahead, behind = ring(feed_in, -1), ring(feed_in, 1)
    fed_own = feed(feed_in, grad_all[0], feed_w)
    ahead, behind, fed_own = lax.optimization_barrier((ahead, behind, fed_own))
    far_top, far_low = ring(ahead[: ROWS // 2], -1), ring(behind[ROWS // 2 :], 1)
    fed_ahead = feed(ahead, grad_all[1], feed_w)
    fed_behind = feed(behind, grad_all[3], feed_w)
    far_top, far_low, fed_ahead, fed_behind = lax.optimization_barrier(
        (far_top, far_low, fed_ahead, fed_behind)
    )
    far = jnp.concatenate([far_top, far_low], 0)
    fed_far = feed(far, grad_all[2], feed_w)
    feed_all = [feed_in, ahead, far, behind]
    fed = [fed_own, fed_ahead, fed_far, fed_behind]
    feed_split = weight_grads(core_scalar, feed_all, grad_all, [f[2] for f in fed], 2, 2)
    db_got = send_ring([f[1] for f in fed])
    db_got, feed_split = lax.optimization_barrier((db_got, feed_split))
    grad_normed_two = add_ring(fed_own[1], db_got)

    gain_two_grad = jnp.sum(grad_normed_two * normed_two, axis=0)
    grad_one = grad_rows.astype(F32) + norm_back(grad_normed_two * gain_two, normed_two, scale_two)

    grad_one_all = gather_direct(grad_one.astype(BF16))
    feed_total = chip_total(feed_split)
    feed_arrived = plane_total(feed_total)
    grad_one_all, feed_total = lax.optimization_barrier((grad_one_all, feed_total))
    grad_one_all = jnp.concatenate(grad_one_all, 0)
    y_parts, grad_one_all = lax.optimization_barrier(([f[0] for f in fed], grad_one_all))
    y_got = send_ring(y_parts)
    grad_att = mm(grad_one_all, attn_w[3]).astype(BF16)
    grad_left, grad_right = grad_att[:, :WIDE], grad_att[:, WIDE:]
    grad_send = jnp.where(low_core, grad_right, grad_left)
    grad_mine = jnp.where(low_core, grad_left, grad_right)
    grad_mine = jnp.concatenate([grad_mine, swap_core(grad_send)], 0)
    d_query, d_key, d_value, bias_sums = attend_back(
        qkv, query_back, key_tail, value_tail, query_tail, grad_mine, attended
    )
    first_part = (jnp.arange(HEAD_DIM) < VARIATES)[None, None]
    bias_sums = jnp.where(first_part, bias_sums[:2].reshape(2, 2, HEAD_DIM), 0.0)
    bias_sums = jnp.sum(bias_sums, axis=2)
    bias_part = jnp.stack([bias_sums[0], bias_sums[1] - bias_sums[0]])
    d_query, y_got, feed_arrived = lax.optimization_barrier((d_query, y_got, feed_arrived))
    mixed = (hidden_one + add_ring(y_parts[0], y_got)).astype(BF16)
    d_mine = jnp.stack([d_query[:PLANE], d_key[:PLANE], d_value[:PLANE]])
    d_got = swap_core(jnp.stack([d_query[PLANE:], d_key[PLANE:], d_value[PLANE:]]))
    grad_proj, in_part, qk_sums = unproject(
        core_scalar, d_mine, d_got, raw, attn_all, attn_w, freq
    )
    in_part = in_part.reshape(RING, ROWS, D)
    in_got = send_ring([in_part[r] for r in range(RING)])
    attn_split = weight_grads(
        core_scalar,
        [attn_all],
        [grad_one_all],
        [jnp.concatenate([grad_proj, att_plane[None]], 0)],
        3,
        1,
    )
    attn_total = chip_total(attn_split)
    in_got, _ = lax.optimization_barrier((in_got, attn_split))
    mixed, _ = lax.optimization_barrier((mixed, attn_total))
    feed_grad = jnp.sum(feed_arrived.astype(F32), axis=0)
    qk_sums = jnp.sum(qk_sums[:2].reshape(2, 4, HEAD_DIM), axis=1)

    small = jnp.zeros((8, WIDE), F32).at[0].set(qk_sums.reshape(WIDE))
    small = small.at[1, :4].set(bias_part.reshape(4))
    tensor_at = (y_at * 2 + core).reshape(1).astype(jnp.int32)
    last = finish(
        in_part[0], in_got, inputs, grad_one, mixed, place, gains, gain_two_grad[None], small, tensor_at
    )
    span = last.shape[1]
    last = last.reshape(DEVICES, 2, span)
    attn_grad, home = plane_rounds(
        attn_total, last, lambda values: lax.all_to_all(values, ALL, 0, 0, tiled=True)
    )
    rows_home = mm(deal, home[:, :, : 2 * D].reshape(ROWS, 2 * D), TN).astype(BF16)
    new_tokens, token_grads = rows_home[:, :D], rows_home[:, D:]
    sums = jnp.sum(home[:, :, 2 * D :].astype(F32), axis=(0, 1))
    gains_grad = sums[:WIDE].reshape(2, 64)
    qk_grad = sums[WIDE : 2 * WIDE].reshape(2, 64)
    bias_grad = sums[2 * WIDE : 2 * WIDE + 4].reshape(2, 2)

    return (
        new_tokens,
        token_grads,
        attn_grad[:3],
        attn_grad[3].T,
        feed_grad[:2],
        feed_grad[2].T,
        gains_grad,
        qk_grad,
        bias_grad,
    )


def solution(mesh):
    fine = Mesh(mesh.devices.reshape(4, 2, 2, 4, 2), ALL)
    dp = ("x", "zh", "core")
    tensor = ("y", "zl")
    in_specs = (
        P(ALL, None),
        P(ALL, None),
        P(ALL),
        P(ALL),
        P(ALL),
        P(dp, None),
        P(None, dp, tensor),
        P(tensor, dp),
        P(None, dp, tensor),
        P(tensor, dp),
        P(None, dp),
        P(),
        P(None, tensor),
    )
    out_specs = (
        P(ALL, None),
        P(ALL, None),
        P(None, dp, tensor),
        P(tensor, dp),
        P(None, dp, tensor),
        P(tensor, dp),
        P(None, dp),
        P(),
        P(None, tensor),
    )
    return jax.shard_map(body, mesh=fine, in_specs=in_specs, out_specs=out_specs, check_vma=False)
```

```python
import functools

import jax
import jax.numpy as jnp
from jax import lax
from jax.experimental import pallas as pl
from jax.experimental.pallas import tpu as pltpu
from jax.sharding import Mesh
from jax.sharding import PartitionSpec as P

HEADS = 16
HEAD_DIM = 64
HALF = HEAD_DIM // 2
D = 1024
FF = 4096
ROWS = 256
RING = 4
PLANE = ROWS * RING
GROUP = 2 * PLANE
DEVICES = 128
VARIATES = 8
SEQS = 4
WIDE = 128
EPS = 1e-06
THETA = 10000.0
LOG2E = 1.4426950408889634
FAR = -16384.0
F32 = jnp.float32
BF16 = jnp.bfloat16

ALL = ("x", "zh", "core", "y", "zl")
FLAT = ("x", "zh", "zl")
NT = (((1,), (1,)), ((), ()))
TN = (((0,), (0,)), ((), ()))


def mm(left, right, dims=(((1,), (0,)), ((), ()))):
    return lax.dot_general(left, right, dims, preferred_element_type=F32)


def root_stats(values):
    return lax.rsqrt(jnp.mean(values * values, axis=-1, keepdims=True) + EPS)


def norm_back(grad_in, normed, scale_inv):
    return scale_inv * (grad_in - normed * jnp.mean(grad_in * normed, axis=-1, keepdims=True))


def pieces(values, count):
    out = []
    for _ in range(count):
        part = lax.reduce_precision(values, 8, 7)
        out.append(part.astype(BF16))
        values = values - part
    return out


def ring(values, step):
    return lax.ppermute(values, "y", [(i, (i + step) % RING) for i in range(RING)])


def swap_core(values):
    return lax.ppermute(values, "core", [(0, 1), (1, 0)])


def gather_ring(values):
    ahead = ring(values, -1)
    behind = ring(values, 1)
    half = values.shape[0] // 2
    far_top = ring(ahead[:half], -1)
    far_low = ring(behind[half:], 1)
    return [values, ahead, jnp.concatenate([far_top, far_low], 0), behind]


def gather_direct(values):
    return [values, ring(values, -1), ring(values, 2), ring(values, 1)]


def send_ring(parts, halves=False):
    half = parts[2].shape[0] // 2
    far = [parts[2][:half], parts[2][half:]] if halves else [parts[2]]
    return [ring(parts[1], 1), ring(parts[3], -1)] + [ring(v, 2) for v in far]


def add_ring(own, got):
    far = got[2] if len(got) == 3 else jnp.concatenate(got[2:], 0)
    return own.astype(F32) + got[0].astype(F32) + got[1].astype(F32) + far.astype(F32)


def gather_round(values, axes, at):
    moves = [[((i + r) % RING, i) for i in range(RING)] for r in range(RING)]
    rows = [values] + [lax.ppermute(values, axes, moves[r]) for r in range(1, RING)]
    return jnp.roll(jnp.stack(rows), at, axis=0)


def flat_gather(shard):
    many = jnp.broadcast_to(shard[None], (16,) + shard.shape)
    return lax.all_to_all(many, FLAT, 0, 0, tiled=True)


def assemble_kernel(core_ref, mine_ref, other_ref, out_ref):
    core = core_ref[0]
    count, _, depth, width = mine_ref.shape
    for ref, side in ((mine_ref, core), (other_ref, 1 - core)):
        for i in range(count):
            at = (i // 2) * 2 * depth + side * depth
            rows = pl.ds(pl.multiple_of(at, depth), depth)
            out_ref[:, rows, (i % 2) * width : (i % 2 + 1) * width] = ref[i]


def assemble(core, mine, other, steps):
    _, kinds, depth, width = mine.shape
    pair = pl.BlockSpec((16 // steps, kinds, depth, width), lambda p: (p, 0, 0, 0))
    return pl.pallas_call(
        assemble_kernel,
        grid=(steps,),
        in_specs=[pl.BlockSpec(memory_space=pltpu.SMEM), pair, pair],
        out_specs=pl.BlockSpec((kinds, 16 // steps * depth, 2 * width), lambda p: (0, p, 0)),
        out_shape=jax.ShapeDtypeStruct((kinds, 16 * depth, 2 * width), BF16),
        compiler_params=pltpu.CompilerParams(vmem_limit_bytes=28 * 2**20),
        cost_estimate=pl.CostEstimate(
            flops=0, bytes_accessed=kinds * 128 * depth * width, transcendentals=0
        ),
    )(core, mine, other)


def chip_total(split):
    return (split[0].astype(F32) + swap_core(split[1]).astype(F32)).astype(BF16)


def send_round(values, axes):
    at = lax.axis_index(axes)
    parts = [lax.dynamic_index_in_dim(values, (at + r) % RING, 0, keepdims=False) for r in range(RING)]
    moves = [[(i, (i + r) % RING) for i in range(RING)] for r in range(RING)]
    return parts[0], [lax.ppermute(parts[r], axes, moves[r]) for r in (1, 3, 2)]


def add_round(own, got):
    return sum((v.astype(F32) for v in got), own.astype(F32))


def trade(values, axes):
    return lax.all_to_all(values.reshape((RING, -1) + values.shape[1:]), axes, 0, 0, tiled=True)


def added(got):
    return jnp.sum(got.astype(F32), axis=0)


def lanes_of(shape):
    return lax.broadcasted_iota(jnp.int32, shape, 1)


QUARTER = D // RING
SPAN = D + WIDE + QUARTER
GAIN_LANE = 16


def deal_kernel(tok_ref, cot_ref, facts_ref, gains_ref, out_ref, deal_ref):
    wide = jnp.concatenate([facts_ref[...], jnp.zeros((WIDE - 8, ROWS), F32)], 0)
    facts = jnp.transpose(wide)
    keys = facts_ref[0:1, :]
    rank = jnp.sum((facts[:, 0:1] < keys).astype(F32), axis=0, keepdims=True)
    at = lax.broadcasted_iota(jnp.int32, (ROWS, ROWS), 0).astype(F32)
    deal_ref[...] = (at == rank).astype(BF16)
    low = jnp.where(lanes_of(facts.shape) == 0, 0.0, facts).astype(BF16)
    row = lax.broadcasted_iota(jnp.int32, (4 * ROWS, 1), 0)
    device, step, odd = row // 8, (row // 2) % RING, row % 2
    ahead = (device // 8) * 8 + ((device // 2 + step) % RING) * 2 + device % 2
    spread = ((2 * ahead + odd).astype(F32) == rank).astype(BF16)
    out_ref[:, :D] = mm(spread, tok_ref[...]).astype(BF16)
    tail = mm(spread, low)
    lane = lanes_of(tail.shape)
    gains = jnp.broadcast_to(gains_ref[...][None], (DEVICES, 8, WIDE)).reshape(tail.shape)
    tail = jnp.where((lane >= GAIN_LANE) & (lane < GAIN_LANE + 16), gains, tail)
    out_ref[:, D : D + WIDE] = tail.astype(BF16)
    own = ((2 * device + (row % 8) // RING).astype(F32) == rank).astype(BF16)
    part = None
    for m in range(RING):
        here = mm(own, cot_ref[:, m * QUARTER : (m + 1) * QUARTER])
        part = here if m == 0 else jnp.where(row % RING == m, here, part)
    out_ref[:, D + WIDE :] = part.astype(BF16)


def deal_rows(tokens, cotangent, facts, gains):
    return pl.pallas_call(
        deal_kernel,
        out_shape=[
            jax.ShapeDtypeStruct((4 * ROWS, SPAN), BF16),
            jax.ShapeDtypeStruct((ROWS, ROWS), BF16),
        ],
        compiler_params=pltpu.CompilerParams(vmem_limit_bytes=28 * 2**20),
        cost_estimate=pl.CostEstimate(
            flops=8 * ROWS * ROWS * 2304, bytes_accessed=ROWS * D * 16, transcendentals=0
        ),
    )(tokens, cotangent, facts, gains)


def receive_kernel(rows_ref, gains_ref, x_ref, g_ref, a_ref, place_ref, gain_ref):
    count = 4 * ROWS
    facts = rows_ref[:, D : D + WIDE]
    slots = jnp.transpose(facts.astype(F32))[1:2, :]
    at = lax.broadcasted_iota(jnp.int32, (ROWS, count), 0)
    arrival = lanes_of((ROWS, count))
    here = at.astype(F32) == slots
    gains = gains_ref[...].astype(F32)
    turned = pltpu.roll(gains, HEAD_DIM, 1)
    left = lanes_of((1, WIDE)) < HEAD_DIM
    one, two = [], []
    for c in range(D // WIDE):
        even, odd = slice(2 * c, 2 * c + 1), slice(2 * c + 1, 2 * c + 2)
        one.append(jnp.where(left, gains[even], turned[odd]))
        two.append(jnp.where(left, turned[even], gains[odd]))
    gain_one = jnp.concatenate(one, 1)
    gain_ref[...] = jnp.zeros_like(gain_ref)
    gain_ref[0:1, :] = gain_one
    gain_ref[1:2, :] = jnp.concatenate(two, 1)
    for r in range(RING):
        place = (here & ((arrival // 2) % RING == r)).astype(BF16)
        rows = mm(place, rows_ref[:, :D])
        block = slice(r * ROWS, (r + 1) * ROWS)
        a_ref[block, :D] = (rows * root_stats(rows) * gain_one).astype(BF16)
        a_ref[block, D:] = mm(place, facts).astype(BF16)
        if r == 0:
            x_ref[...] = rows
            first = place
    pick = ((at // 2) * 8 + at % 2 == arrival).astype(BF16)
    place = mm(first, pick, NT).astype(BF16)
    place_ref[...] = place
    for m in range(RING):
        pick = ((at // 2) * 8 + (at % 2) * RING + m == arrival).astype(BF16)
        quarter = mm(place, pick).astype(BF16)
        g_ref[:, m * QUARTER : (m + 1) * QUARTER] = mm(quarter, rows_ref[:, D + WIDE :]).astype(BF16)


def receive(rows, gains):
    return pl.pallas_call(
        receive_kernel,
        out_shape=[
            jax.ShapeDtypeStruct((ROWS, D), F32),
            jax.ShapeDtypeStruct((ROWS, D), BF16),
            jax.ShapeDtypeStruct((PLANE, D + WIDE), BF16),
            jax.ShapeDtypeStruct((ROWS, ROWS), BF16),
            jax.ShapeDtypeStruct((8, D), F32),
        ],
        compiler_params=pltpu.CompilerParams(vmem_limit_bytes=28 * 2**20),
        cost_estimate=pl.CostEstimate(
            flops=32 * ROWS * ROWS * D, bytes_accessed=ROWS * D * 24, transcendentals=0
        ),
    )(rows, gains)


def finish_kernel(
    own_ref, near_ref, back_ref, far_ref, x_ref, grad_ref, mixed_ref, place_ref,
    gain_ref, two_ref, small_ref, at_ref, out_ref,
):
    rows = x_ref[...]
    scale = root_stats(rows)
    normed = rows * scale
    far = far_ref[...].astype(F32)
    grad = own_ref[...].astype(F32) + near_ref[...].astype(F32) + back_ref[...].astype(F32) + far
    one = jnp.sum(grad * normed, axis=0, keepdims=True)
    two = two_ref[...]
    scaled = grad * gain_ref[0:1, :]
    back = scale * (scaled - normed * jnp.mean(scaled * normed, axis=1, keepdims=True))
    result = (grad_ref[...] + back).astype(BF16)
    count = 4 * ROWS
    row = lax.broadcasted_iota(jnp.int32, (count, 1), 0)
    quarter = row % RING
    pick = (row // RING == lanes_of((count, ROWS))).astype(BF16)
    pick = mm(pick, place_ref[...], NT).astype(BF16)
    part = None
    for m in range(RING):
        cols = slice(m * QUARTER, (m + 1) * QUARTER)
        here = mm(pick, jnp.concatenate([mixed_ref[:, cols], result[:, cols]], 1))
        part = here if m == 0 else jnp.where(quarter == m, here, part)
    out_ref[:, : 2 * QUARTER] = part.astype(BF16)
    left = lanes_of((1, WIDE)) < HEAD_DIM
    tiles = []
    for c in range(D // WIDE):
        cols = slice(c * WIDE, (c + 1) * WIDE)
        a, b = one[:, cols], two[:, cols]
        even = jnp.where(left, a, pltpu.roll(jnp.broadcast_to(b, (8, WIDE)), HEAD_DIM, 1)[0:1])
        odd = jnp.where(left, pltpu.roll(jnp.broadcast_to(a, (8, WIDE)), HEAD_DIM, 1)[0:1], b)
        tiles += [jnp.broadcast_to(even, (64, WIDE)), jnp.broadcast_to(odd, (64, WIDE))]
    value = jnp.concatenate(tiles, 0)
    value = jnp.where(quarter == 1, small_ref[0:1, :], value)
    bias = jnp.where((row // 8) % 8 == at_ref[0], small_ref[1:2, :], 0.0)
    value = jnp.where(quarter == 2, bias, value)
    high = value.astype(BF16).astype(F32)
    value = jnp.where((row // RING) % 2 == 0, high, value - high)
    out_ref[:, 2 * QUARTER :] = value.astype(BF16)


def finish(own, got, rows, grad, mixed, place, gains, two, small, at):
    specs = [pl.BlockSpec(memory_space=pltpu.VMEM)] * 11
    return pl.pallas_call(
        finish_kernel,
        in_specs=specs + [pl.BlockSpec(memory_space=pltpu.SMEM)],
        out_shape=jax.ShapeDtypeStruct((4 * ROWS, 2 * QUARTER + WIDE), BF16),
        compiler_params=pltpu.CompilerParams(vmem_limit_bytes=28 * 2**20),
        cost_estimate=pl.CostEstimate(
            flops=16 * ROWS * ROWS * D, bytes_accessed=ROWS * D * 20, transcendentals=0
        ),
    )(own, *got, rows, grad, mixed, place, gains, two, small, at)


def settle_kernel(home_ref, deal_ref, rows_ref, grads_ref, sums_ref):
    deal = deal_ref[...]
    shape = (ROWS, 4 * ROWS)
    index = lax.broadcasted_iota(jnp.int32, shape, 0)
    for m in range(RING):
        pick = (index * RING + m == lanes_of(shape)).astype(BF16)
        here = mm(pick, home_ref[:, : 2 * QUARTER]).astype(BF16)
        here = mm(deal, here, TN).astype(BF16)
        cols = slice(m * QUARTER, (m + 1) * QUARTER)
        rows_ref[:, cols] = here[:, :QUARTER]
        grads_ref[:, cols] = here[:, QUARTER:]
    small = home_ref[:, 2 * QUARTER :].astype(F32)
    quarter = lax.broadcasted_iota(jnp.int32, small.shape, 0) % RING
    sums_ref[...] = jnp.zeros_like(sums_ref)
    for m in range(3):
        sums_ref[m : m + 1, :] = jnp.sum(jnp.where(quarter == m, small, 0.0), axis=0, keepdims=True)


def settle(home, deal):
    low = jax.ShapeDtypeStruct((ROWS, D), BF16)
    return pl.pallas_call(
        settle_kernel,
        out_shape=[low, low, jax.ShapeDtypeStruct((8, WIDE), F32)],
        compiler_params=pltpu.CompilerParams(vmem_limit_bytes=28 * 2**20),
        cost_estimate=pl.CostEstimate(
            flops=20 * ROWS * ROWS * D, bytes_accessed=ROWS * D * 16, transcendentals=0
        ),
    )(home, deal)


def weight_grad_kernel(core_ref, *refs, parts, switch, steps):
    lefts, others, rights = refs[:parts], refs[parts : 2 * parts], refs[2 * parts : 3 * parts]
    keep_ref, send_ref, turned_ref = refs[3 * parts :]
    low = core_ref[0] == 0
    step = pl.program_id(0)

    def load(sides):
        at = 0
        for side in sides:
            rows = side.shape[0]
            turned_ref[:, at : at + rows] = side[...].T
            at += rows

    @pl.when(step == 0)
    def _():
        load(lefts)

    @pl.when(step == switch * steps)
    def _():
        load(others)

    right = jnp.concatenate([ref[0] for ref in rights], 0)
    total = mm(turned_ref[...], right).astype(BF16)
    depth = total.shape[0] // 16
    width = keep_ref.shape[-1]
    for z in range(total.shape[1] // width):
        cols = slice(z * width, (z + 1) * width)
        for p in range(8):
            at = 2 * p * depth
            even, odd = total[at : at + depth, cols], total[at + depth : at + 2 * depth, cols]
            keep_ref[p, z, 0] = jnp.where(low, even, odd)
            send_ref[p, z, 0] = jnp.where(low, odd, even)


def weight_grads(core, lefts, others, rights, switch, steps):
    parts = len(lefts)
    kinds, _, width = rights[0].shape
    block, half = width // steps, width // 2
    sides = [pl.BlockSpec((v.shape[0], D), lambda s: (0, 0)) for v in list(lefts) + list(others)]
    moving = [
        pl.BlockSpec((1, v.shape[1], block), lambda s: (s // steps, 0, s % steps)) for v in rights
    ]
    rows = sum(v.shape[1] for v in rights)
    out = pl.pallas_call(
        functools.partial(weight_grad_kernel, parts=parts, switch=switch, steps=steps),
        grid=(kinds * steps,),
        in_specs=[pl.BlockSpec(memory_space=pltpu.SMEM)] + sides + moving,
        out_specs=[
            pl.BlockSpec((8, 2 // steps, 1, 64, half), lambda s: (0, s % steps, s // steps, 0, 0))
        ]
        * 2,
        out_shape=[jax.ShapeDtypeStruct((8, 2, kinds, 64, half), BF16)] * 2,
        scratch_shapes=[pltpu.VMEM((D, rows), BF16)],
        compiler_params=pltpu.CompilerParams(vmem_limit_bytes=28 * 2**20),
        cost_estimate=pl.CostEstimate(
            flops=2 * kinds * rows * D * width,
            bytes_accessed=2 * kinds * D * width + 4 * rows * D + 2 * kinds * rows * width,
            transcendentals=0,
        ),
    )(core, *lefts, *others, *rights)
    return [v.reshape(16, kinds, 64, half) for v in out]


def head_sums(values):
    wide = values.shape[1]
    row = lax.broadcasted_iota(jnp.int32, (wide, wide), 0) // HEAD_DIM
    same = (row == lanes_of((wide, wide)) // HEAD_DIM).astype(BF16)
    high = values.astype(BF16)
    low = (values - high.astype(F32)).astype(BF16)
    return mm(high, same) + mm(low, same)


def partner(values):
    wide = values.shape[1]
    first = lanes_of(values.shape) % HEAD_DIM < HALF
    return jnp.where(first, pltpu.roll(values, wide - HALF, 1), pltpu.roll(values, HALF, 1))


def angles_of(facts, freq_ref):
    facts = facts.astype(F32)
    times = facts[:, 3:4] * 32.0 + facts[:, 4:5]
    angle = times * freq_ref[0:1, :WIDE]
    first = lanes_of(angle.shape) % HEAD_DIM < HALF
    cosine = jnp.cos(angle)
    sine = jnp.sin(angle)
    sine = jnp.where(first, -sine, sine)
    return jnp.concatenate([cosine, cosine], 1), jnp.concatenate([sine, sine], 1)


def project_kernel(core_ref, a_ref, w_ref, freq_ref, mine_ref, send_ref, raw_ref):
    low = core_ref[0] == 0
    rows = a_ref[:, :D]
    cosine, sine = angles_of(a_ref[:, D:], freq_ref)

    def emit(kind, value):
        left, right = value[:, :WIDE], value[:, WIDE:]
        mine_ref[kind] = jnp.where(low, left, right).astype(BF16)
        send_ref[kind] = jnp.where(low, right, left).astype(BF16)

    for kind in range(2):
        raw = mm(rows, w_ref[kind])
        raw_ref[kind] = raw
        unit = raw * lax.rsqrt(head_sums(raw * raw) * (1.0 / HEAD_DIM) + EPS)
        value = unit * freq_ref[1 + kind : 2 + kind, :]
        value = value * cosine + partner(value) * sine
        if kind == 0:
            value = value * (HEAD_DIM ** (-0.5) * LOG2E)
        emit(kind, value)
    emit(2, mm(rows, w_ref[2]))


def project(core, rows_all, attn_w, freq):
    block = 512
    both = pl.BlockSpec((3, block, WIDE), lambda i: (0, i, 0))
    low = jax.ShapeDtypeStruct((3, PLANE, WIDE), BF16)
    return pl.pallas_call(
        project_kernel,
        grid=(PLANE // block,),
        in_specs=[
            pl.BlockSpec(memory_space=pltpu.SMEM),
            pl.BlockSpec((block, D + WIDE), lambda i: (i, 0)),
            pl.BlockSpec((3, D, 2 * WIDE), lambda i: (0, 0, 0)),
            pl.BlockSpec((8, 2 * WIDE), lambda i: (0, 0)),
        ],
        out_specs=[both, both, pl.BlockSpec((2, block, 2 * WIDE), lambda i: (0, i, 0))],
        out_shape=[low, low, jax.ShapeDtypeStruct((2, PLANE, 2 * WIDE), F32)],
        compiler_params=pltpu.CompilerParams(vmem_limit_bytes=28 * 2**20),
        cost_estimate=pl.CostEstimate(
            flops=8 * PLANE * D * 2 * WIDE, bytes_accessed=PLANE * D * 8, transcendentals=PLANE * 1024
        ),
    )(core, rows_all, attn_w, freq)


def unproject_kernel(
    core_ref, mine_ref, got_ref, raw_ref, facts_ref, w_ref, freq_ref, dp_ref, part_ref, gain_ref
):
    low = core_ref[0] == 0
    cosine, sine = angles_of(facts_ref[...], freq_ref)

    @pl.when(pl.program_id(0) == 0)
    def _():
        gain_ref[...] = jnp.zeros_like(gain_ref)

    total = None
    for kind in range(3):
        mine, got = mine_ref[kind], got_ref[kind]
        grad = jnp.concatenate([jnp.where(low, mine, got), jnp.where(low, got, mine)], 1)
        if kind < 2:
            grad = grad.astype(F32)
            if kind == 0:
                grad = grad * (HEAD_DIM ** (-0.5))
            raw = raw_ref[kind]
            inv = lax.rsqrt(head_sums(raw * raw) * (1.0 / HEAD_DIM) + EPS)
            unit = raw * inv
            grad = grad * cosine - partner(grad) * sine
            gain_ref[kind : kind + 1, :] += jnp.sum(grad * unit, axis=0, keepdims=True)
            scaled = grad * freq_ref[1 + kind : 2 + kind, :]
            mean = head_sums(scaled * unit) * (1.0 / HEAD_DIM)
            grad = (inv * (scaled - unit * mean)).astype(BF16)
        dp_ref[kind] = grad
        part = mm(grad, w_ref[kind], NT)
        total = part if total is None else total + part
    part_ref[...] = total.astype(BF16)


def unproject(core, mine, got, raw, rows_all, attn_w, freq):
    block = 512
    both = pl.BlockSpec((3, block, WIDE), lambda i: (0, i, 0))
    return pl.pallas_call(
        unproject_kernel,
        grid=(PLANE // block,),
        in_specs=[
            pl.BlockSpec(memory_space=pltpu.SMEM),
            both,
            both,
            pl.BlockSpec((2, block, 2 * WIDE), lambda i: (0, i, 0)),
            pl.BlockSpec((block, WIDE), lambda i: (i, D // WIDE)),
            pl.BlockSpec((3, D, 2 * WIDE), lambda i: (0, 0, 0)),
            pl.BlockSpec((8, 2 * WIDE), lambda i: (0, 0)),
        ],
        out_specs=[
            pl.BlockSpec((3, block, 2 * WIDE), lambda i: (0, i, 0)),
            pl.BlockSpec((block, D), lambda i: (i, 0)),
            pl.BlockSpec((8, 2 * WIDE), lambda i: (0, 0)),
        ],
        out_shape=[
            jax.ShapeDtypeStruct((3, PLANE, 2 * WIDE), BF16),
            jax.ShapeDtypeStruct((PLANE, D), BF16),
            jax.ShapeDtypeStruct((8, 2 * WIDE), F32),
        ],
        compiler_params=pltpu.CompilerParams(vmem_limit_bytes=28 * 2**20),
        cost_estimate=pl.CostEstimate(
            flops=8 * PLANE * D * 2 * WIDE, bytes_accessed=PLANE * D * 8, transcendentals=PLANE * 1024
        ),
    )(core, mine, got, raw, rows_all, attn_w, freq)


LOG_LANE = 3 * VARIATES + SEQS


def with_pieces(base, values, first_lane, lanes):
    for i in range(3):
        part = values.astype(BF16).astype(F32)
        base = jnp.where(lanes == first_lane + i, part, base)
        values = values - part
    return base


def attend_kernel(qkv_ref, all_ref, qt_ref, kt_ref, vt_ref, att_ref, low_ref, tail_ref, *, chunks):
    size = all_ref.shape[1] // chunks
    query = jnp.concatenate([qkv_ref[0], qt_ref[...]], 1)
    zero = jnp.zeros_like(query)
    head_of = (lanes_of(query.shape) // HEAD_DIM) % 2
    lanes = lanes_of((query.shape[0], WIDE))
    out = None
    tail = qt_ref[...].astype(F32)
    for head in range(2):
        masked = jnp.where(head_of == head, query, zero)
        total = None
        for c in range(chunks):
            rows = pl.ds(c * size, size)
            keys = jnp.concatenate([all_ref[1, rows, :], kt_ref[rows, :]], 1)
            values = jnp.concatenate([all_ref[2, rows, :], vt_ref[rows, :]], 1)
            prob = jnp.exp2(mm(masked, keys, NT)).astype(BF16)
            part = mm(prob, values)
            total = part if total is None else total + part
        row_sum = total[:, WIDE : WIDE + 1]
        here = total[:, :WIDE] / row_sum
        out = here if head == 0 else jnp.where(lanes < HEAD_DIM, out, here)
        tail = with_pieces(tail, -jnp.log2(row_sum), head * HEAD_DIM + LOG_LANE, lanes)
    att_ref[...] = out
    low_ref[...] = out.astype(BF16)
    tail_ref[...] = tail.astype(BF16)


def attend(qkv, query_tail, key_tail, value_tail):
    block = 512
    rows = qkv.shape[1]
    moving = pl.BlockSpec((block, WIDE), lambda i: (i, 0))
    fixed = pl.BlockSpec((rows, WIDE), lambda i: (0, 0))
    low = jax.ShapeDtypeStruct((rows, WIDE), BF16)
    return pl.pallas_call(
        functools.partial(attend_kernel, chunks=4),
        grid=(rows // block,),
        in_specs=[
            pl.BlockSpec((1, block, WIDE), lambda i: (0, i, 0)),
            pl.BlockSpec((3, rows, WIDE), lambda i: (0, 0, 0)),
            moving,
            fixed,
            fixed,
        ],
        out_specs=[moving, moving, moving],
        out_shape=[jax.ShapeDtypeStruct((rows, WIDE), F32), low, low],
        compiler_params=pltpu.CompilerParams(vmem_limit_bytes=28 * 2**20),
        cost_estimate=pl.CostEstimate(
            flops=16 * rows * rows * WIDE, bytes_accessed=rows * WIDE * 24, transcendentals=2 * rows * rows
        ),
    )(qkv, qkv, query_tail, key_tail, value_tail)


def attend_back_kernel(
    qkv_ref, all_ref, qt_ref, kt_ref, vt_ref, hot_ref, grad_ref, att_ref,
    dq_ref, dk_ref, dv_ref, bias_ref, dk_sum, dv_sum, *, chunks
):
    size = all_ref.shape[1] // chunks
    step = pl.program_id(0)
    query = jnp.concatenate([qkv_ref[0], qt_ref[...]], 1)
    grad = grad_ref[...]
    zero = jnp.zeros_like(query)
    head_of = (lanes_of(query.shape) // HEAD_DIM) % 2
    lanes = lanes_of((query.shape[0], WIDE))
    overlap = grad.astype(F32) * att_ref[...]

    @pl.when(step == 0)
    def _():
        dk_sum[...] = jnp.zeros_like(dk_sum)
        dv_sum[...] = jnp.zeros_like(dv_sum)

    out = None
    for head in range(2):
        mine = head_of[:, :WIDE] == head
        masked = jnp.where(head_of == head, query, zero)
        grad_here = jnp.where(mine, grad, zero[:, :WIDE])
        dots = jnp.sum(jnp.where(mine, overlap, 0.0), axis=1, keepdims=True)
        extra = with_pieces(jnp.zeros(lanes.shape, F32), -dots, 0, lanes).astype(BF16)
        grad_wide = jnp.concatenate([grad_here, extra], 1)
        total = None
        for c in range(chunks):
            rows = pl.ds(c * size, size)
            keys = all_ref[1, rows, :]
            prob = jnp.exp2(mm(jnp.concatenate([keys, kt_ref[rows, :]], 1), masked, NT))
            slope = mm(jnp.concatenate([all_ref[2, rows, :], vt_ref[rows, :]], 1), grad_wide, NT)
            d_score = (prob * slope).astype(BF16)
            dv_sum[rows, :] += mm(prob.astype(BF16), grad_here)
            dk_sum[rows, :] += mm(d_score, masked)
            part = mm(d_score, keys, TN)
            total = part if total is None else total + part
        out = total if head == 0 else jnp.where(lanes < HEAD_DIM, out, total)
    dq_ref[...] = out.astype(BF16)

    @pl.when(step == pl.num_programs(0) - 1)
    def _():
        dk_ref[...] = (dk_sum[:, :WIDE] * (1.0 / LOG2E)).astype(BF16)
        dv_ref[...] = dv_sum[...].astype(BF16)
        counts = dk_sum[:, WIDE:]
        bias_ref[...] = jnp.zeros_like(bias_ref)
        bias_ref[0:1, :] = jnp.sum(counts * hot_ref[...].astype(F32), axis=0, keepdims=True)
        bias_ref[1:2, :] = jnp.sum(counts, axis=0, keepdims=True)


def attend_back(qkv, query_tail, key_tail, value_tail, query_hot, grad, attended):
    block = 512
    rows = qkv.shape[1]
    moving = pl.BlockSpec((block, WIDE), lambda i: (i, 0))
    fixed = pl.BlockSpec((rows, WIDE), lambda i: (0, 0))
    low = jax.ShapeDtypeStruct((rows, WIDE), BF16)
    return pl.pallas_call(
        functools.partial(attend_back_kernel, chunks=4),
        grid=(rows // block,),
        in_specs=[
            pl.BlockSpec((1, block, WIDE), lambda i: (0, i, 0)),
            pl.BlockSpec((3, rows, WIDE), lambda i: (0, 0, 0)),
            moving,
            fixed,
            fixed,
            fixed,
            moving,
            moving,
        ],
        out_specs=[moving, fixed, fixed, pl.BlockSpec((8, WIDE), lambda i: (0, 0))],
        out_shape=[low, low, low, jax.ShapeDtypeStruct((8, WIDE), F32)],
        scratch_shapes=[pltpu.VMEM((rows, 2 * WIDE), F32), pltpu.VMEM((rows, WIDE), F32)],
        compiler_params=pltpu.CompilerParams(vmem_limit_bytes=28 * 2**20),
        cost_estimate=pl.CostEstimate(
            flops=40 * rows * rows * WIDE, bytes_accessed=rows * WIDE * 24, transcendentals=2 * rows * rows
        ),
    )(qkv, qkv, query_tail, key_tail, value_tail, query_hot, grad, attended)


def feed_kernel(b_ref, g_ref, w_ref, y_ref, db_ref, act_ref, *, cuts):
    rows, grads = b_ref[...], g_ref[...]
    size = w_ref.shape[2] // cuts

    def products(j):
        cols = slice(j * size, (j + 1) * size)
        return mm(rows, w_ref[0, :, cols]), mm(rows, w_ref[1, :, cols]), mm(grads, w_ref[2, :, cols])

    y_sum, db_sum = None, None
    ready = products(0)
    for j in range(cuts):
        gate, up, d_hidden = ready
        if j + 1 < cuts:
            ready = products(j + 1)
        cols = slice(j * size, (j + 1) * size)
        sig = 0.5 + 0.5 * jnp.tanh(0.5 * gate)
        silu = gate * sig
        hidden = (silu * up).astype(BF16)
        d_gate = (d_hidden * up * (sig + silu * (1.0 - sig))).astype(BF16)
        d_up = (d_hidden * silu).astype(BF16)
        act_ref[0, :, cols] = d_gate
        act_ref[1, :, cols] = d_up
        act_ref[2, :, cols] = hidden
        y_part = mm(hidden, w_ref[2, :, cols], NT)
        db_part = mm(d_gate, w_ref[0, :, cols], NT) + mm(d_up, w_ref[1, :, cols], NT)
        y_sum = y_part if y_sum is None else y_sum + y_part
        db_sum = db_part if db_sum is None else db_sum + db_part
    y_ref[...] = y_sum.astype(BF16)
    db_ref[...] = db_sum.astype(BF16)


def feed(rows_b, rows_g, weights):
    rows = rows_b.shape[0]
    width = weights.shape[2]
    low_d = jax.ShapeDtypeStruct((rows, D), BF16)
    low_f = jax.ShapeDtypeStruct((3, rows, width), BF16)
    return pl.pallas_call(
        functools.partial(feed_kernel, cuts=2),
        out_shape=[low_d, low_d, low_f],
        compiler_params=pltpu.CompilerParams(vmem_limit_bytes=28 * 2**20),
        cost_estimate=pl.CostEstimate(
            flops=12 * rows * D * width, bytes_accessed=6 * D * width + rows * D * 8 + rows * width * 6,
            transcendentals=rows * width,
        ),
    )(rows_b, rows_g, weights)


def body(
    tokens,
    cotangent,
    destination,
    variate_ids,
    time_ids,
    seq_lengths,
    qkv_weight,
    out_weight,
    gate_up_weight,
    down_weight,
    norm_gains,
    qk_gains,
    variate_bias,
):
    core = lax.axis_index("core")
    low_core = core == 0
    y_at = lax.axis_index("y")
    zl_at = lax.axis_index("zl")

    core_scalar = core.reshape(1).astype(jnp.int32)

    def side_by_side(mine, other):
        return jnp.concatenate(
            [jnp.where(low_core, mine, other), jnp.where(low_core, other, mine)], axis=-1
        )

    attn_shard = jnp.concatenate([qkv_weight, out_weight.T[None]], 0)
    feed_shard = jnp.concatenate([gate_up_weight, down_weight.T[None]], 0)
    attn_mine = gather_round(attn_shard, ("zh", "zl"), lax.axis_index("zh") * 2 + zl_at)
    attn_mine = gather_round(attn_mine, "x", lax.axis_index("x")).reshape((16,) + attn_shard.shape)

    slot = destination % ROWS
    group_at = destination // GROUP
    block_at = (destination % GROUP) // ROWS
    device_at = ((group_at // 2) * 2 + block_at // 4) * 8 + (block_at % 4) * 2 + group_at % 2
    key = device_at * ROWS + slot
    zero = jnp.zeros_like(slot)
    facts = jnp.stack([key, slot, variate_ids, time_ids // 32, time_ids % 32, zero, zero, zero])
    gains_row = jnp.pad(
        norm_gains.reshape(8, 16), ((0, 0), (GAIN_LANE, WIDE - GAIN_LANE - 16))
    ).astype(F32)
    outgoing, deal = deal_rows(tokens, cotangent, facts.astype(F32), gains_row)
    outgoing, attn_mine = lax.optimization_barrier((outgoing, attn_mine))
    attn_w = assemble(core_scalar, attn_mine, swap_core(attn_mine), 2)
    arrived = lax.all_to_all(outgoing.reshape(DEVICES, 8, SPAN), ALL, 0, 0, tiled=True)
    arrived, attn_w = lax.optimization_barrier((arrived, attn_w))

    lengths_other = swap_core(seq_lengths)
    lengths = jnp.where(zl_at == core, seq_lengths, lengths_other)[0]
    bias_other = lax.ppermute(variate_bias, "zl", [(0, 1), (1, 0)])
    bias_pair = jnp.where(zl_at == core, variate_bias, bias_other)

    all_gains = arrived.reshape(16, 8, 8, SPAN)[:, 0, :, D + GAIN_LANE : D + GAIN_LANE + 16]
    inputs, grad_rows, attn_all, place, gains = receive(
        arrived.reshape(4 * ROWS, SPAN), all_gains.reshape(16, WIDE)
    )
    gain_two = gains[1]
    variates_own = attn_all[:, D + 2].astype(jnp.int32)
    variates = jnp.concatenate([variates_own, swap_core(variates_own)])
    blocks_y = (y_at + jnp.arange(RING)) % RING
    blocks = jnp.concatenate([core * RING + blocks_y, (1 - core) * RING + blocks_y])
    positions = (blocks[:, None] * ROWS + jnp.arange(ROWS)[None, :]).reshape(GROUP)
    segments = jnp.sum((positions[:, None] >= jnp.cumsum(lengths)[None, :]).astype(jnp.int32), 1)

    inverse = THETA ** (-2.0 * jnp.arange(HALF).astype(F32) / HEAD_DIM)
    freq = jnp.concatenate(
        [
            jnp.tile(inverse, 8)[None],
            jnp.tile(qk_gains, (1, 4)),
            jnp.zeros((5, 2 * WIDE), F32),
        ]
    )
    qkv_mine, qkv_send, raw = project(core_scalar, attn_all, attn_w, freq)
    feed_shard, grad_rows, qkv_send = lax.optimization_barrier((feed_shard, grad_rows, qkv_send))
    feed_mine = flat_gather(feed_shard)
    grad_all = gather_direct(grad_rows)
    qkv = jnp.concatenate([qkv_mine, swap_core(qkv_send)], axis=1)

    lane = jnp.arange(WIDE)[None, :]
    tail_lane = lane % HEAD_DIM
    bias_lane = tail_lane < 3 * VARIATES
    seg_lane = (tail_lane >= 3 * VARIATES) & (tail_lane < LOG_LANE)
    one_lane = (tail_lane >= LOG_LANE) & (tail_lane < LOG_LANE + 3)
    equal = bias_lane & (tail_lane % VARIATES == variates[:, None])
    inside = seg_lane & (tail_lane - 3 * VARIATES == segments[:, None])
    query_tail = (equal | inside).astype(BF16)
    bias_parts = jnp.stack(pieces(bias_pair * LOG2E, 3)).astype(F32)
    bias_rows = jnp.repeat(bias_parts, VARIATES, axis=0).transpose(1, 2, 0)
    bias_rows = jnp.pad(bias_rows, ((0, 0), (0, 0), (0, HEAD_DIM - 3 * VARIATES))).reshape(2, WIDE)
    key_tail = jnp.where(equal, bias_rows[0:1], bias_rows[1:2])
    key_tail = jnp.where(seg_lane, jnp.where(inside, 0.0, FAR), key_tail)
    key_tail = jnp.where(one_lane, 1.0, key_tail).astype(BF16)
    value_tail = jnp.broadcast_to((lane < 3).astype(BF16), (GROUP, WIDE))
    attended, att_low, query_back = attend(qkv, query_tail, key_tail, value_tail)
    att_low, grad_all = lax.optimization_barrier((att_low, grad_all))
    att_other = swap_core(att_low[PLANE:])
    att_other, feed_mine = lax.optimization_barrier((att_other, feed_mine))
    feed_w = assemble(core_scalar, feed_mine, swap_core(feed_mine), 4)
    att_plane = side_by_side(att_low[:PLANE], att_other)
    out_part = mm(att_plane, attn_w[3], NT).astype(BF16).reshape(RING, ROWS, D)
    got = send_ring([out_part[r] for r in range(RING)])
    got[0], feed_w = lax.optimization_barrier((got[0], feed_w))
    hidden_one = inputs + add_ring(out_part[0], got)

    scale_two = root_stats(hidden_one)
    normed_two = hidden_one * scale_two
    feed_in = (normed_two * gain_two).astype(BF16)
    ahead, behind = ring(feed_in, -1), ring(feed_in, 1)
    fed_own = feed(feed_in, grad_all[0], feed_w)
    ahead, behind, fed_own = lax.optimization_barrier((ahead, behind, fed_own))
    far_top, far_low = ring(ahead[: ROWS // 2], -1), ring(behind[ROWS // 2 :], 1)
    fed_ahead = feed(ahead, grad_all[1], feed_w)
    fed_behind = feed(behind, grad_all[3], feed_w)
    far_top, far_low, fed_ahead, fed_behind = lax.optimization_barrier(
        (far_top, far_low, fed_ahead, fed_behind)
    )
    far = jnp.concatenate([far_top, far_low], 0)
    fed_far = feed(far, grad_all[2], feed_w)
    feed_all = [feed_in, ahead, far, behind]
    fed = [fed_own, fed_ahead, fed_far, fed_behind]
    feed_split = weight_grads(core_scalar, feed_all, grad_all, [f[2] for f in fed], 2, 2)
    db_got = send_ring([f[1] for f in fed], True)
    db_got, feed_split = lax.optimization_barrier((db_got, feed_split))
    grad_normed_two = add_ring(fed_own[1], db_got)

    gain_two_grad = jnp.sum(grad_normed_two * normed_two, axis=0)
    grad_one = grad_rows.astype(F32) + norm_back(grad_normed_two * gain_two, normed_two, scale_two)

    grad_one_all = gather_direct(grad_one.astype(BF16))
    feed_total = chip_total(feed_split)
    feed_got = trade(feed_total, "x")
    grad_one_all, feed_total = lax.optimization_barrier((grad_one_all, feed_total))
    grad_one_all = jnp.concatenate(grad_one_all, 0)
    y_parts, grad_one_all = lax.optimization_barrier(([f[0] for f in fed], grad_one_all))
    y_got = send_ring(y_parts)
    grad_att = mm(grad_one_all, attn_w[3]).astype(BF16)
    grad_left, grad_right = grad_att[:, :WIDE], grad_att[:, WIDE:]
    grad_send = jnp.where(low_core, grad_right, grad_left)
    grad_mine = jnp.where(low_core, grad_left, grad_right)
    grad_mine = jnp.concatenate([grad_mine, swap_core(grad_send)], 0)
    d_query, d_key, d_value, bias_sums = attend_back(
        qkv, query_back, key_tail, value_tail, query_tail, grad_mine, attended
    )
    first_part = (jnp.arange(HEAD_DIM) < VARIATES)[None, None]
    bias_sums = jnp.where(first_part, bias_sums[:2].reshape(2, 2, HEAD_DIM), 0.0)
    bias_sums = jnp.sum(bias_sums, axis=2)
    bias_part = jnp.stack([bias_sums[0], bias_sums[1] - bias_sums[0]])
    d_query, y_got, feed_got = lax.optimization_barrier((d_query, y_got, feed_got))
    feed_half = added(feed_got).astype(BF16)
    mixed = (hidden_one + add_ring(y_parts[0], y_got)).astype(BF16)
    d_mine = jnp.stack([d_query[:PLANE], d_key[:PLANE], d_value[:PLANE]])
    d_got = swap_core(jnp.stack([d_query[PLANE:], d_key[PLANE:], d_value[PLANE:]]))
    grad_proj, in_part, qk_sums = unproject(
        core_scalar, d_mine, d_got, raw, attn_all, attn_w, freq
    )
    in_part = in_part.reshape(RING, ROWS, D)
    in_got = send_ring([in_part[r] for r in range(RING)])
    attn_split = weight_grads(
        core_scalar,
        [attn_all],
        [grad_one_all],
        [jnp.concatenate([grad_proj, att_plane[None]], 0)],
        3,
        1,
    )
    attn_total = chip_total(attn_split)
    in_got, _ = lax.optimization_barrier((in_got, attn_split))
    mixed, _ = lax.optimization_barrier((mixed, attn_total))
    attn_own, attn_got = send_round(attn_total.reshape((RING, RING) + attn_total.shape[1:]), "x")
    qk_sums = jnp.sum(qk_sums[:2].reshape(2, 4, HEAD_DIM), axis=1)

    small = jnp.zeros((8, WIDE), F32).at[0].set(qk_sums.reshape(WIDE))
    small = small.at[1, :4].set(bias_part.reshape(4))
    tensor_at = (y_at * 2 + core).reshape(1).astype(jnp.int32)
    last = finish(
        in_part[0], in_got, inputs, grad_one, mixed, place, gains, gain_two_grad[None], small, tensor_at
    )
    last = last.reshape(DEVICES, 8, 2 * QUARTER + WIDE)
    last, attn_got, feed_half = lax.optimization_barrier((last, attn_got, feed_half))
    home = lax.all_to_all(last, ALL, 0, 0, tiled=True)
    attn_own, attn_got = send_round(add_round(attn_own, attn_got).astype(BF16), ("zh", "zl"))
    feed_own, feed_got = send_round(feed_half, ("zh", "zl"))
    home, attn_got, feed_got = lax.optimization_barrier((home, attn_got, feed_got))
    attn_grad = add_round(attn_own, attn_got)
    feed_grad = add_round(feed_own, feed_got)
    new_tokens, token_grads, sums = settle(home.reshape(4 * ROWS, 2 * QUARTER + WIDE), deal)
    gains_grad = sums[0].reshape(2, 64)
    qk_grad = sums[1].reshape(2, 64)
    bias_grad = sums[2, :4].reshape(2, 2)

    return (
        new_tokens,
        token_grads,
        attn_grad[:3],
        attn_grad[3].T,
        feed_grad[:2],
        feed_grad[2].T,
        gains_grad,
        qk_grad,
        bias_grad,
    )


def solution(mesh):
    fine = Mesh(mesh.devices.reshape(4, 2, 2, 4, 2), ALL)
    dp = ("x", "zh", "core")
    tensor = ("y", "zl")
    in_specs = (
        P(ALL, None),
        P(ALL, None),
        P(ALL),
        P(ALL),
        P(ALL),
        P(dp, None),
        P(None, dp, tensor),
        P(tensor, dp),
        P(None, dp, tensor),
        P(tensor, dp),
        P(None, dp),
        P(),
        P(None, tensor),
    )
    out_specs = (
        P(ALL, None),
        P(ALL, None),
        P(None, dp, tensor),
        P(tensor, dp),
        P(None, dp, tensor),
        P(tensor, dp),
        P(None, dp),
        P(),
        P(None, tensor),
    )
    return jax.shard_map(body, mesh=fine, in_specs=in_specs, out_specs=out_specs, check_vma=False)
```

```python
import functools

import jax
import jax.numpy as jnp
from jax import lax
from jax.experimental import pallas as pl
from jax.experimental.pallas import tpu as pltpu
from jax.sharding import Mesh
from jax.sharding import PartitionSpec as P

HEADS = 16
HEAD_DIM = 64
HALF = HEAD_DIM // 2
D = 1024
FF = 4096
ROWS = 256
RING = 4
PLANE = ROWS * RING
GROUP = 2 * PLANE
DEVICES = 128
VARIATES = 8
SEQS = 4
WIDE = 128
EPS = 1e-06
THETA = 10000.0
LOG2E = 1.4426950408889634
FAR = -16384.0
F32 = jnp.float32
BF16 = jnp.bfloat16

ALL = ("x", "zh", "core", "y", "zl")
FLAT = ("x", "zh", "zl")
NT = (((1,), (1,)), ((), ()))
TN = (((0,), (0,)), ((), ()))


def mm(left, right, dims=(((1,), (0,)), ((), ()))):
    return lax.dot_general(left, right, dims, preferred_element_type=F32)


def root_stats(values):
    return lax.rsqrt(jnp.mean(values * values, axis=-1, keepdims=True) + EPS)


def norm_back(grad_in, normed, scale_inv):
    return scale_inv * (grad_in - normed * jnp.mean(grad_in * normed, axis=-1, keepdims=True))


def pieces(values, count):
    out = []
    for _ in range(count):
        part = lax.reduce_precision(values, 8, 7)
        out.append(part.astype(BF16))
        values = values - part
    return out


def ring(values, step):
    return lax.ppermute(values, "y", [(i, (i + step) % RING) for i in range(RING)])


def swap_core(values):
    return lax.ppermute(values, "core", [(0, 1), (1, 0)])


def gather_ring(values):
    ahead = ring(values, -1)
    behind = ring(values, 1)
    half = values.shape[0] // 2
    far_top = ring(ahead[:half], -1)
    far_low = ring(behind[half:], 1)
    return [values, ahead, jnp.concatenate([far_top, far_low], 0), behind]


def gather_direct(values):
    return [values, ring(values, -1), ring(values, 2), ring(values, 1)]


def trade_ring(parts):
    return [parts[0]] + [ring(parts[RING - s], -s) for s in range(1, RING)]


def send_ring(parts, halves=False):
    half = parts[2].shape[0] // 2
    far = [parts[2][:half], parts[2][half:]] if halves else [parts[2]]
    return [ring(parts[1], 1), ring(parts[3], -1)] + [ring(v, 2) for v in far]


def add_ring(own, got):
    far = got[2] if len(got) == 3 else jnp.concatenate(got[2:], 0)
    return own.astype(F32) + got[0].astype(F32) + got[1].astype(F32) + far.astype(F32)


def gather_round(values, axes, at):
    moves = [[((i + r) % RING, i) for i in range(RING)] for r in range(RING)]
    rows = [values] + [lax.ppermute(values, axes, moves[r]) for r in range(1, RING)]
    return jnp.roll(jnp.stack(rows), at, axis=0)


def flat_gather(shard):
    many = jnp.broadcast_to(shard[None], (16,) + shard.shape)
    return lax.all_to_all(many, FLAT, 0, 0, tiled=True)


def assemble_kernel(core_ref, mine_ref, other_ref, out_ref):
    core = core_ref[0]
    count, _, depth, width = mine_ref.shape
    for ref, side in ((mine_ref, core), (other_ref, 1 - core)):
        for i in range(count):
            at = (i // 2) * 2 * depth + side * depth
            rows = pl.ds(pl.multiple_of(at, depth), depth)
            out_ref[:, rows, (i % 2) * width : (i % 2 + 1) * width] = ref[i]


def assemble(core, mine, other, steps):
    _, kinds, depth, width = mine.shape
    pair = pl.BlockSpec((16 // steps, kinds, depth, width), lambda p: (p, 0, 0, 0))
    return pl.pallas_call(
        assemble_kernel,
        grid=(steps,),
        in_specs=[pl.BlockSpec(memory_space=pltpu.SMEM), pair, pair],
        out_specs=pl.BlockSpec((kinds, 16 // steps * depth, 2 * width), lambda p: (0, p, 0)),
        out_shape=jax.ShapeDtypeStruct((kinds, 16 * depth, 2 * width), BF16),
        compiler_params=pltpu.CompilerParams(vmem_limit_bytes=48 * 2**20),
        cost_estimate=pl.CostEstimate(
            flops=0, bytes_accessed=kinds * 128 * depth * width, transcendentals=0
        ),
    )(core, mine, other)


def chip_total(split):
    return (split[0].astype(F32) + swap_core(split[1]).astype(F32)).astype(BF16)


def send_round(values, axes):
    at = lax.axis_index(axes)
    parts = [lax.dynamic_index_in_dim(values, (at + r) % RING, 0, keepdims=False) for r in range(RING)]
    moves = [[(i, (i + r) % RING) for i in range(RING)] for r in range(RING)]
    return parts[0], [lax.ppermute(parts[r], axes, moves[r]) for r in (1, 3, 2)]


def add_round(own, got):
    return sum((v.astype(F32) for v in got), own.astype(F32))


def trade(values, axes):
    return lax.all_to_all(values.reshape((RING, -1) + values.shape[1:]), axes, 0, 0, tiled=True)


def added(got):
    return jnp.sum(got.astype(F32), axis=0)


def lanes_of(shape):
    return lax.broadcasted_iota(jnp.int32, shape, 1)


QUARTER = D // RING
PAIR = 2 * QUARTER
SPAN = PAIR + WIDE
GAIN_LANE = 16


def deal_kernel(tok_ref, cot_ref, facts_ref, gains_ref, out_ref, deal_ref):
    wide = jnp.concatenate([facts_ref[...], jnp.zeros((WIDE - 8, ROWS), F32)], 0)
    facts = jnp.transpose(wide)
    keys = facts_ref[0:1, :]
    rank = jnp.sum((facts[:, 0:1] < keys).astype(F32), axis=0, keepdims=True)
    at = lax.broadcasted_iota(jnp.int32, (ROWS, ROWS), 0).astype(F32)
    deal_ref[...] = (at == rank).astype(BF16)
    low = jnp.where(lanes_of(facts.shape) == 0, 0.0, facts).astype(BF16)
    row = lax.broadcasted_iota(jnp.int32, (4 * ROWS, 1), 0)
    own = ((row // RING).astype(F32) == rank).astype(BF16)
    part = None
    for m in range(RING):
        cols = slice(m * QUARTER, (m + 1) * QUARTER)
        here = mm(own, jnp.concatenate([tok_ref[:, cols], cot_ref[:, cols]], 1))
        part = here if m == 0 else jnp.where(row % RING == m, here, part)
    out_ref[:, :PAIR] = part.astype(BF16)
    tail = mm(own, low)
    lane = lanes_of(tail.shape)
    gains = jnp.broadcast_to(gains_ref[...][None], (DEVICES, 8, WIDE)).reshape(tail.shape)
    tail = jnp.where((lane >= GAIN_LANE) & (lane < GAIN_LANE + 16), gains, tail)
    out_ref[:, PAIR:] = tail.astype(BF16)


def deal_rows(tokens, cotangent, facts, gains):
    return pl.pallas_call(
        deal_kernel,
        out_shape=[
            jax.ShapeDtypeStruct((4 * ROWS, SPAN), BF16),
            jax.ShapeDtypeStruct((ROWS, ROWS), BF16),
        ],
        compiler_params=pltpu.CompilerParams(vmem_limit_bytes=48 * 2**20),
        cost_estimate=pl.CostEstimate(
            flops=8 * ROWS * ROWS * 2304, bytes_accessed=ROWS * D * 16, transcendentals=0
        ),
    )(tokens, cotangent, facts, gains)


def receive_kernel(rows_ref, gains_ref, x_ref, g_ref, a_ref, place_ref, gain_ref):
    count = 4 * ROWS
    facts = rows_ref[:, PAIR:]
    slots = jnp.transpose(facts.astype(F32))[1:2, :]
    at = lax.broadcasted_iota(jnp.int32, (ROWS, count), 0)
    arrival = lanes_of((ROWS, count))
    here = at.astype(F32) == slots
    gains = gains_ref[...].astype(F32)
    turned = pltpu.roll(gains, HEAD_DIM, 1)
    left = lanes_of((1, WIDE)) < HEAD_DIM
    one, two = [], []
    for c in range(D // WIDE):
        even, odd = slice(2 * c, 2 * c + 1), slice(2 * c + 1, 2 * c + 2)
        one.append(jnp.where(left, gains[even], turned[odd]))
        two.append(jnp.where(left, turned[even], gains[odd]))
    gain_one = jnp.concatenate(one, 1)
    gain_ref[...] = jnp.zeros_like(gain_ref)
    gain_ref[0:1, :] = gain_one
    gain_ref[1:2, :] = jnp.concatenate(two, 1)
    quarters = []
    for m in range(RING):
        chosen = (here & (arrival % RING == m)).astype(BF16)
        both = mm(chosen, rows_ref[:, :PAIR])
        quarters.append(both[:, :QUARTER])
        g_ref[:, m * QUARTER : (m + 1) * QUARTER] = both[:, QUARTER:].astype(BF16)
        if m == 0:
            a_ref[:, D:] = mm(chosen, facts).astype(BF16)
            pick = (at * RING == arrival).astype(BF16)
            place_ref[...] = mm(chosen, pick, NT).astype(BF16)
    rows = jnp.concatenate(quarters, 1)
    x_ref[...] = rows
    a_ref[:, :D] = (rows * root_stats(rows) * gain_one).astype(BF16)


def receive(rows, gains):
    return pl.pallas_call(
        receive_kernel,
        out_shape=[
            jax.ShapeDtypeStruct((ROWS, D), F32),
            jax.ShapeDtypeStruct((ROWS, D), BF16),
            jax.ShapeDtypeStruct((ROWS, D + WIDE), BF16),
            jax.ShapeDtypeStruct((ROWS, ROWS), BF16),
            jax.ShapeDtypeStruct((8, D), F32),
        ],
        compiler_params=pltpu.CompilerParams(vmem_limit_bytes=48 * 2**20),
        cost_estimate=pl.CostEstimate(
            flops=16 * ROWS * ROWS * D, bytes_accessed=ROWS * D * 24, transcendentals=0
        ),
    )(rows, gains)


OUT_KIND = 3


def out_kernel(*refs):
    att = refs[:RING]
    w_ref, x_ref, gain_ref, h_ref, b_ref = refs[RING:]
    hidden = x_ref[...]
    for r in range(RING):
        hidden = hidden + mm(att[r][...], w_ref[OUT_KIND + r], NT)
    h_ref[...] = hidden
    b_ref[...] = (hidden * root_stats(hidden) * gain_ref[1:2, :]).astype(BF16)


def out_project(att, weights, rows, gains):
    return pl.pallas_call(
        out_kernel,
        out_shape=[jax.ShapeDtypeStruct((ROWS, D), F32), jax.ShapeDtypeStruct((ROWS, D), BF16)],
        compiler_params=pltpu.CompilerParams(vmem_limit_bytes=48 * 2**20),
        cost_estimate=pl.CostEstimate(
            flops=2 * ROWS * D * D, bytes_accessed=2 * D * D + ROWS * D * 14, transcendentals=0
        ),
    )(*att, weights, rows, gains)


def middle_kernel(*refs):
    att, y_parts, w_ref = refs[:RING], refs[RING : 2 * RING], refs[2 * RING]
    refs = refs[2 * RING + 1 :]
    own_ref, near_ref, back_ref, top_ref, low_ref, h_ref, g_ref, gain_ref = refs[:8]
    grad_ref, two_ref, d_ref = refs[8:11]
    both_refs = refs[11:]
    far = jnp.concatenate([top_ref[...], low_ref[...]], 0).astype(F32)
    grad = own_ref[...].astype(F32) + near_ref[...].astype(F32) + back_ref[...].astype(F32) + far
    hidden = h_ref[...]
    scale = root_stats(hidden)
    normed = hidden * scale
    two_ref[...] = jnp.zeros_like(two_ref)
    two_ref[0:1, :] = jnp.sum(grad * normed, axis=0, keepdims=True)
    scaled = grad * gain_ref[1:2, :]
    grad = g_ref[...].astype(F32) + norm_back(scaled, normed, scale)
    grad_ref[...] = grad
    low = grad.astype(BF16)
    for r in range(RING):
        d_ref[r] = mm(low, w_ref[OUT_KIND + r]).astype(BF16)
        both_refs[r][:ROWS] = y_parts[r][...]
        both_refs[r][ROWS:] = mm(att[r][...], low, TN).astype(BF16)


def middle(att, weights, y_parts, own, got, hidden, grad_rows, gains):
    both = jax.ShapeDtypeStruct((2 * ROWS, D), BF16)
    return pl.pallas_call(
        middle_kernel,
        out_shape=[
            jax.ShapeDtypeStruct((ROWS, D), F32),
            jax.ShapeDtypeStruct((8, D), F32),
            jax.ShapeDtypeStruct((RING, ROWS, ROWS), BF16),
        ]
        + [both] * RING,
        compiler_params=pltpu.CompilerParams(vmem_limit_bytes=48 * 2**20),
        cost_estimate=pl.CostEstimate(
            flops=4 * ROWS * D * D, bytes_accessed=2 * D * D + ROWS * D * 40, transcendentals=0
        ),
    )(*att, *y_parts, weights, own, *got, hidden, grad_rows, gains)


def finish_kernel(
    own_ref, near_ref, back_ref, far_ref, x_ref, grad_ref, mixed_ref, place_ref,
    gain_ref, two_ref, small_ref, at_ref, out_ref,
):
    rows = x_ref[...]
    scale = root_stats(rows)
    normed = rows * scale
    far = far_ref[...].astype(F32)
    grad = own_ref[...].astype(F32) + near_ref[...].astype(F32) + back_ref[...].astype(F32) + far
    one = jnp.sum(grad * normed, axis=0, keepdims=True)
    two = two_ref[0:1, :]
    scaled = grad * gain_ref[0:1, :]
    back = scale * (scaled - normed * jnp.mean(scaled * normed, axis=1, keepdims=True))
    result = (grad_ref[...] + back).astype(BF16)
    count = 4 * ROWS
    row = lax.broadcasted_iota(jnp.int32, (count, 1), 0)
    quarter = row % RING
    pick = (row // RING == lanes_of((count, ROWS))).astype(BF16)
    pick = mm(pick, place_ref[...], NT).astype(BF16)
    part = None
    for m in range(RING):
        cols = slice(m * QUARTER, (m + 1) * QUARTER)
        here = mm(pick, jnp.concatenate([mixed_ref[:, cols], result[:, cols]], 1))
        part = here if m == 0 else jnp.where(quarter == m, here, part)
    out_ref[:, : 2 * QUARTER] = part.astype(BF16)
    left = lanes_of((1, WIDE)) < HEAD_DIM
    tiles = []
    for c in range(D // WIDE):
        cols = slice(c * WIDE, (c + 1) * WIDE)
        a, b = one[:, cols], two[:, cols]
        even = jnp.where(left, a, pltpu.roll(jnp.broadcast_to(b, (8, WIDE)), HEAD_DIM, 1)[0:1])
        odd = jnp.where(left, pltpu.roll(jnp.broadcast_to(a, (8, WIDE)), HEAD_DIM, 1)[0:1], b)
        tiles += [jnp.broadcast_to(even, (64, WIDE)), jnp.broadcast_to(odd, (64, WIDE))]
    value = jnp.concatenate(tiles, 0)
    value = jnp.where(quarter == 1, small_ref[0:1, :], value)
    bias = jnp.where((row // 8) % 8 == at_ref[0], small_ref[1:2, :], 0.0)
    value = jnp.where(quarter == 2, bias, value)
    high = value.astype(BF16).astype(F32)
    value = jnp.where((row // RING) % 2 == 0, high, value - high)
    out_ref[:, 2 * QUARTER :] = value.astype(BF16)


def finish(own, got, rows, grad, mixed, place, gains, two, small, at):
    specs = [pl.BlockSpec(memory_space=pltpu.VMEM)] * 11
    return pl.pallas_call(
        finish_kernel,
        in_specs=specs + [pl.BlockSpec(memory_space=pltpu.SMEM)],
        out_shape=jax.ShapeDtypeStruct((4 * ROWS, 2 * QUARTER + WIDE), BF16),
        compiler_params=pltpu.CompilerParams(vmem_limit_bytes=48 * 2**20),
        cost_estimate=pl.CostEstimate(
            flops=16 * ROWS * ROWS * D, bytes_accessed=ROWS * D * 20, transcendentals=0
        ),
    )(own, *got, rows, grad, mixed, place, gains, two, small, at)


def settle_kernel(home_ref, deal_ref, rows_ref, grads_ref, sums_ref):
    deal = deal_ref[...]
    shape = (ROWS, 4 * ROWS)
    index = lax.broadcasted_iota(jnp.int32, shape, 0)
    for m in range(RING):
        pick = (index * RING + m == lanes_of(shape)).astype(BF16)
        here = mm(pick, home_ref[:, : 2 * QUARTER]).astype(BF16)
        here = mm(deal, here, TN).astype(BF16)
        cols = slice(m * QUARTER, (m + 1) * QUARTER)
        rows_ref[:, cols] = here[:, :QUARTER]
        grads_ref[:, cols] = here[:, QUARTER:]
    small = home_ref[:, 2 * QUARTER :].astype(F32)
    quarter = lax.broadcasted_iota(jnp.int32, small.shape, 0) % RING
    sums_ref[...] = jnp.zeros_like(sums_ref)
    for m in range(3):
        sums_ref[m : m + 1, :] = jnp.sum(jnp.where(quarter == m, small, 0.0), axis=0, keepdims=True)


def settle(home, deal):
    low = jax.ShapeDtypeStruct((ROWS, D), BF16)
    return pl.pallas_call(
        settle_kernel,
        out_shape=[low, low, jax.ShapeDtypeStruct((8, WIDE), F32)],
        compiler_params=pltpu.CompilerParams(vmem_limit_bytes=48 * 2**20),
        cost_estimate=pl.CostEstimate(
            flops=20 * ROWS * ROWS * D, bytes_accessed=ROWS * D * 16, transcendentals=0
        ),
    )(home, deal)


def weight_grad_kernel(core_ref, *refs, parts, count, switch, steps):
    given = switch is None
    lefts, others, rights = refs[:parts], refs[parts : parts + count], refs[parts + count : -3]
    keep_ref, send_ref, turned_ref = refs[-3:]
    low = core_ref[0] == 0
    step = pl.program_id(0)

    def load(sides):
        at = 0
        for side in sides:
            rows = side.shape[0]
            turned_ref[:, at : at + rows] = side[...].T
            at += rows

    @pl.when(step == 0)
    def _():
        load(lefts)

    if not given:

        @pl.when(step == switch * steps)
        def _():
            load(others)

    def emit(total):
        depth = total.shape[0] // 16
        width = keep_ref.shape[-1]
        for z in range(total.shape[1] // width):
            cols = slice(z * width, (z + 1) * width)
            for p in range(8):
                at = 2 * p * depth
                even, odd = total[at : at + depth, cols], total[at + depth : at + 2 * depth, cols]
                keep_ref[p, z, 0] = jnp.where(low, even, odd)
                send_ref[p, z, 0] = jnp.where(low, odd, even)

    def product():
        right = jnp.concatenate([ref[0] for ref in rights], 0)
        emit(mm(turned_ref[...], right).astype(BF16))

    if given:
        pl.when(step < pl.num_programs(0) - 1)(product)

        @pl.when(step == pl.num_programs(0) - 1)
        def _():
            emit(others[0][...].T)
    else:
        product()


def weight_grads(core, lefts, others, rights, switch, steps):
    parts = len(lefts)
    made, _, width = rights[0].shape
    kinds = made + 1 if switch is None else made
    block, half = width // steps, width // 2
    sides = [pl.BlockSpec((v.shape[0], D), lambda s: (0, 0)) for v in list(lefts) + list(others)]
    moving = [
        pl.BlockSpec(
            (1, v.shape[1], block), lambda s: (jnp.minimum(s // steps, made - 1), 0, s % steps)
        )
        for v in rights
    ]
    rows = sum(v.shape[1] for v in rights)
    out = pl.pallas_call(
        functools.partial(
            weight_grad_kernel, parts=parts, count=len(others), switch=switch, steps=steps
        ),
        grid=(kinds * steps,),
        in_specs=[pl.BlockSpec(memory_space=pltpu.SMEM)] + sides + moving,
        out_specs=[
            pl.BlockSpec((8, 2 // steps, 1, 64, half), lambda s: (0, s % steps, s // steps, 0, 0))
        ]
        * 2,
        out_shape=[jax.ShapeDtypeStruct((8, 2, kinds, 64, half), BF16)] * 2,
        scratch_shapes=[pltpu.VMEM((D, rows), BF16)],
        compiler_params=pltpu.CompilerParams(vmem_limit_bytes=48 * 2**20),
        cost_estimate=pl.CostEstimate(
            flops=2 * kinds * rows * D * width,
            bytes_accessed=2 * kinds * D * width + 4 * rows * D + 2 * kinds * rows * width,
            transcendentals=0,
        ),
    )(core, *lefts, *others, *rights)
    return [v.reshape(16, kinds, 64, half) for v in out]


def head_sums(values):
    wide = values.shape[1]
    row = lax.broadcasted_iota(jnp.int32, (wide, wide), 0) // HEAD_DIM
    same = (row == lanes_of((wide, wide)) // HEAD_DIM).astype(BF16)
    high = values.astype(BF16)
    low = (values - high.astype(F32)).astype(BF16)
    return mm(high, same) + mm(low, same)


def partner(values):
    wide = values.shape[1]
    first = lanes_of(values.shape) % HEAD_DIM < HALF
    return jnp.where(first, pltpu.roll(values, wide - HALF, 1), pltpu.roll(values, HALF, 1))


def angles_of(facts, freq_ref):
    facts = facts.astype(F32)
    times = facts[:, 3:4] * 32.0 + facts[:, 4:5]
    angle = times * freq_ref[0:1, :WIDE]
    first = lanes_of(angle.shape) % HEAD_DIM < HALF
    cosine = jnp.cos(angle)
    sine = jnp.sin(angle)
    sine = jnp.where(first, -sine, sine)
    return jnp.concatenate([cosine, cosine], 1), jnp.concatenate([sine, sine], 1)


def project_kernel(core_ref, *refs):
    pieces_in = refs[:RING]
    w_ref, freq_ref, mine_ref, send_ref, raw_ref, facts_ref = refs[RING:]
    low = core_ref[0] == 0
    for r in range(RING):
        block = slice(r * ROWS, (r + 1) * ROWS)
        rows = pieces_in[r][:, :D]
        facts = pieces_in[r][:, D:]
        facts_ref[block] = facts
        cosine, sine = angles_of(facts, freq_ref)
        for kind in range(3):
            value = mm(rows, w_ref[kind])
            if kind < 2:
                raw_ref[kind, block] = value
                unit = value * lax.rsqrt(head_sums(value * value) * (1.0 / HEAD_DIM) + EPS)
                value = unit * freq_ref[1 + kind : 2 + kind, :]
                value = value * cosine + partner(value) * sine
            if kind == 0:
                value = value * (HEAD_DIM ** (-0.5) * LOG2E)
            left, right = value[:, :WIDE], value[:, WIDE:]
            mine_ref[kind, block] = jnp.where(low, left, right).astype(BF16)
            send_ref[kind, block] = jnp.where(low, right, left).astype(BF16)


def project(core, rows, attn_w, freq):
    low = jax.ShapeDtypeStruct((3, PLANE, WIDE), BF16)
    whole = pl.BlockSpec(memory_space=pltpu.VMEM)
    return pl.pallas_call(
        project_kernel,
        in_specs=[pl.BlockSpec(memory_space=pltpu.SMEM)] + [whole] * (RING + 2),
        out_shape=[
            low,
            low,
            jax.ShapeDtypeStruct((2, PLANE, 2 * WIDE), F32),
            jax.ShapeDtypeStruct((PLANE, WIDE), BF16),
        ],
        compiler_params=pltpu.CompilerParams(vmem_limit_bytes=48 * 2**20),
        cost_estimate=pl.CostEstimate(
            flops=8 * PLANE * D * 2 * WIDE, bytes_accessed=PLANE * D * 8, transcendentals=PLANE * 1024
        ),
    )(core, *rows, attn_w, freq)


def unproject_kernel(
    core_ref, mine_ref, got_ref, raw_ref, facts_ref, w_ref, freq_ref, dp_ref, part_ref, gain_ref
):
    low = core_ref[0] == 0
    cosine, sine = angles_of(facts_ref[...], freq_ref)

    @pl.when(pl.program_id(0) == 0)
    def _():
        gain_ref[...] = jnp.zeros_like(gain_ref)

    total = None
    for kind in range(3):
        mine, got = mine_ref[kind], got_ref[kind]
        grad = jnp.concatenate([jnp.where(low, mine, got), jnp.where(low, got, mine)], 1)
        if kind < 2:
            grad = grad.astype(F32)
            if kind == 0:
                grad = grad * (HEAD_DIM ** (-0.5))
            raw = raw_ref[kind]
            inv = lax.rsqrt(head_sums(raw * raw) * (1.0 / HEAD_DIM) + EPS)
            unit = raw * inv
            grad = grad * cosine - partner(grad) * sine
            gain_ref[kind : kind + 1, :] += jnp.sum(grad * unit, axis=0, keepdims=True)
            scaled = grad * freq_ref[1 + kind : 2 + kind, :]
            mean = head_sums(scaled * unit) * (1.0 / HEAD_DIM)
            grad = (inv * (scaled - unit * mean)).astype(BF16)
        dp_ref[kind] = grad
        part = mm(grad, w_ref[kind], NT)
        total = part if total is None else total + part
    part_ref[...] = total.astype(BF16)


def unproject(core, mine, got, raw, rows_all, attn_w, freq):
    block = 512
    both = pl.BlockSpec((3, block, WIDE), lambda i: (0, i, 0))
    return pl.pallas_call(
        unproject_kernel,
        grid=(PLANE // block,),
        in_specs=[
            pl.BlockSpec(memory_space=pltpu.SMEM),
            both,
            both,
            pl.BlockSpec((2, block, 2 * WIDE), lambda i: (0, i, 0)),
            pl.BlockSpec((block, WIDE), lambda i: (i, 0)),
            pl.BlockSpec((3, D, 2 * WIDE), lambda i: (0, 0, 0)),
            pl.BlockSpec((8, 2 * WIDE), lambda i: (0, 0)),
        ],
        out_specs=[
            pl.BlockSpec((3, block, 2 * WIDE), lambda i: (0, i, 0)),
            pl.BlockSpec((block, D), lambda i: (i, 0)),
            pl.BlockSpec((8, 2 * WIDE), lambda i: (0, 0)),
        ],
        out_shape=[
            jax.ShapeDtypeStruct((3, PLANE, 2 * WIDE), BF16),
            jax.ShapeDtypeStruct((PLANE, D), BF16),
            jax.ShapeDtypeStruct((8, 2 * WIDE), F32),
        ],
        compiler_params=pltpu.CompilerParams(vmem_limit_bytes=48 * 2**20),
        cost_estimate=pl.CostEstimate(
            flops=8 * PLANE * D * 2 * WIDE, bytes_accessed=PLANE * D * 8, transcendentals=PLANE * 1024
        ),
    )(core, mine, got, raw, rows_all, attn_w, freq)


LOG_LANE = 3 * VARIATES + SEQS


def with_pieces(base, values, first_lane, lanes):
    for i in range(3):
        part = values.astype(BF16).astype(F32)
        base = jnp.where(lanes == first_lane + i, part, base)
        values = values - part
    return base


def value_lanes(rows):
    return (lanes_of((rows, WIDE)) < 3).astype(BF16)


def attend_kernel(
    at_ref, mine_ref, got_ref, own_ref, other_ref, bias_ref,
    att_ref, near_ref, send_ref, tail_ref, kt_ref, all_scr, qt_scr, *, chunks,
):
    step = pl.program_id(0)
    block = att_ref.shape[0]
    size = GROUP // chunks

    @pl.when(step == 0)
    def _():
        all_scr[:, :PLANE] = mine_ref[...]
        all_scr[:, PLANE:] = got_ref[...]
        lane = lanes_of((ROWS, WIDE))
        tail_lane = lane % HEAD_DIM
        bias_lane = tail_lane < 3 * VARIATES
        seg_lane = (tail_lane >= 3 * VARIATES) & (tail_lane < LOG_LANE)
        one_lane = (tail_lane >= LOG_LANE) & (tail_lane < LOG_LANE + 3)
        row = lax.broadcasted_iota(jnp.int32, (ROWS, WIDE), 0)
        for b in range(2 * RING):
            source = own_ref if b < RING else other_ref
            facts = source[(b % RING) * ROWS : (b % RING + 1) * ROWS, :].astype(F32)
            variate = facts[:, 2:3]
            equal = bias_lane & ((tail_lane % VARIATES).astype(F32) == variate)
            position = at_ref[b] + row
            segment = jnp.zeros_like(row)
            for j in range(SEQS):
                segment += (position >= at_ref[2 * RING + j]).astype(jnp.int32)
            inside = seg_lane & (tail_lane - 3 * VARIATES == segment)
            rows = slice(b * ROWS, (b + 1) * ROWS)
            qt_scr[rows] = (equal | inside).astype(BF16)
            tail = jnp.where(equal, bias_ref[0:1, :], bias_ref[1:2, :])
            tail = jnp.where(bias_lane, tail, jnp.where(one_lane, 1.0, 0.0))
            tail = jnp.where(seg_lane & ~inside, FAR, tail)
            kt_ref[rows] = tail.astype(BF16)

    here = pl.ds(pl.multiple_of(step * block, block), block)
    query_tail = qt_scr[here, :]
    query = jnp.concatenate([all_scr[0, here, :], query_tail], 1)
    zero = jnp.zeros_like(query)
    head_of = (lanes_of(query.shape) // HEAD_DIM) % 2
    lanes = lanes_of((block, WIDE))
    ones = value_lanes(size)
    out = None
    tail = query_tail.astype(F32)
    for head in range(2):
        masked = jnp.where(head_of == head, query, zero)
        total = None
        for c in range(chunks):
            rows = slice(c * size, (c + 1) * size)
            keys = jnp.concatenate([all_scr[1, rows, :], kt_ref[rows, :]], 1)
            values = jnp.concatenate([all_scr[2, rows, :], ones], 1)
            prob = jnp.exp2(mm(masked, keys, NT)).astype(BF16)
            part = mm(prob, values)
            total = part if total is None else total + part
        row_sum = total[:, WIDE : WIDE + 1]
        now = total[:, :WIDE] / row_sum
        out = now if head == 0 else jnp.where(lanes < HEAD_DIM, out, now)
        tail = with_pieces(tail, -jnp.log2(row_sum), head * HEAD_DIM + LOG_LANE, lanes)
    att_ref[...] = out
    tail_ref[...] = tail.astype(BF16)
    low = out.astype(BF16)
    half = pl.num_programs(0) // 2

    @pl.when(step < half)
    def _():
        near_ref[here, :] = low

    @pl.when(step >= half)
    def _():
        send_ref[pl.ds(pl.multiple_of((step - half) * block, block), block), :] = low


def attend(at, mine, got, facts, facts_other, bias_rows):
    block = 512
    moving = pl.BlockSpec((block, WIDE), lambda i: (i, 0))
    plane = pl.BlockSpec((PLANE, WIDE), lambda i: (0, 0))
    three = pl.BlockSpec((3, PLANE, WIDE), lambda i: (0, 0, 0))
    low = jax.ShapeDtypeStruct((GROUP, WIDE), BF16)
    low_plane = jax.ShapeDtypeStruct((PLANE, WIDE), BF16)
    return pl.pallas_call(
        functools.partial(attend_kernel, chunks=4),
        grid=(GROUP // block,),
        in_specs=[
            pl.BlockSpec(memory_space=pltpu.SMEM),
            three,
            three,
            plane,
            plane,
            pl.BlockSpec((8, WIDE), lambda i: (0, 0)),
        ],
        out_specs=[moving, plane, plane, moving, pl.BlockSpec((GROUP, WIDE), lambda i: (0, 0))],
        out_shape=[jax.ShapeDtypeStruct((GROUP, WIDE), F32), low_plane, low_plane, low, low],
        scratch_shapes=[pltpu.VMEM((3, GROUP, WIDE), BF16), pltpu.VMEM((GROUP, WIDE), BF16)],
        compiler_params=pltpu.CompilerParams(vmem_limit_bytes=48 * 2**20),
        cost_estimate=pl.CostEstimate(
            flops=16 * GROUP * GROUP * WIDE, bytes_accessed=GROUP * WIDE * 24,
            transcendentals=2 * GROUP * GROUP,
        ),
    )(at, mine, got, facts, facts_other, bias_rows)


def attend_back_kernel(
    mine_ref, got_ref, qt_ref, kt_ref, hot_ref, near_ref, other_ref, att_ref,
    keep_ref, send_ref, bias_ref, all_scr, grad_scr, dk_sum, dv_sum, *, chunks,
):
    size = GROUP // chunks
    step = pl.program_id(0)
    block = qt_ref.shape[0]

    @pl.when(step == 0)
    def _():
        all_scr[:, :PLANE] = mine_ref[...]
        all_scr[:, PLANE:] = got_ref[...]
        grad_scr[:PLANE] = near_ref[...]
        grad_scr[PLANE:] = other_ref[...]
        dk_sum[...] = jnp.zeros_like(dk_sum)
        dv_sum[...] = jnp.zeros_like(dv_sum)

    here = pl.ds(pl.multiple_of(step * block, block), block)
    query = jnp.concatenate([all_scr[0, here, :], qt_ref[...]], 1)
    grad = grad_scr[here, :]
    zero = jnp.zeros_like(query)
    head_of = (lanes_of(query.shape) // HEAD_DIM) % 2
    lanes = lanes_of((block, WIDE))
    overlap = grad.astype(F32) * att_ref[...]
    ones = value_lanes(size)
    out = None
    for head in range(2):
        mine = head_of[:, :WIDE] == head
        masked = jnp.where(head_of == head, query, zero)
        grad_here = jnp.where(mine, grad, zero[:, :WIDE])
        dots = jnp.sum(jnp.where(mine, overlap, 0.0), axis=1, keepdims=True)
        extra = with_pieces(jnp.zeros(lanes.shape, F32), -dots, 0, lanes).astype(BF16)
        grad_wide = jnp.concatenate([grad_here, extra], 1)
        total = None
        for c in range(chunks):
            rows = slice(c * size, (c + 1) * size)
            keys = all_scr[1, rows, :]
            prob = jnp.exp2(mm(jnp.concatenate([keys, kt_ref[rows, :]], 1), masked, NT))
            slope = mm(jnp.concatenate([all_scr[2, rows, :], ones], 1), grad_wide, NT)
            d_score = (prob * slope).astype(BF16)
            dv_sum[rows, :] += mm(prob.astype(BF16), grad_here)
            dk_sum[rows, :] += mm(d_score, masked)
            part = mm(d_score, keys, TN)
            total = part if total is None else total + part
        out = total if head == 0 else jnp.where(lanes < HEAD_DIM, out, total)
    low = out.astype(BF16)
    half = pl.num_programs(0) // 2

    @pl.when(step < half)
    def _():
        keep_ref[0, here, :] = low

    @pl.when(step >= half)
    def _():
        send_ref[0, pl.ds(pl.multiple_of((step - half) * block, block), block), :] = low

    @pl.when(step == pl.num_programs(0) - 1)
    def _():
        for ref, rows in ((keep_ref, slice(0, PLANE)), (send_ref, slice(PLANE, GROUP))):
            ref[1] = (dk_sum[rows, :WIDE] * (1.0 / LOG2E)).astype(BF16)
            ref[2] = dv_sum[rows, :].astype(BF16)
        counts = dk_sum[:, WIDE:]
        bias_ref[...] = jnp.zeros_like(bias_ref)
        bias_ref[0:1, :] = jnp.sum(counts * hot_ref[...].astype(F32), axis=0, keepdims=True)
        bias_ref[1:2, :] = jnp.sum(counts, axis=0, keepdims=True)


def attend_back(mine, got, query_tail, key_tail, near, other, attended):
    block = 512
    moving = pl.BlockSpec((block, WIDE), lambda i: (i, 0))
    fixed = pl.BlockSpec((GROUP, WIDE), lambda i: (0, 0))
    plane = pl.BlockSpec((PLANE, WIDE), lambda i: (0, 0))
    three = pl.BlockSpec((3, PLANE, WIDE), lambda i: (0, 0, 0))
    low = jax.ShapeDtypeStruct((3, PLANE, WIDE), BF16)
    return pl.pallas_call(
        functools.partial(attend_back_kernel, chunks=4),
        grid=(GROUP // block,),
        in_specs=[three, three, moving, fixed, fixed, plane, plane, moving],
        out_specs=[three, three, pl.BlockSpec((8, WIDE), lambda i: (0, 0))],
        out_shape=[low, low, jax.ShapeDtypeStruct((8, WIDE), F32)],
        scratch_shapes=[
            pltpu.VMEM((3, GROUP, WIDE), BF16),
            pltpu.VMEM((GROUP, WIDE), BF16),
            pltpu.VMEM((GROUP, 2 * WIDE), F32),
            pltpu.VMEM((GROUP, WIDE), F32),
        ],
        compiler_params=pltpu.CompilerParams(vmem_limit_bytes=48 * 2**20),
        cost_estimate=pl.CostEstimate(
            flops=40 * GROUP * GROUP * WIDE, bytes_accessed=GROUP * WIDE * 24,
            transcendentals=2 * GROUP * GROUP,
        ),
    )(mine, got, query_tail, key_tail, query_tail, near, other, attended)


def feed_kernel(b_ref, g_ref, w_ref, y_ref, db_ref, act_ref, *, cuts):
    rows, grads = b_ref[...], g_ref[...]
    size = w_ref.shape[2] // cuts

    def products(j):
        cols = slice(j * size, (j + 1) * size)
        return mm(rows, w_ref[0, :, cols]), mm(rows, w_ref[1, :, cols]), mm(grads, w_ref[2, :, cols])

    y_sum, db_sum = None, None
    ready = products(0)
    for j in range(cuts):
        gate, up, d_hidden = ready
        if j + 1 < cuts:
            ready = products(j + 1)
        cols = slice(j * size, (j + 1) * size)
        sig = 0.5 + 0.5 * jnp.tanh(0.5 * gate)
        silu = gate * sig
        hidden = (silu * up).astype(BF16)
        d_gate = (d_hidden * up * (sig + silu * (1.0 - sig))).astype(BF16)
        d_up = (d_hidden * silu).astype(BF16)
        act_ref[0, :, cols] = d_gate
        act_ref[1, :, cols] = d_up
        act_ref[2, :, cols] = hidden
        y_part = mm(hidden, w_ref[2, :, cols], NT)
        db_part = mm(d_gate, w_ref[0, :, cols], NT) + mm(d_up, w_ref[1, :, cols], NT)
        y_sum = y_part if y_sum is None else y_sum + y_part
        db_sum = db_part if db_sum is None else db_sum + db_part
    y_ref[...] = y_sum.astype(BF16)
    db_ref[...] = db_sum.astype(BF16)


def feed(rows_b, rows_g, weights):
    rows = rows_b.shape[0]
    width = weights.shape[2]
    low_d = jax.ShapeDtypeStruct((rows, D), BF16)
    low_f = jax.ShapeDtypeStruct((3, rows, width), BF16)
    return pl.pallas_call(
        functools.partial(feed_kernel, cuts=2),
        out_shape=[low_d, low_d, low_f],
        compiler_params=pltpu.CompilerParams(vmem_limit_bytes=48 * 2**20),
        cost_estimate=pl.CostEstimate(
            flops=12 * rows * D * width, bytes_accessed=6 * D * width + rows * D * 8 + rows * width * 6,
            transcendentals=rows * width,
        ),
    )(rows_b, rows_g, weights)


def body(
    tokens,
    cotangent,
    destination,
    variate_ids,
    time_ids,
    seq_lengths,
    qkv_weight,
    out_weight,
    gate_up_weight,
    down_weight,
    norm_gains,
    qk_gains,
    variate_bias,
):
    core = lax.axis_index("core")
    low_core = core == 0
    y_at = lax.axis_index("y")
    zl_at = lax.axis_index("zl")

    core_scalar = core.reshape(1).astype(jnp.int32)

    def side_by_side(mine, other):
        return jnp.concatenate(
            [jnp.where(low_core, mine, other), jnp.where(low_core, other, mine)], axis=-1
        )

    out_shards = jnp.stack(gather_direct(out_weight.T))
    attn_shard = jnp.concatenate([qkv_weight, out_shards], 0)
    feed_shard = jnp.concatenate([gate_up_weight, down_weight.T[None]], 0)

    slot = destination % ROWS
    group_at = destination // GROUP
    block_at = (destination % GROUP) // ROWS
    device_at = ((group_at // 2) * 2 + block_at // 4) * 8 + (block_at % 4) * 2 + group_at % 2
    key = device_at * ROWS + slot
    zero = jnp.zeros_like(slot)
    facts = jnp.stack([key, slot, variate_ids, time_ids // 32, time_ids % 32, zero, zero, zero])
    gains_row = jnp.pad(
        norm_gains.reshape(8, 16), ((0, 0), (GAIN_LANE, WIDE - GAIN_LANE - 16))
    ).astype(F32)
    outgoing, deal = deal_rows(tokens, cotangent, facts.astype(F32), gains_row)
    arrived = lax.all_to_all(outgoing.reshape(DEVICES, 8, SPAN), ALL, 0, 0, tiled=True)
    attn_mine = gather_round(attn_shard, ("zh", "zl"), lax.axis_index("zh") * 2 + zl_at)
    attn_mine, arrived = lax.optimization_barrier((attn_mine, arrived))
    attn_mine = gather_round(attn_mine, "x", lax.axis_index("x")).reshape((16,) + attn_shard.shape)

    lengths_other = swap_core(seq_lengths)
    lengths = jnp.where(zl_at == core, seq_lengths, lengths_other)[0]
    bias_other = lax.ppermute(variate_bias, "zl", [(0, 1), (1, 0)])
    bias_pair = jnp.where(zl_at == core, variate_bias, bias_other)

    all_gains = arrived.reshape(16, 8, 8, SPAN)[:, 0, :, PAIR + GAIN_LANE : PAIR + GAIN_LANE + 16]
    inputs, grad_rows, attn_in, place, gains = receive(
        arrived.reshape(4 * ROWS, SPAN), all_gains.reshape(16, WIDE)
    )
    ahead, behind = ring(attn_in, -1), ring(attn_in, 1)
    ahead, behind, attn_mine = lax.optimization_barrier((ahead, behind, attn_mine))
    attn_w = assemble(core_scalar, attn_mine, swap_core(attn_mine), 2)
    far_top, far_low = ring(ahead[: ROWS // 2], -1), ring(behind[ROWS // 2 :], 1)
    far_top, attn_w = lax.optimization_barrier((far_top, attn_w))
    attn_all = [attn_in, ahead, jnp.concatenate([far_top, far_low], 0), behind]
    feed_shard, attn_in = lax.optimization_barrier((feed_shard, attn_in))
    feed_mine = flat_gather(feed_shard)
    grad_rows, attn_all = lax.optimization_barrier((grad_rows, attn_all))
    grad_all = gather_direct(grad_rows)

    blocks_y = (y_at + jnp.arange(RING)) % RING
    blocks = jnp.concatenate([core * RING + blocks_y, (1 - core) * RING + blocks_y])
    at = jnp.concatenate([blocks * ROWS, jnp.cumsum(lengths)]).astype(jnp.int32)

    inverse = THETA ** (-2.0 * jnp.arange(HALF).astype(F32) / HEAD_DIM)
    freq = jnp.concatenate(
        [
            jnp.tile(inverse, 8)[None],
            jnp.tile(qk_gains, (1, 4)),
            jnp.zeros((5, 2 * WIDE), F32),
        ]
    )
    qkv_mine, qkv_send, raw, facts_all = project(core_scalar, attn_all, attn_w, freq)
    facts_other = swap_core(facts_all)
    qkv_got = swap_core(qkv_send)

    bias_parts = jnp.stack(pieces(bias_pair * LOG2E, 3)).astype(F32)
    bias_rows = jnp.repeat(bias_parts, VARIATES, axis=0).transpose(1, 2, 0)
    bias_rows = jnp.pad(bias_rows, ((0, 0), (0, 0), (0, HEAD_DIM - 3 * VARIATES))).reshape(2, WIDE)
    bias_rows = jnp.pad(bias_rows, ((0, 6), (0, 0)))
    attended, att_near, att_send, query_back, key_tail = attend(
        at, qkv_mine, qkv_got, facts_all, facts_other, bias_rows
    )
    att_near, grad_all = lax.optimization_barrier((att_near, grad_all))
    att_other = swap_core(att_send)
    att_plane = side_by_side(att_near, att_other).reshape(RING, ROWS, 2 * WIDE)
    att_rows = trade_ring([att_plane[r] for r in range(RING)])
    att_rows[1], feed_mine = lax.optimization_barrier((att_rows[1], feed_mine))
    feed_w = assemble(core_scalar, feed_mine, swap_core(feed_mine), 4)
    hidden_one, feed_in = out_project(att_rows, attn_w, inputs, gains)

    ahead, behind = ring(feed_in, -1), ring(feed_in, 1)
    fed_own = feed(feed_in, grad_all[0], feed_w)
    ahead, behind, fed_own = lax.optimization_barrier((ahead, behind, fed_own))
    far_top, far_low = ring(ahead[: ROWS // 2], -1), ring(behind[ROWS // 2 :], 1)
    fed_ahead = feed(ahead, grad_all[1], feed_w)
    fed_behind = feed(behind, grad_all[3], feed_w)
    far_top, far_low, fed_ahead, fed_behind = lax.optimization_barrier(
        (far_top, far_low, fed_ahead, fed_behind)
    )
    far = jnp.concatenate([far_top, far_low], 0)
    fed_far = feed(far, grad_all[2], feed_w)
    feed_all = [feed_in, ahead, far, behind]
    fed = [fed_own, fed_ahead, fed_far, fed_behind]
    feed_split = weight_grads(core_scalar, feed_all, grad_all, [f[2] for f in fed], 2, 2)
    db_got = send_ring([f[1] for f in fed], True)
    db_got, feed_split = lax.optimization_barrier((db_got, feed_split))
    grad_one, gain_two_grad, d_att, *both = middle(
        att_rows, attn_w, [f[0] for f in fed], fed_own[1], db_got, hidden_one, grad_rows, gains
    )
    feed_total = chip_total(feed_split)
    feed_got = trade(feed_total, "x")

    grad_att = jnp.concatenate(trade_ring([d_att[r] for r in range(RING)]), 0)
    both, grad_att = lax.optimization_barrier((both, grad_att))
    both_got = send_ring(both)
    grad_left, grad_right = grad_att[:, :WIDE], grad_att[:, WIDE:]
    grad_other = swap_core(jnp.where(low_core, grad_right, grad_left))
    grad_near = jnp.where(low_core, grad_left, grad_right)
    d_keep, d_send, bias_sums = attend_back(
        qkv_mine, qkv_got, query_back, key_tail, grad_near, grad_other, attended
    )
    first_part = (jnp.arange(HEAD_DIM) < VARIATES)[None, None]
    bias_sums = jnp.where(first_part, bias_sums[:2].reshape(2, 2, HEAD_DIM), 0.0)
    bias_sums = jnp.sum(bias_sums, axis=2)
    bias_part = jnp.stack([bias_sums[0], bias_sums[1] - bias_sums[0]])
    d_send, both_got, feed_got = lax.optimization_barrier((d_send, both_got, feed_got))
    both_sum = add_ring(both[0], both_got)
    mixed = (hidden_one + both_sum[:ROWS]).astype(BF16)
    out_full = both_sum[ROWS:].astype(BF16)
    feed_half = added(feed_got).astype(BF16)
    grad_proj, in_part, qk_sums = unproject(
        core_scalar, d_keep, swap_core(d_send), raw, facts_all, attn_w, freq
    )
    in_part = in_part.reshape(RING, ROWS, D)
    in_got = send_ring([in_part[r] for r in range(RING)])
    attn_split = weight_grads(core_scalar, attn_all, [out_full], [grad_proj], None, 1)
    attn_total = chip_total(attn_split)
    in_got, _ = lax.optimization_barrier((in_got, attn_split))
    mixed, _ = lax.optimization_barrier((mixed, attn_total))
    attn_own, attn_got = send_round(attn_total.reshape((RING, RING) + attn_total.shape[1:]), "x")
    qk_sums = jnp.sum(qk_sums[:2].reshape(2, 4, HEAD_DIM), axis=1)

    small = jnp.zeros((8, WIDE), F32).at[0].set(qk_sums.reshape(WIDE))
    small = small.at[1, :4].set(bias_part.reshape(4))
    tensor_at = (y_at * 2 + core).reshape(1).astype(jnp.int32)
    last = finish(
        in_part[0], in_got, inputs, grad_one, mixed, place, gains, gain_two_grad, small, tensor_at
    )
    last = last.reshape(DEVICES, 8, 2 * QUARTER + WIDE)
    last, attn_got, feed_half = lax.optimization_barrier((last, attn_got, feed_half))
    home = lax.all_to_all(last, ALL, 0, 0, tiled=True)
    halves = add_round(attn_own, attn_got).astype(BF16).reshape(RING, 64, 512)
    halves = jnp.concatenate([feed_half.reshape(RING, 192, 512), halves], 1)
    own, got = send_round(halves, ("zh", "zl"))
    home, got = lax.optimization_barrier((home, got))
    whole = add_round(own, got)
    feed_grad = whole[:192].reshape(3, 64, 512)
    attn_grad = whole[192:].reshape(4, 64, 128)
    new_tokens, token_grads, sums = settle(home.reshape(4 * ROWS, 2 * QUARTER + WIDE), deal)
    gains_grad = sums[0].reshape(2, 64)
    qk_grad = sums[1].reshape(2, 64)
    bias_grad = sums[2, :4].reshape(2, 2)

    return (
        new_tokens,
        token_grads,
        attn_grad[:3],
        attn_grad[3].T,
        feed_grad[:2],
        feed_grad[2].T,
        gains_grad,
        qk_grad,
        bias_grad,
    )


def solution(mesh):
    fine = Mesh(mesh.devices.reshape(4, 2, 2, 4, 2), ALL)
    dp = ("x", "zh", "core")
    tensor = ("y", "zl")
    in_specs = (
        P(ALL, None),
        P(ALL, None),
        P(ALL),
        P(ALL),
        P(ALL),
        P(dp, None),
        P(None, dp, tensor),
        P(tensor, dp),
        P(None, dp, tensor),
        P(tensor, dp),
        P(None, dp),
        P(),
        P(None, tensor),
    )
    out_specs = (
        P(ALL, None),
        P(ALL, None),
        P(None, dp, tensor),
        P(tensor, dp),
        P(None, dp, tensor),
        P(tensor, dp),
        P(None, dp),
        P(),
        P(None, tensor),
    )
    return jax.shard_map(body, mesh=fine, in_specs=in_specs, out_specs=out_specs, check_vma=False)
```

```python
import functools

import jax
import jax.numpy as jnp
from jax import lax
from jax.experimental import pallas as pl
from jax.experimental.pallas import tpu as pltpu
from jax.sharding import Mesh
from jax.sharding import PartitionSpec as P

HEADS = 16
HEAD_DIM = 64
HALF = HEAD_DIM // 2
D = 1024
FF = 4096
ROWS = 256
RING = 4
PLANE = ROWS * RING
GROUP = 2 * PLANE
DEVICES = 128
VARIATES = 8
SEQS = 4
WIDE = 128
EPS = 1e-06
THETA = 10000.0
LOG2E = 1.4426950408889634
FAR = -16384.0
F32 = jnp.float32
BF16 = jnp.bfloat16

ALL = ("x", "zh", "core", "y", "zl")
FLAT = ("x", "zh", "zl")
NT = (((1,), (1,)), ((), ()))
TN = (((0,), (0,)), ((), ()))


def mm(left, right, dims=(((1,), (0,)), ((), ()))):
    return lax.dot_general(left, right, dims, preferred_element_type=F32)


def root_stats(values):
    return lax.rsqrt(jnp.mean(values * values, axis=-1, keepdims=True) + EPS)


def norm_back(grad_in, normed, scale_inv):
    return scale_inv * (grad_in - normed * jnp.mean(grad_in * normed, axis=-1, keepdims=True))


def pieces(values, count):
    out = []
    for _ in range(count):
        part = lax.reduce_precision(values, 8, 7)
        out.append(part.astype(BF16))
        values = values - part
    return out


def ring(values, step):
    return lax.ppermute(values, "y", [(i, (i + step) % RING) for i in range(RING)])


def swap_core(values):
    return lax.ppermute(values, "core", [(0, 1), (1, 0)])


def gather_ring(values):
    ahead = ring(values, -1)
    behind = ring(values, 1)
    half = values.shape[0] // 2
    far_top = ring(ahead[:half], -1)
    far_low = ring(behind[half:], 1)
    return [values, ahead, jnp.concatenate([far_top, far_low], 0), behind]


def gather_direct(values):
    return [values, ring(values, -1), ring(values, 2), ring(values, 1)]


def trade_ring(parts):
    return [parts[0]] + [ring(parts[RING - s], -s) for s in range(1, RING)]


def send_ring(parts, halves=False):
    half = parts[2].shape[0] // 2
    far = [parts[2][:half], parts[2][half:]] if halves else [parts[2]]
    return [ring(parts[1], 1), ring(parts[3], -1)] + [ring(v, 2) for v in far]


def add_ring(own, got):
    far = got[2] if len(got) == 3 else jnp.concatenate(got[2:], 0)
    return own.astype(F32) + got[0].astype(F32) + got[1].astype(F32) + far.astype(F32)


def gather_ahead(values, axes):
    moves = [[((i + r) % RING, i) for i in range(RING)] for r in range(RING)]
    return [values] + [lax.ppermute(values, axes, moves[r]) for r in range(1, RING)]


def gather_round(values, axes, at):
    return jnp.roll(jnp.stack(gather_ahead(values, axes)), at, axis=0)


def flat_gather(shard):
    many = jnp.broadcast_to(shard[None], (16,) + shard.shape)
    return lax.all_to_all(many, FLAT, 0, 0, tiled=True)


def assemble_kernel(at_ref, mine_ref, other_ref, out_ref):
    core = at_ref[0]
    count, _, depth, width = mine_ref.shape
    for ref, side in ((mine_ref, core), (other_ref, 1 - core)):
        for i in range(count):
            at = (i // 2) * 2 * depth + side * depth
            rows = pl.ds(pl.multiple_of(at, depth), depth)
            out_ref[:, rows, (i % 2) * width : (i % 2 + 1) * width] = ref[i]


def assemble(core, x_at, mine, other):
    _, kinds, depth, width = mine.shape
    pair = pl.BlockSpec((4, kinds, depth, width), lambda p, at: (p, 0, 0, 0))
    return pl.pallas_call(
        assemble_kernel,
        grid_spec=pltpu.PrefetchScalarGridSpec(
            num_scalar_prefetch=1,
            grid=(RING,),
            in_specs=[pair, pair],
            out_specs=pl.BlockSpec(
                (kinds, 4 * depth, 2 * width), lambda p, at: (0, lax.rem(at[1] + p, RING), 0)
            ),
        ),
        out_shape=jax.ShapeDtypeStruct((kinds, 16 * depth, 2 * width), BF16),
        compiler_params=pltpu.CompilerParams(vmem_limit_bytes=28 * 2**20),
        cost_estimate=pl.CostEstimate(
            flops=0, bytes_accessed=kinds * 128 * depth * width, transcendentals=0
        ),
    )(jnp.concatenate([core, x_at]), mine, other)


def chip_total(split):
    return (split[0].astype(F32) + swap_core(split[1]).astype(F32)).astype(BF16)


def send_round(values, axes):
    at = lax.axis_index(axes)
    parts = [lax.dynamic_index_in_dim(values, (at + r) % RING, 0, keepdims=False) for r in range(RING)]
    moves = [[(i, (i + r) % RING) for i in range(RING)] for r in range(RING)]
    return parts[0], [lax.ppermute(parts[r], axes, moves[r]) for r in (1, 3, 2)]


def add_round(own, got):
    return sum((v.astype(F32) for v in got), own.astype(F32))


def trade(values, axes):
    return lax.all_to_all(values.reshape((RING, -1) + values.shape[1:]), axes, 0, 0, tiled=True)


def added(got):
    return jnp.sum(got.astype(F32), axis=0)


def lanes_of(shape):
    return lax.broadcasted_iota(jnp.int32, shape, 1)


QUARTER = D // RING
PAIR = 2 * QUARTER
SPAN = PAIR + WIDE
GAIN_LANE = 16


def deal_kernel(tok_ref, cot_ref, facts_ref, gains_ref, out_ref, deal_ref):
    wide = jnp.concatenate([facts_ref[...], jnp.zeros((WIDE - 8, ROWS), F32)], 0)
    facts = jnp.transpose(wide)
    keys = facts_ref[0:1, :]
    rank = jnp.sum((facts[:, 0:1] < keys).astype(F32), axis=0, keepdims=True)
    at = lax.broadcasted_iota(jnp.int32, (ROWS, ROWS), 0).astype(F32)
    deal_ref[...] = (at == rank).astype(BF16)
    low = jnp.where(lanes_of(facts.shape) == 0, 0.0, facts).astype(BF16)
    row = lax.broadcasted_iota(jnp.int32, (4 * ROWS, 1), 0)
    own = ((row // RING).astype(F32) == rank).astype(BF16)
    part = None
    for m in range(RING):
        cols = slice(m * QUARTER, (m + 1) * QUARTER)
        here = mm(own, jnp.concatenate([tok_ref[:, cols], cot_ref[:, cols]], 1))
        part = here if m == 0 else jnp.where(row % RING == m, here, part)
    out_ref[:, :PAIR] = part.astype(BF16)
    tail = mm(own, low)
    lane = lanes_of(tail.shape)
    gains = jnp.broadcast_to(gains_ref[...][None], (DEVICES, 8, WIDE)).reshape(tail.shape)
    tail = jnp.where((lane >= GAIN_LANE) & (lane < GAIN_LANE + 16), gains, tail)
    out_ref[:, PAIR:] = tail.astype(BF16)


def deal_rows(tokens, cotangent, facts, gains):
    return pl.pallas_call(
        deal_kernel,
        out_shape=[
            jax.ShapeDtypeStruct((4 * ROWS, SPAN), BF16),
            jax.ShapeDtypeStruct((ROWS, ROWS), BF16),
        ],
        compiler_params=pltpu.CompilerParams(vmem_limit_bytes=48 * 2**20),
        cost_estimate=pl.CostEstimate(
            flops=8 * ROWS * ROWS * 2304, bytes_accessed=ROWS * D * 16, transcendentals=0
        ),
    )(tokens, cotangent, facts, gains)


def receive_kernel(rows_ref, gains_ref, x_ref, g_ref, a_ref, place_ref, gain_ref):
    count = 4 * ROWS
    facts = rows_ref[:, PAIR:]
    slots = jnp.transpose(facts.astype(F32))[1:2, :]
    at = lax.broadcasted_iota(jnp.int32, (ROWS, count), 0)
    arrival = lanes_of((ROWS, count))
    here = at.astype(F32) == slots
    gains = gains_ref[...].astype(F32)
    turned = pltpu.roll(gains, HEAD_DIM, 1)
    left = lanes_of((1, WIDE)) < HEAD_DIM
    one, two = [], []
    for c in range(D // WIDE):
        even, odd = slice(2 * c, 2 * c + 1), slice(2 * c + 1, 2 * c + 2)
        one.append(jnp.where(left, gains[even], turned[odd]))
        two.append(jnp.where(left, turned[even], gains[odd]))
    gain_one = jnp.concatenate(one, 1)
    gain_ref[...] = jnp.zeros_like(gain_ref)
    gain_ref[0:1, :] = gain_one
    gain_ref[1:2, :] = jnp.concatenate(two, 1)
    quarters = []
    for m in range(RING):
        chosen = (here & (arrival % RING == m)).astype(BF16)
        both = mm(chosen, rows_ref[:, :PAIR])
        quarters.append(both[:, :QUARTER])
        g_ref[:, m * QUARTER : (m + 1) * QUARTER] = both[:, QUARTER:].astype(BF16)
        if m == 0:
            a_ref[:, D:] = mm(chosen, facts).astype(BF16)
            pick = (at * RING == arrival).astype(BF16)
            place_ref[...] = mm(chosen, pick, NT).astype(BF16)
    rows = jnp.concatenate(quarters, 1)
    x_ref[...] = rows
    a_ref[:, :D] = (rows * root_stats(rows) * gain_one).astype(BF16)


def receive(rows, gains):
    return pl.pallas_call(
        receive_kernel,
        out_shape=[
            jax.ShapeDtypeStruct((ROWS, D), F32),
            jax.ShapeDtypeStruct((ROWS, D), BF16),
            jax.ShapeDtypeStruct((ROWS, D + WIDE), BF16),
            jax.ShapeDtypeStruct((ROWS, ROWS), BF16),
            jax.ShapeDtypeStruct((8, D), F32),
        ],
        compiler_params=pltpu.CompilerParams(vmem_limit_bytes=48 * 2**20),
        cost_estimate=pl.CostEstimate(
            flops=16 * ROWS * ROWS * D, bytes_accessed=ROWS * D * 24, transcendentals=0
        ),
    )(rows, gains)


def out_kernel(*refs):
    att = refs[:RING]
    w_ref, x_ref, gain_ref, h_ref, b_ref = refs[RING:]
    hidden = x_ref[...]
    for r in range(RING):
        hidden = hidden + mm(att[r][...], w_ref[r], NT)
    h_ref[...] = hidden
    b_ref[...] = (hidden * root_stats(hidden) * gain_ref[1:2, :]).astype(BF16)


def out_project(att, weights, rows, gains):
    return pl.pallas_call(
        out_kernel,
        out_shape=[jax.ShapeDtypeStruct((ROWS, D), F32), jax.ShapeDtypeStruct((ROWS, D), BF16)],
        compiler_params=pltpu.CompilerParams(vmem_limit_bytes=48 * 2**20),
        cost_estimate=pl.CostEstimate(
            flops=2 * ROWS * D * D, bytes_accessed=2 * D * D + ROWS * D * 14, transcendentals=0
        ),
    )(*att, weights, rows, gains)


def middle_kernel(*refs):
    att, y_parts, w_ref = refs[:RING], refs[RING : 2 * RING], refs[2 * RING]
    refs = refs[2 * RING + 1 :]
    own_ref, near_ref, back_ref, top_ref, low_ref, h_ref, g_ref, gain_ref = refs[:8]
    grad_ref, two_ref, d_ref = refs[8:11]
    both_refs = refs[11:]
    far = jnp.concatenate([top_ref[...], low_ref[...]], 0).astype(F32)
    grad = own_ref[...].astype(F32) + near_ref[...].astype(F32) + back_ref[...].astype(F32) + far
    hidden = h_ref[...]
    scale = root_stats(hidden)
    normed = hidden * scale
    two_ref[...] = jnp.zeros_like(two_ref)
    two_ref[0:1, :] = jnp.sum(grad * normed, axis=0, keepdims=True)
    scaled = grad * gain_ref[1:2, :]
    grad = g_ref[...].astype(F32) + norm_back(scaled, normed, scale)
    grad_ref[...] = grad
    low = grad.astype(BF16)
    for r in range(RING):
        d_ref[r] = mm(low, w_ref[r]).astype(BF16)
        both_refs[r][:ROWS] = y_parts[r][...]
        both_refs[r][ROWS:] = mm(att[r][...], low, TN).astype(BF16)


def middle(att, weights, y_parts, own, got, hidden, grad_rows, gains):
    both = jax.ShapeDtypeStruct((2 * ROWS, D), BF16)
    return pl.pallas_call(
        middle_kernel,
        out_shape=[
            jax.ShapeDtypeStruct((ROWS, D), F32),
            jax.ShapeDtypeStruct((8, D), F32),
            jax.ShapeDtypeStruct((RING, ROWS, ROWS), BF16),
        ]
        + [both] * RING,
        compiler_params=pltpu.CompilerParams(vmem_limit_bytes=48 * 2**20),
        cost_estimate=pl.CostEstimate(
            flops=4 * ROWS * D * D, bytes_accessed=2 * D * D + ROWS * D * 40, transcendentals=0
        ),
    )(*att, *y_parts, weights, own, *got, hidden, grad_rows, gains)


def finish_kernel(
    own_ref, near_ref, back_ref, far_ref, x_ref, grad_ref, mixed_ref, place_ref,
    gain_ref, two_ref, small_ref, at_ref, out_ref,
):
    rows = x_ref[...]
    scale = root_stats(rows)
    normed = rows * scale
    far = far_ref[...].astype(F32)
    grad = own_ref[...].astype(F32) + near_ref[...].astype(F32) + back_ref[...].astype(F32) + far
    one = jnp.sum(grad * normed, axis=0, keepdims=True)
    two = two_ref[0:1, :]
    scaled = grad * gain_ref[0:1, :]
    back = scale * (scaled - normed * jnp.mean(scaled * normed, axis=1, keepdims=True))
    result = (grad_ref[...] + back).astype(BF16)
    count = 4 * ROWS
    row = lax.broadcasted_iota(jnp.int32, (count, 1), 0)
    quarter = row % RING
    pick = (row // RING == lanes_of((count, ROWS))).astype(BF16)
    pick = mm(pick, place_ref[...], NT).astype(BF16)
    part = None
    for m in range(RING):
        cols = slice(m * QUARTER, (m + 1) * QUARTER)
        here = mm(pick, jnp.concatenate([mixed_ref[:, cols], result[:, cols]], 1))
        part = here if m == 0 else jnp.where(quarter == m, here, part)
    out_ref[:, : 2 * QUARTER] = part.astype(BF16)
    left = lanes_of((1, WIDE)) < HEAD_DIM
    tiles = []
    for c in range(D // WIDE):
        cols = slice(c * WIDE, (c + 1) * WIDE)
        a, b = one[:, cols], two[:, cols]
        even = jnp.where(left, a, pltpu.roll(jnp.broadcast_to(b, (8, WIDE)), HEAD_DIM, 1)[0:1])
        odd = jnp.where(left, pltpu.roll(jnp.broadcast_to(a, (8, WIDE)), HEAD_DIM, 1)[0:1], b)
        tiles += [jnp.broadcast_to(even, (64, WIDE)), jnp.broadcast_to(odd, (64, WIDE))]
    value = jnp.concatenate(tiles, 0)
    value = jnp.where(quarter == 1, small_ref[0:1, :], value)
    bias = jnp.where((row // 8) % 8 == at_ref[0], small_ref[1:2, :], 0.0)
    value = jnp.where(quarter == 2, bias, value)
    high = value.astype(BF16).astype(F32)
    value = jnp.where((row // RING) % 2 == 0, high, value - high)
    out_ref[:, 2 * QUARTER :] = value.astype(BF16)


def finish(own, got, rows, grad, mixed, place, gains, two, small, at):
    specs = [pl.BlockSpec(memory_space=pltpu.VMEM)] * 11
    return pl.pallas_call(
        finish_kernel,
        in_specs=specs + [pl.BlockSpec(memory_space=pltpu.SMEM)],
        out_shape=jax.ShapeDtypeStruct((4 * ROWS, 2 * QUARTER + WIDE), BF16),
        compiler_params=pltpu.CompilerParams(vmem_limit_bytes=48 * 2**20),
        cost_estimate=pl.CostEstimate(
            flops=16 * ROWS * ROWS * D, bytes_accessed=ROWS * D * 20, transcendentals=0
        ),
    )(own, *got, rows, grad, mixed, place, gains, two, small, at)


def settle_kernel(home_ref, deal_ref, rows_ref, grads_ref, sums_ref):
    deal = deal_ref[...]
    shape = (ROWS, 4 * ROWS)
    index = lax.broadcasted_iota(jnp.int32, shape, 0)
    for m in range(RING):
        pick = (index * RING + m == lanes_of(shape)).astype(BF16)
        here = mm(pick, home_ref[:, : 2 * QUARTER]).astype(BF16)
        here = mm(deal, here, TN).astype(BF16)
        cols = slice(m * QUARTER, (m + 1) * QUARTER)
        rows_ref[:, cols] = here[:, :QUARTER]
        grads_ref[:, cols] = here[:, QUARTER:]
    small = home_ref[:, 2 * QUARTER :].astype(F32)
    quarter = lax.broadcasted_iota(jnp.int32, small.shape, 0) % RING
    sums_ref[...] = jnp.zeros_like(sums_ref)
    for m in range(3):
        sums_ref[m : m + 1, :] = jnp.sum(jnp.where(quarter == m, small, 0.0), axis=0, keepdims=True)


def settle(home, deal):
    low = jax.ShapeDtypeStruct((ROWS, D), BF16)
    return pl.pallas_call(
        settle_kernel,
        out_shape=[low, low, jax.ShapeDtypeStruct((8, WIDE), F32)],
        compiler_params=pltpu.CompilerParams(vmem_limit_bytes=48 * 2**20),
        cost_estimate=pl.CostEstimate(
            flops=20 * ROWS * ROWS * D, bytes_accessed=ROWS * D * 16, transcendentals=0
        ),
    )(home, deal)


def weight_grad_kernel(core_ref, *refs, parts, count, switch, steps):
    given = switch is None
    lefts, others, rights = refs[:parts], refs[parts : parts + count], refs[parts + count : -3]
    keep_ref, send_ref, turned_ref = refs[-3:]
    low = core_ref[0] == 0
    step = pl.program_id(0)

    def load(sides):
        at = 0
        for side in sides:
            rows = side.shape[0]
            turned_ref[:, at : at + rows] = side[...].T
            at += rows

    @pl.when(step == 0)
    def _():
        load(lefts)

    if not given:

        @pl.when(step == switch * steps)
        def _():
            load(others)

    def emit(total):
        depth = total.shape[0] // 16
        width = keep_ref.shape[-1]
        for z in range(total.shape[1] // width):
            cols = slice(z * width, (z + 1) * width)
            for p in range(8):
                at = 2 * p * depth
                even, odd = total[at : at + depth, cols], total[at + depth : at + 2 * depth, cols]
                keep_ref[p, z, 0] = jnp.where(low, even, odd)
                send_ref[p, z, 0] = jnp.where(low, odd, even)

    def product():
        right = jnp.concatenate([ref[0] for ref in rights], 0)
        emit(mm(turned_ref[...], right).astype(BF16))

    if given:
        pl.when(step < pl.num_programs(0) - 1)(product)

        @pl.when(step == pl.num_programs(0) - 1)
        def _():
            emit(others[0][...].T)
    else:
        product()


def weight_grads(core, lefts, others, rights, switch, steps):
    parts = len(lefts)
    made, _, width = rights[0].shape
    kinds = made + 1 if switch is None else made
    block, half = width // steps, width // 2
    sides = [pl.BlockSpec((v.shape[0], D), lambda s: (0, 0)) for v in list(lefts) + list(others)]
    moving = [
        pl.BlockSpec(
            (1, v.shape[1], block), lambda s: (jnp.minimum(s // steps, made - 1), 0, s % steps)
        )
        for v in rights
    ]
    rows = sum(v.shape[1] for v in rights)
    out = pl.pallas_call(
        functools.partial(
            weight_grad_kernel, parts=parts, count=len(others), switch=switch, steps=steps
        ),
        grid=(kinds * steps,),
        in_specs=[pl.BlockSpec(memory_space=pltpu.SMEM)] + sides + moving,
        out_specs=[
            pl.BlockSpec((8, 2 // steps, 1, 64, half), lambda s: (0, s % steps, s // steps, 0, 0))
        ]
        * 2,
        out_shape=[jax.ShapeDtypeStruct((8, 2, kinds, 64, half), BF16)] * 2,
        scratch_shapes=[pltpu.VMEM((D, rows), BF16)],
        compiler_params=pltpu.CompilerParams(vmem_limit_bytes=28 * 2**20),
        cost_estimate=pl.CostEstimate(
            flops=2 * kinds * rows * D * width,
            bytes_accessed=2 * kinds * D * width + 4 * rows * D + 2 * kinds * rows * width,
            transcendentals=0,
        ),
    )(core, *lefts, *others, *rights)
    return [v.reshape(16, kinds, 64, half) for v in out]


def head_sums(values):
    wide = values.shape[1]
    row = lax.broadcasted_iota(jnp.int32, (wide, wide), 0) // HEAD_DIM
    same = (row == lanes_of((wide, wide)) // HEAD_DIM).astype(BF16)
    high = values.astype(BF16)
    low = (values - high.astype(F32)).astype(BF16)
    return mm(high, same) + mm(low, same)


def partner(values):
    wide = values.shape[1]
    first = lanes_of(values.shape) % HEAD_DIM < HALF
    return jnp.where(first, pltpu.roll(values, wide - HALF, 1), pltpu.roll(values, HALF, 1))


def angles_of(facts, freq_ref):
    facts = facts.astype(F32)
    times = facts[:, 3:4] * 32.0 + facts[:, 4:5]
    angle = times * freq_ref[0:1, :WIDE]
    first = lanes_of(angle.shape) % HEAD_DIM < HALF
    cosine = jnp.cos(angle)
    sine = jnp.sin(angle)
    sine = jnp.where(first, -sine, sine)
    return jnp.concatenate([cosine, cosine], 1), jnp.concatenate([sine, sine], 1)


def project_kernel(core_ref, *refs):
    pieces_in = refs[:RING]
    w_ref, freq_ref, mine_ref, send_ref, raw_ref, facts_ref = refs[RING:]
    low = core_ref[0] == 0
    for r in range(RING):
        block = slice(r * ROWS, (r + 1) * ROWS)
        rows = pieces_in[r][:, :D]
        facts = pieces_in[r][:, D:]
        facts_ref[block] = facts
        cosine, sine = angles_of(facts, freq_ref)
        for kind in range(3):
            value = mm(rows, w_ref[kind])
            if kind < 2:
                raw_ref[kind, block] = value
                unit = value * lax.rsqrt(head_sums(value * value) * (1.0 / HEAD_DIM) + EPS)
                value = unit * freq_ref[1 + kind : 2 + kind, :]
                value = value * cosine + partner(value) * sine
            if kind == 0:
                value = value * (HEAD_DIM ** (-0.5) * LOG2E)
            left, right = value[:, :WIDE], value[:, WIDE:]
            mine_ref[kind, block] = jnp.where(low, left, right).astype(BF16)
            send_ref[kind, block] = jnp.where(low, right, left).astype(BF16)


def project(core, rows, attn_w, freq):
    low = jax.ShapeDtypeStruct((3, PLANE, WIDE), BF16)
    whole = pl.BlockSpec(memory_space=pltpu.VMEM)
    return pl.pallas_call(
        project_kernel,
        in_specs=[pl.BlockSpec(memory_space=pltpu.SMEM)] + [whole] * (RING + 2),
        out_shape=[
            low,
            low,
            jax.ShapeDtypeStruct((2, PLANE, 2 * WIDE), F32),
            jax.ShapeDtypeStruct((PLANE, WIDE), BF16),
        ],
        compiler_params=pltpu.CompilerParams(vmem_limit_bytes=48 * 2**20),
        cost_estimate=pl.CostEstimate(
            flops=8 * PLANE * D * 2 * WIDE, bytes_accessed=PLANE * D * 8, transcendentals=PLANE * 1024
        ),
    )(core, *rows, attn_w, freq)


def unproject_kernel(
    core_ref, mine_ref, got_ref, raw_ref, facts_ref, w_ref, freq_ref, dp_ref, part_ref, gain_ref
):
    low = core_ref[0] == 0
    cosine, sine = angles_of(facts_ref[...], freq_ref)

    @pl.when(pl.program_id(0) == 0)
    def _():
        gain_ref[...] = jnp.zeros_like(gain_ref)

    total = None
    for kind in range(3):
        mine, got = mine_ref[kind], got_ref[kind]
        grad = jnp.concatenate([jnp.where(low, mine, got), jnp.where(low, got, mine)], 1)
        if kind < 2:
            grad = grad.astype(F32)
            if kind == 0:
                grad = grad * (HEAD_DIM ** (-0.5))
            raw = raw_ref[kind]
            inv = lax.rsqrt(head_sums(raw * raw) * (1.0 / HEAD_DIM) + EPS)
            unit = raw * inv
            grad = grad * cosine - partner(grad) * sine
            gain_ref[kind : kind + 1, :] += jnp.sum(grad * unit, axis=0, keepdims=True)
            scaled = grad * freq_ref[1 + kind : 2 + kind, :]
            mean = head_sums(scaled * unit) * (1.0 / HEAD_DIM)
            grad = (inv * (scaled - unit * mean)).astype(BF16)
        dp_ref[kind] = grad
        part = mm(grad, w_ref[kind], NT)
        total = part if total is None else total + part
    part_ref[...] = total.astype(BF16)


def unproject(core, mine, got, raw, rows_all, attn_w, freq):
    block = 512
    both = pl.BlockSpec((3, block, WIDE), lambda i: (0, i, 0))
    return pl.pallas_call(
        unproject_kernel,
        grid=(PLANE // block,),
        in_specs=[
            pl.BlockSpec(memory_space=pltpu.SMEM),
            both,
            both,
            pl.BlockSpec((2, block, 2 * WIDE), lambda i: (0, i, 0)),
            pl.BlockSpec((block, WIDE), lambda i: (i, 0)),
            pl.BlockSpec((3, D, 2 * WIDE), lambda i: (0, 0, 0)),
            pl.BlockSpec((8, 2 * WIDE), lambda i: (0, 0)),
        ],
        out_specs=[
            pl.BlockSpec((3, block, 2 * WIDE), lambda i: (0, i, 0)),
            pl.BlockSpec((block, D), lambda i: (i, 0)),
            pl.BlockSpec((8, 2 * WIDE), lambda i: (0, 0)),
        ],
        out_shape=[
            jax.ShapeDtypeStruct((3, PLANE, 2 * WIDE), BF16),
            jax.ShapeDtypeStruct((PLANE, D), BF16),
            jax.ShapeDtypeStruct((8, 2 * WIDE), F32),
        ],
        compiler_params=pltpu.CompilerParams(vmem_limit_bytes=48 * 2**20),
        cost_estimate=pl.CostEstimate(
            flops=8 * PLANE * D * 2 * WIDE, bytes_accessed=PLANE * D * 8, transcendentals=PLANE * 1024
        ),
    )(core, mine, got, raw, rows_all, attn_w, freq)


LOG_LANE = 3 * VARIATES + SEQS


def with_pieces(base, values, first_lane, lanes):
    for i in range(3):
        part = values.astype(BF16).astype(F32)
        base = jnp.where(lanes == first_lane + i, part, base)
        values = values - part
    return base


def value_lanes(rows):
    return (lanes_of((rows, WIDE)) < 3).astype(BF16)


def attend_kernel(
    at_ref, mine_ref, got_ref, own_ref, other_ref, bias_ref,
    att_ref, near_ref, send_ref, tail_ref, kt_ref, all_scr, qt_scr, *, chunks,
):
    step = pl.program_id(0)
    block = att_ref.shape[0]
    size = GROUP // chunks

    @pl.when(step == 0)
    def _():
        all_scr[:, :PLANE] = mine_ref[...]
        all_scr[:, PLANE:] = got_ref[...]
        lane = lanes_of((ROWS, WIDE))
        tail_lane = lane % HEAD_DIM
        bias_lane = tail_lane < 3 * VARIATES
        seg_lane = (tail_lane >= 3 * VARIATES) & (tail_lane < LOG_LANE)
        one_lane = (tail_lane >= LOG_LANE) & (tail_lane < LOG_LANE + 3)
        row = lax.broadcasted_iota(jnp.int32, (ROWS, WIDE), 0)
        for b in range(2 * RING):
            source = own_ref if b < RING else other_ref
            facts = source[(b % RING) * ROWS : (b % RING + 1) * ROWS, :].astype(F32)
            variate = facts[:, 2:3]
            equal = bias_lane & ((tail_lane % VARIATES).astype(F32) == variate)
            position = at_ref[b] + row
            segment = jnp.zeros_like(row)
            for j in range(SEQS):
                segment += (position >= at_ref[2 * RING + j]).astype(jnp.int32)
            inside = seg_lane & (tail_lane - 3 * VARIATES == segment)
            rows = slice(b * ROWS, (b + 1) * ROWS)
            qt_scr[rows] = (equal | inside).astype(BF16)
            tail = jnp.where(equal, bias_ref[0:1, :], bias_ref[1:2, :])
            tail = jnp.where(bias_lane, tail, jnp.where(one_lane, 1.0, 0.0))
            tail = jnp.where(seg_lane & ~inside, FAR, tail)
            kt_ref[rows] = tail.astype(BF16)

    here = pl.ds(pl.multiple_of(step * block, block), block)
    query_tail = qt_scr[here, :]
    query = jnp.concatenate([all_scr[0, here, :], query_tail], 1)
    zero = jnp.zeros_like(query)
    head_of = (lanes_of(query.shape) // HEAD_DIM) % 2
    lanes = lanes_of((block, WIDE))
    ones = value_lanes(size)
    out = None
    tail = query_tail.astype(F32)
    for head in range(2):
        masked = jnp.where(head_of == head, query, zero)
        total = None
        for c in range(chunks):
            rows = slice(c * size, (c + 1) * size)
            keys = jnp.concatenate([all_scr[1, rows, :], kt_ref[rows, :]], 1)
            values = jnp.concatenate([all_scr[2, rows, :], ones], 1)
            prob = jnp.exp2(mm(masked, keys, NT)).astype(BF16)
            part = mm(prob, values)
            total = part if total is None else total + part
        row_sum = total[:, WIDE : WIDE + 1]
        now = total[:, :WIDE] / row_sum
        out = now if head == 0 else jnp.where(lanes < HEAD_DIM, out, now)
        tail = with_pieces(tail, -jnp.log2(row_sum), head * HEAD_DIM + LOG_LANE, lanes)
    att_ref[...] = out
    tail_ref[...] = tail.astype(BF16)
    low = out.astype(BF16)
    half = pl.num_programs(0) // 2

    @pl.when(step < half)
    def _():
        near_ref[here, :] = low

    @pl.when(step >= half)
    def _():
        send_ref[pl.ds(pl.multiple_of((step - half) * block, block), block), :] = low


def attend(at, mine, got, facts, facts_other, bias_rows):
    block = 512
    moving = pl.BlockSpec((block, WIDE), lambda i: (i, 0))
    plane = pl.BlockSpec((PLANE, WIDE), lambda i: (0, 0))
    three = pl.BlockSpec((3, PLANE, WIDE), lambda i: (0, 0, 0))
    low = jax.ShapeDtypeStruct((GROUP, WIDE), BF16)
    low_plane = jax.ShapeDtypeStruct((PLANE, WIDE), BF16)
    return pl.pallas_call(
        functools.partial(attend_kernel, chunks=4),
        grid=(GROUP // block,),
        in_specs=[
            pl.BlockSpec(memory_space=pltpu.SMEM),
            three,
            three,
            plane,
            plane,
            pl.BlockSpec((8, WIDE), lambda i: (0, 0)),
        ],
        out_specs=[moving, plane, plane, moving, pl.BlockSpec((GROUP, WIDE), lambda i: (0, 0))],
        out_shape=[jax.ShapeDtypeStruct((GROUP, WIDE), F32), low_plane, low_plane, low, low],
        scratch_shapes=[pltpu.VMEM((3, GROUP, WIDE), BF16), pltpu.VMEM((GROUP, WIDE), BF16)],
        compiler_params=pltpu.CompilerParams(vmem_limit_bytes=48 * 2**20),
        cost_estimate=pl.CostEstimate(
            flops=16 * GROUP * GROUP * WIDE, bytes_accessed=GROUP * WIDE * 24,
            transcendentals=2 * GROUP * GROUP,
        ),
    )(at, mine, got, facts, facts_other, bias_rows)


def attend_back_kernel(
    mine_ref, got_ref, qt_ref, kt_ref, hot_ref, near_ref, other_ref, att_ref,
    keep_ref, send_ref, bias_ref, all_scr, grad_scr, dk_sum, dv_sum, *, chunks,
):
    size = GROUP // chunks
    step = pl.program_id(0)
    block = qt_ref.shape[0]

    @pl.when(step == 0)
    def _():
        all_scr[:, :PLANE] = mine_ref[...]
        all_scr[:, PLANE:] = got_ref[...]
        grad_scr[:PLANE] = near_ref[...]
        grad_scr[PLANE:] = other_ref[...]
        dk_sum[...] = jnp.zeros_like(dk_sum)
        dv_sum[...] = jnp.zeros_like(dv_sum)

    here = pl.ds(pl.multiple_of(step * block, block), block)
    query = jnp.concatenate([all_scr[0, here, :], qt_ref[...]], 1)
    grad = grad_scr[here, :]
    zero = jnp.zeros_like(query)
    head_of = (lanes_of(query.shape) // HEAD_DIM) % 2
    lanes = lanes_of((block, WIDE))
    overlap = grad.astype(F32) * att_ref[...]
    ones = value_lanes(size)
    out = None
    for head in range(2):
        mine = head_of[:, :WIDE] == head
        masked = jnp.where(head_of == head, query, zero)
        grad_here = jnp.where(mine, grad, zero[:, :WIDE])
        dots = jnp.sum(jnp.where(mine, overlap, 0.0), axis=1, keepdims=True)
        extra = with_pieces(jnp.zeros(lanes.shape, F32), -dots, 0, lanes).astype(BF16)
        grad_wide = jnp.concatenate([grad_here, extra], 1)
        total = None
        for c in range(chunks):
            rows = slice(c * size, (c + 1) * size)
            keys = all_scr[1, rows, :]
            prob = jnp.exp2(mm(jnp.concatenate([keys, kt_ref[rows, :]], 1), masked, NT))
            slope = mm(jnp.concatenate([all_scr[2, rows, :], ones], 1), grad_wide, NT)
            d_score = (prob * slope).astype(BF16)
            dv_sum[rows, :] += mm(prob.astype(BF16), grad_here)
            dk_sum[rows, :] += mm(d_score, masked)
            part = mm(d_score, keys, TN)
            total = part if total is None else total + part
        out = total if head == 0 else jnp.where(lanes < HEAD_DIM, out, total)
    low = out.astype(BF16)
    half = pl.num_programs(0) // 2

    @pl.when(step < half)
    def _():
        keep_ref[0, here, :] = low

    @pl.when(step >= half)
    def _():
        send_ref[0, pl.ds(pl.multiple_of((step - half) * block, block), block), :] = low

    @pl.when(step == pl.num_programs(0) - 1)
    def _():
        for ref, rows in ((keep_ref, slice(0, PLANE)), (send_ref, slice(PLANE, GROUP))):
            ref[1] = (dk_sum[rows, :WIDE] * (1.0 / LOG2E)).astype(BF16)
            ref[2] = dv_sum[rows, :].astype(BF16)
        counts = dk_sum[:, WIDE:]
        bias_ref[...] = jnp.zeros_like(bias_ref)
        bias_ref[0:1, :] = jnp.sum(counts * hot_ref[...].astype(F32), axis=0, keepdims=True)
        bias_ref[1:2, :] = jnp.sum(counts, axis=0, keepdims=True)


def attend_back(mine, got, query_tail, key_tail, near, other, attended):
    block = 512
    moving = pl.BlockSpec((block, WIDE), lambda i: (i, 0))
    fixed = pl.BlockSpec((GROUP, WIDE), lambda i: (0, 0))
    plane = pl.BlockSpec((PLANE, WIDE), lambda i: (0, 0))
    three = pl.BlockSpec((3, PLANE, WIDE), lambda i: (0, 0, 0))
    low = jax.ShapeDtypeStruct((3, PLANE, WIDE), BF16)
    return pl.pallas_call(
        functools.partial(attend_back_kernel, chunks=4),
        grid=(GROUP // block,),
        in_specs=[three, three, moving, fixed, fixed, plane, plane, moving],
        out_specs=[three, three, pl.BlockSpec((8, WIDE), lambda i: (0, 0))],
        out_shape=[low, low, jax.ShapeDtypeStruct((8, WIDE), F32)],
        scratch_shapes=[
            pltpu.VMEM((3, GROUP, WIDE), BF16),
            pltpu.VMEM((GROUP, WIDE), BF16),
            pltpu.VMEM((GROUP, 2 * WIDE), F32),
            pltpu.VMEM((GROUP, WIDE), F32),
        ],
        compiler_params=pltpu.CompilerParams(vmem_limit_bytes=48 * 2**20),
        cost_estimate=pl.CostEstimate(
            flops=40 * GROUP * GROUP * WIDE, bytes_accessed=GROUP * WIDE * 24,
            transcendentals=2 * GROUP * GROUP,
        ),
    )(mine, got, query_tail, key_tail, query_tail, near, other, attended)


def feed_kernel(b_ref, g_ref, w_ref, y_ref, db_ref, act_ref, *, cuts):
    rows, grads = b_ref[...], g_ref[...]
    size = w_ref.shape[2] // cuts

    def products(j):
        cols = slice(j * size, (j + 1) * size)
        return mm(rows, w_ref[0, :, cols]), mm(rows, w_ref[1, :, cols]), mm(grads, w_ref[2, :, cols])

    y_sum, db_sum = None, None
    ready = products(0)
    for j in range(cuts):
        gate, up, d_hidden = ready
        if j + 1 < cuts:
            ready = products(j + 1)
        cols = slice(j * size, (j + 1) * size)
        sig = 0.5 + 0.5 * jnp.tanh(0.5 * gate)
        silu = gate * sig
        hidden = (silu * up).astype(BF16)
        d_gate = (d_hidden * up * (sig + silu * (1.0 - sig))).astype(BF16)
        d_up = (d_hidden * silu).astype(BF16)
        act_ref[0, :, cols] = d_gate
        act_ref[1, :, cols] = d_up
        act_ref[2, :, cols] = hidden
        y_part = mm(hidden, w_ref[2, :, cols], NT)
        db_part = mm(d_gate, w_ref[0, :, cols], NT) + mm(d_up, w_ref[1, :, cols], NT)
        y_sum = y_part if y_sum is None else y_sum + y_part
        db_sum = db_part if db_sum is None else db_sum + db_part
    y_ref[...] = y_sum.astype(BF16)
    db_ref[...] = db_sum.astype(BF16)


def feed(rows_b, rows_g, weights):
    rows = rows_b.shape[0]
    width = weights.shape[2]
    low_d = jax.ShapeDtypeStruct((rows, D), BF16)
    low_f = jax.ShapeDtypeStruct((3, rows, width), BF16)
    return pl.pallas_call(
        functools.partial(feed_kernel, cuts=2),
        out_shape=[low_d, low_d, low_f],
        compiler_params=pltpu.CompilerParams(vmem_limit_bytes=26 * 2**20),
        cost_estimate=pl.CostEstimate(
            flops=12 * rows * D * width, bytes_accessed=6 * D * width + rows * D * 8 + rows * width * 6,
            transcendentals=rows * width,
        ),
    )(rows_b, rows_g, weights)


def body(
    tokens,
    cotangent,
    destination,
    variate_ids,
    time_ids,
    seq_lengths,
    qkv_weight,
    out_weight,
    gate_up_weight,
    down_weight,
    norm_gains,
    qk_gains,
    variate_bias,
):
    core = lax.axis_index("core")
    low_core = core == 0
    y_at = lax.axis_index("y")
    zl_at = lax.axis_index("zl")

    core_scalar = core.reshape(1).astype(jnp.int32)

    def side_by_side(mine, other):
        return jnp.concatenate(
            [jnp.where(low_core, mine, other), jnp.where(low_core, other, mine)], axis=-1
        )

    feed_shard = jnp.concatenate([gate_up_weight, down_weight.T[None]], 0)

    slot = destination % ROWS
    group_at = destination // GROUP
    block_at = (destination % GROUP) // ROWS
    device_at = ((group_at // 2) * 2 + block_at // 4) * 8 + (block_at % 4) * 2 + group_at % 2
    key = device_at * ROWS + slot
    zero = jnp.zeros_like(slot)
    facts = jnp.stack([key, slot, variate_ids, time_ids // 32, time_ids % 32, zero, zero, zero])
    gains_row = jnp.pad(
        norm_gains.reshape(8, 16), ((0, 0), (GAIN_LANE, WIDE - GAIN_LANE - 16))
    ).astype(F32)
    outgoing, deal = deal_rows(tokens, cotangent, facts.astype(F32), gains_row)
    arrived = lax.all_to_all(outgoing.reshape(DEVICES, 8, SPAN), ALL, 0, 0, tiled=True)
    out_shard, outgoing = lax.optimization_barrier((out_weight.T, outgoing))
    attn_shard = jnp.concatenate([qkv_weight, jnp.stack(gather_direct(out_shard))], 0)
    attn_mine = gather_round(attn_shard, ("zh", "zl"), lax.axis_index("zh") * 2 + zl_at)
    attn_mine, arrived = lax.optimization_barrier((attn_mine, arrived))
    attn_mine, out_mine = attn_mine[:, :3], attn_mine[:, 3:]
    attn_mine = jnp.stack(gather_ahead(attn_mine, "x")).reshape((16,) + qkv_weight.shape)

    lengths_other = swap_core(seq_lengths)
    lengths = jnp.where(zl_at == core, seq_lengths, lengths_other)[0]
    bias_other = lax.ppermute(variate_bias, "zl", [(0, 1), (1, 0)])
    bias_pair = jnp.where(zl_at == core, variate_bias, bias_other)

    all_gains = arrived.reshape(16, 8, 8, SPAN)[:, 0, :, PAIR + GAIN_LANE : PAIR + GAIN_LANE + 16]
    inputs, grad_rows, attn_in, place, gains = receive(
        arrived.reshape(4 * ROWS, SPAN), all_gains.reshape(16, WIDE)
    )
    feed_shard, attn_in = lax.optimization_barrier((feed_shard, attn_in))
    feed_mine = flat_gather(feed_shard)
    zero_at = jnp.zeros((1,), jnp.int32)
    x_at = lax.axis_index("x").reshape(1).astype(jnp.int32)
    ahead, behind = ring(attn_in, -1), ring(attn_in, 1)
    ahead, behind, attn_mine, out_mine = lax.optimization_barrier((ahead, behind, attn_mine, out_mine))
    out_mine = jnp.stack(gather_ahead(out_mine, "x")).reshape((16, 4, 64, WIDE))
    attn_w = assemble(core_scalar, x_at, attn_mine, swap_core(attn_mine))
    far_top, far_low = ring(ahead[: ROWS // 2], -1), ring(behind[ROWS // 2 :], 1)
    far_top, far_low, attn_w, out_mine = lax.optimization_barrier((far_top, far_low, attn_w, out_mine))
    attn_all = [attn_in, ahead, jnp.concatenate([far_top, far_low], 0), behind]
    grad_rows, attn_all = lax.optimization_barrier((grad_rows, attn_all))
    grad_all = gather_direct(grad_rows)

    blocks_y = (y_at + jnp.arange(RING)) % RING
    blocks = jnp.concatenate([core * RING + blocks_y, (1 - core) * RING + blocks_y])
    at = jnp.concatenate([blocks * ROWS, jnp.cumsum(lengths)]).astype(jnp.int32)

    inverse = THETA ** (-2.0 * jnp.arange(HALF).astype(F32) / HEAD_DIM)
    freq = jnp.concatenate(
        [
            jnp.tile(inverse, 8)[None],
            jnp.tile(qk_gains, (1, 4)),
            jnp.zeros((5, 2 * WIDE), F32),
        ]
    )
    qkv_mine, qkv_send, raw, facts_all = project(core_scalar, attn_all, attn_w, freq)
    facts_other = swap_core(facts_all)
    qkv_got = swap_core(qkv_send)

    bias_parts = jnp.stack(pieces(bias_pair * LOG2E, 3)).astype(F32)
    bias_rows = jnp.repeat(bias_parts, VARIATES, axis=0).transpose(1, 2, 0)
    bias_rows = jnp.pad(bias_rows, ((0, 0), (0, 0), (0, HEAD_DIM - 3 * VARIATES))).reshape(2, WIDE)
    bias_rows = jnp.pad(bias_rows, ((0, 6), (0, 0)))
    attended, att_near, att_send, query_back, key_tail = attend(
        at, qkv_mine, qkv_got, facts_all, facts_other, bias_rows
    )
    att_near, grad_all = lax.optimization_barrier((att_near, grad_all))
    att_other = swap_core(att_send)
    out_w = assemble(core_scalar, x_at, out_mine, swap_core(out_mine))
    att_plane = side_by_side(att_near, att_other).reshape(RING, ROWS, 2 * WIDE)
    att_rows = trade_ring([att_plane[r] for r in range(RING)])
    att_rows, feed_mine = lax.optimization_barrier((att_rows, feed_mine))
    feed_w = assemble(core_scalar, zero_at, feed_mine, swap_core(feed_mine))
    hidden_one, feed_in = out_project(att_rows, out_w, inputs, gains)

    ahead, behind = ring(feed_in, -1), ring(feed_in, 1)
    fed_own = feed(feed_in, grad_all[0], feed_w)
    ahead, behind, fed_own = lax.optimization_barrier((ahead, behind, fed_own))
    far_top, far_low = ring(ahead[: ROWS // 2], -1), ring(behind[ROWS // 2 :], 1)
    fed_ahead = feed(ahead, grad_all[1], feed_w)
    fed_behind = feed(behind, grad_all[3], feed_w)
    far_top, far_low, fed_ahead, fed_behind = lax.optimization_barrier(
        (far_top, far_low, fed_ahead, fed_behind)
    )
    far = jnp.concatenate([far_top, far_low], 0)
    fed_far = feed(far, grad_all[2], feed_w)
    feed_all = [feed_in, ahead, far, behind]
    fed = [fed_own, fed_ahead, fed_far, fed_behind]
    feed_split = weight_grads(core_scalar, feed_all, grad_all, [f[2] for f in fed], 2, 2)
    db_got = send_ring([f[1] for f in fed], True)
    db_got, feed_split = lax.optimization_barrier((db_got, feed_split))
    grad_one, gain_two_grad, d_att, *both = middle(
        att_rows, out_w, [f[0] for f in fed], fed_own[1], db_got, hidden_one, grad_rows, gains
    )
    feed_total = chip_total(feed_split)
    feed_got = trade(feed_total, "x")

    grad_att = trade_ring([d_att[r] for r in range(RING)])
    grad_att[1], feed_total = lax.optimization_barrier((grad_att[1], feed_total))
    grad_att = jnp.concatenate(grad_att, 0)
    both, grad_att = lax.optimization_barrier((both, grad_att))
    both_got = send_ring(both)
    grad_left, grad_right = grad_att[:, :WIDE], grad_att[:, WIDE:]
    grad_other = swap_core(jnp.where(low_core, grad_right, grad_left))
    grad_near = jnp.where(low_core, grad_left, grad_right)
    d_keep, d_send, bias_sums = attend_back(
        qkv_mine, qkv_got, query_back, key_tail, grad_near, grad_other, attended
    )
    first_part = (jnp.arange(HEAD_DIM) < VARIATES)[None, None]
    bias_sums = jnp.where(first_part, bias_sums[:2].reshape(2, 2, HEAD_DIM), 0.0)
    bias_sums = jnp.sum(bias_sums, axis=2)
    bias_part = jnp.stack([bias_sums[0], bias_sums[1] - bias_sums[0]])
    d_send, feed_got = lax.optimization_barrier((d_send, feed_got))
    feed_got = trade(added(feed_got).astype(BF16), ("zh", "zl"))
    grad_proj, in_part, qk_sums = unproject(
        core_scalar, d_keep, swap_core(d_send), raw, facts_all, attn_w, freq
    )
    grad_proj, both_got = lax.optimization_barrier((grad_proj, both_got))
    both_sum = add_ring(both[0], both_got)
    mixed = (hidden_one + both_sum[:ROWS]).astype(BF16)
    out_full = both_sum[ROWS:].astype(BF16)
    in_part = in_part.reshape(RING, ROWS, D)
    in_got = send_ring([in_part[r] for r in range(RING)])
    attn_split = weight_grads(core_scalar, attn_all, [out_full], [grad_proj], None, 1)
    attn_total = chip_total(attn_split)
    in_got, _ = lax.optimization_barrier((in_got, attn_split))
    mixed, _ = lax.optimization_barrier((mixed, attn_total))
    attn_own, attn_got = send_round(attn_total.reshape((RING, RING) + attn_total.shape[1:]), "x")
    qk_sums = jnp.sum(qk_sums[:2].reshape(2, 4, HEAD_DIM), axis=1)

    small = jnp.zeros((8, WIDE), F32).at[0].set(qk_sums.reshape(WIDE))
    small = small.at[1, :4].set(bias_part.reshape(4))
    tensor_at = (y_at * 2 + core).reshape(1).astype(jnp.int32)
    last = finish(
        in_part[0], in_got, inputs, grad_one, mixed, place, gains, gain_two_grad, small, tensor_at
    )
    last = last.reshape(DEVICES, 8, 2 * QUARTER + WIDE)
    last, attn_got, feed_got = lax.optimization_barrier((last, attn_got, feed_got))
    home = lax.all_to_all(last, ALL, 0, 0, tiled=True)
    own, got = send_round(add_round(attn_own, attn_got).astype(BF16), ("zh", "zl"))
    home, got = lax.optimization_barrier((home, got))
    attn_grad = add_round(own, got)
    feed_grad = added(feed_got).reshape(3, 64, 512)
    new_tokens, token_grads, sums = settle(home.reshape(4 * ROWS, 2 * QUARTER + WIDE), deal)
    gains_grad = sums[0].reshape(2, 64)
    qk_grad = sums[1].reshape(2, 64)
    bias_grad = sums[2, :4].reshape(2, 2)

    return (
        new_tokens,
        token_grads,
        attn_grad[:3],
        attn_grad[3].T,
        feed_grad[:2],
        feed_grad[2].T,
        gains_grad,
        qk_grad,
        bias_grad,
    )


def solution(mesh):
    fine = Mesh(mesh.devices.reshape(4, 2, 2, 4, 2), ALL)
    dp = ("x", "zh", "core")
    tensor = ("y", "zl")
    in_specs = (
        P(ALL, None),
        P(ALL, None),
        P(ALL),
        P(ALL),
        P(ALL),
        P(dp, None),
        P(None, dp, tensor),
        P(tensor, dp),
        P(None, dp, tensor),
        P(tensor, dp),
        P(None, dp),
        P(),
        P(None, tensor),
    )
    out_specs = (
        P(ALL, None),
        P(ALL, None),
        P(None, dp, tensor),
        P(tensor, dp),
        P(None, dp, tensor),
        P(tensor, dp),
        P(None, dp),
        P(),
        P(None, tensor),
    )
    return jax.shard_map(body, mesh=fine, in_specs=in_specs, out_specs=out_specs, check_vma=False)
```

```python
import functools

import jax
import jax.numpy as jnp
from jax import lax
from jax.experimental import pallas as pl
from jax.experimental.pallas import tpu as pltpu
from jax.sharding import Mesh
from jax.sharding import PartitionSpec as P

HEADS = 16
HEAD_DIM = 64
HALF = HEAD_DIM // 2
D = 1024
FF = 4096
ROWS = 256
RING = 4
PLANE = ROWS * RING
GROUP = 2 * PLANE
DEVICES = 128
VARIATES = 8
SEQS = 4
WIDE = 128
EPS = 1e-06
THETA = 10000.0
LOG2E = 1.4426950408889634
FAR = -16384.0
F32 = jnp.float32
BF16 = jnp.bfloat16

ALL = ("x", "zh", "core", "y", "zl")
FLAT = ("x", "zh", "zl")
NT = (((1,), (1,)), ((), ()))
TN = (((0,), (0,)), ((), ()))


def mm(left, right, dims=(((1,), (0,)), ((), ()))):
    return lax.dot_general(left, right, dims, preferred_element_type=F32)


def root_stats(values):
    return lax.rsqrt(jnp.mean(values * values, axis=-1, keepdims=True) + EPS)


def norm_back(grad_in, normed, scale_inv):
    return scale_inv * (grad_in - normed * jnp.mean(grad_in * normed, axis=-1, keepdims=True))


def pieces(values, count):
    out = []
    for _ in range(count):
        part = lax.reduce_precision(values, 8, 7)
        out.append(part.astype(BF16))
        values = values - part
    return out


def ring(values, step):
    return lax.ppermute(values, "y", [(i, (i + step) % RING) for i in range(RING)])


def swap_core(values):
    return lax.ppermute(values, "core", [(0, 1), (1, 0)])


def gather_ring(values):
    ahead = ring(values, -1)
    behind = ring(values, 1)
    half = values.shape[0] // 2
    far_top = ring(ahead[:half], -1)
    far_low = ring(behind[half:], 1)
    return [values, ahead, jnp.concatenate([far_top, far_low], 0), behind]


def gather_direct(values):
    return [values, ring(values, -1), ring(values, 2), ring(values, 1)]


def trade_ring(parts):
    return [parts[0]] + [ring(parts[RING - s], -s) for s in range(1, RING)]


def send_ring(parts, halves=False):
    half = parts[2].shape[0] // 2
    far = [parts[2][:half], parts[2][half:]] if halves else [parts[2]]
    return [ring(parts[1], 1), ring(parts[3], -1)] + [ring(v, 2) for v in far]


def add_ring(own, got):
    far = got[2] if len(got) == 3 else jnp.concatenate(got[2:], 0)
    return own.astype(F32) + got[0].astype(F32) + got[1].astype(F32) + far.astype(F32)


def gather_ahead(values, axes):
    moves = [[((i + r) % RING, i) for i in range(RING)] for r in range(RING)]
    return [values] + [lax.ppermute(values, axes, moves[r]) for r in range(1, RING)]


def gather_round(values, axes, at):
    return jnp.roll(jnp.stack(gather_ahead(values, axes)), at, axis=0)


def flat_gather(shard):
    many = jnp.broadcast_to(shard[None], (16,) + shard.shape)
    return lax.all_to_all(many, FLAT, 0, 0, tiled=True)


def assemble_kernel(at_ref, mine_ref, other_ref, out_ref):
    core = at_ref[0]
    count, _, depth, width = mine_ref.shape
    for ref, side in ((mine_ref, core), (other_ref, 1 - core)):
        for i in range(count):
            at = (i // 2) * 2 * depth + side * depth
            rows = pl.ds(pl.multiple_of(at, depth), depth)
            out_ref[:, rows, (i % 2) * width : (i % 2 + 1) * width] = ref[i]


def assemble(core, x_at, mine, other):
    _, kinds, depth, width = mine.shape
    pair = pl.BlockSpec((4, kinds, depth, width), lambda p, at: (p, 0, 0, 0))
    return pl.pallas_call(
        assemble_kernel,
        grid_spec=pltpu.PrefetchScalarGridSpec(
            num_scalar_prefetch=1,
            grid=(RING,),
            in_specs=[pair, pair],
            out_specs=pl.BlockSpec(
                (kinds, 4 * depth, 2 * width), lambda p, at: (0, lax.rem(at[1] + p, RING), 0)
            ),
        ),
        out_shape=jax.ShapeDtypeStruct((kinds, 16 * depth, 2 * width), BF16),
        compiler_params=pltpu.CompilerParams(vmem_limit_bytes=28 * 2**20),
        cost_estimate=pl.CostEstimate(
            flops=0, bytes_accessed=kinds * 128 * depth * width, transcendentals=0
        ),
    )(jnp.concatenate([core, x_at]), mine, other)


def chip_total(split):
    return (split[0].astype(F32) + swap_core(split[1]).astype(F32)).astype(BF16)


def send_round(values, axes):
    at = lax.axis_index(axes)
    parts = [lax.dynamic_index_in_dim(values, (at + r) % RING, 0, keepdims=False) for r in range(RING)]
    moves = [[(i, (i + r) % RING) for i in range(RING)] for r in range(RING)]
    return parts[0], [lax.ppermute(parts[r], axes, moves[r]) for r in (1, 3, 2)]


def add_round(own, got):
    return sum((v.astype(F32) for v in got), own.astype(F32))


def trade(values, axes):
    return lax.all_to_all(values.reshape((RING, -1) + values.shape[1:]), axes, 0, 0, tiled=True)


def added(got):
    return jnp.sum(got.astype(F32), axis=0)


def lanes_of(shape):
    return lax.broadcasted_iota(jnp.int32, shape, 1)


QUARTER = D // RING
PAIR = 2 * QUARTER
SPAN = PAIR + WIDE
GAIN_LANE = 16


def deal_kernel(tok_ref, cot_ref, facts_ref, gains_ref, out_ref, deal_ref):
    wide = jnp.concatenate([facts_ref[...], jnp.zeros((WIDE - 8, ROWS), F32)], 0)
    facts = jnp.transpose(wide)
    keys = facts_ref[0:1, :]
    rank = jnp.sum((facts[:, 0:1] < keys).astype(F32), axis=0, keepdims=True)
    at = lax.broadcasted_iota(jnp.int32, (ROWS, ROWS), 0).astype(F32)
    deal_ref[...] = (at == rank).astype(BF16)
    low = jnp.where(lanes_of(facts.shape) == 0, 0.0, facts).astype(BF16)
    row = lax.broadcasted_iota(jnp.int32, (4 * ROWS, 1), 0)
    own = ((row // RING).astype(F32) == rank).astype(BF16)
    part = None
    for m in range(RING):
        cols = slice(m * QUARTER, (m + 1) * QUARTER)
        here = mm(own, jnp.concatenate([tok_ref[:, cols], cot_ref[:, cols]], 1))
        part = here if m == 0 else jnp.where(row % RING == m, here, part)
    out_ref[:, :PAIR] = part.astype(BF16)
    tail = mm(own, low)
    lane = lanes_of(tail.shape)
    gains = jnp.broadcast_to(gains_ref[...][None], (DEVICES, 8, WIDE)).reshape(tail.shape)
    tail = jnp.where((lane >= GAIN_LANE) & (lane < GAIN_LANE + 16), gains, tail)
    out_ref[:, PAIR:] = tail.astype(BF16)


def deal_rows(tokens, cotangent, facts, gains):
    return pl.pallas_call(
        deal_kernel,
        out_shape=[
            jax.ShapeDtypeStruct((4 * ROWS, SPAN), BF16),
            jax.ShapeDtypeStruct((ROWS, ROWS), BF16),
        ],
        compiler_params=pltpu.CompilerParams(vmem_limit_bytes=48 * 2**20),
        cost_estimate=pl.CostEstimate(
            flops=8 * ROWS * ROWS * 2304, bytes_accessed=ROWS * D * 16, transcendentals=0
        ),
    )(tokens, cotangent, facts, gains)


def receive_kernel(rows_ref, gains_ref, x_ref, g_ref, a_ref, place_ref, gain_ref):
    count = 4 * ROWS
    facts = rows_ref[:, PAIR:]
    slots = jnp.transpose(facts.astype(F32))[1:2, :]
    at = lax.broadcasted_iota(jnp.int32, (ROWS, count), 0)
    arrival = lanes_of((ROWS, count))
    here = at.astype(F32) == slots
    gains = gains_ref[...].astype(F32)
    turned = pltpu.roll(gains, HEAD_DIM, 1)
    left = lanes_of((1, WIDE)) < HEAD_DIM
    one, two = [], []
    for c in range(D // WIDE):
        even, odd = slice(2 * c, 2 * c + 1), slice(2 * c + 1, 2 * c + 2)
        one.append(jnp.where(left, gains[even], turned[odd]))
        two.append(jnp.where(left, turned[even], gains[odd]))
    gain_one = jnp.concatenate(one, 1)
    gain_ref[...] = jnp.zeros_like(gain_ref)
    gain_ref[0:1, :] = gain_one
    gain_ref[1:2, :] = jnp.concatenate(two, 1)
    quarters = []
    for m in range(RING):
        chosen = (here & (arrival % RING == m)).astype(BF16)
        both = mm(chosen, rows_ref[:, :PAIR])
        quarters.append(both[:, :QUARTER])
        g_ref[:, m * QUARTER : (m + 1) * QUARTER] = both[:, QUARTER:].astype(BF16)
        if m == 0:
            a_ref[:, D:] = mm(chosen, facts).astype(BF16)
            pick = (at * RING == arrival).astype(BF16)
            place_ref[...] = mm(chosen, pick, NT).astype(BF16)
    rows = jnp.concatenate(quarters, 1)
    x_ref[...] = rows
    a_ref[:, :D] = (rows * root_stats(rows) * gain_one).astype(BF16)


def receive(rows, gains):
    return pl.pallas_call(
        receive_kernel,
        out_shape=[
            jax.ShapeDtypeStruct((ROWS, D), F32),
            jax.ShapeDtypeStruct((ROWS, D), BF16),
            jax.ShapeDtypeStruct((ROWS, D + WIDE), BF16),
            jax.ShapeDtypeStruct((ROWS, ROWS), BF16),
            jax.ShapeDtypeStruct((8, D), F32),
        ],
        compiler_params=pltpu.CompilerParams(vmem_limit_bytes=48 * 2**20),
        cost_estimate=pl.CostEstimate(
            flops=16 * ROWS * ROWS * D, bytes_accessed=ROWS * D * 24, transcendentals=0
        ),
    )(rows, gains)


OUT_KIND = 3


def out_kernel(*refs):
    att = refs[:RING]
    w_ref, x_ref, gain_ref, h_ref, b_ref = refs[RING:]
    hidden = x_ref[...]
    for r in range(RING):
        hidden = hidden + mm(att[r][...], w_ref[OUT_KIND + r], NT)
    h_ref[...] = hidden
    b_ref[...] = (hidden * root_stats(hidden) * gain_ref[1:2, :]).astype(BF16)


def out_project(att, weights, rows, gains):
    return pl.pallas_call(
        out_kernel,
        out_shape=[jax.ShapeDtypeStruct((ROWS, D), F32), jax.ShapeDtypeStruct((ROWS, D), BF16)],
        compiler_params=pltpu.CompilerParams(vmem_limit_bytes=48 * 2**20),
        cost_estimate=pl.CostEstimate(
            flops=2 * ROWS * D * D, bytes_accessed=2 * D * D + ROWS * D * 14, transcendentals=0
        ),
    )(*att, weights, rows, gains)


def middle_kernel(*refs):
    att, y_parts, w_ref = refs[:RING], refs[RING : 2 * RING], refs[2 * RING]
    refs = refs[2 * RING + 1 :]
    own_ref, near_ref, back_ref, top_ref, low_ref, h_ref, g_ref, gain_ref = refs[:8]
    grad_ref, two_ref, d_ref = refs[8:11]
    both_refs = refs[11:]
    far = jnp.concatenate([top_ref[...], low_ref[...]], 0).astype(F32)
    grad = own_ref[...].astype(F32) + near_ref[...].astype(F32) + back_ref[...].astype(F32) + far
    hidden = h_ref[...]
    scale = root_stats(hidden)
    normed = hidden * scale
    two_ref[...] = jnp.zeros_like(two_ref)
    two_ref[0:1, :] = jnp.sum(grad * normed, axis=0, keepdims=True)
    scaled = grad * gain_ref[1:2, :]
    grad = g_ref[...].astype(F32) + norm_back(scaled, normed, scale)
    grad_ref[...] = grad
    low = grad.astype(BF16)
    for r in range(RING):
        d_ref[r] = mm(low, w_ref[OUT_KIND + r]).astype(BF16)
        both_refs[r][:ROWS] = y_parts[r][...]
        both_refs[r][ROWS:] = mm(att[r][...], low, TN).astype(BF16)


def middle(att, weights, y_parts, own, got, hidden, grad_rows, gains):
    both = jax.ShapeDtypeStruct((2 * ROWS, D), BF16)
    return pl.pallas_call(
        middle_kernel,
        out_shape=[
            jax.ShapeDtypeStruct((ROWS, D), F32),
            jax.ShapeDtypeStruct((8, D), F32),
            jax.ShapeDtypeStruct((RING, ROWS, ROWS), BF16),
        ]
        + [both] * RING,
        compiler_params=pltpu.CompilerParams(vmem_limit_bytes=48 * 2**20),
        cost_estimate=pl.CostEstimate(
            flops=4 * ROWS * D * D, bytes_accessed=2 * D * D + ROWS * D * 40, transcendentals=0
        ),
    )(*att, *y_parts, weights, own, *got, hidden, grad_rows, gains)


def finish_kernel(
    own_ref, near_ref, back_ref, far_ref, x_ref, grad_ref, mixed_ref, place_ref,
    gain_ref, two_ref, small_ref, at_ref, out_ref,
):
    rows = x_ref[...]
    scale = root_stats(rows)
    normed = rows * scale
    far = far_ref[...].astype(F32)
    grad = own_ref[...].astype(F32) + near_ref[...].astype(F32) + back_ref[...].astype(F32) + far
    one = jnp.sum(grad * normed, axis=0, keepdims=True)
    two = two_ref[0:1, :]
    scaled = grad * gain_ref[0:1, :]
    back = scale * (scaled - normed * jnp.mean(scaled * normed, axis=1, keepdims=True))
    result = (grad_ref[...] + back).astype(BF16)
    count = 4 * ROWS
    row = lax.broadcasted_iota(jnp.int32, (count, 1), 0)
    quarter = row % RING
    pick = (row // RING == lanes_of((count, ROWS))).astype(BF16)
    pick = mm(pick, place_ref[...], NT).astype(BF16)
    part = None
    for m in range(RING):
        cols = slice(m * QUARTER, (m + 1) * QUARTER)
        here = mm(pick, jnp.concatenate([mixed_ref[:, cols], result[:, cols]], 1))
        part = here if m == 0 else jnp.where(quarter == m, here, part)
    out_ref[:, : 2 * QUARTER] = part.astype(BF16)
    left = lanes_of((1, WIDE)) < HEAD_DIM
    tiles = []
    for c in range(D // WIDE):
        cols = slice(c * WIDE, (c + 1) * WIDE)
        a, b = one[:, cols], two[:, cols]
        even = jnp.where(left, a, pltpu.roll(jnp.broadcast_to(b, (8, WIDE)), HEAD_DIM, 1)[0:1])
        odd = jnp.where(left, pltpu.roll(jnp.broadcast_to(a, (8, WIDE)), HEAD_DIM, 1)[0:1], b)
        tiles += [jnp.broadcast_to(even, (64, WIDE)), jnp.broadcast_to(odd, (64, WIDE))]
    value = jnp.concatenate(tiles, 0)
    value = jnp.where(quarter == 1, small_ref[0:1, :], value)
    bias = jnp.where((row // 8) % 8 == at_ref[0], small_ref[1:2, :], 0.0)
    value = jnp.where(quarter == 2, bias, value)
    high = value.astype(BF16).astype(F32)
    value = jnp.where((row // RING) % 2 == 0, high, value - high)
    out_ref[:, 2 * QUARTER :] = value.astype(BF16)


def finish(own, got, rows, grad, mixed, place, gains, two, small, at):
    specs = [pl.BlockSpec(memory_space=pltpu.VMEM)] * 11
    return pl.pallas_call(
        finish_kernel,
        in_specs=specs + [pl.BlockSpec(memory_space=pltpu.SMEM)],
        out_shape=jax.ShapeDtypeStruct((4 * ROWS, 2 * QUARTER + WIDE), BF16),
        compiler_params=pltpu.CompilerParams(vmem_limit_bytes=48 * 2**20),
        cost_estimate=pl.CostEstimate(
            flops=16 * ROWS * ROWS * D, bytes_accessed=ROWS * D * 20, transcendentals=0
        ),
    )(own, *got, rows, grad, mixed, place, gains, two, small, at)


def settle_kernel(home_ref, deal_ref, rows_ref, grads_ref, sums_ref):
    deal = deal_ref[...]
    shape = (ROWS, 4 * ROWS)
    index = lax.broadcasted_iota(jnp.int32, shape, 0)
    for m in range(RING):
        pick = (index * RING + m == lanes_of(shape)).astype(BF16)
        here = mm(pick, home_ref[:, : 2 * QUARTER]).astype(BF16)
        here = mm(deal, here, TN).astype(BF16)
        cols = slice(m * QUARTER, (m + 1) * QUARTER)
        rows_ref[:, cols] = here[:, :QUARTER]
        grads_ref[:, cols] = here[:, QUARTER:]
    small = home_ref[:, 2 * QUARTER :].astype(F32)
    quarter = lax.broadcasted_iota(jnp.int32, small.shape, 0) % RING
    sums_ref[...] = jnp.zeros_like(sums_ref)
    for m in range(3):
        sums_ref[m : m + 1, :] = jnp.sum(jnp.where(quarter == m, small, 0.0), axis=0, keepdims=True)


def settle(home, deal):
    low = jax.ShapeDtypeStruct((ROWS, D), BF16)
    return pl.pallas_call(
        settle_kernel,
        out_shape=[low, low, jax.ShapeDtypeStruct((8, WIDE), F32)],
        compiler_params=pltpu.CompilerParams(vmem_limit_bytes=48 * 2**20),
        cost_estimate=pl.CostEstimate(
            flops=20 * ROWS * ROWS * D, bytes_accessed=ROWS * D * 16, transcendentals=0
        ),
    )(home, deal)


def weight_grad_kernel(core_ref, *refs, parts, count, switch, steps):
    given = switch is None
    lefts, others, rights = refs[:parts], refs[parts : parts + count], refs[parts + count : -3]
    keep_ref, send_ref, turned_ref = refs[-3:]
    low = core_ref[0] == 0
    step = pl.program_id(0)

    def load(sides):
        at = 0
        for side in sides:
            rows = side.shape[0]
            turned_ref[:, at : at + rows] = side[...].T
            at += rows

    @pl.when(step == 0)
    def _():
        load(lefts)

    if not given:

        @pl.when(step == switch * steps)
        def _():
            load(others)

    def emit(total):
        depth = total.shape[0] // 16
        width = keep_ref.shape[-1]
        for z in range(total.shape[1] // width):
            cols = slice(z * width, (z + 1) * width)
            for p in range(8):
                at = 2 * p * depth
                even, odd = total[at : at + depth, cols], total[at + depth : at + 2 * depth, cols]
                keep_ref[p, z, 0] = jnp.where(low, even, odd)
                send_ref[p, z, 0] = jnp.where(low, odd, even)

    def product():
        right = jnp.concatenate([ref[0] for ref in rights], 0)
        emit(mm(turned_ref[...], right).astype(BF16))

    if given:
        pl.when(step < pl.num_programs(0) - 1)(product)

        @pl.when(step == pl.num_programs(0) - 1)
        def _():
            emit(others[0][...].T)
    else:
        product()


def weight_grads(core, lefts, others, rights, switch, steps):
    parts = len(lefts)
    made, _, width = rights[0].shape
    kinds = made + 1 if switch is None else made
    block, half = width // steps, width // 2
    sides = [pl.BlockSpec((v.shape[0], D), lambda s: (0, 0)) for v in list(lefts) + list(others)]
    moving = [
        pl.BlockSpec(
            (1, v.shape[1], block), lambda s: (jnp.minimum(s // steps, made - 1), 0, s % steps)
        )
        for v in rights
    ]
    rows = sum(v.shape[1] for v in rights)
    out = pl.pallas_call(
        functools.partial(
            weight_grad_kernel, parts=parts, count=len(others), switch=switch, steps=steps
        ),
        grid=(kinds * steps,),
        in_specs=[pl.BlockSpec(memory_space=pltpu.SMEM)] + sides + moving,
        out_specs=[
            pl.BlockSpec((8, 2 // steps, 1, 64, half), lambda s: (0, s % steps, s // steps, 0, 0))
        ]
        * 2,
        out_shape=[jax.ShapeDtypeStruct((8, 2, kinds, 64, half), BF16)] * 2,
        scratch_shapes=[pltpu.VMEM((D, rows), BF16)],
        compiler_params=pltpu.CompilerParams(vmem_limit_bytes=48 * 2**20),
        cost_estimate=pl.CostEstimate(
            flops=2 * kinds * rows * D * width,
            bytes_accessed=2 * kinds * D * width + 4 * rows * D + 2 * kinds * rows * width,
            transcendentals=0,
        ),
    )(core, *lefts, *others, *rights)
    return [v.reshape(16, kinds, 64, half) for v in out]


def head_sums(values):
    wide = values.shape[1]
    row = lax.broadcasted_iota(jnp.int32, (wide, wide), 0) // HEAD_DIM
    same = (row == lanes_of((wide, wide)) // HEAD_DIM).astype(BF16)
    high = values.astype(BF16)
    low = (values - high.astype(F32)).astype(BF16)
    return mm(high, same) + mm(low, same)


def partner(values):
    wide = values.shape[1]
    first = lanes_of(values.shape) % HEAD_DIM < HALF
    return jnp.where(first, pltpu.roll(values, wide - HALF, 1), pltpu.roll(values, HALF, 1))


def angles_of(facts, freq_ref):
    facts = facts.astype(F32)
    times = facts[:, 3:4] * 32.0 + facts[:, 4:5]
    angle = times * freq_ref[0:1, :WIDE]
    first = lanes_of(angle.shape) % HEAD_DIM < HALF
    cosine = jnp.cos(angle)
    sine = jnp.sin(angle)
    sine = jnp.where(first, -sine, sine)
    return jnp.concatenate([cosine, cosine], 1), jnp.concatenate([sine, sine], 1)


def project_kernel(core_ref, *refs):
    pieces_in = refs[:RING]
    w_ref, freq_ref, mine_ref, send_ref, raw_ref, facts_ref = refs[RING:]
    low = core_ref[0] == 0
    for r in range(RING):
        block = slice(r * ROWS, (r + 1) * ROWS)
        rows = pieces_in[r][:, :D]
        facts = pieces_in[r][:, D:]
        facts_ref[block] = facts
        cosine, sine = angles_of(facts, freq_ref)
        for kind in range(3):
            value = mm(rows, w_ref[kind])
            if kind < 2:
                raw_ref[kind, block] = value
                unit = value * lax.rsqrt(head_sums(value * value) * (1.0 / HEAD_DIM) + EPS)
                value = unit * freq_ref[1 + kind : 2 + kind, :]
                value = value * cosine + partner(value) * sine
            if kind == 0:
                value = value * (HEAD_DIM ** (-0.5) * LOG2E)
            left, right = value[:, :WIDE], value[:, WIDE:]
            mine_ref[kind, block] = jnp.where(low, left, right).astype(BF16)
            send_ref[kind, block] = jnp.where(low, right, left).astype(BF16)


def project(core, rows, attn_w, freq):
    low = jax.ShapeDtypeStruct((3, PLANE, WIDE), BF16)
    whole = pl.BlockSpec(memory_space=pltpu.VMEM)
    return pl.pallas_call(
        project_kernel,
        in_specs=[pl.BlockSpec(memory_space=pltpu.SMEM)] + [whole] * (RING + 2),
        out_shape=[
            low,
            low,
            jax.ShapeDtypeStruct((2, PLANE, 2 * WIDE), F32),
            jax.ShapeDtypeStruct((PLANE, WIDE), BF16),
        ],
        compiler_params=pltpu.CompilerParams(vmem_limit_bytes=48 * 2**20),
        cost_estimate=pl.CostEstimate(
            flops=8 * PLANE * D * 2 * WIDE, bytes_accessed=PLANE * D * 8, transcendentals=PLANE * 1024
        ),
    )(core, *rows, attn_w, freq)


def unproject_kernel(core_ref, mine_ref, got_ref, raw_ref, facts_ref, w_ref, freq_ref, dp_ref, gain_ref, *part_refs):
    low = core_ref[0] == 0
    gains = [0.0, 0.0]
    for r in range(RING):
        block = slice(r * ROWS, (r + 1) * ROWS)
        cosine, sine = angles_of(facts_ref[block], freq_ref)
        total = None
        for kind in range(3):
            mine, got = mine_ref[kind, block], got_ref[kind, block]
            grad = jnp.concatenate([jnp.where(low, mine, got), jnp.where(low, got, mine)], 1)
            if kind < 2:
                grad = grad.astype(F32)
                if kind == 0:
                    grad = grad * (HEAD_DIM ** (-0.5))
                raw = raw_ref[kind, block]
                inv = lax.rsqrt(head_sums(raw * raw) * (1.0 / HEAD_DIM) + EPS)
                unit = raw * inv
                grad = grad * cosine - partner(grad) * sine
                gains[kind] += jnp.sum(grad * unit, axis=0, keepdims=True)
                scaled = grad * freq_ref[1 + kind : 2 + kind, :]
                mean = head_sums(scaled * unit) * (1.0 / HEAD_DIM)
                grad = (inv * (scaled - unit * mean)).astype(BF16)
            dp_ref[kind, block] = grad
            part = mm(grad, w_ref[kind], NT)
            total = part if total is None else total + part
        part_refs[r][...] = total.astype(BF16)
    gain_ref[...] = jnp.zeros_like(gain_ref)
    gain_ref[0:1, :] = gains[0]
    gain_ref[1:2, :] = gains[1]


def unproject(core, mine, got, raw, facts, attn_w, freq):
    three = pl.BlockSpec((3, D, 2 * WIDE), lambda i: (0, 0, 0))

    def whole(v):
        return pl.BlockSpec(v.shape, lambda i: (0,) * v.ndim)

    shapes = [
        jax.ShapeDtypeStruct((3, PLANE, 2 * WIDE), BF16),
        jax.ShapeDtypeStruct((8, 2 * WIDE), F32),
    ] + [jax.ShapeDtypeStruct((ROWS, D), BF16)] * RING
    return pl.pallas_call(
        unproject_kernel,
        grid=(1,),
        in_specs=[pl.BlockSpec(memory_space=pltpu.SMEM)]
        + [whole(v) for v in (mine, got, raw, facts)]
        + [three, whole(freq)],
        out_specs=[whole(v) for v in shapes],
        out_shape=shapes,
        compiler_params=pltpu.CompilerParams(vmem_limit_bytes=48 * 2**20),
        cost_estimate=pl.CostEstimate(
            flops=8 * PLANE * D * 2 * WIDE, bytes_accessed=PLANE * D * 8, transcendentals=PLANE * 1024
        ),
    )(core, mine, got, raw, facts, attn_w, freq)


LOG_LANE = 3 * VARIATES + SEQS


def with_pieces(base, values, first_lane, lanes):
    for i in range(3):
        part = values.astype(BF16).astype(F32)
        base = jnp.where(lanes == first_lane + i, part, base)
        values = values - part
    return base


def value_lanes(rows):
    return (lanes_of((rows, WIDE)) < 3).astype(BF16)


def attend_kernel(
    at_ref, mine_ref, got_ref, own_ref, other_ref, bias_ref,
    att_ref, near_ref, send_ref, tail_ref, kt_ref, all_scr, qt_scr, *, chunks,
):
    step = pl.program_id(0)
    block = att_ref.shape[0]
    size = GROUP // chunks

    @pl.when(step == 0)
    def _():
        all_scr[:, :PLANE] = mine_ref[...]
        all_scr[:, PLANE:] = got_ref[...]
        lane = lanes_of((ROWS, WIDE))
        tail_lane = lane % HEAD_DIM
        bias_lane = tail_lane < 3 * VARIATES
        seg_lane = (tail_lane >= 3 * VARIATES) & (tail_lane < LOG_LANE)
        one_lane = (tail_lane >= LOG_LANE) & (tail_lane < LOG_LANE + 3)
        row = lax.broadcasted_iota(jnp.int32, (ROWS, WIDE), 0)
        for b in range(2 * RING):
            source = own_ref if b < RING else other_ref
            facts = source[(b % RING) * ROWS : (b % RING + 1) * ROWS, :].astype(F32)
            variate = facts[:, 2:3]
            equal = bias_lane & ((tail_lane % VARIATES).astype(F32) == variate)
            position = at_ref[b] + row
            segment = jnp.zeros_like(row)
            for j in range(SEQS):
                segment += (position >= at_ref[2 * RING + j]).astype(jnp.int32)
            inside = seg_lane & (tail_lane - 3 * VARIATES == segment)
            rows = slice(b * ROWS, (b + 1) * ROWS)
            qt_scr[rows] = (equal | inside).astype(BF16)
            tail = jnp.where(equal, bias_ref[0:1, :], bias_ref[1:2, :])
            tail = jnp.where(bias_lane, tail, jnp.where(one_lane, 1.0, 0.0))
            tail = jnp.where(seg_lane & ~inside, FAR, tail)
            kt_ref[rows] = tail.astype(BF16)

    here = pl.ds(pl.multiple_of(step * block, block), block)
    query_tail = qt_scr[here, :]
    query = jnp.concatenate([all_scr[0, here, :], query_tail], 1)
    zero = jnp.zeros_like(query)
    head_of = (lanes_of(query.shape) // HEAD_DIM) % 2
    lanes = lanes_of((block, WIDE))
    ones = value_lanes(size)
    out = None
    tail = query_tail.astype(F32)
    for head in range(2):
        masked = jnp.where(head_of == head, query, zero)
        total = None
        for c in range(chunks):
            rows = slice(c * size, (c + 1) * size)
            keys = jnp.concatenate([all_scr[1, rows, :], kt_ref[rows, :]], 1)
            values = jnp.concatenate([all_scr[2, rows, :], ones], 1)
            prob = jnp.exp2(mm(masked, keys, NT)).astype(BF16)
            part = mm(prob, values)
            total = part if total is None else total + part
        row_sum = total[:, WIDE : WIDE + 1]
        now = total[:, :WIDE] / row_sum
        out = now if head == 0 else jnp.where(lanes < HEAD_DIM, out, now)
        tail = with_pieces(tail, -jnp.log2(row_sum), head * HEAD_DIM + LOG_LANE, lanes)
    att_ref[...] = out
    tail_ref[...] = tail.astype(BF16)
    low = out.astype(BF16)
    half = pl.num_programs(0) // 2

    @pl.when(step < half)
    def _():
        near_ref[here, :] = low

    @pl.when(step >= half)
    def _():
        send_ref[pl.ds(pl.multiple_of((step - half) * block, block), block), :] = low


def attend(at, mine, got, facts, facts_other, bias_rows):
    block = 512
    moving = pl.BlockSpec((block, WIDE), lambda i: (i, 0))
    plane = pl.BlockSpec((PLANE, WIDE), lambda i: (0, 0))
    three = pl.BlockSpec((3, PLANE, WIDE), lambda i: (0, 0, 0))
    low = jax.ShapeDtypeStruct((GROUP, WIDE), BF16)
    low_plane = jax.ShapeDtypeStruct((PLANE, WIDE), BF16)
    return pl.pallas_call(
        functools.partial(attend_kernel, chunks=4),
        grid=(GROUP // block,),
        in_specs=[
            pl.BlockSpec(memory_space=pltpu.SMEM),
            three,
            three,
            plane,
            plane,
            pl.BlockSpec((8, WIDE), lambda i: (0, 0)),
        ],
        out_specs=[moving, plane, plane, moving, pl.BlockSpec((GROUP, WIDE), lambda i: (0, 0))],
        out_shape=[jax.ShapeDtypeStruct((GROUP, WIDE), F32), low_plane, low_plane, low, low],
        scratch_shapes=[pltpu.VMEM((3, GROUP, WIDE), BF16), pltpu.VMEM((GROUP, WIDE), BF16)],
        compiler_params=pltpu.CompilerParams(vmem_limit_bytes=48 * 2**20),
        cost_estimate=pl.CostEstimate(
            flops=16 * GROUP * GROUP * WIDE, bytes_accessed=GROUP * WIDE * 24,
            transcendentals=2 * GROUP * GROUP,
        ),
    )(at, mine, got, facts, facts_other, bias_rows)


def attend_back_kernel(
    mine_ref, got_ref, qt_ref, kt_ref, hot_ref, near_ref, other_ref, att_ref,
    keep_ref, send_ref, bias_ref, all_scr, grad_scr, dk_sum, dv_sum, *, chunks,
):
    size = GROUP // chunks
    step = pl.program_id(0)
    block = qt_ref.shape[0]

    @pl.when(step == 0)
    def _():
        all_scr[:, :PLANE] = mine_ref[...]
        all_scr[:, PLANE:] = got_ref[...]
        grad_scr[:PLANE] = near_ref[...]
        grad_scr[PLANE:] = other_ref[...]
        dk_sum[...] = jnp.zeros_like(dk_sum)
        dv_sum[...] = jnp.zeros_like(dv_sum)

    here = pl.ds(pl.multiple_of(step * block, block), block)
    query = jnp.concatenate([all_scr[0, here, :], qt_ref[...]], 1)
    grad = grad_scr[here, :]
    zero = jnp.zeros_like(query)
    head_of = (lanes_of(query.shape) // HEAD_DIM) % 2
    lanes = lanes_of((block, WIDE))
    overlap = grad.astype(F32) * att_ref[...]
    ones = value_lanes(size)
    out = None
    for head in range(2):
        mine = head_of[:, :WIDE] == head
        masked = jnp.where(head_of == head, query, zero)
        grad_here = jnp.where(mine, grad, zero[:, :WIDE])
        dots = jnp.sum(jnp.where(mine, overlap, 0.0), axis=1, keepdims=True)
        extra = with_pieces(jnp.zeros(lanes.shape, F32), -dots, 0, lanes).astype(BF16)
        grad_wide = jnp.concatenate([grad_here, extra], 1)
        total = None
        for c in range(chunks):
            rows = slice(c * size, (c + 1) * size)
            keys = all_scr[1, rows, :]
            prob = jnp.exp2(mm(jnp.concatenate([keys, kt_ref[rows, :]], 1), masked, NT))
            slope = mm(jnp.concatenate([all_scr[2, rows, :], ones], 1), grad_wide, NT)
            d_score = (prob * slope).astype(BF16)
            dv_sum[rows, :] += mm(prob.astype(BF16), grad_here)
            dk_sum[rows, :] += mm(d_score, masked)
            part = mm(d_score, keys, TN)
            total = part if total is None else total + part
        out = total if head == 0 else jnp.where(lanes < HEAD_DIM, out, total)
    low = out.astype(BF16)
    half = pl.num_programs(0) // 2

    @pl.when(step < half)
    def _():
        keep_ref[0, here, :] = low

    @pl.when(step >= half)
    def _():
        send_ref[0, pl.ds(pl.multiple_of((step - half) * block, block), block), :] = low

    @pl.when(step == pl.num_programs(0) - 1)
    def _():
        for ref, rows in ((keep_ref, slice(0, PLANE)), (send_ref, slice(PLANE, GROUP))):
            ref[1] = (dk_sum[rows, :WIDE] * (1.0 / LOG2E)).astype(BF16)
            ref[2] = dv_sum[rows, :].astype(BF16)
        counts = dk_sum[:, WIDE:]
        bias_ref[...] = jnp.zeros_like(bias_ref)
        bias_ref[0:1, :] = jnp.sum(counts * hot_ref[...].astype(F32), axis=0, keepdims=True)
        bias_ref[1:2, :] = jnp.sum(counts, axis=0, keepdims=True)


def attend_back(mine, got, query_tail, key_tail, near, other, attended):
    block = 512
    moving = pl.BlockSpec((block, WIDE), lambda i: (i, 0))
    fixed = pl.BlockSpec((GROUP, WIDE), lambda i: (0, 0))
    plane = pl.BlockSpec((PLANE, WIDE), lambda i: (0, 0))
    three = pl.BlockSpec((3, PLANE, WIDE), lambda i: (0, 0, 0))
    low = jax.ShapeDtypeStruct((3, PLANE, WIDE), BF16)
    return pl.pallas_call(
        functools.partial(attend_back_kernel, chunks=4),
        grid=(GROUP // block,),
        in_specs=[three, three, moving, fixed, fixed, plane, plane, moving],
        out_specs=[three, three, pl.BlockSpec((8, WIDE), lambda i: (0, 0))],
        out_shape=[low, low, jax.ShapeDtypeStruct((8, WIDE), F32)],
        scratch_shapes=[
            pltpu.VMEM((3, GROUP, WIDE), BF16),
            pltpu.VMEM((GROUP, WIDE), BF16),
            pltpu.VMEM((GROUP, 2 * WIDE), F32),
            pltpu.VMEM((GROUP, WIDE), F32),
        ],
        compiler_params=pltpu.CompilerParams(vmem_limit_bytes=48 * 2**20),
        cost_estimate=pl.CostEstimate(
            flops=40 * GROUP * GROUP * WIDE, bytes_accessed=GROUP * WIDE * 24,
            transcendentals=2 * GROUP * GROUP,
        ),
    )(mine, got, query_tail, key_tail, query_tail, near, other, attended)


def feed_kernel(b_ref, g_ref, w_ref, y_ref, db_ref, act_ref, *, cuts):
    rows, grads = b_ref[...], g_ref[...]
    size = w_ref.shape[2] // cuts

    def products(j):
        cols = slice(j * size, (j + 1) * size)
        return mm(rows, w_ref[0, :, cols]), mm(rows, w_ref[1, :, cols]), mm(grads, w_ref[2, :, cols])

    y_sum, db_sum = None, None
    ready = products(0)
    for j in range(cuts):
        gate, up, d_hidden = ready
        if j + 1 < cuts:
            ready = products(j + 1)
        cols = slice(j * size, (j + 1) * size)
        sig = 0.5 + 0.5 * jnp.tanh(0.5 * gate)
        silu = gate * sig
        hidden = (silu * up).astype(BF16)
        d_gate = (d_hidden * up * (sig + silu * (1.0 - sig))).astype(BF16)
        d_up = (d_hidden * silu).astype(BF16)
        act_ref[0, :, cols] = d_gate
        act_ref[1, :, cols] = d_up
        act_ref[2, :, cols] = hidden
        y_part = mm(hidden, w_ref[2, :, cols], NT)
        db_part = mm(d_gate, w_ref[0, :, cols], NT) + mm(d_up, w_ref[1, :, cols], NT)
        y_sum = y_part if y_sum is None else y_sum + y_part
        db_sum = db_part if db_sum is None else db_sum + db_part
    y_ref[...] = y_sum.astype(BF16)
    db_ref[...] = db_sum.astype(BF16)


def feed(rows_b, rows_g, weights):
    rows = rows_b.shape[0]
    width = weights.shape[2]
    low_d = jax.ShapeDtypeStruct((rows, D), BF16)
    low_f = jax.ShapeDtypeStruct((3, rows, width), BF16)
    return pl.pallas_call(
        functools.partial(feed_kernel, cuts=2),
        out_shape=[low_d, low_d, low_f],
        compiler_params=pltpu.CompilerParams(vmem_limit_bytes=26 * 2**20),
        cost_estimate=pl.CostEstimate(
            flops=12 * rows * D * width, bytes_accessed=6 * D * width + rows * D * 8 + rows * width * 6,
            transcendentals=rows * width,
        ),
    )(rows_b, rows_g, weights)


def body(
    tokens,
    cotangent,
    destination,
    variate_ids,
    time_ids,
    seq_lengths,
    qkv_weight,
    out_weight,
    gate_up_weight,
    down_weight,
    norm_gains,
    qk_gains,
    variate_bias,
):
    core = lax.axis_index("core")
    low_core = core == 0
    y_at = lax.axis_index("y")
    zl_at = lax.axis_index("zl")

    core_scalar = core.reshape(1).astype(jnp.int32)

    def side_by_side(mine, other):
        return jnp.concatenate(
            [jnp.where(low_core, mine, other), jnp.where(low_core, other, mine)], axis=-1
        )

    feed_shard = jnp.concatenate([gate_up_weight, down_weight.T[None]], 0)

    slot = destination % ROWS
    group_at = destination // GROUP
    block_at = (destination % GROUP) // ROWS
    device_at = ((group_at // 2) * 2 + block_at // 4) * 8 + (block_at % 4) * 2 + group_at % 2
    key = device_at * ROWS + slot
    zero = jnp.zeros_like(slot)
    facts = jnp.stack([key, slot, variate_ids, time_ids // 32, time_ids % 32, zero, zero, zero])
    gains_row = jnp.pad(
        norm_gains.reshape(8, 16), ((0, 0), (GAIN_LANE, WIDE - GAIN_LANE - 16))
    ).astype(F32)
    outgoing, deal = deal_rows(tokens, cotangent, facts.astype(F32), gains_row)
    arrived = lax.all_to_all(outgoing.reshape(DEVICES, 8, SPAN), ALL, 0, 0, tiled=True)
    out_shard, outgoing = lax.optimization_barrier((out_weight.T, outgoing))
    attn_shard = jnp.concatenate([qkv_weight, jnp.stack(gather_direct(out_shard))], 0)
    attn_mine = gather_round(attn_shard, ("zh", "zl"), lax.axis_index("zh") * 2 + zl_at)
    attn_mine, arrived = lax.optimization_barrier((attn_mine, arrived))
    attn_mine = jnp.stack(gather_ahead(attn_mine, "x")).reshape((16,) + attn_shard.shape)

    lengths_other = swap_core(seq_lengths)
    lengths = jnp.where(zl_at == core, seq_lengths, lengths_other)[0]
    bias_other = lax.ppermute(variate_bias, "zl", [(0, 1), (1, 0)])
    bias_pair = jnp.where(zl_at == core, variate_bias, bias_other)

    arrived, lengths, bias_pair = lax.optimization_barrier((arrived, lengths, bias_pair))
    all_gains = arrived.reshape(16, 8, 8, SPAN)[:, 0, :, PAIR + GAIN_LANE : PAIR + GAIN_LANE + 16]
    inputs, grad_rows, attn_in, place, gains = receive(
        arrived.reshape(4 * ROWS, SPAN), all_gains.reshape(16, WIDE)
    )
    feed_shard, attn_in = lax.optimization_barrier((feed_shard, attn_in))
    feed_mine = flat_gather(feed_shard)
    zero_at = jnp.zeros((1,), jnp.int32)
    x_at = lax.axis_index("x").reshape(1).astype(jnp.int32)
    ahead, behind = ring(attn_in, -1), ring(attn_in, 1)
    far_top, far_low = ring(ahead[: ROWS // 2], -1), ring(behind[ROWS // 2 :], 1)
    far_top, far_low, attn_mine = lax.optimization_barrier((far_top, far_low, attn_mine))
    attn_w = assemble(core_scalar, x_at, attn_mine, swap_core(attn_mine))
    attn_all = [attn_in, ahead, jnp.concatenate([far_top, far_low], 0), behind]
    grad_rows, attn_all = lax.optimization_barrier((grad_rows, attn_all))
    grad_all = gather_direct(grad_rows)

    blocks_y = (y_at + jnp.arange(RING)) % RING
    blocks = jnp.concatenate([core * RING + blocks_y, (1 - core) * RING + blocks_y])
    at = jnp.concatenate([blocks * ROWS, jnp.cumsum(lengths)]).astype(jnp.int32)

    inverse = THETA ** (-2.0 * jnp.arange(HALF).astype(F32) / HEAD_DIM)
    freq = jnp.concatenate(
        [
            jnp.tile(inverse, 8)[None],
            jnp.tile(qk_gains, (1, 4)),
            jnp.zeros((5, 2 * WIDE), F32),
        ]
    )
    qkv_mine, qkv_send, raw, facts_all = project(core_scalar, attn_all, attn_w, freq)
    facts_other = swap_core(facts_all)
    qkv_got = swap_core(qkv_send)

    bias_parts = jnp.stack(pieces(bias_pair * LOG2E, 3)).astype(F32)
    bias_rows = jnp.repeat(bias_parts, VARIATES, axis=0).transpose(1, 2, 0)
    bias_rows = jnp.pad(bias_rows, ((0, 0), (0, 0), (0, HEAD_DIM - 3 * VARIATES))).reshape(2, WIDE)
    bias_rows = jnp.pad(bias_rows, ((0, 6), (0, 0)))
    attended, att_near, att_send, query_back, key_tail = attend(
        at, qkv_mine, qkv_got, facts_all, facts_other, bias_rows
    )
    att_near, grad_all = lax.optimization_barrier((att_near, grad_all))
    att_other = swap_core(att_send)
    att_plane = side_by_side(att_near, att_other).reshape(RING, ROWS, 2 * WIDE)
    att_rows = trade_ring([att_plane[r] for r in range(RING)])
    att_rows, feed_mine = lax.optimization_barrier((att_rows, feed_mine))
    feed_w = assemble(core_scalar, zero_at, feed_mine, swap_core(feed_mine))
    hidden_one, feed_in = out_project(att_rows, attn_w, inputs, gains)

    ahead, behind = ring(feed_in, -1), ring(feed_in, 1)
    fed_own = feed(feed_in, grad_all[0], feed_w)
    ahead, behind, fed_own = lax.optimization_barrier((ahead, behind, fed_own))
    far_top, far_low = ring(ahead[: ROWS // 2], -1), ring(behind[ROWS // 2 :], 1)
    fed_ahead = feed(ahead, grad_all[1], feed_w)
    fed_behind = feed(behind, grad_all[3], feed_w)
    far_top, far_low, fed_ahead, fed_behind = lax.optimization_barrier(
        (far_top, far_low, fed_ahead, fed_behind)
    )
    far = jnp.concatenate([far_top, far_low], 0)
    fed_far = feed(far, grad_all[2], feed_w)
    feed_all = [feed_in, ahead, far, behind]
    fed = [fed_own, fed_ahead, fed_far, fed_behind]
    feed_split = weight_grads(core_scalar, feed_all, grad_all, [f[2] for f in fed], 2, 2)
    db_got = send_ring([f[1] for f in fed], True)
    db_got, feed_split = lax.optimization_barrier((db_got, feed_split))
    grad_one, gain_two_grad, d_att, *both = middle(
        att_rows, attn_w, [f[0] for f in fed], fed_own[1], db_got, hidden_one, grad_rows, gains
    )
    feed_total = chip_total(feed_split)
    feed_got = trade(feed_total, "x")

    grad_att = trade_ring([d_att[r] for r in range(RING)])
    grad_att[1], feed_total = lax.optimization_barrier((grad_att[1], feed_total))
    grad_att = jnp.concatenate(grad_att, 0)
    both, grad_att = lax.optimization_barrier((both, grad_att))
    both_got = send_ring(both)
    grad_left, grad_right = grad_att[:, :WIDE], grad_att[:, WIDE:]
    grad_other = swap_core(jnp.where(low_core, grad_right, grad_left))
    grad_near = jnp.where(low_core, grad_left, grad_right)
    d_keep, d_send, bias_sums = attend_back(
        qkv_mine, qkv_got, query_back, key_tail, grad_near, grad_other, attended
    )
    first_part = (jnp.arange(HEAD_DIM) < VARIATES)[None, None]
    bias_sums = jnp.where(first_part, bias_sums[:2].reshape(2, 2, HEAD_DIM), 0.0)
    bias_sums = jnp.sum(bias_sums, axis=2)
    bias_part = jnp.stack([bias_sums[0], bias_sums[1] - bias_sums[0]])
    d_send, feed_got = lax.optimization_barrier((d_send, feed_got))
    feed_half = added(feed_got).astype(BF16)
    d_got, feed_half = lax.optimization_barrier((swap_core(d_send), feed_half))
    grad_proj, qk_sums, *in_part = unproject(
        core_scalar, d_keep, d_got, raw, facts_all, attn_w, freq
    )
    in_got = send_ring(in_part)
    in_got[0], feed_half = lax.optimization_barrier((in_got[0], feed_half))
    grad_proj, both_got = lax.optimization_barrier((grad_proj, both_got))
    both_sum = add_ring(both[0], both_got)
    mixed = (hidden_one + both_sum[:ROWS]).astype(BF16)
    out_full = both_sum[ROWS:].astype(BF16)
    attn_split = weight_grads(core_scalar, attn_all, [out_full], [grad_proj], None, 1)
    attn_total = chip_total(attn_split)
    in_got, _ = lax.optimization_barrier((in_got, attn_split))
    feed_got = trade(feed_half, ("zh", "zl"))
    mixed, _ = lax.optimization_barrier((mixed, attn_total))
    attn_own, attn_got = send_round(attn_total.reshape((RING, RING) + attn_total.shape[1:]), "x")
    qk_sums = jnp.sum(qk_sums[:2].reshape(2, 4, HEAD_DIM), axis=1)

    small = jnp.zeros((8, WIDE), F32).at[0].set(qk_sums.reshape(WIDE))
    small = small.at[1, :4].set(bias_part.reshape(4))
    tensor_at = (y_at * 2 + core).reshape(1).astype(jnp.int32)
    last = finish(
        in_part[0], in_got, inputs, grad_one, mixed, place, gains, gain_two_grad, small, tensor_at
    )
    last = last.reshape(DEVICES, 8, 2 * QUARTER + WIDE)
    last, attn_got, feed_got = lax.optimization_barrier((last, attn_got, feed_got))
    home = lax.all_to_all(last, ALL, 0, 0, tiled=True)
    own, got = send_round(add_round(attn_own, attn_got).astype(BF16), ("zh", "zl"))
    home, got = lax.optimization_barrier((home, got))
    attn_grad = add_round(own, got)
    feed_grad = added(feed_got).reshape(3, 64, 512)
    new_tokens, token_grads, sums = settle(home.reshape(4 * ROWS, 2 * QUARTER + WIDE), deal)
    gains_grad = sums[0].reshape(2, 64)
    qk_grad = sums[1].reshape(2, 64)
    bias_grad = sums[2, :4].reshape(2, 2)

    return (
        new_tokens,
        token_grads,
        attn_grad[:3],
        attn_grad[3].T,
        feed_grad[:2],
        feed_grad[2].T,
        gains_grad,
        qk_grad,
        bias_grad,
    )


def solution(mesh):
    fine = Mesh(mesh.devices.reshape(4, 2, 2, 4, 2), ALL)
    dp = ("x", "zh", "core")
    tensor = ("y", "zl")
    in_specs = (
        P(ALL, None),
        P(ALL, None),
        P(ALL),
        P(ALL),
        P(ALL),
        P(dp, None),
        P(None, dp, tensor),
        P(tensor, dp),
        P(None, dp, tensor),
        P(tensor, dp),
        P(None, dp),
        P(),
        P(None, tensor),
    )
    out_specs = (
        P(ALL, None),
        P(ALL, None),
        P(None, dp, tensor),
        P(tensor, dp),
        P(None, dp, tensor),
        P(tensor, dp),
        P(None, dp),
        P(),
        P(None, tensor),
    )
    return jax.shard_map(body, mesh=fine, in_specs=in_specs, out_specs=out_specs, check_vma=False)
```

```python
import functools

import jax
import jax.numpy as jnp
from jax import lax
from jax.experimental import pallas as pl
from jax.experimental.pallas import tpu as pltpu
from jax.sharding import Mesh
from jax.sharding import PartitionSpec as P

HEADS = 16
HEAD_DIM = 64
HALF = HEAD_DIM // 2
D = 1024
FF = 4096
ROWS = 256
RING = 4
PLANE = ROWS * RING
GROUP = 2 * PLANE
DEVICES = 128
VARIATES = 8
SEQS = 4
WIDE = 128
EPS = 1e-06
THETA = 10000.0
LOG2E = 1.4426950408889634
FAR = -16384.0
F32 = jnp.float32
BF16 = jnp.bfloat16

ALL = ("x", "zh", "core", "y", "zl")
FLAT = ("x", "zh", "zl")
NT = (((1,), (1,)), ((), ()))
TN = (((0,), (0,)), ((), ()))


def mm(left, right, dims=(((1,), (0,)), ((), ()))):
    return lax.dot_general(left, right, dims, preferred_element_type=F32)


def root_stats(values):
    return lax.rsqrt(jnp.mean(values * values, axis=-1, keepdims=True) + EPS)


def norm_back(grad_in, normed, scale_inv):
    return scale_inv * (grad_in - normed * jnp.mean(grad_in * normed, axis=-1, keepdims=True))


def pieces(values, count):
    out = []
    for _ in range(count):
        part = lax.reduce_precision(values, 8, 7)
        out.append(part.astype(BF16))
        values = values - part
    return out


def ring(values, step):
    return lax.ppermute(values, "y", [(i, (i + step) % RING) for i in range(RING)])


def swap_core(values):
    return lax.ppermute(values, "core", [(0, 1), (1, 0)])


def gather_ring(values):
    ahead = ring(values, -1)
    behind = ring(values, 1)
    half = values.shape[0] // 2
    far_top = ring(ahead[:half], -1)
    far_low = ring(behind[half:], 1)
    return [values, ahead, jnp.concatenate([far_top, far_low], 0), behind]


def gather_direct(values):
    return [values, ring(values, -1), ring(values, 2), ring(values, 1)]


def trade_ring(parts):
    return [parts[0]] + [ring(parts[RING - s], -s) for s in range(1, RING)]


def send_ring(parts, halves=False):
    half = parts[2].shape[0] // 2
    far = [parts[2][:half], parts[2][half:]] if halves else [parts[2]]
    return [ring(parts[1], 1), ring(parts[3], -1)] + [ring(v, 2) for v in far]


def add_ring(own, got):
    far = got[2] if len(got) == 3 else jnp.concatenate(got[2:], 0)
    return own.astype(F32) + got[0].astype(F32) + got[1].astype(F32) + far.astype(F32)


def gather_ahead(values, axes):
    moves = [[((i + r) % RING, i) for i in range(RING)] for r in range(RING)]
    return [values] + [lax.ppermute(values, axes, moves[r]) for r in range(1, RING)]


def gather_round(values, axes, at):
    return jnp.roll(jnp.stack(gather_ahead(values, axes)), at, axis=0)


def flat_gather(shard):
    many = jnp.broadcast_to(shard[None], (16,) + shard.shape)
    return lax.all_to_all(many, FLAT, 0, 0, tiled=True)


def assemble_kernel(at_ref, mine_ref, other_ref, out_ref):
    core = at_ref[0]
    count, _, depth, width = mine_ref.shape
    for ref, side in ((mine_ref, core), (other_ref, 1 - core)):
        for i in range(count):
            at = (i // 2) * 2 * depth + side * depth
            rows = pl.ds(pl.multiple_of(at, depth), depth)
            out_ref[:, rows, (i % 2) * width : (i % 2 + 1) * width] = ref[i]


def assemble(core, x_at, mine, other):
    _, kinds, depth, width = mine.shape
    pair = pl.BlockSpec((4, kinds, depth, width), lambda p, at: (p, 0, 0, 0))
    return pl.pallas_call(
        assemble_kernel,
        grid_spec=pltpu.PrefetchScalarGridSpec(
            num_scalar_prefetch=1,
            grid=(RING,),
            in_specs=[pair, pair],
            out_specs=pl.BlockSpec(
                (kinds, 4 * depth, 2 * width), lambda p, at: (0, lax.rem(at[1] + p, RING), 0)
            ),
        ),
        out_shape=jax.ShapeDtypeStruct((kinds, 16 * depth, 2 * width), BF16),
        compiler_params=pltpu.CompilerParams(vmem_limit_bytes=28 * 2**20),
        cost_estimate=pl.CostEstimate(
            flops=0, bytes_accessed=kinds * 128 * depth * width, transcendentals=0
        ),
    )(jnp.concatenate([core, x_at]), mine, other)


def chip_total(split):
    return (split[0].astype(F32) + swap_core(split[1]).astype(F32)).astype(BF16)


def send_round(values, axes):
    at = lax.axis_index(axes)
    parts = [lax.dynamic_index_in_dim(values, (at + r) % RING, 0, keepdims=False) for r in range(RING)]
    moves = [[(i, (i + r) % RING) for i in range(RING)] for r in range(RING)]
    return parts[0], [lax.ppermute(parts[r], axes, moves[r]) for r in (1, 3, 2)]


def add_round(own, got):
    return sum((v.astype(F32) for v in got), own.astype(F32))


def trade(values, axes):
    return lax.all_to_all(values.reshape((RING, -1) + values.shape[1:]), axes, 0, 0, tiled=True)


def added(got):
    return jnp.sum(got.astype(F32), axis=0)


def lanes_of(shape):
    return lax.broadcasted_iota(jnp.int32, shape, 1)


QUARTER = D // RING
PAIR = 2 * QUARTER
SPAN = PAIR + WIDE
GAIN_LANE = 16


def deal_kernel(tok_ref, cot_ref, facts_ref, gains_ref, out_ref, deal_ref):
    wide = jnp.concatenate([facts_ref[...], jnp.zeros((WIDE - 8, ROWS), F32)], 0)
    facts = jnp.transpose(wide)
    keys = facts_ref[0:1, :]
    rank = jnp.sum((facts[:, 0:1] < keys).astype(F32), axis=0, keepdims=True)
    at = lax.broadcasted_iota(jnp.int32, (ROWS, ROWS), 0).astype(F32)
    deal_ref[...] = (at == rank).astype(BF16)
    low = jnp.where(lanes_of(facts.shape) == 0, 0.0, facts).astype(BF16)
    row = lax.broadcasted_iota(jnp.int32, (4 * ROWS, 1), 0)
    own = ((row // RING).astype(F32) == rank).astype(BF16)
    part = None
    for m in range(RING):
        cols = slice(m * QUARTER, (m + 1) * QUARTER)
        here = mm(own, jnp.concatenate([tok_ref[:, cols], cot_ref[:, cols]], 1))
        part = here if m == 0 else jnp.where(row % RING == m, here, part)
    out_ref[:, :PAIR] = part.astype(BF16)
    tail = mm(own, low)
    lane = lanes_of(tail.shape)
    gains = jnp.broadcast_to(gains_ref[...][None], (DEVICES, 8, WIDE)).reshape(tail.shape)
    tail = jnp.where((lane >= GAIN_LANE) & (lane < GAIN_LANE + 16), gains, tail)
    out_ref[:, PAIR:] = tail.astype(BF16)


def deal_rows(tokens, cotangent, facts, gains):
    return pl.pallas_call(
        deal_kernel,
        out_shape=[
            jax.ShapeDtypeStruct((4 * ROWS, SPAN), BF16),
            jax.ShapeDtypeStruct((ROWS, ROWS), BF16),
        ],
        compiler_params=pltpu.CompilerParams(vmem_limit_bytes=48 * 2**20),
        cost_estimate=pl.CostEstimate(
            flops=8 * ROWS * ROWS * 2304, bytes_accessed=ROWS * D * 16, transcendentals=0
        ),
    )(tokens, cotangent, facts, gains)


def receive_kernel(rows_ref, gains_ref, x_ref, g_ref, a_ref, place_ref, gain_ref):
    count = 4 * ROWS
    facts = rows_ref[:, PAIR:]
    slots = jnp.transpose(facts.astype(F32))[1:2, :]
    at = lax.broadcasted_iota(jnp.int32, (ROWS, count), 0)
    arrival = lanes_of((ROWS, count))
    here = at.astype(F32) == slots
    gains = gains_ref[...].astype(F32)
    turned = pltpu.roll(gains, HEAD_DIM, 1)
    left = lanes_of((1, WIDE)) < HEAD_DIM
    one, two = [], []
    for c in range(D // WIDE):
        even, odd = slice(2 * c, 2 * c + 1), slice(2 * c + 1, 2 * c + 2)
        one.append(jnp.where(left, gains[even], turned[odd]))
        two.append(jnp.where(left, turned[even], gains[odd]))
    gain_one = jnp.concatenate(one, 1)
    gain_ref[...] = jnp.zeros_like(gain_ref)
    gain_ref[0:1, :] = gain_one
    gain_ref[1:2, :] = jnp.concatenate(two, 1)
    quarters = []
    for m in range(RING):
        chosen = (here & (arrival % RING == m)).astype(BF16)
        both = mm(chosen, rows_ref[:, :PAIR])
        quarters.append(both[:, :QUARTER])
        g_ref[:, m * QUARTER : (m + 1) * QUARTER] = both[:, QUARTER:].astype(BF16)
        if m == 0:
            a_ref[:, D:] = mm(chosen, facts).astype(BF16)
            pick = (at * RING == arrival).astype(BF16)
            place_ref[...] = mm(chosen, pick, NT).astype(BF16)
    rows = jnp.concatenate(quarters, 1)
    x_ref[...] = rows
    a_ref[:, :D] = (rows * root_stats(rows) * gain_one).astype(BF16)


def receive(rows, gains):
    return pl.pallas_call(
        receive_kernel,
        out_shape=[
            jax.ShapeDtypeStruct((ROWS, D), F32),
            jax.ShapeDtypeStruct((ROWS, D), BF16),
            jax.ShapeDtypeStruct((ROWS, D + WIDE), BF16),
            jax.ShapeDtypeStruct((ROWS, ROWS), BF16),
            jax.ShapeDtypeStruct((8, D), F32),
        ],
        compiler_params=pltpu.CompilerParams(vmem_limit_bytes=48 * 2**20),
        cost_estimate=pl.CostEstimate(
            flops=16 * ROWS * ROWS * D, bytes_accessed=ROWS * D * 24, transcendentals=0
        ),
    )(rows, gains)


OUT_KIND = 3


def out_kernel(*refs):
    att = refs[:RING]
    w_ref, x_ref, gain_ref, h_ref, b_ref = refs[RING:]
    hidden = x_ref[...]
    for r in range(RING):
        hidden = hidden + mm(att[r][...], w_ref[OUT_KIND + r], NT)
    h_ref[...] = hidden
    b_ref[...] = (hidden * root_stats(hidden) * gain_ref[1:2, :]).astype(BF16)


def out_project(att, weights, rows, gains):
    return pl.pallas_call(
        out_kernel,
        out_shape=[jax.ShapeDtypeStruct((ROWS, D), F32), jax.ShapeDtypeStruct((ROWS, D), BF16)],
        compiler_params=pltpu.CompilerParams(vmem_limit_bytes=48 * 2**20),
        cost_estimate=pl.CostEstimate(
            flops=2 * ROWS * D * D, bytes_accessed=2 * D * D + ROWS * D * 14, transcendentals=0
        ),
    )(*att, weights, rows, gains)


def middle_kernel(*refs):
    att, y_parts, w_ref = refs[:RING], refs[RING : 2 * RING], refs[2 * RING]
    refs = refs[2 * RING + 1 :]
    own_ref, near_ref, back_ref, top_ref, low_ref, h_ref, g_ref, gain_ref = refs[:8]
    grad_ref, two_ref, d_ref = refs[8:11]
    both_refs = refs[11:]
    far = jnp.concatenate([top_ref[...], low_ref[...]], 0).astype(F32)
    grad = own_ref[...].astype(F32) + near_ref[...].astype(F32) + back_ref[...].astype(F32) + far
    hidden = h_ref[...]
    scale = root_stats(hidden)
    normed = hidden * scale
    two_ref[...] = jnp.zeros_like(two_ref)
    two_ref[0:1, :] = jnp.sum(grad * normed, axis=0, keepdims=True)
    scaled = grad * gain_ref[1:2, :]
    grad = g_ref[...].astype(F32) + norm_back(scaled, normed, scale)
    grad_ref[...] = grad
    low = grad.astype(BF16)
    for r in range(RING):
        d_ref[r] = mm(low, w_ref[OUT_KIND + r]).astype(BF16)
        both_refs[r][:ROWS] = y_parts[r][...]
        both_refs[r][ROWS:] = mm(att[r][...], low, TN).astype(BF16)


def middle(att, weights, y_parts, own, got, hidden, grad_rows, gains):
    both = jax.ShapeDtypeStruct((2 * ROWS, D), BF16)
    return pl.pallas_call(
        middle_kernel,
        out_shape=[
            jax.ShapeDtypeStruct((ROWS, D), F32),
            jax.ShapeDtypeStruct((8, D), F32),
            jax.ShapeDtypeStruct((RING, ROWS, ROWS), BF16),
        ]
        + [both] * RING,
        compiler_params=pltpu.CompilerParams(vmem_limit_bytes=48 * 2**20),
        cost_estimate=pl.CostEstimate(
            flops=4 * ROWS * D * D, bytes_accessed=2 * D * D + ROWS * D * 40, transcendentals=0
        ),
    )(*att, *y_parts, weights, own, *got, hidden, grad_rows, gains)


def finish_kernel(
    own_ref, near_ref, back_ref, far_ref, x_ref, grad_ref, mixed_ref, place_ref,
    gain_ref, two_ref, small_ref, at_ref, out_ref,
):
    rows = x_ref[...]
    scale = root_stats(rows)
    normed = rows * scale
    far = far_ref[...].astype(F32)
    grad = own_ref[...].astype(F32) + near_ref[...].astype(F32) + back_ref[...].astype(F32) + far
    one = jnp.sum(grad * normed, axis=0, keepdims=True)
    two = two_ref[0:1, :]
    scaled = grad * gain_ref[0:1, :]
    back = scale * (scaled - normed * jnp.mean(scaled * normed, axis=1, keepdims=True))
    result = (grad_ref[...] + back).astype(BF16)
    count = 4 * ROWS
    row = lax.broadcasted_iota(jnp.int32, (count, 1), 0)
    quarter = row % RING
    pick = (row // RING == lanes_of((count, ROWS))).astype(BF16)
    pick = mm(pick, place_ref[...], NT).astype(BF16)
    part = None
    for m in range(RING):
        cols = slice(m * QUARTER, (m + 1) * QUARTER)
        here = mm(pick, jnp.concatenate([mixed_ref[:, cols], result[:, cols]], 1))
        part = here if m == 0 else jnp.where(quarter == m, here, part)
    out_ref[:, : 2 * QUARTER] = part.astype(BF16)
    left = lanes_of((1, WIDE)) < HEAD_DIM
    tiles = []
    for c in range(D // WIDE):
        cols = slice(c * WIDE, (c + 1) * WIDE)
        a, b = one[:, cols], two[:, cols]
        even = jnp.where(left, a, pltpu.roll(jnp.broadcast_to(b, (8, WIDE)), HEAD_DIM, 1)[0:1])
        odd = jnp.where(left, pltpu.roll(jnp.broadcast_to(a, (8, WIDE)), HEAD_DIM, 1)[0:1], b)
        tiles += [jnp.broadcast_to(even, (64, WIDE)), jnp.broadcast_to(odd, (64, WIDE))]
    value = jnp.concatenate(tiles, 0)
    value = jnp.where(quarter == 1, small_ref[0:1, :], value)
    bias = jnp.where((row // 8) % 8 == at_ref[0], small_ref[1:2, :], 0.0)
    value = jnp.where(quarter == 2, bias, value)
    high = value.astype(BF16).astype(F32)
    value = jnp.where((row // RING) % 2 == 0, high, value - high)
    out_ref[:, 2 * QUARTER :] = value.astype(BF16)


def finish(own, got, rows, grad, mixed, place, gains, two, small, at):
    specs = [pl.BlockSpec(memory_space=pltpu.VMEM)] * 11
    return pl.pallas_call(
        finish_kernel,
        in_specs=specs + [pl.BlockSpec(memory_space=pltpu.SMEM)],
        out_shape=jax.ShapeDtypeStruct((4 * ROWS, 2 * QUARTER + WIDE), BF16),
        compiler_params=pltpu.CompilerParams(vmem_limit_bytes=48 * 2**20),
        cost_estimate=pl.CostEstimate(
            flops=16 * ROWS * ROWS * D, bytes_accessed=ROWS * D * 20, transcendentals=0
        ),
    )(own, *got, rows, grad, mixed, place, gains, two, small, at)


def settle_kernel(home_ref, deal_ref, rows_ref, grads_ref, sums_ref):
    deal = deal_ref[...]
    shape = (ROWS, 4 * ROWS)
    index = lax.broadcasted_iota(jnp.int32, shape, 0)
    for m in range(RING):
        pick = (index * RING + m == lanes_of(shape)).astype(BF16)
        here = mm(pick, home_ref[:, : 2 * QUARTER]).astype(BF16)
        here = mm(deal, here, TN).astype(BF16)
        cols = slice(m * QUARTER, (m + 1) * QUARTER)
        rows_ref[:, cols] = here[:, :QUARTER]
        grads_ref[:, cols] = here[:, QUARTER:]
    small = home_ref[:, 2 * QUARTER :].astype(F32)
    quarter = lax.broadcasted_iota(jnp.int32, small.shape, 0) % RING
    sums_ref[...] = jnp.zeros_like(sums_ref)
    for m in range(3):
        sums_ref[m : m + 1, :] = jnp.sum(jnp.where(quarter == m, small, 0.0), axis=0, keepdims=True)


def settle(home, deal):
    low = jax.ShapeDtypeStruct((ROWS, D), BF16)
    return pl.pallas_call(
        settle_kernel,
        out_shape=[low, low, jax.ShapeDtypeStruct((8, WIDE), F32)],
        compiler_params=pltpu.CompilerParams(vmem_limit_bytes=48 * 2**20),
        cost_estimate=pl.CostEstimate(
            flops=20 * ROWS * ROWS * D, bytes_accessed=ROWS * D * 16, transcendentals=0
        ),
    )(home, deal)


def weight_grad_kernel(core_ref, *refs, parts, count, switch, steps):
    given = switch is None
    lefts, others, rights = refs[:parts], refs[parts : parts + count], refs[parts + count : -3]
    keep_ref, send_ref, turned_ref = refs[-3:]
    low = core_ref[0] == 0
    step = pl.program_id(0)

    def load(sides):
        at = 0
        for side in sides:
            rows = side.shape[0]
            turned_ref[:, at : at + rows] = side[...].T
            at += rows

    @pl.when(step == 0)
    def _():
        load(lefts)

    if not given:

        @pl.when(step == switch * steps)
        def _():
            load(others)

    def emit(total):
        depth = total.shape[0] // 16
        width = keep_ref.shape[-1]
        for z in range(total.shape[1] // width):
            cols = slice(z * width, (z + 1) * width)
            for p in range(8):
                at = 2 * p * depth
                even, odd = total[at : at + depth, cols], total[at + depth : at + 2 * depth, cols]
                keep_ref[p, z, 0] = jnp.where(low, even, odd)
                send_ref[p, z, 0] = jnp.where(low, odd, even)

    def product():
        right = jnp.concatenate([ref[0] for ref in rights], 0)
        emit(mm(turned_ref[...], right).astype(BF16))

    if given:
        pl.when(step < pl.num_programs(0) - 1)(product)

        @pl.when(step == pl.num_programs(0) - 1)
        def _():
            emit(others[0][...].T)
    else:
        product()


def weight_grads(core, lefts, others, rights, switch, steps):
    parts = len(lefts)
    made, _, width = rights[0].shape
    kinds = made + 1 if switch is None else made
    block, half = width // steps, width // 2
    sides = [pl.BlockSpec((v.shape[0], D), lambda s: (0, 0)) for v in list(lefts) + list(others)]
    moving = [
        pl.BlockSpec(
            (1, v.shape[1], block), lambda s: (jnp.minimum(s // steps, made - 1), 0, s % steps)
        )
        for v in rights
    ]
    rows = sum(v.shape[1] for v in rights)
    out = pl.pallas_call(
        functools.partial(
            weight_grad_kernel, parts=parts, count=len(others), switch=switch, steps=steps
        ),
        grid=(kinds * steps,),
        in_specs=[pl.BlockSpec(memory_space=pltpu.SMEM)] + sides + moving,
        out_specs=[
            pl.BlockSpec((8, 2 // steps, 1, 64, half), lambda s: (0, s % steps, s // steps, 0, 0))
        ]
        * 2,
        out_shape=[jax.ShapeDtypeStruct((8, 2, kinds, 64, half), BF16)] * 2,
        scratch_shapes=[pltpu.VMEM((D, rows), BF16)],
        compiler_params=pltpu.CompilerParams(vmem_limit_bytes=48 * 2**20),
        cost_estimate=pl.CostEstimate(
            flops=2 * kinds * rows * D * width,
            bytes_accessed=2 * kinds * D * width + 4 * rows * D + 2 * kinds * rows * width,
            transcendentals=0,
        ),
    )(core, *lefts, *others, *rights)
    return [v.reshape(16, kinds, 64, half) for v in out]


def head_sums(values):
    wide = values.shape[1]
    row = lax.broadcasted_iota(jnp.int32, (wide, wide), 0) // HEAD_DIM
    same = (row == lanes_of((wide, wide)) // HEAD_DIM).astype(BF16)
    high = values.astype(BF16)
    low = (values - high.astype(F32)).astype(BF16)
    return mm(high, same) + mm(low, same)


def partner(values):
    wide = values.shape[1]
    first = lanes_of(values.shape) % HEAD_DIM < HALF
    return jnp.where(first, pltpu.roll(values, wide - HALF, 1), pltpu.roll(values, HALF, 1))


def angles_of(facts, freq_ref):
    facts = facts.astype(F32)
    times = facts[:, 3:4] * 32.0 + facts[:, 4:5]
    angle = times * freq_ref[0:1, :WIDE]
    first = lanes_of(angle.shape) % HEAD_DIM < HALF
    cosine = jnp.cos(angle)
    sine = jnp.sin(angle)
    sine = jnp.where(first, -sine, sine)
    return jnp.concatenate([cosine, cosine], 1), jnp.concatenate([sine, sine], 1)


def project_kernel(core_ref, *refs):
    pieces_in = refs[:RING]
    w_ref, freq_ref, mine_ref, send_ref, raw_ref, facts_ref = refs[RING:]
    low = core_ref[0] == 0
    for r in range(RING):
        block = slice(r * ROWS, (r + 1) * ROWS)
        rows = pieces_in[r][:, :D]
        facts = pieces_in[r][:, D:]
        facts_ref[block] = facts
        cosine, sine = angles_of(facts, freq_ref)
        for kind in range(3):
            value = mm(rows, w_ref[kind])
            if kind < 2:
                raw_ref[kind, block] = value
                unit = value * lax.rsqrt(head_sums(value * value) * (1.0 / HEAD_DIM) + EPS)
                value = unit * freq_ref[1 + kind : 2 + kind, :]
                value = value * cosine + partner(value) * sine
            if kind == 0:
                value = value * (HEAD_DIM ** (-0.5) * LOG2E)
            left, right = value[:, :WIDE], value[:, WIDE:]
            mine_ref[kind, block] = jnp.where(low, left, right).astype(BF16)
            send_ref[kind, block] = jnp.where(low, right, left).astype(BF16)


def project(core, rows, attn_w, freq):
    low = jax.ShapeDtypeStruct((3, PLANE, WIDE), BF16)
    whole = pl.BlockSpec(memory_space=pltpu.VMEM)
    return pl.pallas_call(
        project_kernel,
        in_specs=[pl.BlockSpec(memory_space=pltpu.SMEM)] + [whole] * (RING + 2),
        out_shape=[
            low,
            low,
            jax.ShapeDtypeStruct((2, PLANE, 2 * WIDE), F32),
            jax.ShapeDtypeStruct((PLANE, WIDE), BF16),
        ],
        compiler_params=pltpu.CompilerParams(vmem_limit_bytes=48 * 2**20),
        cost_estimate=pl.CostEstimate(
            flops=8 * PLANE * D * 2 * WIDE, bytes_accessed=PLANE * D * 8, transcendentals=PLANE * 1024
        ),
    )(core, *rows, attn_w, freq)


def unproject_kernel(core_ref, mine_ref, got_ref, raw_ref, facts_ref, w_ref, freq_ref, dp_ref, gain_ref, *part_refs):
    low = core_ref[0] == 0
    gains = [0.0, 0.0]
    for r in range(RING):
        block = slice(r * ROWS, (r + 1) * ROWS)
        cosine, sine = angles_of(facts_ref[block], freq_ref)
        total = None
        for kind in range(3):
            mine, got = mine_ref[kind, block], got_ref[kind, block]
            grad = jnp.concatenate([jnp.where(low, mine, got), jnp.where(low, got, mine)], 1)
            if kind < 2:
                grad = grad.astype(F32)
                if kind == 0:
                    grad = grad * (HEAD_DIM ** (-0.5))
                raw = raw_ref[kind, block]
                inv = lax.rsqrt(head_sums(raw * raw) * (1.0 / HEAD_DIM) + EPS)
                unit = raw * inv
                grad = grad * cosine - partner(grad) * sine
                gains[kind] += jnp.sum(grad * unit, axis=0, keepdims=True)
                scaled = grad * freq_ref[1 + kind : 2 + kind, :]
                mean = head_sums(scaled * unit) * (1.0 / HEAD_DIM)
                grad = (inv * (scaled - unit * mean)).astype(BF16)
            dp_ref[kind, block] = grad
            part = mm(grad, w_ref[kind], NT)
            total = part if total is None else total + part
        part_refs[r][...] = total.astype(BF16)
    gain_ref[...] = jnp.zeros_like(gain_ref)
    gain_ref[0:1, :] = gains[0]
    gain_ref[1:2, :] = gains[1]


def unproject(core, mine, got, raw, facts, attn_w, freq):
    three = pl.BlockSpec((3, D, 2 * WIDE), lambda i: (0, 0, 0))

    def whole(v):
        return pl.BlockSpec(v.shape, lambda i: (0,) * v.ndim)

    shapes = [
        jax.ShapeDtypeStruct((3, PLANE, 2 * WIDE), BF16),
        jax.ShapeDtypeStruct((8, 2 * WIDE), F32),
    ] + [jax.ShapeDtypeStruct((ROWS, D), BF16)] * RING
    return pl.pallas_call(
        unproject_kernel,
        grid=(1,),
        in_specs=[pl.BlockSpec(memory_space=pltpu.SMEM)]
        + [whole(v) for v in (mine, got, raw, facts)]
        + [three, whole(freq)],
        out_specs=[whole(v) for v in shapes],
        out_shape=shapes,
        compiler_params=pltpu.CompilerParams(vmem_limit_bytes=48 * 2**20),
        cost_estimate=pl.CostEstimate(
            flops=8 * PLANE * D * 2 * WIDE, bytes_accessed=PLANE * D * 8, transcendentals=PLANE * 1024
        ),
    )(core, mine, got, raw, facts, attn_w, freq)


LOG_LANE = 3 * VARIATES + SEQS


def with_pieces(base, values, first_lane, lanes):
    for i in range(3):
        part = values.astype(BF16).astype(F32)
        base = jnp.where(lanes == first_lane + i, part, base)
        values = values - part
    return base


def value_lanes(rows):
    return (lanes_of((rows, WIDE)) < 3).astype(BF16)


def attend_kernel(
    at_ref, mine_ref, got_ref, own_ref, other_ref, bias_ref,
    att_ref, near_ref, send_ref, tail_ref, kt_ref, all_scr, qt_scr, *, chunks,
):
    step = pl.program_id(0)
    block = att_ref.shape[0]
    size = GROUP // chunks

    @pl.when(step == 0)
    def _():
        all_scr[:, :PLANE] = mine_ref[...]
        all_scr[:, PLANE:] = got_ref[...]
        lane = lanes_of((ROWS, WIDE))
        tail_lane = lane % HEAD_DIM
        bias_lane = tail_lane < 3 * VARIATES
        seg_lane = (tail_lane >= 3 * VARIATES) & (tail_lane < LOG_LANE)
        one_lane = (tail_lane >= LOG_LANE) & (tail_lane < LOG_LANE + 3)
        row = lax.broadcasted_iota(jnp.int32, (ROWS, WIDE), 0)
        for b in range(2 * RING):
            source = own_ref if b < RING else other_ref
            facts = source[(b % RING) * ROWS : (b % RING + 1) * ROWS, :].astype(F32)
            variate = facts[:, 2:3]
            equal = bias_lane & ((tail_lane % VARIATES).astype(F32) == variate)
            position = at_ref[b] + row
            segment = jnp.zeros_like(row)
            for j in range(SEQS):
                segment += (position >= at_ref[2 * RING + j]).astype(jnp.int32)
            inside = seg_lane & (tail_lane - 3 * VARIATES == segment)
            rows = slice(b * ROWS, (b + 1) * ROWS)
            qt_scr[rows] = (equal | inside).astype(BF16)
            tail = jnp.where(equal, bias_ref[0:1, :], bias_ref[1:2, :])
            tail = jnp.where(bias_lane, tail, jnp.where(one_lane, 1.0, 0.0))
            tail = jnp.where(seg_lane & ~inside, FAR, tail)
            kt_ref[rows] = tail.astype(BF16)

    here = pl.ds(pl.multiple_of(step * block, block), block)
    query_tail = qt_scr[here, :]
    query = jnp.concatenate([all_scr[0, here, :], query_tail], 1)
    zero = jnp.zeros_like(query)
    head_of = (lanes_of(query.shape) // HEAD_DIM) % 2
    lanes = lanes_of((block, WIDE))
    ones = value_lanes(size)
    out = None
    tail = query_tail.astype(F32)
    for head in range(2):
        masked = jnp.where(head_of == head, query, zero)
        total = None
        for c in range(chunks):
            rows = slice(c * size, (c + 1) * size)
            keys = jnp.concatenate([all_scr[1, rows, :], kt_ref[rows, :]], 1)
            values = jnp.concatenate([all_scr[2, rows, :], ones], 1)
            prob = jnp.exp2(mm(masked, keys, NT)).astype(BF16)
            part = mm(prob, values)
            total = part if total is None else total + part
        row_sum = total[:, WIDE : WIDE + 1]
        now = total[:, :WIDE] / row_sum
        out = now if head == 0 else jnp.where(lanes < HEAD_DIM, out, now)
        tail = with_pieces(tail, -jnp.log2(row_sum), head * HEAD_DIM + LOG_LANE, lanes)
    att_ref[...] = out
    tail_ref[...] = tail.astype(BF16)
    low = out.astype(BF16)
    half = pl.num_programs(0) // 2

    @pl.when(step < half)
    def _():
        near_ref[here, :] = low

    @pl.when(step >= half)
    def _():
        send_ref[pl.ds(pl.multiple_of((step - half) * block, block), block), :] = low


def attend(at, mine, got, facts, facts_other, bias_rows):
    block = 512
    moving = pl.BlockSpec((block, WIDE), lambda i: (i, 0))
    plane = pl.BlockSpec((PLANE, WIDE), lambda i: (0, 0))
    three = pl.BlockSpec((3, PLANE, WIDE), lambda i: (0, 0, 0))
    low = jax.ShapeDtypeStruct((GROUP, WIDE), BF16)
    low_plane = jax.ShapeDtypeStruct((PLANE, WIDE), BF16)
    return pl.pallas_call(
        functools.partial(attend_kernel, chunks=4),
        grid=(GROUP // block,),
        in_specs=[
            pl.BlockSpec(memory_space=pltpu.SMEM),
            three,
            three,
            plane,
            plane,
            pl.BlockSpec((8, WIDE), lambda i: (0, 0)),
        ],
        out_specs=[moving, plane, plane, moving, pl.BlockSpec((GROUP, WIDE), lambda i: (0, 0))],
        out_shape=[jax.ShapeDtypeStruct((GROUP, WIDE), F32), low_plane, low_plane, low, low],
        scratch_shapes=[pltpu.VMEM((3, GROUP, WIDE), BF16), pltpu.VMEM((GROUP, WIDE), BF16)],
        compiler_params=pltpu.CompilerParams(vmem_limit_bytes=48 * 2**20),
        cost_estimate=pl.CostEstimate(
            flops=16 * GROUP * GROUP * WIDE, bytes_accessed=GROUP * WIDE * 24,
            transcendentals=2 * GROUP * GROUP,
        ),
    )(at, mine, got, facts, facts_other, bias_rows)


def attend_back_kernel(
    mine_ref, got_ref, qt_ref, kt_ref, hot_ref, near_ref, other_ref, att_ref,
    keep_ref, send_ref, bias_ref, all_scr, grad_scr, dk_sum, dv_sum, *, chunks,
):
    size = GROUP // chunks
    step = pl.program_id(0)
    block = qt_ref.shape[0]

    @pl.when(step == 0)
    def _():
        all_scr[:, :PLANE] = mine_ref[...]
        all_scr[:, PLANE:] = got_ref[...]
        grad_scr[:PLANE] = near_ref[...]
        grad_scr[PLANE:] = other_ref[...]
        dk_sum[...] = jnp.zeros_like(dk_sum)
        dv_sum[...] = jnp.zeros_like(dv_sum)

    here = pl.ds(pl.multiple_of(step * block, block), block)
    query = jnp.concatenate([all_scr[0, here, :], qt_ref[...]], 1)
    grad = grad_scr[here, :]
    zero = jnp.zeros_like(query)
    head_of = (lanes_of(query.shape) // HEAD_DIM) % 2
    lanes = lanes_of((block, WIDE))
    overlap = grad.astype(F32) * att_ref[...]
    ones = value_lanes(size)
    out = None
    for head in range(2):
        mine = head_of[:, :WIDE] == head
        masked = jnp.where(head_of == head, query, zero)
        grad_here = jnp.where(mine, grad, zero[:, :WIDE])
        dots = jnp.sum(jnp.where(mine, overlap, 0.0), axis=1, keepdims=True)
        extra = with_pieces(jnp.zeros(lanes.shape, F32), -dots, 0, lanes).astype(BF16)
        grad_wide = jnp.concatenate([grad_here, extra], 1)
        total = None
        for c in range(chunks):
            rows = slice(c * size, (c + 1) * size)
            keys = all_scr[1, rows, :]
            prob = jnp.exp2(mm(jnp.concatenate([keys, kt_ref[rows, :]], 1), masked, NT))
            slope = mm(jnp.concatenate([all_scr[2, rows, :], ones], 1), grad_wide, NT)
            d_score = (prob * slope).astype(BF16)
            dv_sum[rows, :] += mm(prob.astype(BF16), grad_here)
            dk_sum[rows, :] += mm(d_score, masked)
            part = mm(d_score, keys, TN)
            total = part if total is None else total + part
        out = total if head == 0 else jnp.where(lanes < HEAD_DIM, out, total)
    low = out.astype(BF16)
    half = pl.num_programs(0) // 2

    @pl.when(step < half)
    def _():
        keep_ref[0, here, :] = low

    @pl.when(step >= half)
    def _():
        send_ref[0, pl.ds(pl.multiple_of((step - half) * block, block), block), :] = low

    @pl.when(step == pl.num_programs(0) - 1)
    def _():
        for ref, rows in ((keep_ref, slice(0, PLANE)), (send_ref, slice(PLANE, GROUP))):
            ref[1] = (dk_sum[rows, :WIDE] * (1.0 / LOG2E)).astype(BF16)
            ref[2] = dv_sum[rows, :].astype(BF16)
        counts = dk_sum[:, WIDE:]
        bias_ref[...] = jnp.zeros_like(bias_ref)
        bias_ref[0:1, :] = jnp.sum(counts * hot_ref[...].astype(F32), axis=0, keepdims=True)
        bias_ref[1:2, :] = jnp.sum(counts, axis=0, keepdims=True)


def attend_back(mine, got, query_tail, key_tail, near, other, attended):
    block = 512
    moving = pl.BlockSpec((block, WIDE), lambda i: (i, 0))
    fixed = pl.BlockSpec((GROUP, WIDE), lambda i: (0, 0))
    plane = pl.BlockSpec((PLANE, WIDE), lambda i: (0, 0))
    three = pl.BlockSpec((3, PLANE, WIDE), lambda i: (0, 0, 0))
    low = jax.ShapeDtypeStruct((3, PLANE, WIDE), BF16)
    return pl.pallas_call(
        functools.partial(attend_back_kernel, chunks=4),
        grid=(GROUP // block,),
        in_specs=[three, three, moving, fixed, fixed, plane, plane, moving],
        out_specs=[three, three, pl.BlockSpec((8, WIDE), lambda i: (0, 0))],
        out_shape=[low, low, jax.ShapeDtypeStruct((8, WIDE), F32)],
        scratch_shapes=[
            pltpu.VMEM((3, GROUP, WIDE), BF16),
            pltpu.VMEM((GROUP, WIDE), BF16),
            pltpu.VMEM((GROUP, 2 * WIDE), F32),
            pltpu.VMEM((GROUP, WIDE), F32),
        ],
        compiler_params=pltpu.CompilerParams(vmem_limit_bytes=48 * 2**20),
        cost_estimate=pl.CostEstimate(
            flops=40 * GROUP * GROUP * WIDE, bytes_accessed=GROUP * WIDE * 24,
            transcendentals=2 * GROUP * GROUP,
        ),
    )(mine, got, query_tail, key_tail, query_tail, near, other, attended)


def feed_kernel(b_ref, g_ref, w_ref, y_ref, db_ref, act_ref, *, cuts):
    rows, grads = b_ref[...], g_ref[...]
    size = w_ref.shape[2] // cuts

    def products(j):
        cols = slice(j * size, (j + 1) * size)
        return mm(rows, w_ref[0, :, cols]), mm(rows, w_ref[1, :, cols]), mm(grads, w_ref[2, :, cols])

    y_sum, db_sum = None, None
    ready = products(0)
    for j in range(cuts):
        gate, up, d_hidden = ready
        if j + 1 < cuts:
            ready = products(j + 1)
        cols = slice(j * size, (j + 1) * size)
        sig = 0.5 + 0.5 * jnp.tanh(0.5 * gate)
        silu = gate * sig
        hidden = (silu * up).astype(BF16)
        d_gate = (d_hidden * up * (sig + silu * (1.0 - sig))).astype(BF16)
        d_up = (d_hidden * silu).astype(BF16)
        act_ref[0, :, cols] = d_gate
        act_ref[1, :, cols] = d_up
        act_ref[2, :, cols] = hidden
        y_part = mm(hidden, w_ref[2, :, cols], NT)
        db_part = mm(d_gate, w_ref[0, :, cols], NT) + mm(d_up, w_ref[1, :, cols], NT)
        y_sum = y_part if y_sum is None else y_sum + y_part
        db_sum = db_part if db_sum is None else db_sum + db_part
    y_ref[...] = y_sum.astype(BF16)
    db_ref[...] = db_sum.astype(BF16)


def feed(rows_b, rows_g, weights):
    rows = rows_b.shape[0]
    width = weights.shape[2]
    low_d = jax.ShapeDtypeStruct((rows, D), BF16)
    low_f = jax.ShapeDtypeStruct((3, rows, width), BF16)
    return pl.pallas_call(
        functools.partial(feed_kernel, cuts=2),
        out_shape=[low_d, low_d, low_f],
        compiler_params=pltpu.CompilerParams(vmem_limit_bytes=26 * 2**20),
        cost_estimate=pl.CostEstimate(
            flops=12 * rows * D * width, bytes_accessed=6 * D * width + rows * D * 8 + rows * width * 6,
            transcendentals=rows * width,
        ),
    )(rows_b, rows_g, weights)


def body(
    tokens,
    cotangent,
    destination,
    variate_ids,
    time_ids,
    seq_lengths,
    qkv_weight,
    out_weight,
    gate_up_weight,
    down_weight,
    norm_gains,
    qk_gains,
    variate_bias,
):
    core = lax.axis_index("core")
    low_core = core == 0
    y_at = lax.axis_index("y")
    zl_at = lax.axis_index("zl")

    core_scalar = core.reshape(1).astype(jnp.int32)

    def side_by_side(mine, other):
        return jnp.concatenate(
            [jnp.where(low_core, mine, other), jnp.where(low_core, other, mine)], axis=-1
        )

    feed_shard = jnp.concatenate([gate_up_weight, down_weight.T[None]], 0)

    slot = destination % ROWS
    group_at = destination // GROUP
    block_at = (destination % GROUP) // ROWS
    device_at = ((group_at // 2) * 2 + block_at // 4) * 8 + (block_at % 4) * 2 + group_at % 2
    key = device_at * ROWS + slot
    zero = jnp.zeros_like(slot)
    facts = jnp.stack([key, slot, variate_ids, time_ids // 32, time_ids % 32, zero, zero, zero])
    gains_row = jnp.pad(
        norm_gains.reshape(8, 16), ((0, 0), (GAIN_LANE, WIDE - GAIN_LANE - 16))
    ).astype(F32)
    outgoing, deal = deal_rows(tokens, cotangent, facts.astype(F32), gains_row)
    arrived = lax.all_to_all(outgoing.reshape(DEVICES, 8, SPAN), ALL, 0, 0, tiled=True)
    out_shard, outgoing = lax.optimization_barrier((out_weight.T, outgoing))
    attn_shard = jnp.concatenate([qkv_weight, jnp.stack(gather_direct(out_shard))], 0)
    attn_mine = gather_round(attn_shard, ("zh", "zl"), lax.axis_index("zh") * 2 + zl_at)
    attn_mine, arrived = lax.optimization_barrier((attn_mine, arrived))
    attn_mine = jnp.stack(gather_ahead(attn_mine, "x")).reshape((16,) + attn_shard.shape)

    lengths_other = swap_core(seq_lengths)
    lengths = jnp.where(zl_at == core, seq_lengths, lengths_other)[0]
    bias_other = lax.ppermute(variate_bias, "zl", [(0, 1), (1, 0)])
    bias_pair = jnp.where(zl_at == core, variate_bias, bias_other)

    arrived, lengths, bias_pair = lax.optimization_barrier((arrived, lengths, bias_pair))
    all_gains = arrived.reshape(16, 8, 8, SPAN)[:, 0, :, PAIR + GAIN_LANE : PAIR + GAIN_LANE + 16]
    inputs, grad_rows, attn_in, place, gains = receive(
        arrived.reshape(4 * ROWS, SPAN), all_gains.reshape(16, WIDE)
    )
    feed_shard, attn_in = lax.optimization_barrier((feed_shard, attn_in))
    feed_mine = flat_gather(feed_shard)
    zero_at = jnp.zeros((1,), jnp.int32)
    x_at = lax.axis_index("x").reshape(1).astype(jnp.int32)
    ahead, behind = ring(attn_in, -1), ring(attn_in, 1)
    far_top, far_low = ring(ahead[: ROWS // 2], -1), ring(behind[ROWS // 2 :], 1)
    far_top, far_low, attn_mine = lax.optimization_barrier((far_top, far_low, attn_mine))
    attn_w = assemble(core_scalar, x_at, attn_mine, swap_core(attn_mine))
    attn_all = [attn_in, ahead, jnp.concatenate([far_top, far_low], 0), behind]
    grad_rows, attn_all = lax.optimization_barrier((grad_rows, attn_all))
    grad_all = gather_direct(grad_rows)

    blocks_y = (y_at + jnp.arange(RING)) % RING
    blocks = jnp.concatenate([core * RING + blocks_y, (1 - core) * RING + blocks_y])
    at = jnp.concatenate([blocks * ROWS, jnp.cumsum(lengths)]).astype(jnp.int32)

    inverse = THETA ** (-2.0 * jnp.arange(HALF).astype(F32) / HEAD_DIM)
    freq = jnp.concatenate(
        [
            jnp.tile(inverse, 8)[None],
            jnp.tile(qk_gains, (1, 4)),
            jnp.zeros((5, 2 * WIDE), F32),
        ]
    )
    qkv_mine, qkv_send, raw, facts_all = project(core_scalar, attn_all, attn_w, freq)
    facts_other = swap_core(facts_all)
    qkv_got = swap_core(qkv_send)

    bias_parts = jnp.stack(pieces(bias_pair * LOG2E, 3)).astype(F32)
    bias_rows = jnp.repeat(bias_parts, VARIATES, axis=0).transpose(1, 2, 0)
    bias_rows = jnp.pad(bias_rows, ((0, 0), (0, 0), (0, HEAD_DIM - 3 * VARIATES))).reshape(2, WIDE)
    bias_rows = jnp.pad(bias_rows, ((0, 6), (0, 0)))
    attended, att_near, att_send, query_back, key_tail = attend(
        at, qkv_mine, qkv_got, facts_all, facts_other, bias_rows
    )
    att_other = swap_core(att_send)
    att_other, grad_all = lax.optimization_barrier((att_other, grad_all))
    att_plane = side_by_side(att_near, att_other).reshape(RING, ROWS, 2 * WIDE)
    att_rows = trade_ring([att_plane[r] for r in range(RING)])
    att_rows, feed_mine = lax.optimization_barrier((att_rows, feed_mine))
    feed_w = assemble(core_scalar, zero_at, feed_mine, swap_core(feed_mine))
    hidden_one, feed_in = out_project(att_rows, attn_w, inputs, gains)

    ahead, behind = ring(feed_in, -1), ring(feed_in, 1)
    fed_own = feed(feed_in, grad_all[0], feed_w)
    ahead, behind, fed_own = lax.optimization_barrier((ahead, behind, fed_own))
    far_top, far_low = ring(ahead[: ROWS // 2], -1), ring(behind[ROWS // 2 :], 1)
    fed_ahead = feed(ahead, grad_all[1], feed_w)
    fed_behind = feed(behind, grad_all[3], feed_w)
    far_top, far_low, fed_ahead, fed_behind = lax.optimization_barrier(
        (far_top, far_low, fed_ahead, fed_behind)
    )
    far = jnp.concatenate([far_top, far_low], 0)
    fed_far = feed(far, grad_all[2], feed_w)
    feed_all = [feed_in, ahead, far, behind]
    fed = [fed_own, fed_ahead, fed_far, fed_behind]
    feed_split = weight_grads(core_scalar, feed_all, grad_all, [f[2] for f in fed], 2, 2)
    db_got = send_ring([f[1] for f in fed], True)
    db_got, feed_split = lax.optimization_barrier((db_got, feed_split))
    grad_one, gain_two_grad, d_att, *both = middle(
        att_rows, attn_w, [f[0] for f in fed], fed_own[1], db_got, hidden_one, grad_rows, gains
    )
    feed_total = chip_total(feed_split)
    feed_got = trade(feed_total, "x")

    grad_att = trade_ring([d_att[r] for r in range(RING)])
    grad_att[1], feed_total = lax.optimization_barrier((grad_att[1], feed_total))
    grad_att = jnp.concatenate(grad_att, 0)
    both, grad_att = lax.optimization_barrier((both, grad_att))
    both_got = send_ring(both)
    grad_left, grad_right = grad_att[:, :WIDE], grad_att[:, WIDE:]
    grad_other = swap_core(jnp.where(low_core, grad_right, grad_left))
    grad_near = jnp.where(low_core, grad_left, grad_right)
    d_keep, d_send, bias_sums = attend_back(
        qkv_mine, qkv_got, query_back, key_tail, grad_near, grad_other, attended
    )
    first_part = (jnp.arange(HEAD_DIM) < VARIATES)[None, None]
    bias_sums = jnp.where(first_part, bias_sums[:2].reshape(2, 2, HEAD_DIM), 0.0)
    bias_sums = jnp.sum(bias_sums, axis=2)
    bias_part = jnp.stack([bias_sums[0], bias_sums[1] - bias_sums[0]])
    d_got = swap_core(d_send)
    grad_proj, qk_sums, *in_part = unproject(
        core_scalar, d_keep, d_got, raw, facts_all, attn_w, freq
    )
    in_got = send_ring(in_part)
    feed_half = added(feed_got).astype(BF16)
    in_got[0], feed_half = lax.optimization_barrier((in_got[0], feed_half))
    grad_proj, both_got = lax.optimization_barrier((grad_proj, both_got))
    both_sum = add_ring(both[0], both_got)
    mixed = (hidden_one + both_sum[:ROWS]).astype(BF16)
    out_full = both_sum[ROWS:].astype(BF16)
    attn_split = weight_grads(core_scalar, attn_all, [out_full], [grad_proj], None, 1)
    attn_total = chip_total(attn_split)
    in_got, _ = lax.optimization_barrier((in_got, attn_split))
    mixed, _ = lax.optimization_barrier((mixed, attn_total))
    feed_got = trade(feed_half, ("zh", "zl"))
    attn_own, attn_got = send_round(attn_total.reshape((RING, RING) + attn_total.shape[1:]), "x")
    qk_sums = jnp.sum(qk_sums[:2].reshape(2, 4, HEAD_DIM), axis=1)

    small = jnp.zeros((8, WIDE), F32).at[0].set(qk_sums.reshape(WIDE))
    small = small.at[1, :4].set(bias_part.reshape(4))
    tensor_at = (y_at * 2 + core).reshape(1).astype(jnp.int32)
    last = finish(
        in_part[0], in_got, inputs, grad_one, mixed, place, gains, gain_two_grad, small, tensor_at
    )
    last = last.reshape(DEVICES, 8, 2 * QUARTER + WIDE)
    last, attn_got, feed_got = lax.optimization_barrier((last, attn_got, feed_got))
    home = lax.all_to_all(last, ALL, 0, 0, tiled=True)
    own, got = send_round(add_round(attn_own, attn_got).astype(BF16), ("zh", "zl"))
    home, got = lax.optimization_barrier((home, got))
    attn_grad = add_round(own, got)
    feed_grad = added(feed_got).reshape(3, 64, 512)
    new_tokens, token_grads, sums = settle(home.reshape(4 * ROWS, 2 * QUARTER + WIDE), deal)
    gains_grad = sums[0].reshape(2, 64)
    qk_grad = sums[1].reshape(2, 64)
    bias_grad = sums[2, :4].reshape(2, 2)

    return (
        new_tokens,
        token_grads,
        attn_grad[:3],
        attn_grad[3].T,
        feed_grad[:2],
        feed_grad[2].T,
        gains_grad,
        qk_grad,
        bias_grad,
    )


def solution(mesh):
    fine = Mesh(mesh.devices.reshape(4, 2, 2, 4, 2), ALL)
    dp = ("x", "zh", "core")
    tensor = ("y", "zl")
    in_specs = (
        P(ALL, None),
        P(ALL, None),
        P(ALL),
        P(ALL),
        P(ALL),
        P(dp, None),
        P(None, dp, tensor),
        P(tensor, dp),
        P(None, dp, tensor),
        P(tensor, dp),
        P(None, dp),
        P(),
        P(None, tensor),
    )
    out_specs = (
        P(ALL, None),
        P(ALL, None),
        P(None, dp, tensor),
        P(tensor, dp),
        P(None, dp, tensor),
        P(tensor, dp),
        P(None, dp),
        P(),
        P(None, tensor),
    )
    return jax.shard_map(body, mesh=fine, in_specs=in_specs, out_specs=out_specs, check_vma=False)
```

```python
import functools

import jax
import jax.numpy as jnp
from jax import lax
from jax.experimental import pallas as pl
from jax.experimental.pallas import tpu as pltpu
from jax.sharding import Mesh
from jax.sharding import PartitionSpec as P

HEADS = 16
HEAD_DIM = 64
HALF = HEAD_DIM // 2
D = 1024
FF = 4096
ROWS = 256
RING = 4
PLANE = ROWS * RING
GROUP = 2 * PLANE
DEVICES = 128
VARIATES = 8
SEQS = 4
WIDE = 128
EPS = 1e-06
THETA = 10000.0
LOG2E = 1.4426950408889634
FAR = -16384.0
F32 = jnp.float32
BF16 = jnp.bfloat16

ALL = ("x", "zh", "core", "y", "zl")
FLAT = ("x", "zh", "zl")
NT = (((1,), (1,)), ((), ()))
TN = (((0,), (0,)), ((), ()))


def mm(left, right, dims=(((1,), (0,)), ((), ()))):
    return lax.dot_general(left, right, dims, preferred_element_type=F32)


def root_stats(values):
    return lax.rsqrt(jnp.mean(values * values, axis=-1, keepdims=True) + EPS)


def norm_back(grad_in, normed, scale_inv):
    return scale_inv * (grad_in - normed * jnp.mean(grad_in * normed, axis=-1, keepdims=True))


def pieces(values, count):
    out = []
    for _ in range(count):
        part = lax.reduce_precision(values, 8, 7)
        out.append(part.astype(BF16))
        values = values - part
    return out


def ring(values, step):
    return lax.ppermute(values, "y", [(i, (i + step) % RING) for i in range(RING)])


def swap_core(values):
    return lax.ppermute(values, "core", [(0, 1), (1, 0)])


def gather_ring(values):
    ahead = ring(values, -1)
    behind = ring(values, 1)
    half = values.shape[0] // 2
    far_top = ring(ahead[:half], -1)
    far_low = ring(behind[half:], 1)
    return [values, ahead, jnp.concatenate([far_top, far_low], 0), behind]


def gather_direct(values):
    return [values, ring(values, -1), ring(values, 2), ring(values, 1)]


def trade_ring(parts):
    return [parts[0]] + [ring(parts[RING - s], -s) for s in range(1, RING)]


def send_ring(parts, halves=False):
    half = parts[2].shape[0] // 2
    far = [parts[2][:half], parts[2][half:]] if halves else [parts[2]]
    return [ring(parts[1], 1), ring(parts[3], -1)] + [ring(v, 2) for v in far]


def add_ring(own, got):
    far = got[2] if len(got) == 3 else jnp.concatenate(got[2:], 0)
    return own.astype(F32) + got[0].astype(F32) + got[1].astype(F32) + far.astype(F32)


def gather_ahead(values, axes):
    moves = [[((i + r) % RING, i) for i in range(RING)] for r in range(RING)]
    return [values] + [lax.ppermute(values, axes, moves[r]) for r in range(1, RING)]


def gather_round(values, axes, at):
    return jnp.roll(jnp.stack(gather_ahead(values, axes)), at, axis=0)


def flat_gather(shard):
    many = jnp.broadcast_to(shard[None], (16,) + shard.shape)
    return lax.all_to_all(many, FLAT, 0, 0, tiled=True)


def assemble_kernel(at_ref, mine_ref, other_ref, out_ref):
    core = at_ref[0]
    count, _, depth, width = mine_ref.shape
    for ref, side in ((mine_ref, core), (other_ref, 1 - core)):
        for i in range(count):
            at = (i // 2) * 2 * depth + side * depth
            rows = pl.ds(pl.multiple_of(at, depth), depth)
            out_ref[:, rows, (i % 2) * width : (i % 2 + 1) * width] = ref[i]


def assemble(core, x_at, mine, other):
    _, kinds, depth, width = mine.shape
    pair = pl.BlockSpec((4, kinds, depth, width), lambda p, at: (p, 0, 0, 0))
    return pl.pallas_call(
        assemble_kernel,
        grid_spec=pltpu.PrefetchScalarGridSpec(
            num_scalar_prefetch=1,
            grid=(RING,),
            in_specs=[pair, pair],
            out_specs=pl.BlockSpec(
                (kinds, 4 * depth, 2 * width), lambda p, at: (0, lax.rem(at[1] + p, RING), 0)
            ),
        ),
        out_shape=jax.ShapeDtypeStruct((kinds, 16 * depth, 2 * width), BF16),
        compiler_params=pltpu.CompilerParams(vmem_limit_bytes=28 * 2**20),
        cost_estimate=pl.CostEstimate(
            flops=0, bytes_accessed=kinds * 128 * depth * width, transcendentals=0
        ),
    )(jnp.concatenate([core, x_at]), mine, other)


def chip_total(split):
    return (split[0].astype(F32) + swap_core(split[1]).astype(F32)).astype(BF16)


def send_round(values, axes):
    at = lax.axis_index(axes)
    parts = [lax.dynamic_index_in_dim(values, (at + r) % RING, 0, keepdims=False) for r in range(RING)]
    moves = [[(i, (i + r) % RING) for i in range(RING)] for r in range(RING)]
    return parts[0], [lax.ppermute(parts[r], axes, moves[r]) for r in (1, 3, 2)]


def add_round(own, got):
    return sum((v.astype(F32) for v in got), own.astype(F32))


def trade(values, axes):
    return lax.all_to_all(values.reshape((RING, -1) + values.shape[1:]), axes, 0, 0, tiled=True)


def added(got):
    return jnp.sum(got.astype(F32), axis=0)


def lanes_of(shape):
    return lax.broadcasted_iota(jnp.int32, shape, 1)


QUARTER = D // RING
PAIR = 2 * QUARTER
SPAN = PAIR + WIDE
GAIN_LANE = 16


def deal_kernel(tok_ref, cot_ref, facts_ref, gains_ref, out_ref, deal_ref):
    wide = jnp.concatenate([facts_ref[...], jnp.zeros((WIDE - 8, ROWS), F32)], 0)
    facts = jnp.transpose(wide)
    keys = facts_ref[0:1, :]
    rank = jnp.sum((facts[:, 0:1] < keys).astype(F32), axis=0, keepdims=True)
    at = lax.broadcasted_iota(jnp.int32, (ROWS, ROWS), 0).astype(F32)
    deal_ref[...] = (at == rank).astype(BF16)
    low = jnp.where(lanes_of(facts.shape) == 0, 0.0, facts).astype(BF16)
    row = lax.broadcasted_iota(jnp.int32, (4 * ROWS, 1), 0)
    own = ((row // RING).astype(F32) == rank).astype(BF16)
    part = None
    for m in range(RING):
        cols = slice(m * QUARTER, (m + 1) * QUARTER)
        here = mm(own, jnp.concatenate([tok_ref[:, cols], cot_ref[:, cols]], 1))
        part = here if m == 0 else jnp.where(row % RING == m, here, part)
    out_ref[:, :PAIR] = part.astype(BF16)
    tail = mm(own, low)
    lane = lanes_of(tail.shape)
    gains = jnp.broadcast_to(gains_ref[...][None], (DEVICES, 8, WIDE)).reshape(tail.shape)
    tail = jnp.where((lane >= GAIN_LANE) & (lane < GAIN_LANE + 16), gains, tail)
    out_ref[:, PAIR:] = tail.astype(BF16)


def deal_rows(tokens, cotangent, facts, gains):
    return pl.pallas_call(
        deal_kernel,
        out_shape=[
            jax.ShapeDtypeStruct((4 * ROWS, SPAN), BF16),
            jax.ShapeDtypeStruct((ROWS, ROWS), BF16),
        ],
        compiler_params=pltpu.CompilerParams(vmem_limit_bytes=48 * 2**20),
        cost_estimate=pl.CostEstimate(
            flops=8 * ROWS * ROWS * 2304, bytes_accessed=ROWS * D * 16, transcendentals=0
        ),
    )(tokens, cotangent, facts, gains)


def receive_kernel(rows_ref, gains_ref, x_ref, g_ref, a_ref, place_ref, gain_ref):
    count = 4 * ROWS
    facts = rows_ref[:, PAIR:]
    slots = jnp.transpose(facts.astype(F32))[1:2, :]
    at = lax.broadcasted_iota(jnp.int32, (ROWS, count), 0)
    arrival = lanes_of((ROWS, count))
    here = at.astype(F32) == slots
    gains = gains_ref[...].astype(F32)
    turned = pltpu.roll(gains, HEAD_DIM, 1)
    left = lanes_of((1, WIDE)) < HEAD_DIM
    one, two = [], []
    for c in range(D // WIDE):
        even, odd = slice(2 * c, 2 * c + 1), slice(2 * c + 1, 2 * c + 2)
        one.append(jnp.where(left, gains[even], turned[odd]))
        two.append(jnp.where(left, turned[even], gains[odd]))
    gain_one = jnp.concatenate(one, 1)
    gain_ref[...] = jnp.zeros_like(gain_ref)
    gain_ref[0:1, :] = gain_one
    gain_ref[1:2, :] = jnp.concatenate(two, 1)
    quarters = []
    for m in range(RING):
        chosen = (here & (arrival % RING == m)).astype(BF16)
        both = mm(chosen, rows_ref[:, :PAIR])
        quarters.append(both[:, :QUARTER])
        g_ref[:, m * QUARTER : (m + 1) * QUARTER] = both[:, QUARTER:].astype(BF16)
        if m == 0:
            a_ref[:, D:] = mm(chosen, facts).astype(BF16)
            pick = (at * RING == arrival).astype(BF16)
            place_ref[...] = mm(chosen, pick, NT).astype(BF16)
    rows = jnp.concatenate(quarters, 1)
    x_ref[...] = rows
    a_ref[:, :D] = (rows * root_stats(rows) * gain_one).astype(BF16)


def receive(rows, gains):
    return pl.pallas_call(
        receive_kernel,
        out_shape=[
            jax.ShapeDtypeStruct((ROWS, D), F32),
            jax.ShapeDtypeStruct((ROWS, D), BF16),
            jax.ShapeDtypeStruct((ROWS, D + WIDE), BF16),
            jax.ShapeDtypeStruct((ROWS, ROWS), BF16),
            jax.ShapeDtypeStruct((8, D), F32),
        ],
        compiler_params=pltpu.CompilerParams(vmem_limit_bytes=48 * 2**20),
        cost_estimate=pl.CostEstimate(
            flops=16 * ROWS * ROWS * D, bytes_accessed=ROWS * D * 24, transcendentals=0
        ),
    )(rows, gains)


def out_kernel(*refs):
    att = refs[:RING]
    w_ref, x_ref, gain_ref, h_ref, b_ref = refs[RING:]
    hidden = x_ref[...]
    for r in range(RING):
        hidden = hidden + mm(att[r][...], w_ref[r], NT)
    h_ref[...] = hidden
    b_ref[...] = (hidden * root_stats(hidden) * gain_ref[1:2, :]).astype(BF16)


def out_project(att, weights, rows, gains):
    return pl.pallas_call(
        out_kernel,
        out_shape=[jax.ShapeDtypeStruct((ROWS, D), F32), jax.ShapeDtypeStruct((ROWS, D), BF16)],
        compiler_params=pltpu.CompilerParams(vmem_limit_bytes=48 * 2**20),
        cost_estimate=pl.CostEstimate(
            flops=2 * ROWS * D * D, bytes_accessed=2 * D * D + ROWS * D * 14, transcendentals=0
        ),
    )(*att, weights, rows, gains)


def middle_kernel(*refs):
    att, y_parts, w_ref = refs[:RING], refs[RING : 2 * RING], refs[2 * RING]
    refs = refs[2 * RING + 1 :]
    own_ref, near_ref, back_ref, top_ref, low_ref, h_ref, g_ref, gain_ref = refs[:8]
    grad_ref, two_ref, d_ref = refs[8:11]
    both_refs = refs[11:]
    far = jnp.concatenate([top_ref[...], low_ref[...]], 0).astype(F32)
    grad = own_ref[...].astype(F32) + near_ref[...].astype(F32) + back_ref[...].astype(F32) + far
    hidden = h_ref[...]
    scale = root_stats(hidden)
    normed = hidden * scale
    two_ref[...] = jnp.zeros_like(two_ref)
    two_ref[0:1, :] = jnp.sum(grad * normed, axis=0, keepdims=True)
    scaled = grad * gain_ref[1:2, :]
    grad = g_ref[...].astype(F32) + norm_back(scaled, normed, scale)
    grad_ref[...] = grad
    low = grad.astype(BF16)
    for r in range(RING):
        d_ref[r] = mm(low, w_ref[r]).astype(BF16)
        both_refs[r][:ROWS] = y_parts[r][...]
        both_refs[r][ROWS:] = mm(att[r][...], low, TN).astype(BF16)


def middle(att, weights, y_parts, own, got, hidden, grad_rows, gains):
    both = jax.ShapeDtypeStruct((2 * ROWS, D), BF16)
    return pl.pallas_call(
        middle_kernel,
        out_shape=[
            jax.ShapeDtypeStruct((ROWS, D), F32),
            jax.ShapeDtypeStruct((8, D), F32),
            jax.ShapeDtypeStruct((RING, ROWS, ROWS), BF16),
        ]
        + [both] * RING,
        compiler_params=pltpu.CompilerParams(vmem_limit_bytes=48 * 2**20),
        cost_estimate=pl.CostEstimate(
            flops=4 * ROWS * D * D, bytes_accessed=2 * D * D + ROWS * D * 40, transcendentals=0
        ),
    )(*att, *y_parts, weights, own, *got, hidden, grad_rows, gains)


def finish_kernel(
    own_ref, near_ref, back_ref, far_ref, x_ref, grad_ref, mixed_ref, place_ref,
    gain_ref, two_ref, small_ref, at_ref, out_ref,
):
    rows = x_ref[...]
    scale = root_stats(rows)
    normed = rows * scale
    far = far_ref[...].astype(F32)
    grad = own_ref[...].astype(F32) + near_ref[...].astype(F32) + back_ref[...].astype(F32) + far
    one = jnp.sum(grad * normed, axis=0, keepdims=True)
    two = two_ref[0:1, :]
    scaled = grad * gain_ref[0:1, :]
    back = scale * (scaled - normed * jnp.mean(scaled * normed, axis=1, keepdims=True))
    result = (grad_ref[...] + back).astype(BF16)
    count = 4 * ROWS
    row = lax.broadcasted_iota(jnp.int32, (count, 1), 0)
    quarter = row % RING
    pick = (row // RING == lanes_of((count, ROWS))).astype(BF16)
    pick = mm(pick, place_ref[...], NT).astype(BF16)
    part = None
    for m in range(RING):
        cols = slice(m * QUARTER, (m + 1) * QUARTER)
        here = mm(pick, jnp.concatenate([mixed_ref[:, cols], result[:, cols]], 1))
        part = here if m == 0 else jnp.where(quarter == m, here, part)
    out_ref[:, : 2 * QUARTER] = part.astype(BF16)
    left = lanes_of((1, WIDE)) < HEAD_DIM
    tiles = []
    for c in range(D // WIDE):
        cols = slice(c * WIDE, (c + 1) * WIDE)
        a, b = one[:, cols], two[:, cols]
        even = jnp.where(left, a, pltpu.roll(jnp.broadcast_to(b, (8, WIDE)), HEAD_DIM, 1)[0:1])
        odd = jnp.where(left, pltpu.roll(jnp.broadcast_to(a, (8, WIDE)), HEAD_DIM, 1)[0:1], b)
        tiles += [jnp.broadcast_to(even, (64, WIDE)), jnp.broadcast_to(odd, (64, WIDE))]
    value = jnp.concatenate(tiles, 0)
    value = jnp.where(quarter == 1, small_ref[0:1, :], value)
    bias = jnp.where((row // 8) % 8 == at_ref[0], small_ref[1:2, :], 0.0)
    value = jnp.where(quarter == 2, bias, value)
    high = value.astype(BF16).astype(F32)
    value = jnp.where((row // RING) % 2 == 0, high, value - high)
    out_ref[:, 2 * QUARTER :] = value.astype(BF16)


def finish(own, got, rows, grad, mixed, place, gains, two, small, at):
    specs = [pl.BlockSpec(memory_space=pltpu.VMEM)] * 11
    return pl.pallas_call(
        finish_kernel,
        in_specs=specs + [pl.BlockSpec(memory_space=pltpu.SMEM)],
        out_shape=jax.ShapeDtypeStruct((4 * ROWS, 2 * QUARTER + WIDE), BF16),
        compiler_params=pltpu.CompilerParams(vmem_limit_bytes=48 * 2**20),
        cost_estimate=pl.CostEstimate(
            flops=16 * ROWS * ROWS * D, bytes_accessed=ROWS * D * 20, transcendentals=0
        ),
    )(own, *got, rows, grad, mixed, place, gains, two, small, at)


def settle_kernel(home_ref, deal_ref, rows_ref, grads_ref, sums_ref):
    deal = deal_ref[...]
    shape = (ROWS, 4 * ROWS)
    index = lax.broadcasted_iota(jnp.int32, shape, 0)
    for m in range(RING):
        pick = (index * RING + m == lanes_of(shape)).astype(BF16)
        here = mm(pick, home_ref[:, : 2 * QUARTER]).astype(BF16)
        here = mm(deal, here, TN).astype(BF16)
        cols = slice(m * QUARTER, (m + 1) * QUARTER)
        rows_ref[:, cols] = here[:, :QUARTER]
        grads_ref[:, cols] = here[:, QUARTER:]
    small = home_ref[:, 2 * QUARTER :].astype(F32)
    quarter = lax.broadcasted_iota(jnp.int32, small.shape, 0) % RING
    sums_ref[...] = jnp.zeros_like(sums_ref)
    for m in range(3):
        sums_ref[m : m + 1, :] = jnp.sum(jnp.where(quarter == m, small, 0.0), axis=0, keepdims=True)


def settle(home, deal):
    low = jax.ShapeDtypeStruct((ROWS, D), BF16)
    return pl.pallas_call(
        settle_kernel,
        out_shape=[low, low, jax.ShapeDtypeStruct((8, WIDE), F32)],
        compiler_params=pltpu.CompilerParams(vmem_limit_bytes=48 * 2**20),
        cost_estimate=pl.CostEstimate(
            flops=20 * ROWS * ROWS * D, bytes_accessed=ROWS * D * 16, transcendentals=0
        ),
    )(home, deal)


def weight_grad_kernel(core_ref, *refs, parts, count, switch, steps):
    given = switch is None
    lefts, others, rights = refs[:parts], refs[parts : parts + count], refs[parts + count : -3]
    keep_ref, send_ref, turned_ref = refs[-3:]
    low = core_ref[0] == 0
    step = pl.program_id(0)

    def load(sides):
        at = 0
        for side in sides:
            rows = side.shape[0]
            turned_ref[:, at : at + rows] = side[...].T
            at += rows

    @pl.when(step == 0)
    def _():
        load(lefts)

    if not given:

        @pl.when(step == switch * steps)
        def _():
            load(others)

    def emit(total):
        depth = total.shape[0] // 16
        width = keep_ref.shape[-1]
        for z in range(total.shape[1] // width):
            cols = slice(z * width, (z + 1) * width)
            for p in range(8):
                at = 2 * p * depth
                even, odd = total[at : at + depth, cols], total[at + depth : at + 2 * depth, cols]
                keep_ref[p, z, 0] = jnp.where(low, even, odd)
                send_ref[p, z, 0] = jnp.where(low, odd, even)

    def product():
        right = jnp.concatenate([ref[0] for ref in rights], 0)
        emit(mm(turned_ref[...], right).astype(BF16))

    if given:
        pl.when(step < pl.num_programs(0) - 1)(product)

        @pl.when(step == pl.num_programs(0) - 1)
        def _():
            emit(others[0][...].T)
    else:
        product()


def weight_grads(core, lefts, others, rights, switch, steps):
    parts = len(lefts)
    made, _, width = rights[0].shape
    kinds = made + 1 if switch is None else made
    block, half = width // steps, width // 2
    sides = [pl.BlockSpec((v.shape[0], D), lambda s: (0, 0)) for v in list(lefts) + list(others)]
    moving = [
        pl.BlockSpec(
            (1, v.shape[1], block), lambda s: (jnp.minimum(s // steps, made - 1), 0, s % steps)
        )
        for v in rights
    ]
    rows = sum(v.shape[1] for v in rights)
    out = pl.pallas_call(
        functools.partial(
            weight_grad_kernel, parts=parts, count=len(others), switch=switch, steps=steps
        ),
        grid=(kinds * steps,),
        in_specs=[pl.BlockSpec(memory_space=pltpu.SMEM)] + sides + moving,
        out_specs=[
            pl.BlockSpec((8, 2 // steps, 1, 64, half), lambda s: (0, s % steps, s // steps, 0, 0))
        ]
        * 2,
        out_shape=[jax.ShapeDtypeStruct((8, 2, kinds, 64, half), BF16)] * 2,
        scratch_shapes=[pltpu.VMEM((D, rows), BF16)],
        compiler_params=pltpu.CompilerParams(vmem_limit_bytes=48 * 2**20),
        cost_estimate=pl.CostEstimate(
            flops=2 * kinds * rows * D * width,
            bytes_accessed=2 * kinds * D * width + 4 * rows * D + 2 * kinds * rows * width,
            transcendentals=0,
        ),
    )(core, *lefts, *others, *rights)
    return [v.reshape(16, kinds, 64, half) for v in out]


def head_sums(values):
    wide = values.shape[1]
    row = lax.broadcasted_iota(jnp.int32, (wide, wide), 0) // HEAD_DIM
    same = (row == lanes_of((wide, wide)) // HEAD_DIM).astype(BF16)
    high = values.astype(BF16)
    low = (values - high.astype(F32)).astype(BF16)
    return mm(high, same) + mm(low, same)


def partner(values):
    wide = values.shape[1]
    first = lanes_of(values.shape) % HEAD_DIM < HALF
    return jnp.where(first, pltpu.roll(values, wide - HALF, 1), pltpu.roll(values, HALF, 1))


def angles_of(facts, freq_ref):
    facts = facts.astype(F32)
    times = facts[:, 3:4] * 32.0 + facts[:, 4:5]
    angle = times * freq_ref[0:1, :WIDE]
    first = lanes_of(angle.shape) % HEAD_DIM < HALF
    cosine = jnp.cos(angle)
    sine = jnp.sin(angle)
    sine = jnp.where(first, -sine, sine)
    return jnp.concatenate([cosine, cosine], 1), jnp.concatenate([sine, sine], 1)


def project_kernel(core_ref, *refs):
    pieces_in = refs[:RING]
    w_ref, freq_ref, mine_ref, send_ref, raw_ref, facts_ref = refs[RING:]
    low = core_ref[0] == 0
    for r in range(RING):
        block = slice(r * ROWS, (r + 1) * ROWS)
        rows = pieces_in[r][:, :D]
        facts = pieces_in[r][:, D:]
        facts_ref[block] = facts
        cosine, sine = angles_of(facts, freq_ref)
        for kind in range(3):
            value = mm(rows, w_ref[kind])
            if kind < 2:
                raw_ref[kind, block] = value
                unit = value * lax.rsqrt(head_sums(value * value) * (1.0 / HEAD_DIM) + EPS)
                value = unit * freq_ref[1 + kind : 2 + kind, :]
                value = value * cosine + partner(value) * sine
            if kind == 0:
                value = value * (HEAD_DIM ** (-0.5) * LOG2E)
            left, right = value[:, :WIDE], value[:, WIDE:]
            mine_ref[kind, block] = jnp.where(low, left, right).astype(BF16)
            send_ref[kind, block] = jnp.where(low, right, left).astype(BF16)


def project(core, rows, attn_w, freq):
    low = jax.ShapeDtypeStruct((3, PLANE, WIDE), BF16)
    whole = pl.BlockSpec(memory_space=pltpu.VMEM)
    return pl.pallas_call(
        project_kernel,
        in_specs=[pl.BlockSpec(memory_space=pltpu.SMEM)] + [whole] * (RING + 2),
        out_shape=[
            low,
            low,
            jax.ShapeDtypeStruct((2, PLANE, 2 * WIDE), F32),
            jax.ShapeDtypeStruct((PLANE, WIDE), BF16),
        ],
        compiler_params=pltpu.CompilerParams(vmem_limit_bytes=48 * 2**20),
        cost_estimate=pl.CostEstimate(
            flops=8 * PLANE * D * 2 * WIDE, bytes_accessed=PLANE * D * 8, transcendentals=PLANE * 1024
        ),
    )(core, *rows, attn_w, freq)


def unproject_kernel(core_ref, mine_ref, got_ref, raw_ref, facts_ref, w_ref, freq_ref, dp_ref, gain_ref, *part_refs):
    low = core_ref[0] == 0
    gains = [0.0, 0.0]
    for r in range(RING):
        block = slice(r * ROWS, (r + 1) * ROWS)
        cosine, sine = angles_of(facts_ref[block], freq_ref)
        total = None
        for kind in range(3):
            mine, got = mine_ref[kind, block], got_ref[kind, block]
            grad = jnp.concatenate([jnp.where(low, mine, got), jnp.where(low, got, mine)], 1)
            if kind < 2:
                grad = grad.astype(F32)
                if kind == 0:
                    grad = grad * (HEAD_DIM ** (-0.5))
                raw = raw_ref[kind, block]
                inv = lax.rsqrt(head_sums(raw * raw) * (1.0 / HEAD_DIM) + EPS)
                unit = raw * inv
                grad = grad * cosine - partner(grad) * sine
                gains[kind] += jnp.sum(grad * unit, axis=0, keepdims=True)
                scaled = grad * freq_ref[1 + kind : 2 + kind, :]
                mean = head_sums(scaled * unit) * (1.0 / HEAD_DIM)
                grad = (inv * (scaled - unit * mean)).astype(BF16)
            dp_ref[kind, block] = grad
            part = mm(grad, w_ref[kind], NT)
            total = part if total is None else total + part
        part_refs[r][...] = total.astype(BF16)
    gain_ref[...] = jnp.zeros_like(gain_ref)
    gain_ref[0:1, :] = gains[0]
    gain_ref[1:2, :] = gains[1]


def unproject(core, mine, got, raw, facts, attn_w, freq):
    three = pl.BlockSpec((3, D, 2 * WIDE), lambda i: (0, 0, 0))

    def whole(v):
        return pl.BlockSpec(v.shape, lambda i: (0,) * v.ndim)

    shapes = [
        jax.ShapeDtypeStruct((3, PLANE, 2 * WIDE), BF16),
        jax.ShapeDtypeStruct((8, 2 * WIDE), F32),
    ] + [jax.ShapeDtypeStruct((ROWS, D), BF16)] * RING
    return pl.pallas_call(
        unproject_kernel,
        grid=(1,),
        in_specs=[pl.BlockSpec(memory_space=pltpu.SMEM)]
        + [whole(v) for v in (mine, got, raw, facts)]
        + [three, whole(freq)],
        out_specs=[whole(v) for v in shapes],
        out_shape=shapes,
        compiler_params=pltpu.CompilerParams(vmem_limit_bytes=48 * 2**20),
        cost_estimate=pl.CostEstimate(
            flops=8 * PLANE * D * 2 * WIDE, bytes_accessed=PLANE * D * 8, transcendentals=PLANE * 1024
        ),
    )(core, mine, got, raw, facts, attn_w, freq)


LOG_LANE = 3 * VARIATES + SEQS


def with_pieces(base, values, first_lane, lanes):
    for i in range(3):
        part = values.astype(BF16).astype(F32)
        base = jnp.where(lanes == first_lane + i, part, base)
        values = values - part
    return base


def key_rows(mine_ref, got_ref, start, size):
    if start < PLANE:
        return mine_ref, slice(start, start + size)
    return got_ref, slice(start - PLANE, start - PLANE + size)


def value_lanes(rows):
    return (lanes_of((rows, WIDE)) < 3).astype(BF16)


def attend_kernel(
    at_ref, mine_ref, got_ref, own_ref, other_ref, bias_ref,
    att_ref, near_ref, send_ref, tail_ref, kt_ref, q_scr, qt_scr, *, chunks,
):
    step = pl.program_id(0)
    block = att_ref.shape[0]
    size = GROUP // chunks

    @pl.when(step == 0)
    def _():
        q_scr[:PLANE] = mine_ref[0]
        q_scr[PLANE:] = got_ref[0]
        lane = lanes_of((ROWS, WIDE))
        tail_lane = lane % HEAD_DIM
        bias_lane = tail_lane < 3 * VARIATES
        seg_lane = (tail_lane >= 3 * VARIATES) & (tail_lane < LOG_LANE)
        one_lane = (tail_lane >= LOG_LANE) & (tail_lane < LOG_LANE + 3)
        row = lax.broadcasted_iota(jnp.int32, (ROWS, WIDE), 0)
        for b in range(2 * RING):
            source = own_ref if b < RING else other_ref
            facts = source[(b % RING) * ROWS : (b % RING + 1) * ROWS, :].astype(F32)
            variate = facts[:, 2:3]
            equal = bias_lane & ((tail_lane % VARIATES).astype(F32) == variate)
            position = at_ref[b] + row
            segment = jnp.zeros_like(row)
            for j in range(SEQS):
                segment += (position >= at_ref[2 * RING + j]).astype(jnp.int32)
            inside = seg_lane & (tail_lane - 3 * VARIATES == segment)
            rows = slice(b * ROWS, (b + 1) * ROWS)
            qt_scr[rows] = (equal | inside).astype(BF16)
            tail = jnp.where(equal, bias_ref[0:1, :], bias_ref[1:2, :])
            tail = jnp.where(bias_lane, tail, jnp.where(one_lane, 1.0, 0.0))
            tail = jnp.where(seg_lane & ~inside, FAR, tail)
            kt_ref[rows] = tail.astype(BF16)

    here = pl.ds(pl.multiple_of(step * block, block), block)
    query_tail = qt_scr[here, :]
    query = jnp.concatenate([q_scr[here, :], query_tail], 1)
    zero = jnp.zeros_like(query)
    head_of = (lanes_of(query.shape) // HEAD_DIM) % 2
    lanes = lanes_of((block, WIDE))
    ones = value_lanes(size)
    out = None
    tail = query_tail.astype(F32)
    for head in range(2):
        masked = jnp.where(head_of == head, query, zero)
        total = None
        for c in range(chunks):
            rows = slice(c * size, (c + 1) * size)
            ref, at = key_rows(mine_ref, got_ref, c * size, size)
            keys = jnp.concatenate([ref[1, at, :], kt_ref[rows, :]], 1)
            values = jnp.concatenate([ref[2, at, :], ones], 1)
            prob = jnp.exp2(mm(masked, keys, NT)).astype(BF16)
            part = mm(prob, values)
            total = part if total is None else total + part
        row_sum = total[:, WIDE : WIDE + 1]
        now = total[:, :WIDE] / row_sum
        out = now if head == 0 else jnp.where(lanes < HEAD_DIM, out, now)
        tail = with_pieces(tail, -jnp.log2(row_sum), head * HEAD_DIM + LOG_LANE, lanes)
    att_ref[...] = out
    tail_ref[...] = tail.astype(BF16)
    low = out.astype(BF16)
    half = pl.num_programs(0) // 2

    @pl.when(step < half)
    def _():
        near_ref[here, :] = low

    @pl.when(step >= half)
    def _():
        send_ref[pl.ds(pl.multiple_of((step - half) * block, block), block), :] = low


def attend(at, mine, got, facts, facts_other, bias_rows):
    block = 512
    moving = pl.BlockSpec((block, WIDE), lambda i: (i, 0))
    plane = pl.BlockSpec((PLANE, WIDE), lambda i: (0, 0))
    three = pl.BlockSpec((3, PLANE, WIDE), lambda i: (0, 0, 0))
    low = jax.ShapeDtypeStruct((GROUP, WIDE), BF16)
    low_plane = jax.ShapeDtypeStruct((PLANE, WIDE), BF16)
    return pl.pallas_call(
        functools.partial(attend_kernel, chunks=4),
        grid=(GROUP // block,),
        in_specs=[
            pl.BlockSpec(memory_space=pltpu.SMEM),
            three,
            three,
            plane,
            plane,
            pl.BlockSpec((8, WIDE), lambda i: (0, 0)),
        ],
        out_specs=[moving, plane, plane, moving, pl.BlockSpec((GROUP, WIDE), lambda i: (0, 0))],
        out_shape=[jax.ShapeDtypeStruct((GROUP, WIDE), F32), low_plane, low_plane, low, low],
        scratch_shapes=[pltpu.VMEM((GROUP, WIDE), BF16)] * 2,
        compiler_params=pltpu.CompilerParams(vmem_limit_bytes=48 * 2**20),
        cost_estimate=pl.CostEstimate(
            flops=16 * GROUP * GROUP * WIDE, bytes_accessed=GROUP * WIDE * 24,
            transcendentals=2 * GROUP * GROUP,
        ),
    )(at, mine, got, facts, facts_other, bias_rows)


def attend_back_kernel(
    mine_ref, got_ref, qt_ref, kt_ref, hot_ref, near_ref, other_ref, att_ref,
    keep_ref, send_ref, bias_ref, q_scr, grad_scr, dk_sum, dv_sum, *, chunks,
):
    size = GROUP // chunks
    step = pl.program_id(0)
    block = qt_ref.shape[0]

    @pl.when(step == 0)
    def _():
        q_scr[:PLANE] = mine_ref[0]
        q_scr[PLANE:] = got_ref[0]
        grad_scr[:PLANE] = near_ref[...]
        grad_scr[PLANE:] = other_ref[...]
        dk_sum[...] = jnp.zeros_like(dk_sum)
        dv_sum[...] = jnp.zeros_like(dv_sum)

    here = pl.ds(pl.multiple_of(step * block, block), block)
    query = jnp.concatenate([q_scr[here, :], qt_ref[...]], 1)
    grad = grad_scr[here, :]
    zero = jnp.zeros_like(query)
    head_of = (lanes_of(query.shape) // HEAD_DIM) % 2
    lanes = lanes_of((block, WIDE))
    overlap = grad.astype(F32) * att_ref[...]
    ones = value_lanes(size)
    out = None
    for head in range(2):
        mine = head_of[:, :WIDE] == head
        masked = jnp.where(head_of == head, query, zero)
        grad_here = jnp.where(mine, grad, zero[:, :WIDE])
        dots = jnp.sum(jnp.where(mine, overlap, 0.0), axis=1, keepdims=True)
        extra = with_pieces(jnp.zeros(lanes.shape, F32), -dots, 0, lanes).astype(BF16)
        grad_wide = jnp.concatenate([grad_here, extra], 1)
        total = None
        for c in range(chunks):
            rows = slice(c * size, (c + 1) * size)
            ref, at = key_rows(mine_ref, got_ref, c * size, size)
            keys = ref[1, at, :]
            prob = jnp.exp2(mm(jnp.concatenate([keys, kt_ref[rows, :]], 1), masked, NT))
            slope = mm(jnp.concatenate([ref[2, at, :], ones], 1), grad_wide, NT)
            d_score = (prob * slope).astype(BF16)
            dv_sum[rows, :] += mm(prob.astype(BF16), grad_here)
            dk_sum[rows, :] += mm(d_score, masked)
            part = mm(d_score, keys, TN)
            total = part if total is None else total + part
        out = total if head == 0 else jnp.where(lanes < HEAD_DIM, out, total)
    low = out.astype(BF16)
    half = pl.num_programs(0) // 2

    @pl.when(step < half)
    def _():
        keep_ref[0, here, :] = low

    @pl.when(step >= half)
    def _():
        send_ref[0, pl.ds(pl.multiple_of((step - half) * block, block), block), :] = low

    @pl.when(step == pl.num_programs(0) - 1)
    def _():
        for ref, rows in ((keep_ref, slice(0, PLANE)), (send_ref, slice(PLANE, GROUP))):
            ref[1] = (dk_sum[rows, :WIDE] * (1.0 / LOG2E)).astype(BF16)
            ref[2] = dv_sum[rows, :].astype(BF16)
        counts = dk_sum[:, WIDE:]
        bias_ref[...] = jnp.zeros_like(bias_ref)
        bias_ref[0:1, :] = jnp.sum(counts * hot_ref[...].astype(F32), axis=0, keepdims=True)
        bias_ref[1:2, :] = jnp.sum(counts, axis=0, keepdims=True)


def attend_back(mine, got, query_tail, key_tail, near, other, attended):
    block = 512
    moving = pl.BlockSpec((block, WIDE), lambda i: (i, 0))
    fixed = pl.BlockSpec((GROUP, WIDE), lambda i: (0, 0))
    plane = pl.BlockSpec((PLANE, WIDE), lambda i: (0, 0))
    three = pl.BlockSpec((3, PLANE, WIDE), lambda i: (0, 0, 0))
    low = jax.ShapeDtypeStruct((3, PLANE, WIDE), BF16)
    return pl.pallas_call(
        functools.partial(attend_back_kernel, chunks=4),
        grid=(GROUP // block,),
        in_specs=[three, three, moving, fixed, fixed, plane, plane, moving],
        out_specs=[three, three, pl.BlockSpec((8, WIDE), lambda i: (0, 0))],
        out_shape=[low, low, jax.ShapeDtypeStruct((8, WIDE), F32)],
        scratch_shapes=[
            pltpu.VMEM((GROUP, WIDE), BF16),
            pltpu.VMEM((GROUP, WIDE), BF16),
            pltpu.VMEM((GROUP, 2 * WIDE), F32),
            pltpu.VMEM((GROUP, WIDE), F32),
        ],
        compiler_params=pltpu.CompilerParams(vmem_limit_bytes=48 * 2**20),
        cost_estimate=pl.CostEstimate(
            flops=40 * GROUP * GROUP * WIDE, bytes_accessed=GROUP * WIDE * 24,
            transcendentals=2 * GROUP * GROUP,
        ),
    )(mine, got, query_tail, key_tail, query_tail, near, other, attended)


def feed_kernel(b_ref, g_ref, w_ref, y_ref, db_ref, act_ref, *, cuts):
    rows, grads = b_ref[...], g_ref[...]
    size = w_ref.shape[2] // cuts

    def products(j):
        cols = slice(j * size, (j + 1) * size)
        return mm(rows, w_ref[0, :, cols]), mm(rows, w_ref[1, :, cols]), mm(grads, w_ref[2, :, cols])

    y_sum, db_sum = None, None
    ready = products(0)
    for j in range(cuts):
        gate, up, d_hidden = ready
        if j + 1 < cuts:
            ready = products(j + 1)
        cols = slice(j * size, (j + 1) * size)
        sig = 0.5 + 0.5 * jnp.tanh(0.5 * gate)
        silu = gate * sig
        hidden = (silu * up).astype(BF16)
        d_gate = (d_hidden * up * (sig + silu * (1.0 - sig))).astype(BF16)
        d_up = (d_hidden * silu).astype(BF16)
        act_ref[0, :, cols] = d_gate
        act_ref[1, :, cols] = d_up
        act_ref[2, :, cols] = hidden
        y_part = mm(hidden, w_ref[2, :, cols], NT)
        db_part = mm(d_gate, w_ref[0, :, cols], NT) + mm(d_up, w_ref[1, :, cols], NT)
        y_sum = y_part if y_sum is None else y_sum + y_part
        db_sum = db_part if db_sum is None else db_sum + db_part
    y_ref[...] = y_sum.astype(BF16)
    db_ref[...] = db_sum.astype(BF16)


def feed(rows_b, rows_g, weights):
    rows = rows_b.shape[0]
    width = weights.shape[2]
    low_d = jax.ShapeDtypeStruct((rows, D), BF16)
    low_f = jax.ShapeDtypeStruct((3, rows, width), BF16)
    return pl.pallas_call(
        functools.partial(feed_kernel, cuts=2),
        out_shape=[low_d, low_d, low_f],
        compiler_params=pltpu.CompilerParams(vmem_limit_bytes=26 * 2**20),
        cost_estimate=pl.CostEstimate(
            flops=12 * rows * D * width, bytes_accessed=6 * D * width + rows * D * 8 + rows * width * 6,
            transcendentals=rows * width,
        ),
    )(rows_b, rows_g, weights)


def body(
    tokens,
    cotangent,
    destination,
    variate_ids,
    time_ids,
    seq_lengths,
    qkv_weight,
    out_weight,
    gate_up_weight,
    down_weight,
    norm_gains,
    qk_gains,
    variate_bias,
):
    core = lax.axis_index("core")
    low_core = core == 0
    y_at = lax.axis_index("y")
    zl_at = lax.axis_index("zl")

    core_scalar = core.reshape(1).astype(jnp.int32)

    def side_by_side(mine, other):
        return jnp.concatenate(
            [jnp.where(low_core, mine, other), jnp.where(low_core, other, mine)], axis=-1
        )

    feed_shard = jnp.concatenate([gate_up_weight, down_weight.T[None]], 0)

    slot = destination % ROWS
    group_at = destination // GROUP
    block_at = (destination % GROUP) // ROWS
    device_at = ((group_at // 2) * 2 + block_at // 4) * 8 + (block_at % 4) * 2 + group_at % 2
    key = device_at * ROWS + slot
    zero = jnp.zeros_like(slot)
    facts = jnp.stack([key, slot, variate_ids, time_ids // 32, time_ids % 32, zero, zero, zero])
    gains_row = jnp.pad(
        norm_gains.reshape(8, 16), ((0, 0), (GAIN_LANE, WIDE - GAIN_LANE - 16))
    ).astype(F32)
    outgoing, deal = deal_rows(tokens, cotangent, facts.astype(F32), gains_row)
    arrived = lax.all_to_all(outgoing.reshape(DEVICES, 8, SPAN), ALL, 0, 0, tiled=True)
    out_shard, outgoing = lax.optimization_barrier((out_weight.T, outgoing))
    attn_shard = jnp.concatenate([qkv_weight, jnp.stack(gather_direct(out_shard))], 0)
    attn_mine = gather_round(attn_shard, ("zh", "zl"), lax.axis_index("zh") * 2 + zl_at)
    attn_mine, arrived = lax.optimization_barrier((attn_mine, arrived))
    attn_mine, out_mine = attn_mine[:, :3], attn_mine[:, 3:]
    attn_mine = jnp.stack(gather_ahead(attn_mine, "x")).reshape((16,) + qkv_weight.shape)

    lengths_other = swap_core(seq_lengths)
    lengths = jnp.where(zl_at == core, seq_lengths, lengths_other)[0]
    bias_other = lax.ppermute(variate_bias, "zl", [(0, 1), (1, 0)])
    bias_pair = jnp.where(zl_at == core, variate_bias, bias_other)

    arrived, lengths, bias_pair = lax.optimization_barrier((arrived, lengths, bias_pair))
    all_gains = arrived.reshape(16, 8, 8, SPAN)[:, 0, :, PAIR + GAIN_LANE : PAIR + GAIN_LANE + 16]
    inputs, grad_rows, attn_in, place, gains = receive(
        arrived.reshape(4 * ROWS, SPAN), all_gains.reshape(16, WIDE)
    )
    feed_shard, attn_in = lax.optimization_barrier((feed_shard, attn_in))
    feed_mine = flat_gather(feed_shard)
    zero_at = jnp.zeros((1,), jnp.int32)
    x_at = lax.axis_index("x").reshape(1).astype(jnp.int32)
    ahead, behind = ring(attn_in, -1), ring(attn_in, 1)
    ahead, behind, attn_mine = lax.optimization_barrier((ahead, behind, attn_mine))
    attn_w = assemble(core_scalar, x_at, attn_mine, swap_core(attn_mine))
    far_top, far_low = ring(ahead[: ROWS // 2], -1), ring(behind[ROWS // 2 :], 1)
    far_top, far_low, attn_w = lax.optimization_barrier((far_top, far_low, attn_w))
    attn_all = [attn_in, ahead, jnp.concatenate([far_top, far_low], 0), behind]
    grad_rows, attn_all = lax.optimization_barrier((grad_rows, attn_all))
    grad_all = gather_direct(grad_rows)

    blocks_y = (y_at + jnp.arange(RING)) % RING
    blocks = jnp.concatenate([core * RING + blocks_y, (1 - core) * RING + blocks_y])
    at = jnp.concatenate([blocks * ROWS, jnp.cumsum(lengths)]).astype(jnp.int32)

    inverse = THETA ** (-2.0 * jnp.arange(HALF).astype(F32) / HEAD_DIM)
    freq = jnp.concatenate(
        [
            jnp.tile(inverse, 8)[None],
            jnp.tile(qk_gains, (1, 4)),
            jnp.zeros((5, 2 * WIDE), F32),
        ]
    )
    qkv_mine, qkv_send, raw, facts_all = project(core_scalar, attn_all, attn_w, freq)
    facts_other = swap_core(facts_all)
    qkv_got = swap_core(qkv_send)

    bias_parts = jnp.stack(pieces(bias_pair * LOG2E, 3)).astype(F32)
    bias_rows = jnp.repeat(bias_parts, VARIATES, axis=0).transpose(1, 2, 0)
    bias_rows = jnp.pad(bias_rows, ((0, 0), (0, 0), (0, HEAD_DIM - 3 * VARIATES))).reshape(2, WIDE)
    bias_rows = jnp.pad(bias_rows, ((0, 6), (0, 0)))
    attended, att_near, att_send, query_back, key_tail = attend(
        at, qkv_mine, qkv_got, facts_all, facts_other, bias_rows
    )
    att_other = swap_core(att_send)
    att_other, grad_all = lax.optimization_barrier((att_other, grad_all))
    out_mine, att_send, feed_mine = lax.optimization_barrier((out_mine, att_send, feed_mine))
    out_mine = jnp.broadcast_to(out_mine[None], (RING,) + out_mine.shape)
    out_mine = lax.all_to_all(out_mine, "x", 0, 0, tiled=True).reshape(16, RING, 64, WIDE)
    att_plane = side_by_side(att_near, att_other).reshape(RING, ROWS, 2 * WIDE)
    att_rows = trade_ring([att_plane[r] for r in range(RING)])
    att_rows, feed_mine, out_mine = lax.optimization_barrier((att_rows, feed_mine, out_mine))
    out_other, feed_mine = lax.optimization_barrier((swap_core(out_mine), feed_mine))
    out_w = assemble(core_scalar, zero_at, out_mine, out_other)
    feed_w = assemble(core_scalar, zero_at, feed_mine, swap_core(feed_mine))
    hidden_one, feed_in = out_project(att_rows, out_w, inputs, gains)

    ahead, behind = ring(feed_in, -1), ring(feed_in, 1)
    fed_own = feed(feed_in, grad_all[0], feed_w)
    ahead, behind, fed_own = lax.optimization_barrier((ahead, behind, fed_own))
    far_top, far_low = ring(ahead[: ROWS // 2], -1), ring(behind[ROWS // 2 :], 1)
    fed_ahead = feed(ahead, grad_all[1], feed_w)
    fed_behind = feed(behind, grad_all[3], feed_w)
    far_top, far_low, fed_ahead, fed_behind = lax.optimization_barrier(
        (far_top, far_low, fed_ahead, fed_behind)
    )
    far = jnp.concatenate([far_top, far_low], 0)
    fed_far = feed(far, grad_all[2], feed_w)
    feed_all = [feed_in, ahead, far, behind]
    fed = [fed_own, fed_ahead, fed_far, fed_behind]
    feed_split = weight_grads(core_scalar, feed_all, grad_all, [f[2] for f in fed], 2, 2)
    db_got = send_ring([f[1] for f in fed], True)
    db_got, feed_split = lax.optimization_barrier((db_got, feed_split))
    grad_one, gain_two_grad, d_att, *both = middle(
        att_rows, out_w, [f[0] for f in fed], fed_own[1], db_got, hidden_one, grad_rows, gains
    )
    feed_total = chip_total(feed_split)
    feed_got = trade(feed_total, "x")

    grad_att = trade_ring([d_att[r] for r in range(RING)])
    grad_att[1], feed_total = lax.optimization_barrier((grad_att[1], feed_total))
    grad_att = jnp.concatenate(grad_att, 0)
    both, grad_att = lax.optimization_barrier((both, grad_att))
    both_got = send_ring(both)
    grad_left, grad_right = grad_att[:, :WIDE], grad_att[:, WIDE:]
    grad_other = swap_core(jnp.where(low_core, grad_right, grad_left))
    grad_near = jnp.where(low_core, grad_left, grad_right)
    d_keep, d_send, bias_sums = attend_back(
        qkv_mine, qkv_got, query_back, key_tail, grad_near, grad_other, attended
    )
    first_part = (jnp.arange(HEAD_DIM) < VARIATES)[None, None]
    bias_sums = jnp.where(first_part, bias_sums[:2].reshape(2, 2, HEAD_DIM), 0.0)
    bias_sums = jnp.sum(bias_sums, axis=2)
    bias_part = jnp.stack([bias_sums[0], bias_sums[1] - bias_sums[0]])
    d_got = swap_core(d_send)
    grad_proj, qk_sums, *in_part = unproject(
        core_scalar, d_keep, d_got, raw, facts_all, attn_w, freq
    )
    in_got = send_ring(in_part)
    feed_half = added(feed_got).astype(BF16)
    in_got[0], feed_half = lax.optimization_barrier((in_got[0], feed_half))
    grad_proj, both_got = lax.optimization_barrier((grad_proj, both_got))
    both_sum = add_ring(both[0], both_got)
    mixed = (hidden_one + both_sum[:ROWS]).astype(BF16)
    out_full = both_sum[ROWS:].astype(BF16)
    attn_split = weight_grads(core_scalar, attn_all, [out_full], [grad_proj], None, 1)
    attn_total = chip_total(attn_split)
    mixed, _ = lax.optimization_barrier((mixed, attn_total))
    feed_got = trade(feed_half, ("zh", "zl"))
    attn_own, attn_got = send_round(attn_total.reshape((RING, RING) + attn_total.shape[1:]), "x")
    in_got[2], attn_got = lax.optimization_barrier((in_got[2], attn_got))
    qk_sums = jnp.sum(qk_sums[:2].reshape(2, 4, HEAD_DIM), axis=1)

    small = jnp.zeros((8, WIDE), F32).at[0].set(qk_sums.reshape(WIDE))
    small = small.at[1, :4].set(bias_part.reshape(4))
    tensor_at = (y_at * 2 + core).reshape(1).astype(jnp.int32)
    last = finish(
        in_part[0], in_got, inputs, grad_one, mixed, place, gains, gain_two_grad, small, tensor_at
    )
    last = last.reshape(DEVICES, 8, 2 * QUARTER + WIDE)
    last, attn_got, feed_got = lax.optimization_barrier((last, attn_got, feed_got))
    home = lax.all_to_all(last, ALL, 0, 0, tiled=True)
    own, got = send_round(add_round(attn_own, attn_got).astype(BF16), ("zh", "zl"))
    home, got = lax.optimization_barrier((home, got))
    attn_grad = add_round(own, got)
    feed_grad = added(feed_got).reshape(3, 64, 512)
    new_tokens, token_grads, sums = settle(home.reshape(4 * ROWS, 2 * QUARTER + WIDE), deal)
    gains_grad = sums[0].reshape(2, 64)
    qk_grad = sums[1].reshape(2, 64)
    bias_grad = sums[2, :4].reshape(2, 2)

    return (
        new_tokens,
        token_grads,
        attn_grad[:3],
        attn_grad[3].T,
        feed_grad[:2],
        feed_grad[2].T,
        gains_grad,
        qk_grad,
        bias_grad,
    )


def solution(mesh):
    fine = Mesh(mesh.devices.reshape(4, 2, 2, 4, 2), ALL)
    dp = ("x", "zh", "core")
    tensor = ("y", "zl")
    in_specs = (
        P(ALL, None),
        P(ALL, None),
        P(ALL),
        P(ALL),
        P(ALL),
        P(dp, None),
        P(None, dp, tensor),
        P(tensor, dp),
        P(None, dp, tensor),
        P(tensor, dp),
        P(None, dp),
        P(),
        P(None, tensor),
    )
    out_specs = (
        P(ALL, None),
        P(ALL, None),
        P(None, dp, tensor),
        P(tensor, dp),
        P(None, dp, tensor),
        P(tensor, dp),
        P(None, dp),
        P(),
        P(None, tensor),
    )
    return jax.shard_map(body, mesh=fine, in_specs=in_specs, out_specs=out_specs, check_vma=False)
```

```python
import functools

import jax
import jax.numpy as jnp
from jax import lax
from jax.experimental import pallas as pl
from jax.experimental.pallas import tpu as pltpu
from jax.sharding import Mesh
from jax.sharding import PartitionSpec as P

HEADS = 16
HEAD_DIM = 64
HALF = HEAD_DIM // 2
D = 1024
FF = 4096
ROWS = 256
RING = 4
PLANE = ROWS * RING
GROUP = 2 * PLANE
DEVICES = 128
VARIATES = 8
SEQS = 4
WIDE = 128
EPS = 1e-06
THETA = 10000.0
LOG2E = 1.4426950408889634
FAR = -16384.0
F32 = jnp.float32
BF16 = jnp.bfloat16

ALL = ("x", "zh", "core", "y", "zl")
FLAT = ("x", "zh", "zl")
NT = (((1,), (1,)), ((), ()))
TN = (((0,), (0,)), ((), ()))


def mm(left, right, dims=(((1,), (0,)), ((), ()))):
    return lax.dot_general(left, right, dims, preferred_element_type=F32)


def root_stats(values):
    return lax.rsqrt(jnp.mean(values * values, axis=-1, keepdims=True) + EPS)


def norm_back(grad_in, normed, scale_inv):
    return scale_inv * (grad_in - normed * jnp.mean(grad_in * normed, axis=-1, keepdims=True))


def pieces(values, count):
    out = []
    for _ in range(count):
        part = lax.reduce_precision(values, 8, 7)
        out.append(part.astype(BF16))
        values = values - part
    return out


def ring(values, step):
    return lax.ppermute(values, "y", [(i, (i + step) % RING) for i in range(RING)])


def swap_core(values):
    return lax.ppermute(values, "core", [(0, 1), (1, 0)])


def gather_ring(values):
    ahead = ring(values, -1)
    behind = ring(values, 1)
    half = values.shape[0] // 2
    far_top = ring(ahead[:half], -1)
    far_low = ring(behind[half:], 1)
    return [values, ahead, jnp.concatenate([far_top, far_low], 0), behind]


def gather_direct(values):
    return [values, ring(values, -1), ring(values, 2), ring(values, 1)]


def trade_ring(parts):
    return [parts[0]] + [ring(parts[RING - s], -s) for s in range(1, RING)]


def send_ring(parts, halves=False):
    half = parts[2].shape[0] // 2
    far = [parts[2][:half], parts[2][half:]] if halves else [parts[2]]
    return [ring(parts[1], 1), ring(parts[3], -1)] + [ring(v, 2) for v in far]


def add_ring(own, got):
    far = got[2] if len(got) == 3 else jnp.concatenate(got[2:], 0)
    return own.astype(F32) + got[0].astype(F32) + got[1].astype(F32) + far.astype(F32)


def gather_ahead(values, axes):
    moves = [[((i + r) % RING, i) for i in range(RING)] for r in range(RING)]
    return [values] + [lax.ppermute(values, axes, moves[r]) for r in range(1, RING)]


def gather_round(values, axes, at):
    return jnp.roll(jnp.stack(gather_ahead(values, axes)), at, axis=0)


def flat_gather(shard):
    many = jnp.broadcast_to(shard[None], (16,) + shard.shape)
    return lax.all_to_all(many, FLAT, 0, 0, tiled=True)


def assemble_kernel(at_ref, mine_ref, other_ref, out_ref):
    core = at_ref[0]
    count, _, depth, width = mine_ref.shape
    for ref, side in ((mine_ref, core), (other_ref, 1 - core)):
        for i in range(count):
            at = (i // 2) * 2 * depth + side * depth
            rows = pl.ds(pl.multiple_of(at, depth), depth)
            out_ref[:, rows, (i % 2) * width : (i % 2 + 1) * width] = ref[i]


def assemble(core, x_at, mine, other):
    _, kinds, depth, width = mine.shape
    pair = pl.BlockSpec((4, kinds, depth, width), lambda p, at: (p, 0, 0, 0))
    return pl.pallas_call(
        assemble_kernel,
        grid_spec=pltpu.PrefetchScalarGridSpec(
            num_scalar_prefetch=1,
            grid=(RING,),
            in_specs=[pair, pair],
            out_specs=pl.BlockSpec(
                (kinds, 4 * depth, 2 * width), lambda p, at: (0, lax.rem(at[1] + p, RING), 0)
            ),
        ),
        out_shape=jax.ShapeDtypeStruct((kinds, 16 * depth, 2 * width), BF16),
        compiler_params=pltpu.CompilerParams(vmem_limit_bytes=28 * 2**20),
        cost_estimate=pl.CostEstimate(
            flops=0, bytes_accessed=kinds * 128 * depth * width, transcendentals=0
        ),
    )(jnp.concatenate([core, x_at]), mine, other)


def chip_total(split):
    return (split[0].astype(F32) + swap_core(split[1]).astype(F32)).astype(BF16)


def send_round(values, axes):
    at = lax.axis_index(axes)
    parts = [lax.dynamic_index_in_dim(values, (at + r) % RING, 0, keepdims=False) for r in range(RING)]
    moves = [[(i, (i + r) % RING) for i in range(RING)] for r in range(RING)]
    return parts[0], [lax.ppermute(parts[r], axes, moves[r]) for r in (1, 3, 2)]


def add_round(own, got):
    return sum((v.astype(F32) for v in got), own.astype(F32))


def trade(values, axes):
    return lax.all_to_all(values.reshape((RING, -1) + values.shape[1:]), axes, 0, 0, tiled=True)


def added(got):
    return jnp.sum(got.astype(F32), axis=0)


def lanes_of(shape):
    return lax.broadcasted_iota(jnp.int32, shape, 1)


QUARTER = D // RING
PAIR = 2 * QUARTER
SPAN = PAIR + WIDE
GAIN_LANE = 16


def deal_kernel(tok_ref, cot_ref, facts_ref, gains_ref, out_ref, deal_ref):
    wide = jnp.concatenate([facts_ref[...], jnp.zeros((WIDE - 8, ROWS), F32)], 0)
    facts = jnp.transpose(wide)
    keys = facts_ref[0:1, :]
    rank = jnp.sum((facts[:, 0:1] < keys).astype(F32), axis=0, keepdims=True)
    at = lax.broadcasted_iota(jnp.int32, (ROWS, ROWS), 0).astype(F32)
    deal_ref[...] = (at == rank).astype(BF16)
    low = jnp.where(lanes_of(facts.shape) == 0, 0.0, facts).astype(BF16)
    row = lax.broadcasted_iota(jnp.int32, (4 * ROWS, 1), 0)
    own = ((row // RING).astype(F32) == rank).astype(BF16)
    part = None
    for m in range(RING):
        cols = slice(m * QUARTER, (m + 1) * QUARTER)
        here = mm(own, jnp.concatenate([tok_ref[:, cols], cot_ref[:, cols]], 1))
        part = here if m == 0 else jnp.where(row % RING == m, here, part)
    out_ref[:, :PAIR] = part.astype(BF16)
    tail = mm(own, low)
    lane = lanes_of(tail.shape)
    gains = jnp.broadcast_to(gains_ref[...][None], (DEVICES, 8, WIDE)).reshape(tail.shape)
    tail = jnp.where((lane >= GAIN_LANE) & (lane < GAIN_LANE + 16), gains, tail)
    out_ref[:, PAIR:] = tail.astype(BF16)


def deal_rows(tokens, cotangent, facts, gains):
    return pl.pallas_call(
        deal_kernel,
        out_shape=[
            jax.ShapeDtypeStruct((4 * ROWS, SPAN), BF16),
            jax.ShapeDtypeStruct((ROWS, ROWS), BF16),
        ],
        compiler_params=pltpu.CompilerParams(vmem_limit_bytes=48 * 2**20),
        cost_estimate=pl.CostEstimate(
            flops=8 * ROWS * ROWS * 2304, bytes_accessed=ROWS * D * 16, transcendentals=0
        ),
    )(tokens, cotangent, facts, gains)


def receive_kernel(rows_ref, gains_ref, x_ref, g_ref, a_ref, place_ref, gain_ref):
    count = 4 * ROWS
    facts = rows_ref[:, PAIR:]
    slots = jnp.transpose(facts.astype(F32))[1:2, :]
    at = lax.broadcasted_iota(jnp.int32, (ROWS, count), 0)
    arrival = lanes_of((ROWS, count))
    here = at.astype(F32) == slots
    gains = gains_ref[...].astype(F32)
    turned = pltpu.roll(gains, HEAD_DIM, 1)
    left = lanes_of((1, WIDE)) < HEAD_DIM
    one, two = [], []
    for c in range(D // WIDE):
        even, odd = slice(2 * c, 2 * c + 1), slice(2 * c + 1, 2 * c + 2)
        one.append(jnp.where(left, gains[even], turned[odd]))
        two.append(jnp.where(left, turned[even], gains[odd]))
    gain_one = jnp.concatenate(one, 1)
    gain_ref[...] = jnp.zeros_like(gain_ref)
    gain_ref[0:1, :] = gain_one
    gain_ref[1:2, :] = jnp.concatenate(two, 1)
    quarters = []
    for m in range(RING):
        chosen = (here & (arrival % RING == m)).astype(BF16)
        both = mm(chosen, rows_ref[:, :PAIR])
        quarters.append(both[:, :QUARTER])
        g_ref[:, m * QUARTER : (m + 1) * QUARTER] = both[:, QUARTER:].astype(BF16)
        if m == 0:
            a_ref[:, D:] = mm(chosen, facts).astype(BF16)
            pick = (at * RING == arrival).astype(BF16)
            place_ref[...] = mm(chosen, pick, NT).astype(BF16)
    rows = jnp.concatenate(quarters, 1)
    x_ref[...] = rows
    a_ref[:, :D] = (rows * root_stats(rows) * gain_one).astype(BF16)


def receive(rows, gains):
    return pl.pallas_call(
        receive_kernel,
        out_shape=[
            jax.ShapeDtypeStruct((ROWS, D), F32),
            jax.ShapeDtypeStruct((ROWS, D), BF16),
            jax.ShapeDtypeStruct((ROWS, D + WIDE), BF16),
            jax.ShapeDtypeStruct((ROWS, ROWS), BF16),
            jax.ShapeDtypeStruct((8, D), F32),
        ],
        compiler_params=pltpu.CompilerParams(vmem_limit_bytes=48 * 2**20),
        cost_estimate=pl.CostEstimate(
            flops=16 * ROWS * ROWS * D, bytes_accessed=ROWS * D * 24, transcendentals=0
        ),
    )(rows, gains)


def out_kernel(*refs):
    att = refs[:RING]
    weights = refs[RING : 2 * RING]
    x_ref, gain_ref, h_ref, b_ref = refs[2 * RING :]
    hidden = x_ref[...]
    for r in range(RING):
        hidden = hidden + mm(att[r][...], weights[r][...], NT)
    h_ref[...] = hidden
    b_ref[...] = (hidden * root_stats(hidden) * gain_ref[1:2, :]).astype(BF16)


def out_project(att, weights, rows, gains):
    return pl.pallas_call(
        out_kernel,
        out_shape=[jax.ShapeDtypeStruct((ROWS, D), F32), jax.ShapeDtypeStruct((ROWS, D), BF16)],
        compiler_params=pltpu.CompilerParams(vmem_limit_bytes=48 * 2**20),
        cost_estimate=pl.CostEstimate(
            flops=2 * ROWS * D * D, bytes_accessed=2 * D * D + ROWS * D * 14, transcendentals=0
        ),
    )(*att, *weights, rows, gains)


def middle_kernel(*refs):
    att, y_parts, weights = refs[:RING], refs[RING : 2 * RING], refs[2 * RING : 3 * RING]
    refs = refs[3 * RING :]
    own_ref, near_ref, back_ref, top_ref, low_ref, h_ref, g_ref, gain_ref = refs[:8]
    grad_ref, two_ref, d_ref = refs[8:11]
    both_refs = refs[11:]
    far = jnp.concatenate([top_ref[...], low_ref[...]], 0).astype(F32)
    grad = own_ref[...].astype(F32) + near_ref[...].astype(F32) + back_ref[...].astype(F32) + far
    hidden = h_ref[...]
    scale = root_stats(hidden)
    normed = hidden * scale
    two_ref[...] = jnp.zeros_like(two_ref)
    two_ref[0:1, :] = jnp.sum(grad * normed, axis=0, keepdims=True)
    scaled = grad * gain_ref[1:2, :]
    grad = g_ref[...].astype(F32) + norm_back(scaled, normed, scale)
    grad_ref[...] = grad
    low = grad.astype(BF16)
    for r in range(RING):
        d_ref[r] = mm(low, weights[r][...]).astype(BF16)
        both_refs[r][:ROWS] = y_parts[r][...]
        both_refs[r][ROWS:] = mm(att[r][...], low, TN).astype(BF16)


def middle(att, weights, y_parts, own, got, hidden, grad_rows, gains):
    both = jax.ShapeDtypeStruct((2 * ROWS, D), BF16)
    return pl.pallas_call(
        middle_kernel,
        out_shape=[
            jax.ShapeDtypeStruct((ROWS, D), F32),
            jax.ShapeDtypeStruct((8, D), F32),
            jax.ShapeDtypeStruct((RING, ROWS, ROWS), BF16),
        ]
        + [both] * RING,
        compiler_params=pltpu.CompilerParams(vmem_limit_bytes=48 * 2**20),
        cost_estimate=pl.CostEstimate(
            flops=4 * ROWS * D * D, bytes_accessed=2 * D * D + ROWS * D * 40, transcendentals=0
        ),
    )(*att, *y_parts, *weights, own, *got, hidden, grad_rows, gains)


def finish_kernel(
    own_ref, near_ref, back_ref, far_ref, x_ref, grad_ref, mixed_ref, place_ref,
    gain_ref, two_ref, small_ref, at_ref, out_ref,
):
    rows = x_ref[...]
    scale = root_stats(rows)
    normed = rows * scale
    far = far_ref[...].astype(F32)
    grad = own_ref[...].astype(F32) + near_ref[...].astype(F32) + back_ref[...].astype(F32) + far
    one = jnp.sum(grad * normed, axis=0, keepdims=True)
    two = two_ref[0:1, :]
    scaled = grad * gain_ref[0:1, :]
    back = scale * (scaled - normed * jnp.mean(scaled * normed, axis=1, keepdims=True))
    result = (grad_ref[...] + back).astype(BF16)
    count = 4 * ROWS
    row = lax.broadcasted_iota(jnp.int32, (count, 1), 0)
    quarter = row % RING
    pick = (row // RING == lanes_of((count, ROWS))).astype(BF16)
    pick = mm(pick, place_ref[...], NT).astype(BF16)
    part = None
    for m in range(RING):
        cols = slice(m * QUARTER, (m + 1) * QUARTER)
        here = mm(pick, jnp.concatenate([mixed_ref[:, cols], result[:, cols]], 1))
        part = here if m == 0 else jnp.where(quarter == m, here, part)
    out_ref[:, : 2 * QUARTER] = part.astype(BF16)
    left = lanes_of((1, WIDE)) < HEAD_DIM
    tiles = []
    for c in range(D // WIDE):
        cols = slice(c * WIDE, (c + 1) * WIDE)
        a, b = one[:, cols], two[:, cols]
        even = jnp.where(left, a, pltpu.roll(jnp.broadcast_to(b, (8, WIDE)), HEAD_DIM, 1)[0:1])
        odd = jnp.where(left, pltpu.roll(jnp.broadcast_to(a, (8, WIDE)), HEAD_DIM, 1)[0:1], b)
        tiles += [jnp.broadcast_to(even, (64, WIDE)), jnp.broadcast_to(odd, (64, WIDE))]
    value = jnp.concatenate(tiles, 0)
    value = jnp.where(quarter == 1, small_ref[0:1, :], value)
    bias = jnp.where((row // 8) % 8 == at_ref[0], small_ref[1:2, :], 0.0)
    value = jnp.where(quarter == 2, bias, value)
    high = value.astype(BF16).astype(F32)
    value = jnp.where((row // RING) % 2 == 0, high, value - high)
    out_ref[:, 2 * QUARTER :] = value.astype(BF16)


def finish(own, got, rows, grad, mixed, place, gains, two, small, at):
    specs = [pl.BlockSpec(memory_space=pltpu.VMEM)] * 11
    return pl.pallas_call(
        finish_kernel,
        in_specs=specs + [pl.BlockSpec(memory_space=pltpu.SMEM)],
        out_shape=jax.ShapeDtypeStruct((4 * ROWS, 2 * QUARTER + WIDE), BF16),
        compiler_params=pltpu.CompilerParams(vmem_limit_bytes=48 * 2**20),
        cost_estimate=pl.CostEstimate(
            flops=16 * ROWS * ROWS * D, bytes_accessed=ROWS * D * 20, transcendentals=0
        ),
    )(own, *got, rows, grad, mixed, place, gains, two, small, at)


def settle_kernel(home_ref, deal_ref, rows_ref, grads_ref, sums_ref):
    deal = deal_ref[...]
    shape = (ROWS, 4 * ROWS)
    index = lax.broadcasted_iota(jnp.int32, shape, 0)
    for m in range(RING):
        pick = (index * RING + m == lanes_of(shape)).astype(BF16)
        here = mm(pick, home_ref[:, : 2 * QUARTER]).astype(BF16)
        here = mm(deal, here, TN).astype(BF16)
        cols = slice(m * QUARTER, (m + 1) * QUARTER)
        rows_ref[:, cols] = here[:, :QUARTER]
        grads_ref[:, cols] = here[:, QUARTER:]
    small = home_ref[:, 2 * QUARTER :].astype(F32)
    quarter = lax.broadcasted_iota(jnp.int32, small.shape, 0) % RING
    sums_ref[...] = jnp.zeros_like(sums_ref)
    for m in range(3):
        sums_ref[m : m + 1, :] = jnp.sum(jnp.where(quarter == m, small, 0.0), axis=0, keepdims=True)


def settle(home, deal):
    low = jax.ShapeDtypeStruct((ROWS, D), BF16)
    return pl.pallas_call(
        settle_kernel,
        out_shape=[low, low, jax.ShapeDtypeStruct((8, WIDE), F32)],
        compiler_params=pltpu.CompilerParams(vmem_limit_bytes=48 * 2**20),
        cost_estimate=pl.CostEstimate(
            flops=20 * ROWS * ROWS * D, bytes_accessed=ROWS * D * 16, transcendentals=0
        ),
    )(home, deal)


def weight_grad_kernel(core_ref, *refs, parts, count, switch, steps):
    given = switch is None
    lefts, others, rights = refs[:parts], refs[parts : parts + count], refs[parts + count : -3]
    keep_ref, send_ref, turned_ref = refs[-3:]
    low = core_ref[0] == 0
    step = pl.program_id(0)

    def load(sides):
        at = 0
        for side in sides:
            rows = side.shape[0]
            turned_ref[:, at : at + rows] = side[...].T
            at += rows

    @pl.when(step == 0)
    def _():
        load(lefts)

    if not given:

        @pl.when(step == switch * steps)
        def _():
            load(others)

    def emit(total):
        depth = total.shape[0] // 16
        width = keep_ref.shape[-1]
        for z in range(total.shape[1] // width):
            cols = slice(z * width, (z + 1) * width)
            for p in range(8):
                at = 2 * p * depth
                even, odd = total[at : at + depth, cols], total[at + depth : at + 2 * depth, cols]
                keep_ref[p, z, 0] = jnp.where(low, even, odd)
                send_ref[p, z, 0] = jnp.where(low, odd, even)

    def product():
        right = jnp.concatenate([ref[0] for ref in rights], 0)
        emit(mm(turned_ref[...], right).astype(BF16))

    if given:
        pl.when(step < pl.num_programs(0) - 1)(product)

        @pl.when(step == pl.num_programs(0) - 1)
        def _():
            emit(others[0][...].T)
    else:
        product()


def weight_grads(core, lefts, others, rights, switch, steps):
    parts = len(lefts)
    made, _, width = rights[0].shape
    kinds = made + 1 if switch is None else made
    block, half = width // steps, width // 2
    sides = [pl.BlockSpec((v.shape[0], D), lambda s: (0, 0)) for v in list(lefts) + list(others)]
    moving = [
        pl.BlockSpec(
            (1, v.shape[1], block), lambda s: (jnp.minimum(s // steps, made - 1), 0, s % steps)
        )
        for v in rights
    ]
    rows = sum(v.shape[1] for v in rights)
    out = pl.pallas_call(
        functools.partial(
            weight_grad_kernel, parts=parts, count=len(others), switch=switch, steps=steps
        ),
        grid=(kinds * steps,),
        in_specs=[pl.BlockSpec(memory_space=pltpu.SMEM)] + sides + moving,
        out_specs=[
            pl.BlockSpec((8, 2 // steps, 1, 64, half), lambda s: (0, s % steps, s // steps, 0, 0))
        ]
        * 2,
        out_shape=[jax.ShapeDtypeStruct((8, 2, kinds, 64, half), BF16)] * 2,
        scratch_shapes=[pltpu.VMEM((D, rows), BF16)],
        compiler_params=pltpu.CompilerParams(vmem_limit_bytes=48 * 2**20),
        cost_estimate=pl.CostEstimate(
            flops=2 * kinds * rows * D * width,
            bytes_accessed=2 * kinds * D * width + 4 * rows * D + 2 * kinds * rows * width,
            transcendentals=0,
        ),
    )(core, *lefts, *others, *rights)
    return [v.reshape(16, kinds, 64, half) for v in out]


def head_sums(values):
    wide = values.shape[1]
    row = lax.broadcasted_iota(jnp.int32, (wide, wide), 0) // HEAD_DIM
    same = (row == lanes_of((wide, wide)) // HEAD_DIM).astype(BF16)
    high = values.astype(BF16)
    low = (values - high.astype(F32)).astype(BF16)
    return mm(high, same) + mm(low, same)


def partner(values):
    wide = values.shape[1]
    first = lanes_of(values.shape) % HEAD_DIM < HALF
    return jnp.where(first, pltpu.roll(values, wide - HALF, 1), pltpu.roll(values, HALF, 1))


def angles_of(facts, freq_ref):
    facts = facts.astype(F32)
    times = facts[:, 3:4] * 32.0 + facts[:, 4:5]
    angle = times * freq_ref[0:1, :WIDE]
    first = lanes_of(angle.shape) % HEAD_DIM < HALF
    cosine = jnp.cos(angle)
    sine = jnp.sin(angle)
    sine = jnp.where(first, -sine, sine)
    return jnp.concatenate([cosine, cosine], 1), jnp.concatenate([sine, sine], 1)


def project_kernel(core_ref, *refs):
    pieces_in = refs[:RING]
    w_ref, freq_ref, mine_ref, send_ref, raw_ref, facts_ref = refs[RING:]
    low = core_ref[0] == 0
    for r in range(RING):
        block = slice(r * ROWS, (r + 1) * ROWS)
        rows = pieces_in[r][:, :D]
        facts = pieces_in[r][:, D:]
        facts_ref[block] = facts
        cosine, sine = angles_of(facts, freq_ref)
        for kind in range(3):
            value = mm(rows, w_ref[kind])
            if kind < 2:
                raw_ref[kind, block] = value
                unit = value * lax.rsqrt(head_sums(value * value) * (1.0 / HEAD_DIM) + EPS)
                value = unit * freq_ref[1 + kind : 2 + kind, :]
                value = value * cosine + partner(value) * sine
            if kind == 0:
                value = value * (HEAD_DIM ** (-0.5) * LOG2E)
            left, right = value[:, :WIDE], value[:, WIDE:]
            mine_ref[kind, block] = jnp.where(low, left, right).astype(BF16)
            send_ref[kind, block] = jnp.where(low, right, left).astype(BF16)


def project(core, rows, attn_w, freq):
    low = jax.ShapeDtypeStruct((3, PLANE, WIDE), BF16)

    def whole(v):
        return pl.BlockSpec(v.shape, lambda i: (0,) * v.ndim)

    shapes = [
        low,
        low,
        jax.ShapeDtypeStruct((2, PLANE, 2 * WIDE), F32),
        jax.ShapeDtypeStruct((PLANE, WIDE), BF16),
    ]
    return pl.pallas_call(
        project_kernel,
        grid=(1,),
        in_specs=[pl.BlockSpec(memory_space=pltpu.SMEM)]
        + [whole(v) for v in rows]
        + [pl.BlockSpec((3, D, 2 * WIDE), lambda i: (0, 0, 0)), whole(freq)],
        out_specs=[whole(v) for v in shapes],
        out_shape=shapes,
        compiler_params=pltpu.CompilerParams(vmem_limit_bytes=48 * 2**20),
        cost_estimate=pl.CostEstimate(
            flops=8 * PLANE * D * 2 * WIDE, bytes_accessed=PLANE * D * 8, transcendentals=PLANE * 1024
        ),
    )(core, *rows, attn_w, freq)


def unproject_kernel(core_ref, mine_ref, got_ref, raw_ref, facts_ref, w_ref, freq_ref, dp_ref, gain_ref, *part_refs):
    low = core_ref[0] == 0
    gains = [0.0, 0.0]
    for r in range(RING):
        block = slice(r * ROWS, (r + 1) * ROWS)
        cosine, sine = angles_of(facts_ref[block], freq_ref)
        total = None
        for kind in range(3):
            mine, got = mine_ref[kind, block], got_ref[kind, block]
            grad = jnp.concatenate([jnp.where(low, mine, got), jnp.where(low, got, mine)], 1)
            if kind < 2:
                grad = grad.astype(F32)
                if kind == 0:
                    grad = grad * (HEAD_DIM ** (-0.5))
                raw = raw_ref[kind, block]
                inv = lax.rsqrt(head_sums(raw * raw) * (1.0 / HEAD_DIM) + EPS)
                unit = raw * inv
                grad = grad * cosine - partner(grad) * sine
                gains[kind] += jnp.sum(grad * unit, axis=0, keepdims=True)
                scaled = grad * freq_ref[1 + kind : 2 + kind, :]
                mean = head_sums(scaled * unit) * (1.0 / HEAD_DIM)
                grad = (inv * (scaled - unit * mean)).astype(BF16)
            dp_ref[kind, block] = grad
            part = mm(grad, w_ref[kind], NT)
            total = part if total is None else total + part
        part_refs[r][...] = total.astype(BF16)
    gain_ref[...] = jnp.zeros_like(gain_ref)
    gain_ref[0:1, :] = gains[0]
    gain_ref[1:2, :] = gains[1]


def unproject(core, mine, got, raw, facts, attn_w, freq):
    three = pl.BlockSpec((3, D, 2 * WIDE), lambda i: (0, 0, 0))

    def whole(v):
        return pl.BlockSpec(v.shape, lambda i: (0,) * v.ndim)

    shapes = [
        jax.ShapeDtypeStruct((3, PLANE, 2 * WIDE), BF16),
        jax.ShapeDtypeStruct((8, 2 * WIDE), F32),
    ] + [jax.ShapeDtypeStruct((ROWS, D), BF16)] * RING
    return pl.pallas_call(
        unproject_kernel,
        grid=(1,),
        in_specs=[pl.BlockSpec(memory_space=pltpu.SMEM)]
        + [whole(v) for v in (mine, got, raw, facts)]
        + [three, whole(freq)],
        out_specs=[whole(v) for v in shapes],
        out_shape=shapes,
        compiler_params=pltpu.CompilerParams(vmem_limit_bytes=48 * 2**20),
        cost_estimate=pl.CostEstimate(
            flops=8 * PLANE * D * 2 * WIDE, bytes_accessed=PLANE * D * 8, transcendentals=PLANE * 1024
        ),
    )(core, mine, got, raw, facts, attn_w, freq)


LOG_LANE = 3 * VARIATES + SEQS


def with_pieces(base, values, first_lane, lanes):
    for i in range(3):
        part = values.astype(BF16).astype(F32)
        base = jnp.where(lanes == first_lane + i, part, base)
        values = values - part
    return base


def key_rows(mine_ref, got_ref, start, size):
    if start < PLANE:
        return mine_ref, slice(start, start + size)
    return got_ref, slice(start - PLANE, start - PLANE + size)


def value_lanes(rows):
    return (lanes_of((rows, WIDE)) < 3).astype(BF16)


def attend_kernel(
    at_ref, mine_ref, got_ref, own_ref, other_ref, bias_ref,
    att_ref, near_ref, send_ref, tail_ref, kt_ref, q_scr, qt_scr, *, chunks,
):
    step = pl.program_id(0)
    block = att_ref.shape[0]
    size = GROUP // chunks

    @pl.when(step == 0)
    def _():
        q_scr[:PLANE] = mine_ref[0]
        q_scr[PLANE:] = got_ref[0]
        lane = lanes_of((ROWS, WIDE))
        tail_lane = lane % HEAD_DIM
        bias_lane = tail_lane < 3 * VARIATES
        seg_lane = (tail_lane >= 3 * VARIATES) & (tail_lane < LOG_LANE)
        one_lane = (tail_lane >= LOG_LANE) & (tail_lane < LOG_LANE + 3)
        row = lax.broadcasted_iota(jnp.int32, (ROWS, WIDE), 0)
        for b in range(2 * RING):
            source = own_ref if b < RING else other_ref
            facts = source[(b % RING) * ROWS : (b % RING + 1) * ROWS, :].astype(F32)
            variate = facts[:, 2:3]
            equal = bias_lane & ((tail_lane % VARIATES).astype(F32) == variate)
            position = at_ref[b] + row
            segment = jnp.zeros_like(row)
            for j in range(SEQS):
                segment += (position >= at_ref[2 * RING + j]).astype(jnp.int32)
            inside = seg_lane & (tail_lane - 3 * VARIATES == segment)
            rows = slice(b * ROWS, (b + 1) * ROWS)
            qt_scr[rows] = (equal | inside).astype(BF16)
            tail = jnp.where(equal, bias_ref[0:1, :], bias_ref[1:2, :])
            tail = jnp.where(bias_lane, tail, jnp.where(one_lane, 1.0, 0.0))
            tail = jnp.where(seg_lane & ~inside, FAR, tail)
            kt_ref[rows] = tail.astype(BF16)

    here = pl.ds(pl.multiple_of(step * block, block), block)
    query_tail = qt_scr[here, :]
    query = jnp.concatenate([q_scr[here, :], query_tail], 1)
    zero = jnp.zeros_like(query)
    head_of = (lanes_of(query.shape) // HEAD_DIM) % 2
    lanes = lanes_of((block, WIDE))
    ones = value_lanes(size)
    out = None
    tail = query_tail.astype(F32)
    for head in range(2):
        masked = jnp.where(head_of == head, query, zero)
        total = None
        for c in range(chunks):
            rows = slice(c * size, (c + 1) * size)
            ref, at = key_rows(mine_ref, got_ref, c * size, size)
            keys = jnp.concatenate([ref[1, at, :], kt_ref[rows, :]], 1)
            values = jnp.concatenate([ref[2, at, :], ones], 1)
            prob = jnp.exp2(mm(masked, keys, NT)).astype(BF16)
            part = mm(prob, values)
            total = part if total is None else total + part
        row_sum = total[:, WIDE : WIDE + 1]
        now = total[:, :WIDE] / row_sum
        out = now if head == 0 else jnp.where(lanes < HEAD_DIM, out, now)
        tail = with_pieces(tail, -jnp.log2(row_sum), head * HEAD_DIM + LOG_LANE, lanes)
    att_ref[...] = out
    tail_ref[...] = tail.astype(BF16)
    low = out.astype(BF16)
    half = pl.num_programs(0) // 2

    @pl.when(step < half)
    def _():
        near_ref[here, :] = low

    @pl.when(step >= half)
    def _():
        send_ref[pl.ds(pl.multiple_of((step - half) * block, block), block), :] = low


def attend(at, mine, got, facts, facts_other, bias_rows):
    block = 512
    moving = pl.BlockSpec((block, WIDE), lambda i: (i, 0))
    plane = pl.BlockSpec((PLANE, WIDE), lambda i: (0, 0))
    three = pl.BlockSpec((3, PLANE, WIDE), lambda i: (0, 0, 0))
    low = jax.ShapeDtypeStruct((GROUP, WIDE), BF16)
    low_plane = jax.ShapeDtypeStruct((PLANE, WIDE), BF16)
    return pl.pallas_call(
        functools.partial(attend_kernel, chunks=4),
        grid=(GROUP // block,),
        in_specs=[
            pl.BlockSpec(memory_space=pltpu.SMEM),
            three,
            three,
            plane,
            plane,
            pl.BlockSpec((8, WIDE), lambda i: (0, 0)),
        ],
        out_specs=[moving, plane, plane, moving, pl.BlockSpec((GROUP, WIDE), lambda i: (0, 0))],
        out_shape=[jax.ShapeDtypeStruct((GROUP, WIDE), F32), low_plane, low_plane, low, low],
        scratch_shapes=[pltpu.VMEM((GROUP, WIDE), BF16)] * 2,
        compiler_params=pltpu.CompilerParams(vmem_limit_bytes=48 * 2**20),
        cost_estimate=pl.CostEstimate(
            flops=16 * GROUP * GROUP * WIDE, bytes_accessed=GROUP * WIDE * 24,
            transcendentals=2 * GROUP * GROUP,
        ),
    )(at, mine, got, facts, facts_other, bias_rows)


def attend_back_kernel(
    mine_ref, got_ref, qt_ref, kt_ref, hot_ref, near_ref, other_ref, att_ref,
    keep_ref, send_ref, bias_ref, q_scr, grad_scr, dk_sum, dv_sum, *, chunks,
):
    size = GROUP // chunks
    step = pl.program_id(0)
    block = qt_ref.shape[0]

    @pl.when(step == 0)
    def _():
        q_scr[:PLANE] = mine_ref[0]
        q_scr[PLANE:] = got_ref[0]
        grad_scr[:PLANE] = near_ref[...]
        grad_scr[PLANE:] = other_ref[...]
        dk_sum[...] = jnp.zeros_like(dk_sum)
        dv_sum[...] = jnp.zeros_like(dv_sum)

    here = pl.ds(pl.multiple_of(step * block, block), block)
    query = jnp.concatenate([q_scr[here, :], qt_ref[...]], 1)
    grad = grad_scr[here, :]
    zero = jnp.zeros_like(query)
    head_of = (lanes_of(query.shape) // HEAD_DIM) % 2
    lanes = lanes_of((block, WIDE))
    overlap = grad.astype(F32) * att_ref[...]
    ones = value_lanes(size)
    out = None
    for head in range(2):
        mine = head_of[:, :WIDE] == head
        masked = jnp.where(head_of == head, query, zero)
        grad_here = jnp.where(mine, grad, zero[:, :WIDE])
        dots = jnp.sum(jnp.where(mine, overlap, 0.0), axis=1, keepdims=True)
        extra = with_pieces(jnp.zeros(lanes.shape, F32), -dots, 0, lanes).astype(BF16)
        grad_wide = jnp.concatenate([grad_here, extra], 1)
        total = None
        for c in range(chunks):
            rows = slice(c * size, (c + 1) * size)
            ref, at = key_rows(mine_ref, got_ref, c * size, size)
            keys = ref[1, at, :]
            prob = jnp.exp2(mm(jnp.concatenate([keys, kt_ref[rows, :]], 1), masked, NT))
            slope = mm(jnp.concatenate([ref[2, at, :], ones], 1), grad_wide, NT)
            d_score = (prob * slope).astype(BF16)
            dv_sum[rows, :] += mm(prob.astype(BF16), grad_here)
            dk_sum[rows, :] += mm(d_score, masked)
            part = mm(d_score, keys, TN)
            total = part if total is None else total + part
        out = total if head == 0 else jnp.where(lanes < HEAD_DIM, out, total)
    low = out.astype(BF16)
    half = pl.num_programs(0) // 2

    @pl.when(step < half)
    def _():
        keep_ref[0, here, :] = low

    @pl.when(step >= half)
    def _():
        send_ref[0, pl.ds(pl.multiple_of((step - half) * block, block), block), :] = low

    @pl.when(step == pl.num_programs(0) - 1)
    def _():
        for ref, rows in ((keep_ref, slice(0, PLANE)), (send_ref, slice(PLANE, GROUP))):
            ref[1] = (dk_sum[rows, :WIDE] * (1.0 / LOG2E)).astype(BF16)
            ref[2] = dv_sum[rows, :].astype(BF16)
        counts = dk_sum[:, WIDE:]
        bias_ref[...] = jnp.zeros_like(bias_ref)
        bias_ref[0:1, :] = jnp.sum(counts * hot_ref[...].astype(F32), axis=0, keepdims=True)
        bias_ref[1:2, :] = jnp.sum(counts, axis=0, keepdims=True)


def attend_back(mine, got, query_tail, key_tail, near, other, attended):
    block = 512
    moving = pl.BlockSpec((block, WIDE), lambda i: (i, 0))
    fixed = pl.BlockSpec((GROUP, WIDE), lambda i: (0, 0))
    plane = pl.BlockSpec((PLANE, WIDE), lambda i: (0, 0))
    three = pl.BlockSpec((3, PLANE, WIDE), lambda i: (0, 0, 0))
    low = jax.ShapeDtypeStruct((3, PLANE, WIDE), BF16)
    return pl.pallas_call(
        functools.partial(attend_back_kernel, chunks=4),
        grid=(GROUP // block,),
        in_specs=[three, three, moving, fixed, fixed, plane, plane, moving],
        out_specs=[three, three, pl.BlockSpec((8, WIDE), lambda i: (0, 0))],
        out_shape=[low, low, jax.ShapeDtypeStruct((8, WIDE), F32)],
        scratch_shapes=[
            pltpu.VMEM((GROUP, WIDE), BF16),
            pltpu.VMEM((GROUP, WIDE), BF16),
            pltpu.VMEM((GROUP, 2 * WIDE), F32),
            pltpu.VMEM((GROUP, WIDE), F32),
        ],
        compiler_params=pltpu.CompilerParams(vmem_limit_bytes=48 * 2**20),
        cost_estimate=pl.CostEstimate(
            flops=40 * GROUP * GROUP * WIDE, bytes_accessed=GROUP * WIDE * 24,
            transcendentals=2 * GROUP * GROUP,
        ),
    )(mine, got, query_tail, key_tail, query_tail, near, other, attended)


def feed_kernel(b_ref, g_ref, w_ref, y_ref, db_ref, act_ref, *, cuts):
    rows, grads = b_ref[...], g_ref[...]
    size = w_ref.shape[2] // cuts

    def products(j):
        cols = slice(j * size, (j + 1) * size)
        return mm(rows, w_ref[0, :, cols]), mm(rows, w_ref[1, :, cols]), mm(grads, w_ref[2, :, cols])

    y_sum, db_sum = None, None
    ready = products(0)
    for j in range(cuts):
        gate, up, d_hidden = ready
        if j + 1 < cuts:
            ready = products(j + 1)
        cols = slice(j * size, (j + 1) * size)
        sig = 0.5 + 0.5 * jnp.tanh(0.5 * gate)
        silu = gate * sig
        hidden = (silu * up).astype(BF16)
        d_gate = (d_hidden * up * (sig + silu * (1.0 - sig))).astype(BF16)
        d_up = (d_hidden * silu).astype(BF16)
        act_ref[0, :, cols] = d_gate
        act_ref[1, :, cols] = d_up
        act_ref[2, :, cols] = hidden
        y_part = mm(hidden, w_ref[2, :, cols], NT)
        db_part = mm(d_gate, w_ref[0, :, cols], NT) + mm(d_up, w_ref[1, :, cols], NT)
        y_sum = y_part if y_sum is None else y_sum + y_part
        db_sum = db_part if db_sum is None else db_sum + db_part
    y_ref[...] = y_sum.astype(BF16)
    db_ref[...] = db_sum.astype(BF16)


def feed(rows_b, rows_g, weights):
    rows = rows_b.shape[0]
    width = weights.shape[2]
    low_d = jax.ShapeDtypeStruct((rows, D), BF16)
    low_f = jax.ShapeDtypeStruct((3, rows, width), BF16)
    return pl.pallas_call(
        functools.partial(feed_kernel, cuts=2),
        out_shape=[low_d, low_d, low_f],
        compiler_params=pltpu.CompilerParams(vmem_limit_bytes=26 * 2**20),
        cost_estimate=pl.CostEstimate(
            flops=12 * rows * D * width, bytes_accessed=6 * D * width + rows * D * 8 + rows * width * 6,
            transcendentals=rows * width,
        ),
    )(rows_b, rows_g, weights)


def body(
    tokens,
    cotangent,
    destination,
    variate_ids,
    time_ids,
    seq_lengths,
    qkv_weight,
    out_weight,
    gate_up_weight,
    down_weight,
    norm_gains,
    qk_gains,
    variate_bias,
):
    core = lax.axis_index("core")
    low_core = core == 0
    y_at = lax.axis_index("y")
    zl_at = lax.axis_index("zl")

    core_scalar = core.reshape(1).astype(jnp.int32)

    def side_by_side(mine, other):
        return jnp.concatenate(
            [jnp.where(low_core, mine, other), jnp.where(low_core, other, mine)], axis=-1
        )

    feed_shard = jnp.concatenate([gate_up_weight, down_weight.T[None]], 0)

    slot = destination % ROWS
    group_at = destination // GROUP
    block_at = (destination % GROUP) // ROWS
    device_at = ((group_at // 2) * 2 + block_at // 4) * 8 + (block_at % 4) * 2 + group_at % 2
    key = device_at * ROWS + slot
    zero = jnp.zeros_like(slot)
    facts = jnp.stack([key, slot, variate_ids, time_ids // 32, time_ids % 32, zero, zero, zero])
    gains_row = jnp.pad(
        norm_gains.reshape(8, 16), ((0, 0), (GAIN_LANE, WIDE - GAIN_LANE - 16))
    ).astype(F32)
    outgoing, deal = deal_rows(tokens, cotangent, facts.astype(F32), gains_row)
    arrived = lax.all_to_all(outgoing.reshape(DEVICES, 8, SPAN), ALL, 0, 0, tiled=True)
    attn_shard = jnp.concatenate([qkv_weight, out_weight.T[None]], 0)
    lengths_other = swap_core(seq_lengths)
    lengths = jnp.where(zl_at == core, seq_lengths, lengths_other)[0]
    bias_here, outgoing = lax.optimization_barrier((variate_bias, outgoing))
    bias_other = lax.ppermute(bias_here, "zl", [(0, 1), (1, 0)])
    bias_pair = jnp.where(zl_at == core, variate_bias, bias_other)
    attn_shard, bias_other = lax.optimization_barrier((attn_shard, bias_other))
    attn_mine = gather_round(attn_shard, ("zh", "zl"), lax.axis_index("zh") * 2 + zl_at)
    attn_mine, arrived = lax.optimization_barrier((attn_mine, arrived))
    attn_mine = jnp.stack(gather_ahead(attn_mine, "x")).reshape((16,) + attn_shard.shape)


    arrived, lengths, bias_pair = lax.optimization_barrier((arrived, lengths, bias_pair))
    all_gains = arrived.reshape(16, 8, 8, SPAN)[:, 0, :, PAIR + GAIN_LANE : PAIR + GAIN_LANE + 16]
    inputs, grad_rows, attn_in, place, gains = receive(
        arrived.reshape(4 * ROWS, SPAN), all_gains.reshape(16, WIDE)
    )
    feed_shard, attn_in = lax.optimization_barrier((feed_shard, attn_in))
    feed_mine = flat_gather(feed_shard)
    zero_at = jnp.zeros((1,), jnp.int32)
    x_at = lax.axis_index("x").reshape(1).astype(jnp.int32)
    ahead, behind = ring(attn_in, -1), ring(attn_in, 1)
    far_top, far_low = ring(ahead[: ROWS // 2], -1), ring(behind[ROWS // 2 :], 1)
    far_top, far_low, attn_mine = lax.optimization_barrier((far_top, far_low, attn_mine))
    attn_w = assemble(core_scalar, x_at, attn_mine, swap_core(attn_mine))
    attn_all = [attn_in, ahead, jnp.concatenate([far_top, far_low], 0), behind]
    out_w = gather_direct(attn_w[3])

    blocks_y = (y_at + jnp.arange(RING)) % RING
    blocks = jnp.concatenate([core * RING + blocks_y, (1 - core) * RING + blocks_y])
    at = jnp.concatenate([blocks * ROWS, jnp.cumsum(lengths)]).astype(jnp.int32)

    inverse = THETA ** (-2.0 * jnp.arange(HALF).astype(F32) / HEAD_DIM)
    freq = jnp.concatenate(
        [
            jnp.tile(inverse, 8)[None],
            jnp.tile(qk_gains, (1, 4)),
            jnp.zeros((5, 2 * WIDE), F32),
        ]
    )
    qkv_mine, qkv_send, raw, facts_all = project(core_scalar, attn_all, attn_w, freq)
    facts_other = swap_core(facts_all)
    qkv_got = swap_core(qkv_send)

    bias_parts = jnp.stack(pieces(bias_pair * LOG2E, 3)).astype(F32)
    bias_rows = jnp.repeat(bias_parts, VARIATES, axis=0).transpose(1, 2, 0)
    bias_rows = jnp.pad(bias_rows, ((0, 0), (0, 0), (0, HEAD_DIM - 3 * VARIATES))).reshape(2, WIDE)
    bias_rows = jnp.pad(bias_rows, ((0, 6), (0, 0)))
    attended, att_near, att_send, query_back, key_tail = attend(
        at, qkv_mine, qkv_got, facts_all, facts_other, bias_rows
    )
    att_send, feed_mine, out_w, grad_rows = lax.optimization_barrier(
        (att_send, feed_mine, out_w, grad_rows)
    )
    grad_all = gather_direct(grad_rows)
    att_other = swap_core(att_send)
    att_plane = side_by_side(att_near, att_other).reshape(RING, ROWS, 2 * WIDE)
    att_rows = trade_ring([att_plane[r] for r in range(RING)])
    att_rows, feed_mine, grad_all = lax.optimization_barrier((att_rows, feed_mine, grad_all))
    feed_w = assemble(core_scalar, zero_at, feed_mine, swap_core(feed_mine))
    hidden_one, feed_in = out_project(att_rows, out_w, inputs, gains)

    ahead, behind = ring(feed_in, -1), ring(feed_in, 1)
    fed_own = feed(feed_in, grad_all[0], feed_w)
    ahead, behind, fed_own = lax.optimization_barrier((ahead, behind, fed_own))
    far_top, far_low = ring(ahead[: ROWS // 2], -1), ring(behind[ROWS // 2 :], 1)
    fed_ahead = feed(ahead, grad_all[1], feed_w)
    fed_behind = feed(behind, grad_all[3], feed_w)
    far_top, far_low, fed_ahead, fed_behind = lax.optimization_barrier(
        (far_top, far_low, fed_ahead, fed_behind)
    )
    far = jnp.concatenate([far_top, far_low], 0)
    fed_far = feed(far, grad_all[2], feed_w)
    feed_all = [feed_in, ahead, far, behind]
    fed = [fed_own, fed_ahead, fed_far, fed_behind]
    feed_split = weight_grads(core_scalar, feed_all, grad_all, [f[2] for f in fed], 2, 2)
    db_got = send_ring([f[1] for f in fed], True)
    db_got, feed_split = lax.optimization_barrier((db_got, feed_split))
    grad_one, gain_two_grad, d_att, *both = middle(
        att_rows, out_w, [f[0] for f in fed], fed_own[1], db_got, hidden_one, grad_rows, gains
    )
    feed_total = chip_total(feed_split)
    feed_got = trade(feed_total, "x")

    grad_att = trade_ring([d_att[r] for r in range(RING)])
    grad_att[1], feed_total = lax.optimization_barrier((grad_att[1], feed_total))
    grad_att = jnp.concatenate(grad_att, 0)
    both, grad_att = lax.optimization_barrier((both, grad_att))
    both_got = send_ring(both)
    grad_left, grad_right = grad_att[:, :WIDE], grad_att[:, WIDE:]
    grad_other = swap_core(jnp.where(low_core, grad_right, grad_left))
    grad_near = jnp.where(low_core, grad_left, grad_right)
    d_keep, d_send, bias_sums = attend_back(
        qkv_mine, qkv_got, query_back, key_tail, grad_near, grad_other, attended
    )
    first_part = (jnp.arange(HEAD_DIM) < VARIATES)[None, None]
    bias_sums = jnp.where(first_part, bias_sums[:2].reshape(2, 2, HEAD_DIM), 0.0)
    bias_sums = jnp.sum(bias_sums, axis=2)
    bias_part = jnp.stack([bias_sums[0], bias_sums[1] - bias_sums[0]])
    d_got = swap_core(d_send)
    grad_proj, qk_sums, *in_part = unproject(
        core_scalar, d_keep, d_got, raw, facts_all, attn_w, freq
    )
    in_got = send_ring(in_part)
    feed_half = added(feed_got).astype(BF16)
    in_got[0], feed_half = lax.optimization_barrier((in_got[0], feed_half))
    grad_proj, both_got = lax.optimization_barrier((grad_proj, both_got))
    both_sum = add_ring(both[0], both_got)
    mixed = (hidden_one + both_sum[:ROWS]).astype(BF16)
    out_full = both_sum[ROWS:].astype(BF16)
    attn_split = weight_grads(core_scalar, attn_all, [out_full], [grad_proj], None, 1)
    attn_total = chip_total(attn_split)
    in_got, _ = lax.optimization_barrier((in_got, attn_split))
    mixed, _ = lax.optimization_barrier((mixed, attn_total))
    feed_got = trade(feed_half, ("zh", "zl"))
    attn_own, attn_got = send_round(attn_total.reshape((RING, RING) + attn_total.shape[1:]), "x")
    qk_sums = jnp.sum(qk_sums[:2].reshape(2, 4, HEAD_DIM), axis=1)

    small = jnp.zeros((8, WIDE), F32).at[0].set(qk_sums.reshape(WIDE))
    small = small.at[1, :4].set(bias_part.reshape(4))
    tensor_at = (y_at * 2 + core).reshape(1).astype(jnp.int32)
    last = finish(
        in_part[0], in_got, inputs, grad_one, mixed, place, gains, gain_two_grad, small, tensor_at
    )
    last = last.reshape(DEVICES, 8, 2 * QUARTER + WIDE)
    last, attn_got, feed_got = lax.optimization_barrier((last, attn_got, feed_got))
    home = lax.all_to_all(last, ALL, 0, 0, tiled=True)
    own, got = send_round(add_round(attn_own, attn_got).astype(BF16), ("zh", "zl"))
    home, got = lax.optimization_barrier((home, got))
    attn_grad = add_round(own, got)
    feed_grad = added(feed_got).reshape(3, 64, 512)
    new_tokens, token_grads, sums = settle(home.reshape(4 * ROWS, 2 * QUARTER + WIDE), deal)
    gains_grad = sums[0].reshape(2, 64)
    qk_grad = sums[1].reshape(2, 64)
    bias_grad = sums[2, :4].reshape(2, 2)

    return (
        new_tokens,
        token_grads,
        attn_grad[:3],
        attn_grad[3].T,
        feed_grad[:2],
        feed_grad[2].T,
        gains_grad,
        qk_grad,
        bias_grad,
    )


def solution(mesh):
    fine = Mesh(mesh.devices.reshape(4, 2, 2, 4, 2), ALL)
    dp = ("x", "zh", "core")
    tensor = ("y", "zl")
    in_specs = (
        P(ALL, None),
        P(ALL, None),
        P(ALL),
        P(ALL),
        P(ALL),
        P(dp, None),
        P(None, dp, tensor),
        P(tensor, dp),
        P(None, dp, tensor),
        P(tensor, dp),
        P(None, dp),
        P(),
        P(None, tensor),
    )
    out_specs = (
        P(ALL, None),
        P(ALL, None),
        P(None, dp, tensor),
        P(tensor, dp),
        P(None, dp, tensor),
        P(tensor, dp),
        P(None, dp),
        P(),
        P(None, tensor),
    )
    return jax.shard_map(body, mesh=fine, in_specs=in_specs, out_specs=out_specs, check_vma=False)
```

```python
import functools

import jax
import jax.numpy as jnp
from jax import lax
from jax.experimental import pallas as pl
from jax.experimental.pallas import tpu as pltpu
from jax.sharding import Mesh
from jax.sharding import PartitionSpec as P

HEADS = 16
HEAD_DIM = 64
HALF = HEAD_DIM // 2
D = 1024
FF = 4096
ROWS = 256
RING = 4
PLANE = ROWS * RING
GROUP = 2 * PLANE
DEVICES = 128
VARIATES = 8
SEQS = 4
WIDE = 128
EPS = 1e-06
THETA = 10000.0
LOG2E = 1.4426950408889634
FAR = -16384.0
F32 = jnp.float32
BF16 = jnp.bfloat16

ALL = ("x", "zh", "core", "y", "zl")
FLAT = ("x", "zh", "zl")
NT = (((1,), (1,)), ((), ()))
TN = (((0,), (0,)), ((), ()))


def mm(left, right, dims=(((1,), (0,)), ((), ()))):
    return lax.dot_general(left, right, dims, preferred_element_type=F32)


def root_stats(values):
    return lax.rsqrt(jnp.mean(values * values, axis=-1, keepdims=True) + EPS)


def norm_back(grad_in, normed, scale_inv):
    return scale_inv * (grad_in - normed * jnp.mean(grad_in * normed, axis=-1, keepdims=True))


def pieces(values, count):
    out = []
    for _ in range(count):
        part = lax.reduce_precision(values, 8, 7)
        out.append(part.astype(BF16))
        values = values - part
    return out


def ring(values, step):
    return lax.ppermute(values, "y", [(i, (i + step) % RING) for i in range(RING)])


def swap_core(values):
    return lax.ppermute(values, "core", [(0, 1), (1, 0)])


def gather_ring(values):
    ahead = ring(values, -1)
    behind = ring(values, 1)
    half = values.shape[0] // 2
    far_top = ring(ahead[:half], -1)
    far_low = ring(behind[half:], 1)
    return [values, ahead, jnp.concatenate([far_top, far_low], 0), behind]


def gather_direct(values):
    return [values, ring(values, -1), ring(values, 2), ring(values, 1)]


def trade_ring(parts):
    return [parts[0]] + [ring(parts[RING - s], -s) for s in range(1, RING)]


def send_ring(parts, halves=False):
    half = parts[2].shape[0] // 2
    far = [parts[2][:half], parts[2][half:]] if halves else [parts[2]]
    return [ring(parts[1], 1), ring(parts[3], -1)] + [ring(v, 2) for v in far]


def add_ring(own, got):
    far = got[2] if len(got) == 3 else jnp.concatenate(got[2:], 0)
    return own.astype(F32) + got[0].astype(F32) + got[1].astype(F32) + far.astype(F32)


def gather_ahead(values, axes):
    moves = [[((i + r) % RING, i) for i in range(RING)] for r in range(RING)]
    return [values] + [lax.ppermute(values, axes, moves[r]) for r in range(1, RING)]


def gather_round(values, axes, at):
    return jnp.roll(jnp.stack(gather_ahead(values, axes)), at, axis=0)


def assemble_kernel(at_ref, mine_ref, other_ref, out_ref):
    core = at_ref[0]
    count, _, depth, width = mine_ref.shape
    for ref, side in ((mine_ref, core), (other_ref, 1 - core)):
        for i in range(count):
            at = (i // 2) * 2 * depth + side * depth
            rows = pl.ds(pl.multiple_of(at, depth), depth)
            out_ref[:, rows, (i % 2) * width : (i % 2 + 1) * width] = ref[i]


def assemble(core, x_at, mine, other):
    _, kinds, depth, width = mine.shape
    pair = pl.BlockSpec((4, kinds, depth, width), lambda p, at: (p, 0, 0, 0))
    return pl.pallas_call(
        assemble_kernel,
        grid_spec=pltpu.PrefetchScalarGridSpec(
            num_scalar_prefetch=1,
            grid=(RING,),
            in_specs=[pair, pair],
            out_specs=pl.BlockSpec(
                (kinds, 4 * depth, 2 * width), lambda p, at: (0, lax.rem(at[1] + p, RING), 0)
            ),
        ),
        out_shape=jax.ShapeDtypeStruct((kinds, 16 * depth, 2 * width), BF16),
        compiler_params=pltpu.CompilerParams(vmem_limit_bytes=28 * 2**20),
        cost_estimate=pl.CostEstimate(
            flops=0, bytes_accessed=kinds * 128 * depth * width, transcendentals=0
        ),
    )(jnp.concatenate([core, x_at]), mine, other)


def chip_total(split):
    return (split[0].astype(F32) + swap_core(split[1]).astype(F32)).astype(BF16)


def send_round(values, axes):
    at = lax.axis_index(axes)
    parts = [lax.dynamic_index_in_dim(values, (at + r) % RING, 0, keepdims=False) for r in range(RING)]
    moves = [[(i, (i + r) % RING) for i in range(RING)] for r in range(RING)]
    return parts[0], [lax.ppermute(parts[r], axes, moves[r]) for r in (1, 3, 2)]


def add_round(own, got):
    return sum((v.astype(F32) for v in got), own.astype(F32))


def trade(values, axes):
    return lax.all_to_all(values.reshape((RING, -1) + values.shape[1:]), axes, 0, 0, tiled=True)


def added(got):
    return jnp.sum(got.astype(F32), axis=0)


def lanes_of(shape):
    return lax.broadcasted_iota(jnp.int32, shape, 1)


QUARTER = D // RING
PAIR = 2 * QUARTER
SPAN = PAIR + WIDE
GAIN_LANE = 16


def deal_kernel(tok_ref, cot_ref, facts_ref, gains_ref, out_ref, deal_ref):
    wide = jnp.concatenate([facts_ref[...], jnp.zeros((WIDE - 8, ROWS), F32)], 0)
    facts = jnp.transpose(wide)
    keys = facts_ref[0:1, :]
    rank = jnp.sum((facts[:, 0:1] < keys).astype(F32), axis=0, keepdims=True)
    at = lax.broadcasted_iota(jnp.int32, (ROWS, ROWS), 0).astype(F32)
    deal_ref[...] = (at == rank).astype(BF16)
    low = jnp.where(lanes_of(facts.shape) == 0, 0.0, facts).astype(BF16)
    row = lax.broadcasted_iota(jnp.int32, (4 * ROWS, 1), 0)
    own = ((row // RING).astype(F32) == rank).astype(BF16)
    part = None
    for m in range(RING):
        cols = slice(m * QUARTER, (m + 1) * QUARTER)
        here = mm(own, jnp.concatenate([tok_ref[:, cols], cot_ref[:, cols]], 1))
        part = here if m == 0 else jnp.where(row % RING == m, here, part)
    out_ref[:, :PAIR] = part.astype(BF16)
    tail = mm(own, low)
    lane = lanes_of(tail.shape)
    gains = jnp.broadcast_to(gains_ref[...][None], (DEVICES, 8, WIDE)).reshape(tail.shape)
    tail = jnp.where((lane >= GAIN_LANE) & (lane < GAIN_LANE + 16), gains, tail)
    out_ref[:, PAIR:] = tail.astype(BF16)


def deal_rows(tokens, cotangent, facts, gains):
    return pl.pallas_call(
        deal_kernel,
        out_shape=[
            jax.ShapeDtypeStruct((4 * ROWS, SPAN), BF16),
            jax.ShapeDtypeStruct((ROWS, ROWS), BF16),
        ],
        compiler_params=pltpu.CompilerParams(vmem_limit_bytes=48 * 2**20),
        cost_estimate=pl.CostEstimate(
            flops=8 * ROWS * ROWS * 2304, bytes_accessed=ROWS * D * 16, transcendentals=0
        ),
    )(tokens, cotangent, facts, gains)


def receive_kernel(rows_ref, gains_ref, x_ref, g_ref, a_ref, place_ref, gain_ref):
    count = 4 * ROWS
    facts = rows_ref[:, PAIR:]
    slots = jnp.transpose(facts.astype(F32))[1:2, :]
    at = lax.broadcasted_iota(jnp.int32, (ROWS, count), 0)
    arrival = lanes_of((ROWS, count))
    here = at.astype(F32) == slots
    gains = gains_ref[...].astype(F32)
    turned = pltpu.roll(gains, HEAD_DIM, 1)
    left = lanes_of((1, WIDE)) < HEAD_DIM
    one, two = [], []
    for c in range(D // WIDE):
        even, odd = slice(2 * c, 2 * c + 1), slice(2 * c + 1, 2 * c + 2)
        one.append(jnp.where(left, gains[even], turned[odd]))
        two.append(jnp.where(left, turned[even], gains[odd]))
    gain_one = jnp.concatenate(one, 1)
    gain_ref[...] = jnp.zeros_like(gain_ref)
    gain_ref[0:1, :] = gain_one
    gain_ref[1:2, :] = jnp.concatenate(two, 1)
    quarters = []
    for m in range(RING):
        chosen = (here & (arrival % RING == m)).astype(BF16)
        both = mm(chosen, rows_ref[:, :PAIR])
        quarters.append(both[:, :QUARTER])
        g_ref[:, m * QUARTER : (m + 1) * QUARTER] = both[:, QUARTER:].astype(BF16)
        if m == 0:
            a_ref[:, D:] = mm(chosen, facts).astype(BF16)
            pick = (at * RING == arrival).astype(BF16)
            place_ref[...] = mm(chosen, pick, NT).astype(BF16)
    rows = jnp.concatenate(quarters, 1)
    x_ref[...] = rows
    a_ref[:, :D] = (rows * root_stats(rows) * gain_one).astype(BF16)


def receive(rows, gains):
    return pl.pallas_call(
        receive_kernel,
        out_shape=[
            jax.ShapeDtypeStruct((ROWS, D), F32),
            jax.ShapeDtypeStruct((ROWS, D), BF16),
            jax.ShapeDtypeStruct((ROWS, D + WIDE), BF16),
            jax.ShapeDtypeStruct((ROWS, ROWS), BF16),
            jax.ShapeDtypeStruct((8, D), F32),
        ],
        compiler_params=pltpu.CompilerParams(vmem_limit_bytes=48 * 2**20),
        cost_estimate=pl.CostEstimate(
            flops=16 * ROWS * ROWS * D, bytes_accessed=ROWS * D * 24, transcendentals=0
        ),
    )(rows, gains)


OUT_KIND = 3


def out_kernel(*refs):
    att = refs[:RING]
    w_ref, x_ref, gain_ref, h_ref, b_ref = refs[RING:]
    hidden = x_ref[...]
    for r in range(RING):
        hidden = hidden + mm(att[r][...], w_ref[OUT_KIND + r], NT)
    h_ref[...] = hidden
    b_ref[...] = (hidden * root_stats(hidden) * gain_ref[1:2, :]).astype(BF16)


def out_project(att, weights, rows, gains):
    return pl.pallas_call(
        out_kernel,
        out_shape=[jax.ShapeDtypeStruct((ROWS, D), F32), jax.ShapeDtypeStruct((ROWS, D), BF16)],
        compiler_params=pltpu.CompilerParams(vmem_limit_bytes=48 * 2**20),
        cost_estimate=pl.CostEstimate(
            flops=2 * ROWS * D * D, bytes_accessed=2 * D * D + ROWS * D * 14, transcendentals=0
        ),
    )(*att, weights, rows, gains)


def middle_kernel(*refs):
    att, y_parts, w_ref = refs[:RING], refs[RING : 2 * RING], refs[2 * RING]
    refs = refs[2 * RING + 1 :]
    own_ref, near_ref, back_ref, top_ref, low_ref, h_ref, g_ref, gain_ref = refs[:8]
    grad_ref, two_ref, d_ref = refs[8:11]
    both_refs = refs[11:]
    far = jnp.concatenate([top_ref[...], low_ref[...]], 0).astype(F32)
    grad = own_ref[...].astype(F32) + near_ref[...].astype(F32) + back_ref[...].astype(F32) + far
    hidden = h_ref[...]
    scale = root_stats(hidden)
    normed = hidden * scale
    two_ref[...] = jnp.zeros_like(two_ref)
    two_ref[0:1, :] = jnp.sum(grad * normed, axis=0, keepdims=True)
    scaled = grad * gain_ref[1:2, :]
    grad = g_ref[...].astype(F32) + norm_back(scaled, normed, scale)
    grad_ref[...] = grad
    low = grad.astype(BF16)
    for r in range(RING):
        d_ref[r] = mm(low, w_ref[OUT_KIND + r]).astype(BF16)
        both_refs[r][:ROWS] = y_parts[r][...]
        both_refs[r][ROWS:] = mm(att[r][...], low, TN).astype(BF16)


def middle(att, weights, y_parts, own, got, hidden, grad_rows, gains):
    both = jax.ShapeDtypeStruct((2 * ROWS, D), BF16)
    return pl.pallas_call(
        middle_kernel,
        out_shape=[
            jax.ShapeDtypeStruct((ROWS, D), F32),
            jax.ShapeDtypeStruct((8, D), F32),
            jax.ShapeDtypeStruct((RING, ROWS, ROWS), BF16),
        ]
        + [both] * RING,
        compiler_params=pltpu.CompilerParams(vmem_limit_bytes=48 * 2**20),
        cost_estimate=pl.CostEstimate(
            flops=4 * ROWS * D * D, bytes_accessed=2 * D * D + ROWS * D * 40, transcendentals=0
        ),
    )(*att, *y_parts, weights, own, *got, hidden, grad_rows, gains)


def finish_kernel(
    own_ref, near_ref, back_ref, far_ref, x_ref, grad_ref, mixed_ref, place_ref,
    gain_ref, two_ref, small_ref, at_ref, out_ref,
):
    rows = x_ref[...]
    scale = root_stats(rows)
    normed = rows * scale
    far = far_ref[...].astype(F32)
    grad = own_ref[...].astype(F32) + near_ref[...].astype(F32) + back_ref[...].astype(F32) + far
    one = jnp.sum(grad * normed, axis=0, keepdims=True)
    two = two_ref[0:1, :]
    scaled = grad * gain_ref[0:1, :]
    back = scale * (scaled - normed * jnp.mean(scaled * normed, axis=1, keepdims=True))
    result = (grad_ref[...] + back).astype(BF16)
    count = 4 * ROWS
    row = lax.broadcasted_iota(jnp.int32, (count, 1), 0)
    quarter = row % RING
    pick = (row // RING == lanes_of((count, ROWS))).astype(BF16)
    pick = mm(pick, place_ref[...], NT).astype(BF16)
    part = None
    for m in range(RING):
        cols = slice(m * QUARTER, (m + 1) * QUARTER)
        here = mm(pick, jnp.concatenate([mixed_ref[:, cols], result[:, cols]], 1))
        part = here if m == 0 else jnp.where(quarter == m, here, part)
    out_ref[:, : 2 * QUARTER] = part.astype(BF16)
    left = lanes_of((1, WIDE)) < HEAD_DIM
    tiles = []
    for c in range(D // WIDE):
        cols = slice(c * WIDE, (c + 1) * WIDE)
        a, b = one[:, cols], two[:, cols]
        even = jnp.where(left, a, pltpu.roll(jnp.broadcast_to(b, (8, WIDE)), HEAD_DIM, 1)[0:1])
        odd = jnp.where(left, pltpu.roll(jnp.broadcast_to(a, (8, WIDE)), HEAD_DIM, 1)[0:1], b)
        tiles += [jnp.broadcast_to(even, (64, WIDE)), jnp.broadcast_to(odd, (64, WIDE))]
    value = jnp.concatenate(tiles, 0)
    value = jnp.where(quarter == 1, small_ref[0:1, :], value)
    bias = jnp.where((row // 8) % 8 == at_ref[0], small_ref[1:2, :], 0.0)
    value = jnp.where(quarter == 2, bias, value)
    high = value.astype(BF16).astype(F32)
    value = jnp.where((row // RING) % 2 == 0, high, value - high)
    out_ref[:, 2 * QUARTER :] = value.astype(BF16)


def finish(own, got, rows, grad, mixed, place, gains, two, small, at):
    specs = [pl.BlockSpec(memory_space=pltpu.VMEM)] * 11
    return pl.pallas_call(
        finish_kernel,
        in_specs=specs + [pl.BlockSpec(memory_space=pltpu.SMEM)],
        out_shape=jax.ShapeDtypeStruct((4 * ROWS, 2 * QUARTER + WIDE), BF16),
        compiler_params=pltpu.CompilerParams(vmem_limit_bytes=48 * 2**20),
        cost_estimate=pl.CostEstimate(
            flops=16 * ROWS * ROWS * D, bytes_accessed=ROWS * D * 20, transcendentals=0
        ),
    )(own, *got, rows, grad, mixed, place, gains, two, small, at)


def settle_kernel(home_ref, deal_ref, rows_ref, grads_ref, sums_ref):
    deal = deal_ref[...]
    shape = (ROWS, 4 * ROWS)
    index = lax.broadcasted_iota(jnp.int32, shape, 0)
    for m in range(RING):
        pick = (index * RING + m == lanes_of(shape)).astype(BF16)
        here = mm(pick, home_ref[:, : 2 * QUARTER]).astype(BF16)
        here = mm(deal, here, TN).astype(BF16)
        cols = slice(m * QUARTER, (m + 1) * QUARTER)
        rows_ref[:, cols] = here[:, :QUARTER]
        grads_ref[:, cols] = here[:, QUARTER:]
    small = home_ref[:, 2 * QUARTER :].astype(F32)
    quarter = lax.broadcasted_iota(jnp.int32, small.shape, 0) % RING
    sums_ref[...] = jnp.zeros_like(sums_ref)
    for m in range(3):
        sums_ref[m : m + 1, :] = jnp.sum(jnp.where(quarter == m, small, 0.0), axis=0, keepdims=True)


def settle(home, deal):
    low = jax.ShapeDtypeStruct((ROWS, D), BF16)
    return pl.pallas_call(
        settle_kernel,
        out_shape=[low, low, jax.ShapeDtypeStruct((8, WIDE), F32)],
        compiler_params=pltpu.CompilerParams(vmem_limit_bytes=48 * 2**20),
        cost_estimate=pl.CostEstimate(
            flops=20 * ROWS * ROWS * D, bytes_accessed=ROWS * D * 16, transcendentals=0
        ),
    )(home, deal)


def weight_grad_kernel(core_ref, *refs, parts, count, switch, steps):
    given = switch is None
    lefts, others, rights = refs[:parts], refs[parts : parts + count], refs[parts + count : -3]
    keep_ref, send_ref, turned_ref = refs[-3:]
    low = core_ref[0] == 0
    step = pl.program_id(0)

    def load(sides):
        at = 0
        for side in sides:
            rows = side.shape[0]
            turned_ref[:, at : at + rows] = side[...].T
            at += rows

    @pl.when(step == 0)
    def _():
        load(lefts)

    if not given:

        @pl.when(step == switch * steps)
        def _():
            load(others)

    def emit(total):
        depth = total.shape[0] // 16
        width = keep_ref.shape[-1]
        for z in range(total.shape[1] // width):
            cols = slice(z * width, (z + 1) * width)
            for p in range(8):
                at = 2 * p * depth
                even, odd = total[at : at + depth, cols], total[at + depth : at + 2 * depth, cols]
                keep_ref[p, z, 0] = jnp.where(low, even, odd)
                send_ref[p, z, 0] = jnp.where(low, odd, even)

    def product():
        right = jnp.concatenate([ref[0] for ref in rights], 0)
        emit(mm(turned_ref[...], right).astype(BF16))

    if given:
        pl.when(step < pl.num_programs(0) - 1)(product)

        @pl.when(step == pl.num_programs(0) - 1)
        def _():
            emit(others[0][...].T)
    else:
        product()


def weight_grads(core, lefts, others, rights, switch, steps):
    parts = len(lefts)
    made, _, width = rights[0].shape
    kinds = made + 1 if switch is None else made
    block, half = width // steps, width // 2
    sides = [pl.BlockSpec((v.shape[0], D), lambda s: (0, 0)) for v in list(lefts) + list(others)]
    moving = [
        pl.BlockSpec(
            (1, v.shape[1], block), lambda s: (jnp.minimum(s // steps, made - 1), 0, s % steps)
        )
        for v in rights
    ]
    rows = sum(v.shape[1] for v in rights)
    out = pl.pallas_call(
        functools.partial(
            weight_grad_kernel, parts=parts, count=len(others), switch=switch, steps=steps
        ),
        grid=(kinds * steps,),
        in_specs=[pl.BlockSpec(memory_space=pltpu.SMEM)] + sides + moving,
        out_specs=[
            pl.BlockSpec((8, 2 // steps, 1, 64, half), lambda s: (0, s % steps, s // steps, 0, 0))
        ]
        * 2,
        out_shape=[jax.ShapeDtypeStruct((8, 2, kinds, 64, half), BF16)] * 2,
        scratch_shapes=[pltpu.VMEM((D, rows), BF16)],
        compiler_params=pltpu.CompilerParams(vmem_limit_bytes=48 * 2**20),
        cost_estimate=pl.CostEstimate(
            flops=2 * kinds * rows * D * width,
            bytes_accessed=2 * kinds * D * width + 4 * rows * D + 2 * kinds * rows * width,
            transcendentals=0,
        ),
    )(core, *lefts, *others, *rights)
    return [v.reshape(16, kinds, 64, half) for v in out]


def head_sums(values):
    wide = values.shape[1]
    row = lax.broadcasted_iota(jnp.int32, (wide, wide), 0) // HEAD_DIM
    same = (row == lanes_of((wide, wide)) // HEAD_DIM).astype(BF16)
    high = values.astype(BF16)
    low = (values - high.astype(F32)).astype(BF16)
    return mm(high, same) + mm(low, same)


def partner(values):
    wide = values.shape[1]
    first = lanes_of(values.shape) % HEAD_DIM < HALF
    return jnp.where(first, pltpu.roll(values, wide - HALF, 1), pltpu.roll(values, HALF, 1))


def angles_of(facts, freq_ref):
    facts = facts.astype(F32)
    times = facts[:, 3:4] * 32.0 + facts[:, 4:5]
    angle = times * freq_ref[0:1, :WIDE]
    first = lanes_of(angle.shape) % HEAD_DIM < HALF
    cosine = jnp.cos(angle)
    sine = jnp.sin(angle)
    sine = jnp.where(first, -sine, sine)
    return jnp.concatenate([cosine, cosine], 1), jnp.concatenate([sine, sine], 1)


def project_kernel(core_ref, *refs):
    pieces_in = refs[:RING]
    w_ref, freq_ref, mine_ref, send_ref, raw_ref, facts_ref = refs[RING:]
    low = core_ref[0] == 0
    for r in range(RING):
        block = slice(r * ROWS, (r + 1) * ROWS)
        rows = pieces_in[r][:, :D]
        facts = pieces_in[r][:, D:]
        facts_ref[block] = facts
        cosine, sine = angles_of(facts, freq_ref)
        for kind in range(3):
            value = mm(rows, w_ref[kind])
            if kind < 2:
                raw_ref[kind, block] = value
                unit = value * lax.rsqrt(head_sums(value * value) * (1.0 / HEAD_DIM) + EPS)
                value = unit * freq_ref[1 + kind : 2 + kind, :]
                value = value * cosine + partner(value) * sine
            if kind == 0:
                value = value * (HEAD_DIM ** (-0.5) * LOG2E)
            left, right = value[:, :WIDE], value[:, WIDE:]
            mine_ref[kind, block] = jnp.where(low, left, right).astype(BF16)
            send_ref[kind, block] = jnp.where(low, right, left).astype(BF16)


def project(core, rows, attn_w, freq):
    low = jax.ShapeDtypeStruct((3, PLANE, WIDE), BF16)

    def whole(v):
        return pl.BlockSpec(v.shape, lambda i: (0,) * v.ndim)

    shapes = [
        low,
        low,
        jax.ShapeDtypeStruct((2, PLANE, 2 * WIDE), F32),
        jax.ShapeDtypeStruct((PLANE, WIDE), BF16),
    ]
    return pl.pallas_call(
        project_kernel,
        grid=(1,),
        in_specs=[pl.BlockSpec(memory_space=pltpu.SMEM)]
        + [whole(v) for v in rows]
        + [pl.BlockSpec((3, D, 2 * WIDE), lambda i: (0, 0, 0)), whole(freq)],
        out_specs=[whole(v) for v in shapes],
        out_shape=shapes,
        compiler_params=pltpu.CompilerParams(vmem_limit_bytes=48 * 2**20),
        cost_estimate=pl.CostEstimate(
            flops=8 * PLANE * D * 2 * WIDE, bytes_accessed=PLANE * D * 8, transcendentals=PLANE * 1024
        ),
    )(core, *rows, attn_w, freq)


def unproject_kernel(core_ref, mine_ref, got_ref, raw_ref, facts_ref, w_ref, freq_ref, dp_ref, gain_ref, *part_refs):
    low = core_ref[0] == 0
    gains = [0.0, 0.0]
    for r in range(RING):
        block = slice(r * ROWS, (r + 1) * ROWS)
        cosine, sine = angles_of(facts_ref[block], freq_ref)
        total = None
        for kind in range(3):
            mine, got = mine_ref[kind, block], got_ref[kind, block]
            grad = jnp.concatenate([jnp.where(low, mine, got), jnp.where(low, got, mine)], 1)
            if kind < 2:
                grad = grad.astype(F32)
                if kind == 0:
                    grad = grad * (HEAD_DIM ** (-0.5))
                raw = raw_ref[kind, block]
                inv = lax.rsqrt(head_sums(raw * raw) * (1.0 / HEAD_DIM) + EPS)
                unit = raw * inv
                grad = grad * cosine - partner(grad) * sine
                gains[kind] += jnp.sum(grad * unit, axis=0, keepdims=True)
                scaled = grad * freq_ref[1 + kind : 2 + kind, :]
                mean = head_sums(scaled * unit) * (1.0 / HEAD_DIM)
                grad = (inv * (scaled - unit * mean)).astype(BF16)
            dp_ref[kind, block] = grad
            part = mm(grad, w_ref[kind], NT)
            total = part if total is None else total + part
        part_refs[r][...] = total.astype(BF16)
    gain_ref[...] = jnp.zeros_like(gain_ref)
    gain_ref[0:1, :] = gains[0]
    gain_ref[1:2, :] = gains[1]


def unproject(core, mine, got, raw, facts, attn_w, freq):
    three = pl.BlockSpec((3, D, 2 * WIDE), lambda i: (0, 0, 0))

    def whole(v):
        return pl.BlockSpec(v.shape, lambda i: (0,) * v.ndim)

    shapes = [
        jax.ShapeDtypeStruct((3, PLANE, 2 * WIDE), BF16),
        jax.ShapeDtypeStruct((8, 2 * WIDE), F32),
    ] + [jax.ShapeDtypeStruct((ROWS, D), BF16)] * RING
    return pl.pallas_call(
        unproject_kernel,
        grid=(1,),
        in_specs=[pl.BlockSpec(memory_space=pltpu.SMEM)]
        + [whole(v) for v in (mine, got, raw, facts)]
        + [three, whole(freq)],
        out_specs=[whole(v) for v in shapes],
        out_shape=shapes,
        compiler_params=pltpu.CompilerParams(vmem_limit_bytes=48 * 2**20),
        cost_estimate=pl.CostEstimate(
            flops=8 * PLANE * D * 2 * WIDE, bytes_accessed=PLANE * D * 8, transcendentals=PLANE * 1024
        ),
    )(core, mine, got, raw, facts, attn_w, freq)


LOG_LANE = 3 * VARIATES + SEQS


def with_pieces(base, values, first_lane, lanes):
    for i in range(3):
        part = values.astype(BF16).astype(F32)
        base = jnp.where(lanes == first_lane + i, part, base)
        values = values - part
    return base


def key_rows(mine_ref, got_ref, start, size):
    if start < PLANE:
        return mine_ref, slice(start, start + size)
    return got_ref, slice(start - PLANE, start - PLANE + size)


def value_lanes(rows):
    return (lanes_of((rows, WIDE)) < 3).astype(BF16)


def attend_kernel(
    at_ref, mine_ref, got_ref, own_ref, other_ref, bias_ref,
    att_ref, near_ref, send_ref, tail_ref, kt_ref, q_scr, qt_scr, *, chunks,
):
    step = pl.program_id(0)
    block = att_ref.shape[0]
    size = GROUP // chunks

    @pl.when(step == 0)
    def _():
        q_scr[:PLANE] = mine_ref[0]
        q_scr[PLANE:] = got_ref[0]
        lane = lanes_of((ROWS, WIDE))
        tail_lane = lane % HEAD_DIM
        bias_lane = tail_lane < 3 * VARIATES
        seg_lane = (tail_lane >= 3 * VARIATES) & (tail_lane < LOG_LANE)
        one_lane = (tail_lane >= LOG_LANE) & (tail_lane < LOG_LANE + 3)
        row = lax.broadcasted_iota(jnp.int32, (ROWS, WIDE), 0)
        for b in range(2 * RING):
            source = own_ref if b < RING else other_ref
            facts = source[(b % RING) * ROWS : (b % RING + 1) * ROWS, :].astype(F32)
            variate = facts[:, 2:3]
            equal = bias_lane & ((tail_lane % VARIATES).astype(F32) == variate)
            position = at_ref[b] + row
            segment = jnp.zeros_like(row)
            for j in range(SEQS):
                segment += (position >= at_ref[2 * RING + j]).astype(jnp.int32)
            inside = seg_lane & (tail_lane - 3 * VARIATES == segment)
            rows = slice(b * ROWS, (b + 1) * ROWS)
            qt_scr[rows] = (equal | inside).astype(BF16)
            tail = jnp.where(equal, bias_ref[0:1, :], bias_ref[1:2, :])
            tail = jnp.where(bias_lane, tail, jnp.where(one_lane, 1.0, 0.0))
            tail = jnp.where(seg_lane & ~inside, FAR, tail)
            kt_ref[rows] = tail.astype(BF16)

    here = pl.ds(pl.multiple_of(step * block, block), block)
    query_tail = qt_scr[here, :]
    query = jnp.concatenate([q_scr[here, :], query_tail], 1)
    zero = jnp.zeros_like(query)
    head_of = (lanes_of(query.shape) // HEAD_DIM) % 2
    lanes = lanes_of((block, WIDE))
    ones = value_lanes(size)
    out = None
    tail = query_tail.astype(F32)
    for head in range(2):
        masked = jnp.where(head_of == head, query, zero)
        total = None
        for c in range(chunks):
            rows = slice(c * size, (c + 1) * size)
            ref, at = key_rows(mine_ref, got_ref, c * size, size)
            keys = jnp.concatenate([ref[1, at, :], kt_ref[rows, :]], 1)
            values = jnp.concatenate([ref[2, at, :], ones], 1)
            prob = jnp.exp2(mm(masked, keys, NT)).astype(BF16)
            part = mm(prob, values)
            total = part if total is None else total + part
        row_sum = total[:, WIDE : WIDE + 1]
        now = total[:, :WIDE] / row_sum
        out = now if head == 0 else jnp.where(lanes < HEAD_DIM, out, now)
        tail = with_pieces(tail, -jnp.log2(row_sum), head * HEAD_DIM + LOG_LANE, lanes)
    att_ref[...] = out
    tail_ref[...] = tail.astype(BF16)
    low = out.astype(BF16)
    half = pl.num_programs(0) // 2

    @pl.when(step < half)
    def _():
        near_ref[here, :] = low

    @pl.when(step >= half)
    def _():
        send_ref[pl.ds(pl.multiple_of((step - half) * block, block), block), :] = low


def attend(at, mine, got, facts, facts_other, bias_rows):
    block = 512
    moving = pl.BlockSpec((block, WIDE), lambda i: (i, 0))
    plane = pl.BlockSpec((PLANE, WIDE), lambda i: (0, 0))
    three = pl.BlockSpec((3, PLANE, WIDE), lambda i: (0, 0, 0))
    low = jax.ShapeDtypeStruct((GROUP, WIDE), BF16)
    low_plane = jax.ShapeDtypeStruct((PLANE, WIDE), BF16)
    return pl.pallas_call(
        functools.partial(attend_kernel, chunks=4),
        grid=(GROUP // block,),
        in_specs=[
            pl.BlockSpec(memory_space=pltpu.SMEM),
            three,
            three,
            plane,
            plane,
            pl.BlockSpec((8, WIDE), lambda i: (0, 0)),
        ],
        out_specs=[moving, plane, plane, moving, pl.BlockSpec((GROUP, WIDE), lambda i: (0, 0))],
        out_shape=[jax.ShapeDtypeStruct((GROUP, WIDE), F32), low_plane, low_plane, low, low],
        scratch_shapes=[pltpu.VMEM((GROUP, WIDE), BF16)] * 2,
        compiler_params=pltpu.CompilerParams(vmem_limit_bytes=48 * 2**20),
        cost_estimate=pl.CostEstimate(
            flops=16 * GROUP * GROUP * WIDE, bytes_accessed=GROUP * WIDE * 24,
            transcendentals=2 * GROUP * GROUP,
        ),
    )(at, mine, got, facts, facts_other, bias_rows)


def attend_back_kernel(
    mine_ref, got_ref, qt_ref, kt_ref, hot_ref, near_ref, other_ref, att_ref,
    keep_ref, send_ref, bias_ref, q_scr, grad_scr, dk_sum, dv_sum, *, chunks,
):
    size = GROUP // chunks
    step = pl.program_id(0)
    block = qt_ref.shape[0]

    @pl.when(step == 0)
    def _():
        q_scr[:PLANE] = mine_ref[0]
        q_scr[PLANE:] = got_ref[0]
        grad_scr[:PLANE] = near_ref[...]
        grad_scr[PLANE:] = other_ref[...]
        dk_sum[...] = jnp.zeros_like(dk_sum)
        dv_sum[...] = jnp.zeros_like(dv_sum)

    here = pl.ds(pl.multiple_of(step * block, block), block)
    query = jnp.concatenate([q_scr[here, :], qt_ref[...]], 1)
    grad = grad_scr[here, :]
    zero = jnp.zeros_like(query)
    head_of = (lanes_of(query.shape) // HEAD_DIM) % 2
    lanes = lanes_of((block, WIDE))
    overlap = grad.astype(F32) * att_ref[...]
    ones = value_lanes(size)
    out = None
    for head in range(2):
        mine = head_of[:, :WIDE] == head
        masked = jnp.where(head_of == head, query, zero)
        grad_here = jnp.where(mine, grad, zero[:, :WIDE])
        dots = jnp.sum(jnp.where(mine, overlap, 0.0), axis=1, keepdims=True)
        extra = with_pieces(jnp.zeros(lanes.shape, F32), -dots, 0, lanes).astype(BF16)
        grad_wide = jnp.concatenate([grad_here, extra], 1)
        total = None
        for c in range(chunks):
            rows = slice(c * size, (c + 1) * size)
            ref, at = key_rows(mine_ref, got_ref, c * size, size)
            keys = ref[1, at, :]
            prob = jnp.exp2(mm(jnp.concatenate([keys, kt_ref[rows, :]], 1), masked, NT))
            slope = mm(jnp.concatenate([ref[2, at, :], ones], 1), grad_wide, NT)
            d_score = (prob * slope).astype(BF16)
            dv_sum[rows, :] += mm(prob.astype(BF16), grad_here)
            dk_sum[rows, :] += mm(d_score, masked)
            part = mm(d_score, keys, TN)
            total = part if total is None else total + part
        out = total if head == 0 else jnp.where(lanes < HEAD_DIM, out, total)
    low = out.astype(BF16)
    half = pl.num_programs(0) // 2

    @pl.when(step < half)
    def _():
        keep_ref[0, here, :] = low

    @pl.when(step >= half)
    def _():
        send_ref[0, pl.ds(pl.multiple_of((step - half) * block, block), block), :] = low

    @pl.when(step == pl.num_programs(0) - 1)
    def _():
        for ref, rows in ((keep_ref, slice(0, PLANE)), (send_ref, slice(PLANE, GROUP))):
            ref[1] = (dk_sum[rows, :WIDE] * (1.0 / LOG2E)).astype(BF16)
            ref[2] = dv_sum[rows, :].astype(BF16)
        counts = dk_sum[:, WIDE:]
        bias_ref[...] = jnp.zeros_like(bias_ref)
        bias_ref[0:1, :] = jnp.sum(counts * hot_ref[...].astype(F32), axis=0, keepdims=True)
        bias_ref[1:2, :] = jnp.sum(counts, axis=0, keepdims=True)


def attend_back(mine, got, query_tail, key_tail, near, other, attended):
    block = 512
    moving = pl.BlockSpec((block, WIDE), lambda i: (i, 0))
    fixed = pl.BlockSpec((GROUP, WIDE), lambda i: (0, 0))
    plane = pl.BlockSpec((PLANE, WIDE), lambda i: (0, 0))
    three = pl.BlockSpec((3, PLANE, WIDE), lambda i: (0, 0, 0))
    low = jax.ShapeDtypeStruct((3, PLANE, WIDE), BF16)
    return pl.pallas_call(
        functools.partial(attend_back_kernel, chunks=4),
        grid=(GROUP // block,),
        in_specs=[three, three, moving, fixed, fixed, plane, plane, moving],
        out_specs=[three, three, pl.BlockSpec((8, WIDE), lambda i: (0, 0))],
        out_shape=[low, low, jax.ShapeDtypeStruct((8, WIDE), F32)],
        scratch_shapes=[
            pltpu.VMEM((GROUP, WIDE), BF16),
            pltpu.VMEM((GROUP, WIDE), BF16),
            pltpu.VMEM((GROUP, 2 * WIDE), F32),
            pltpu.VMEM((GROUP, WIDE), F32),
        ],
        compiler_params=pltpu.CompilerParams(vmem_limit_bytes=48 * 2**20),
        cost_estimate=pl.CostEstimate(
            flops=40 * GROUP * GROUP * WIDE, bytes_accessed=GROUP * WIDE * 24,
            transcendentals=2 * GROUP * GROUP,
        ),
    )(mine, got, query_tail, key_tail, query_tail, near, other, attended)


def feed_kernel(b_ref, g_ref, w_ref, y_ref, db_ref, act_ref, *, cuts):
    rows, grads = b_ref[...], g_ref[...]
    size = w_ref.shape[2] // cuts

    def products(j):
        cols = slice(j * size, (j + 1) * size)
        return mm(rows, w_ref[0, :, cols]), mm(rows, w_ref[1, :, cols]), mm(grads, w_ref[2, :, cols])

    y_sum, db_sum = None, None
    ready = products(0)
    for j in range(cuts):
        gate, up, d_hidden = ready
        if j + 1 < cuts:
            ready = products(j + 1)
        cols = slice(j * size, (j + 1) * size)
        sig = 0.5 + 0.5 * jnp.tanh(0.5 * gate)
        silu = gate * sig
        hidden = (silu * up).astype(BF16)
        d_gate = (d_hidden * up * (sig + silu * (1.0 - sig))).astype(BF16)
        d_up = (d_hidden * silu).astype(BF16)
        act_ref[0, :, cols] = d_gate
        act_ref[1, :, cols] = d_up
        act_ref[2, :, cols] = hidden
        y_part = mm(hidden, w_ref[2, :, cols], NT)
        db_part = mm(d_gate, w_ref[0, :, cols], NT) + mm(d_up, w_ref[1, :, cols], NT)
        y_sum = y_part if y_sum is None else y_sum + y_part
        db_sum = db_part if db_sum is None else db_sum + db_part
    y_ref[...] = y_sum.astype(BF16)
    db_ref[...] = db_sum.astype(BF16)


def feed(rows_b, rows_g, weights):
    rows = rows_b.shape[0]
    width = weights.shape[2]
    low_d = jax.ShapeDtypeStruct((rows, D), BF16)
    low_f = jax.ShapeDtypeStruct((3, rows, width), BF16)
    return pl.pallas_call(
        functools.partial(feed_kernel, cuts=2),
        out_shape=[low_d, low_d, low_f],
        compiler_params=pltpu.CompilerParams(vmem_limit_bytes=26 * 2**20),
        cost_estimate=pl.CostEstimate(
            flops=12 * rows * D * width, bytes_accessed=6 * D * width + rows * D * 8 + rows * width * 6,
            transcendentals=rows * width,
        ),
    )(rows_b, rows_g, weights)


def body(
    tokens,
    cotangent,
    destination,
    variate_ids,
    time_ids,
    seq_lengths,
    qkv_weight,
    out_weight,
    gate_up_weight,
    down_weight,
    norm_gains,
    qk_gains,
    variate_bias,
):
    core = lax.axis_index("core")
    low_core = core == 0
    y_at = lax.axis_index("y")
    zl_at = lax.axis_index("zl")

    core_scalar = core.reshape(1).astype(jnp.int32)

    def side_by_side(mine, other):
        return jnp.concatenate(
            [jnp.where(low_core, mine, other), jnp.where(low_core, other, mine)], axis=-1
        )

    feed_shard = jnp.concatenate([gate_up_weight, down_weight.T[None]], 0)

    slot = destination % ROWS
    group_at = destination // GROUP
    block_at = (destination % GROUP) // ROWS
    device_at = ((group_at // 2) * 2 + block_at // 4) * 8 + (block_at % 4) * 2 + group_at % 2
    key = device_at * ROWS + slot
    zero = jnp.zeros_like(slot)
    facts = jnp.stack([key, slot, variate_ids, time_ids // 32, time_ids % 32, zero, zero, zero])
    gains_row = jnp.pad(
        norm_gains.reshape(8, 16), ((0, 0), (GAIN_LANE, WIDE - GAIN_LANE - 16))
    ).astype(F32)
    outgoing, deal = deal_rows(tokens, cotangent, facts.astype(F32), gains_row)
    arrived = lax.all_to_all(outgoing.reshape(DEVICES, 8, SPAN), ALL, 0, 0, tiled=True)
    out_shard, outgoing = lax.optimization_barrier((out_weight.T, outgoing))
    attn_shard = jnp.concatenate([qkv_weight, jnp.stack(gather_direct(out_shard))], 0)
    attn_mine = gather_round(attn_shard, ("zh", "zl"), lax.axis_index("zh") * 2 + zl_at)
    attn_mine, arrived = lax.optimization_barrier((attn_mine, arrived))
    attn_mine = jnp.stack(gather_ahead(attn_mine, "x")).reshape((16,) + attn_shard.shape)

    lengths_other = swap_core(seq_lengths)
    lengths = jnp.where(zl_at == core, seq_lengths, lengths_other)[0]
    bias_other = lax.ppermute(variate_bias, "zl", [(0, 1), (1, 0)])
    bias_pair = jnp.where(zl_at == core, variate_bias, bias_other)

    arrived, lengths, bias_pair = lax.optimization_barrier((arrived, lengths, bias_pair))
    all_gains = arrived.reshape(16, 8, 8, SPAN)[:, 0, :, PAIR + GAIN_LANE : PAIR + GAIN_LANE + 16]
    inputs, grad_rows, attn_in, place, gains = receive(
        arrived.reshape(4 * ROWS, SPAN), all_gains.reshape(16, WIDE)
    )
    feed_shard, attn_in = lax.optimization_barrier((feed_shard, attn_in))
    feed_many = jnp.broadcast_to(feed_shard[None], (16,) + feed_shard.shape)
    zero_at = jnp.zeros((1,), jnp.int32)
    x_at = lax.axis_index("x").reshape(1).astype(jnp.int32)
    ahead, behind = ring(attn_in, -1), ring(attn_in, 1)
    ahead, feed_many = lax.optimization_barrier((ahead, feed_many))
    far_top, far_low = ring(ahead[: ROWS // 2], -1), ring(behind[ROWS // 2 :], 1)
    far_top, far_low, attn_mine, feed_many = lax.optimization_barrier(
        (far_top, far_low, attn_mine, feed_many)
    )
    feed_mine = lax.all_to_all(feed_many, FLAT, 0, 0, tiled=True)
    attn_w = assemble(core_scalar, x_at, attn_mine, swap_core(attn_mine))
    attn_all = [attn_in, ahead, jnp.concatenate([far_top, far_low], 0), behind]
    grad_rows, attn_all = lax.optimization_barrier((grad_rows, attn_all))
    grad_all = gather_direct(grad_rows)

    blocks_y = (y_at + jnp.arange(RING)) % RING
    blocks = jnp.concatenate([core * RING + blocks_y, (1 - core) * RING + blocks_y])
    at = jnp.concatenate([blocks * ROWS, jnp.cumsum(lengths)]).astype(jnp.int32)

    inverse = THETA ** (-2.0 * jnp.arange(HALF).astype(F32) / HEAD_DIM)
    freq = jnp.concatenate(
        [
            jnp.tile(inverse, 8)[None],
            jnp.tile(qk_gains, (1, 4)),
            jnp.zeros((5, 2 * WIDE), F32),
        ]
    )
    qkv_mine, qkv_send, raw, facts_all = project(core_scalar, attn_all, attn_w, freq)
    facts_other = swap_core(facts_all)
    qkv_got = swap_core(qkv_send)

    bias_parts = jnp.stack(pieces(bias_pair * LOG2E, 3)).astype(F32)
    bias_rows = jnp.repeat(bias_parts, VARIATES, axis=0).transpose(1, 2, 0)
    bias_rows = jnp.pad(bias_rows, ((0, 0), (0, 0), (0, HEAD_DIM - 3 * VARIATES))).reshape(2, WIDE)
    bias_rows = jnp.pad(bias_rows, ((0, 6), (0, 0)))
    attended, att_near, att_send, query_back, key_tail = attend(
        at, qkv_mine, qkv_got, facts_all, facts_other, bias_rows
    )
    att_send, feed_mine = lax.optimization_barrier((att_send, feed_mine))
    att_other = swap_core(att_send)
    att_other, grad_all = lax.optimization_barrier((att_other, grad_all))
    att_plane = side_by_side(att_near, att_other).reshape(RING, ROWS, 2 * WIDE)
    att_rows = trade_ring([att_plane[r] for r in range(RING)])
    att_rows, feed_mine = lax.optimization_barrier((att_rows, feed_mine))
    feed_w = assemble(core_scalar, zero_at, feed_mine, swap_core(feed_mine))
    hidden_one, feed_in = out_project(att_rows, attn_w, inputs, gains)

    ahead, behind = ring(feed_in, -1), ring(feed_in, 1)
    fed_own = feed(feed_in, grad_all[0], feed_w)
    ahead, behind, fed_own = lax.optimization_barrier((ahead, behind, fed_own))
    far_top, far_low = ring(ahead[: ROWS // 2], -1), ring(behind[ROWS // 2 :], 1)
    fed_ahead = feed(ahead, grad_all[1], feed_w)
    fed_behind = feed(behind, grad_all[3], feed_w)
    far_top, far_low, fed_ahead, fed_behind = lax.optimization_barrier(
        (far_top, far_low, fed_ahead, fed_behind)
    )
    far = jnp.concatenate([far_top, far_low], 0)
    fed_far = feed(far, grad_all[2], feed_w)
    feed_all = [feed_in, ahead, far, behind]
    fed = [fed_own, fed_ahead, fed_far, fed_behind]
    feed_split = weight_grads(core_scalar, feed_all, grad_all, [f[2] for f in fed], 2, 2)
    db_got = send_ring([f[1] for f in fed], True)
    db_got, feed_split = lax.optimization_barrier((db_got, feed_split))
    grad_one, gain_two_grad, d_att, *both = middle(
        att_rows, attn_w, [f[0] for f in fed], fed_own[1], db_got, hidden_one, grad_rows, gains
    )
    feed_total = chip_total(feed_split)
    feed_got = trade(feed_total, "x")

    grad_att = trade_ring([d_att[r] for r in range(RING)])
    grad_att[1], feed_total = lax.optimization_barrier((grad_att[1], feed_total))
    grad_att = jnp.concatenate(grad_att, 0)
    both, grad_att = lax.optimization_barrier((both, grad_att))
    both_got = send_ring(both)
    grad_left, grad_right = grad_att[:, :WIDE], grad_att[:, WIDE:]
    grad_other = swap_core(jnp.where(low_core, grad_right, grad_left))
    grad_near = jnp.where(low_core, grad_left, grad_right)
    d_keep, d_send, bias_sums = attend_back(
        qkv_mine, qkv_got, query_back, key_tail, grad_near, grad_other, attended
    )
    first_part = (jnp.arange(HEAD_DIM) < VARIATES)[None, None]
    bias_sums = jnp.where(first_part, bias_sums[:2].reshape(2, 2, HEAD_DIM), 0.0)
    bias_sums = jnp.sum(bias_sums, axis=2)
    bias_part = jnp.stack([bias_sums[0], bias_sums[1] - bias_sums[0]])
    d_got = swap_core(d_send)
    grad_proj, qk_sums, *in_part = unproject(
        core_scalar, d_keep, d_got, raw, facts_all, attn_w, freq
    )
    in_got = send_ring(in_part)
    feed_half = added(feed_got).astype(BF16)
    in_got[0], feed_half = lax.optimization_barrier((in_got[0], feed_half))
    grad_proj, both_got = lax.optimization_barrier((grad_proj, both_got))
    both_sum = add_ring(both[0], both_got)
    mixed = (hidden_one + both_sum[:ROWS]).astype(BF16)
    out_full = both_sum[ROWS:].astype(BF16)
    attn_split = weight_grads(core_scalar, attn_all, [out_full], [grad_proj], None, 1)
    attn_total = chip_total(attn_split)
    in_got, _ = lax.optimization_barrier((in_got, attn_split))
    mixed, _ = lax.optimization_barrier((mixed, attn_total))
    feed_got = trade(feed_half, ("zh", "zl"))
    attn_own, attn_got = send_round(attn_total.reshape((RING, RING) + attn_total.shape[1:]), "x")
    qk_sums = jnp.sum(qk_sums[:2].reshape(2, 4, HEAD_DIM), axis=1)

    small = jnp.zeros((8, WIDE), F32).at[0].set(qk_sums.reshape(WIDE))
    small = small.at[1, :4].set(bias_part.reshape(4))
    tensor_at = (y_at * 2 + core).reshape(1).astype(jnp.int32)
    last = finish(
        in_part[0], in_got, inputs, grad_one, mixed, place, gains, gain_two_grad, small, tensor_at
    )
    last = last.reshape(DEVICES, 8, 2 * QUARTER + WIDE)
    last, attn_got, feed_got = lax.optimization_barrier((last, attn_got, feed_got))
    home = lax.all_to_all(last, ALL, 0, 0, tiled=True)
    own, got = send_round(add_round(attn_own, attn_got).astype(BF16), ("zh", "zl"))
    home, got = lax.optimization_barrier((home, got))
    attn_grad = add_round(own, got)
    feed_grad = added(feed_got).reshape(3, 64, 512)
    new_tokens, token_grads, sums = settle(home.reshape(4 * ROWS, 2 * QUARTER + WIDE), deal)
    gains_grad = sums[0].reshape(2, 64)
    qk_grad = sums[1].reshape(2, 64)
    bias_grad = sums[2, :4].reshape(2, 2)

    return (
        new_tokens,
        token_grads,
        attn_grad[:3],
        attn_grad[3].T,
        feed_grad[:2],
        feed_grad[2].T,
        gains_grad,
        qk_grad,
        bias_grad,
    )


def solution(mesh):
    fine = Mesh(mesh.devices.reshape(4, 2, 2, 4, 2), ALL)
    dp = ("x", "zh", "core")
    tensor = ("y", "zl")
    in_specs = (
        P(ALL, None),
        P(ALL, None),
        P(ALL),
        P(ALL),
        P(ALL),
        P(dp, None),
        P(None, dp, tensor),
        P(tensor, dp),
        P(None, dp, tensor),
        P(tensor, dp),
        P(None, dp),
        P(),
        P(None, tensor),
    )
    out_specs = (
        P(ALL, None),
        P(ALL, None),
        P(None, dp, tensor),
        P(tensor, dp),
        P(None, dp, tensor),
        P(tensor, dp),
        P(None, dp),
        P(),
        P(None, tensor),
    )
    return jax.shard_map(body, mesh=fine, in_specs=in_specs, out_specs=out_specs, check_vma=False)
```

```python
import functools

import jax
import jax.numpy as jnp
from jax import lax
from jax.experimental import pallas as pl
from jax.experimental.pallas import tpu as pltpu
from jax.sharding import Mesh
from jax.sharding import PartitionSpec as P

HEADS = 16
HEAD_DIM = 64
HALF = HEAD_DIM // 2
D = 1024
FF = 4096
ROWS = 256
RING = 4
PLANE = ROWS * RING
GROUP = 2 * PLANE
DEVICES = 128
VARIATES = 8
SEQS = 4
WIDE = 128
EPS = 1e-06
THETA = 10000.0
LOG2E = 1.4426950408889634
FAR = -16384.0
F32 = jnp.float32
BF16 = jnp.bfloat16

ALL = ("x", "zh", "core", "y", "zl")
FLAT = ("x", "zh", "zl")
NT = (((1,), (1,)), ((), ()))
TN = (((0,), (0,)), ((), ()))


def mm(left, right, dims=(((1,), (0,)), ((), ()))):
    return lax.dot_general(left, right, dims, preferred_element_type=F32)


def root_stats(values):
    return lax.rsqrt(jnp.mean(values * values, axis=-1, keepdims=True) + EPS)


def norm_back(grad_in, normed, scale_inv):
    return scale_inv * (grad_in - normed * jnp.mean(grad_in * normed, axis=-1, keepdims=True))


def pieces(values, count):
    out = []
    for _ in range(count):
        part = lax.reduce_precision(values, 8, 7)
        out.append(part.astype(BF16))
        values = values - part
    return out


def ring(values, step):
    return lax.ppermute(values, "y", [(i, (i + step) % RING) for i in range(RING)])


def swap_core(values):
    return lax.ppermute(values, "core", [(0, 1), (1, 0)])


def gather_ring(values):
    ahead = ring(values, -1)
    behind = ring(values, 1)
    half = values.shape[0] // 2
    far_top = ring(ahead[:half], -1)
    far_low = ring(behind[half:], 1)
    return [values, ahead, jnp.concatenate([far_top, far_low], 0), behind]


def gather_direct(values):
    return [values, ring(values, -1), ring(values, 2), ring(values, 1)]


def trade_ring(parts):
    return [parts[0]] + [ring(parts[RING - s], -s) for s in range(1, RING)]


def send_ring(parts, halves=False):
    half = parts[2].shape[0] // 2
    far = [parts[2][:half], parts[2][half:]] if halves else [parts[2]]
    return [ring(parts[1], 1), ring(parts[3], -1)] + [ring(v, 2) for v in far]


def add_ring(own, got):
    far = got[2] if len(got) == 3 else jnp.concatenate(got[2:], 0)
    return own.astype(F32) + got[0].astype(F32) + got[1].astype(F32) + far.astype(F32)


def gather_ahead(values, axes):
    moves = [[((i + r) % RING, i) for i in range(RING)] for r in range(RING)]
    return [values] + [lax.ppermute(values, axes, moves[r]) for r in range(1, RING)]


def gather_round(values, axes, at):
    return jnp.roll(jnp.stack(gather_ahead(values, axes)), at, axis=0)


def assemble_kernel(at_ref, mine_ref, other_ref, out_ref):
    core = at_ref[0]
    count, _, depth, width = mine_ref.shape
    for ref, side in ((mine_ref, core), (other_ref, 1 - core)):
        for i in range(count):
            at = (i // 2) * 2 * depth + side * depth
            rows = pl.ds(pl.multiple_of(at, depth), depth)
            out_ref[:, rows, (i % 2) * width : (i % 2 + 1) * width] = ref[i]


def assemble(core, x_at, mine, other):
    _, kinds, depth, width = mine.shape
    pair = pl.BlockSpec((4, kinds, depth, width), lambda p, at: (p, 0, 0, 0))
    return pl.pallas_call(
        assemble_kernel,
        grid_spec=pltpu.PrefetchScalarGridSpec(
            num_scalar_prefetch=1,
            grid=(RING,),
            in_specs=[pair, pair],
            out_specs=pl.BlockSpec(
                (kinds, 4 * depth, 2 * width), lambda p, at: (0, lax.rem(at[1] + p, RING), 0)
            ),
        ),
        out_shape=jax.ShapeDtypeStruct((kinds, 16 * depth, 2 * width), BF16),
        compiler_params=pltpu.CompilerParams(vmem_limit_bytes=28 * 2**20),
        cost_estimate=pl.CostEstimate(
            flops=0, bytes_accessed=kinds * 128 * depth * width, transcendentals=0
        ),
    )(jnp.concatenate([core, x_at]), mine, other)


def chip_total(split):
    return (split[0].astype(F32) + swap_core(split[1]).astype(F32)).astype(BF16)


def send_round(values, axes):
    at = lax.axis_index(axes)
    parts = [lax.dynamic_index_in_dim(values, (at + r) % RING, 0, keepdims=False) for r in range(RING)]
    moves = [[(i, (i + r) % RING) for i in range(RING)] for r in range(RING)]
    return parts[0], [lax.ppermute(parts[r], axes, moves[r]) for r in (1, 3, 2)]


def add_round(own, got):
    return sum((v.astype(F32) for v in got), own.astype(F32))


def trade(values, axes):
    return lax.all_to_all(values.reshape((RING, -1) + values.shape[1:]), axes, 0, 0, tiled=True)


def added(got):
    return jnp.sum(got.astype(F32), axis=0)


def lanes_of(shape):
    return lax.broadcasted_iota(jnp.int32, shape, 1)


QUARTER = D // RING
PAIR = 2 * QUARTER
SPAN = PAIR + WIDE
GAIN_LANE = 16


def deal_kernel(tok_ref, cot_ref, facts_ref, gains_ref, out_ref, deal_ref):
    wide = jnp.concatenate([facts_ref[...], jnp.zeros((WIDE - 8, ROWS), F32)], 0)
    facts = jnp.transpose(wide)
    keys = facts_ref[0:1, :]
    rank = jnp.sum((facts[:, 0:1] < keys).astype(F32), axis=0, keepdims=True)
    at = lax.broadcasted_iota(jnp.int32, (ROWS, ROWS), 0).astype(F32)
    deal_ref[...] = (at == rank).astype(BF16)
    low = jnp.where(lanes_of(facts.shape) == 0, 0.0, facts).astype(BF16)
    row = lax.broadcasted_iota(jnp.int32, (4 * ROWS, 1), 0)
    own = ((row // RING).astype(F32) == rank).astype(BF16)
    part = None
    for m in range(RING):
        cols = slice(m * QUARTER, (m + 1) * QUARTER)
        here = mm(own, jnp.concatenate([tok_ref[:, cols], cot_ref[:, cols]], 1))
        part = here if m == 0 else jnp.where(row % RING == m, here, part)
    out_ref[:, :PAIR] = part.astype(BF16)
    tail = mm(own, low)
    lane = lanes_of(tail.shape)
    gains = jnp.broadcast_to(gains_ref[...][None], (DEVICES, 8, WIDE)).reshape(tail.shape)
    tail = jnp.where((lane >= GAIN_LANE) & (lane < GAIN_LANE + 16), gains, tail)
    out_ref[:, PAIR:] = tail.astype(BF16)


def deal_rows(tokens, cotangent, facts, gains):
    return pl.pallas_call(
        deal_kernel,
        out_shape=[
            jax.ShapeDtypeStruct((4 * ROWS, SPAN), BF16),
            jax.ShapeDtypeStruct((ROWS, ROWS), BF16),
        ],
        compiler_params=pltpu.CompilerParams(vmem_limit_bytes=48 * 2**20),
        cost_estimate=pl.CostEstimate(
            flops=8 * ROWS * ROWS * 2304, bytes_accessed=ROWS * D * 16, transcendentals=0
        ),
    )(tokens, cotangent, facts, gains)


def receive_kernel(rows_ref, gains_ref, x_ref, g_ref, a_ref, place_ref, gain_ref):
    count = 4 * ROWS
    facts = rows_ref[:, PAIR:]
    slots = jnp.transpose(facts.astype(F32))[1:2, :]
    at = lax.broadcasted_iota(jnp.int32, (ROWS, count), 0)
    arrival = lanes_of((ROWS, count))
    here = at.astype(F32) == slots
    gains = gains_ref[...].astype(F32)
    turned = pltpu.roll(gains, HEAD_DIM, 1)
    left = lanes_of((1, WIDE)) < HEAD_DIM
    one, two = [], []
    for c in range(D // WIDE):
        even, odd = slice(2 * c, 2 * c + 1), slice(2 * c + 1, 2 * c + 2)
        one.append(jnp.where(left, gains[even], turned[odd]))
        two.append(jnp.where(left, turned[even], gains[odd]))
    gain_one = jnp.concatenate(one, 1)
    gain_ref[...] = jnp.zeros_like(gain_ref)
    gain_ref[0:1, :] = gain_one
    gain_ref[1:2, :] = jnp.concatenate(two, 1)
    quarters = []
    for m in range(RING):
        chosen = (here & (arrival % RING == m)).astype(BF16)
        both = mm(chosen, rows_ref[:, :PAIR])
        quarters.append(both[:, :QUARTER])
        g_ref[:, m * QUARTER : (m + 1) * QUARTER] = both[:, QUARTER:].astype(BF16)
        if m == 0:
            a_ref[:, D:] = mm(chosen, facts).astype(BF16)
            pick = (at * RING == arrival).astype(BF16)
            place_ref[...] = mm(chosen, pick, NT).astype(BF16)
    rows = jnp.concatenate(quarters, 1)
    x_ref[...] = rows
    a_ref[:, :D] = (rows * root_stats(rows) * gain_one).astype(BF16)


def receive(rows, gains):
    return pl.pallas_call(
        receive_kernel,
        out_shape=[
            jax.ShapeDtypeStruct((ROWS, D), F32),
            jax.ShapeDtypeStruct((ROWS, D), BF16),
            jax.ShapeDtypeStruct((ROWS, D + WIDE), BF16),
            jax.ShapeDtypeStruct((ROWS, ROWS), BF16),
            jax.ShapeDtypeStruct((8, D), F32),
        ],
        compiler_params=pltpu.CompilerParams(vmem_limit_bytes=48 * 2**20),
        cost_estimate=pl.CostEstimate(
            flops=16 * ROWS * ROWS * D, bytes_accessed=ROWS * D * 24, transcendentals=0
        ),
    )(rows, gains)


OUT_KIND = 3


def out_kernel(*refs):
    att = refs[:RING]
    w_ref, x_ref, gain_ref, h_ref, b_ref = refs[RING:]
    hidden = x_ref[...]
    for r in range(RING):
        hidden = hidden + mm(att[r][...], w_ref[OUT_KIND + r], NT)
    h_ref[...] = hidden
    b_ref[...] = (hidden * root_stats(hidden) * gain_ref[1:2, :]).astype(BF16)


def out_project(att, weights, rows, gains):
    return pl.pallas_call(
        out_kernel,
        out_shape=[jax.ShapeDtypeStruct((ROWS, D), F32), jax.ShapeDtypeStruct((ROWS, D), BF16)],
        compiler_params=pltpu.CompilerParams(vmem_limit_bytes=48 * 2**20),
        cost_estimate=pl.CostEstimate(
            flops=2 * ROWS * D * D, bytes_accessed=2 * D * D + ROWS * D * 14, transcendentals=0
        ),
    )(*att, weights, rows, gains)


def middle_kernel(*refs):
    att, y_parts, w_ref = refs[:RING], refs[RING : 2 * RING], refs[2 * RING]
    refs = refs[2 * RING + 1 :]
    own_ref, near_ref, back_ref, top_ref, low_ref, h_ref, g_ref, gain_ref = refs[:8]
    grad_ref, two_ref, d_ref = refs[8:11]
    both_refs = refs[11:]
    far = jnp.concatenate([top_ref[...], low_ref[...]], 0).astype(F32)
    grad = own_ref[...].astype(F32) + near_ref[...].astype(F32) + back_ref[...].astype(F32) + far
    hidden = h_ref[...]
    scale = root_stats(hidden)
    normed = hidden * scale
    two_ref[...] = jnp.zeros_like(two_ref)
    two_ref[0:1, :] = jnp.sum(grad * normed, axis=0, keepdims=True)
    scaled = grad * gain_ref[1:2, :]
    grad = g_ref[...].astype(F32) + norm_back(scaled, normed, scale)
    grad_ref[...] = grad
    low = grad.astype(BF16)
    for r in range(RING):
        d_ref[r] = mm(low, w_ref[OUT_KIND + r]).astype(BF16)
        both_refs[r][:ROWS] = y_parts[r][...]
        both_refs[r][ROWS:] = mm(att[r][...], low, TN).astype(BF16)


def middle(att, weights, y_parts, own, got, hidden, grad_rows, gains):
    both = jax.ShapeDtypeStruct((2 * ROWS, D), BF16)
    return pl.pallas_call(
        middle_kernel,
        out_shape=[
            jax.ShapeDtypeStruct((ROWS, D), F32),
            jax.ShapeDtypeStruct((8, D), F32),
            jax.ShapeDtypeStruct((RING, ROWS, ROWS), BF16),
        ]
        + [both] * RING,
        compiler_params=pltpu.CompilerParams(vmem_limit_bytes=48 * 2**20),
        cost_estimate=pl.CostEstimate(
            flops=4 * ROWS * D * D, bytes_accessed=2 * D * D + ROWS * D * 40, transcendentals=0
        ),
    )(*att, *y_parts, weights, own, *got, hidden, grad_rows, gains)


def finish_kernel(
    own_ref, near_ref, back_ref, far_ref, x_ref, grad_ref, mixed_ref, place_ref,
    gain_ref, two_ref, small_ref, at_ref, out_ref,
):
    rows = x_ref[...]
    scale = root_stats(rows)
    normed = rows * scale
    far = far_ref[...].astype(F32)
    grad = own_ref[...].astype(F32) + near_ref[...].astype(F32) + back_ref[...].astype(F32) + far
    one = jnp.sum(grad * normed, axis=0, keepdims=True)
    two = two_ref[0:1, :]
    scaled = grad * gain_ref[0:1, :]
    back = scale * (scaled - normed * jnp.mean(scaled * normed, axis=1, keepdims=True))
    result = (grad_ref[...] + back).astype(BF16)
    count = 4 * ROWS
    row = lax.broadcasted_iota(jnp.int32, (count, 1), 0)
    quarter = row % RING
    pick = (row // RING == lanes_of((count, ROWS))).astype(BF16)
    pick = mm(pick, place_ref[...], NT).astype(BF16)
    part = None
    for m in range(RING):
        cols = slice(m * QUARTER, (m + 1) * QUARTER)
        here = mm(pick, jnp.concatenate([mixed_ref[:, cols], result[:, cols]], 1))
        part = here if m == 0 else jnp.where(quarter == m, here, part)
    out_ref[:, : 2 * QUARTER] = part.astype(BF16)
    left = lanes_of((1, WIDE)) < HEAD_DIM
    tiles = []
    for c in range(D // WIDE):
        cols = slice(c * WIDE, (c + 1) * WIDE)
        a, b = one[:, cols], two[:, cols]
        even = jnp.where(left, a, pltpu.roll(jnp.broadcast_to(b, (8, WIDE)), HEAD_DIM, 1)[0:1])
        odd = jnp.where(left, pltpu.roll(jnp.broadcast_to(a, (8, WIDE)), HEAD_DIM, 1)[0:1], b)
        tiles += [jnp.broadcast_to(even, (64, WIDE)), jnp.broadcast_to(odd, (64, WIDE))]
    value = jnp.concatenate(tiles, 0)
    value = jnp.where(quarter == 1, small_ref[0:1, :], value)
    bias = jnp.where((row // 8) % 8 == at_ref[0], small_ref[1:2, :], 0.0)
    value = jnp.where(quarter == 2, bias, value)
    high = value.astype(BF16).astype(F32)
    value = jnp.where((row // RING) % 2 == 0, high, value - high)
    out_ref[:, 2 * QUARTER :] = value.astype(BF16)


def finish(own, got, rows, grad, mixed, place, gains, two, small, at):
    specs = [pl.BlockSpec(memory_space=pltpu.VMEM)] * 11
    return pl.pallas_call(
        finish_kernel,
        in_specs=specs + [pl.BlockSpec(memory_space=pltpu.SMEM)],
        out_shape=jax.ShapeDtypeStruct((4 * ROWS, 2 * QUARTER + WIDE), BF16),
        compiler_params=pltpu.CompilerParams(vmem_limit_bytes=48 * 2**20),
        cost_estimate=pl.CostEstimate(
            flops=16 * ROWS * ROWS * D, bytes_accessed=ROWS * D * 20, transcendentals=0
        ),
    )(own, *got, rows, grad, mixed, place, gains, two, small, at)


def settle_kernel(home_ref, deal_ref, rows_ref, grads_ref, sums_ref):
    deal = deal_ref[...]
    shape = (ROWS, 4 * ROWS)
    index = lax.broadcasted_iota(jnp.int32, shape, 0)
    for m in range(RING):
        pick = (index * RING + m == lanes_of(shape)).astype(BF16)
        here = mm(pick, home_ref[:, : 2 * QUARTER]).astype(BF16)
        here = mm(deal, here, TN).astype(BF16)
        cols = slice(m * QUARTER, (m + 1) * QUARTER)
        rows_ref[:, cols] = here[:, :QUARTER]
        grads_ref[:, cols] = here[:, QUARTER:]
    small = home_ref[:, 2 * QUARTER :].astype(F32)
    quarter = lax.broadcasted_iota(jnp.int32, small.shape, 0) % RING
    sums_ref[...] = jnp.zeros_like(sums_ref)
    for m in range(3):
        sums_ref[m : m + 1, :] = jnp.sum(jnp.where(quarter == m, small, 0.0), axis=0, keepdims=True)


def settle(home, deal):
    low = jax.ShapeDtypeStruct((ROWS, D), BF16)
    return pl.pallas_call(
        settle_kernel,
        out_shape=[low, low, jax.ShapeDtypeStruct((8, WIDE), F32)],
        compiler_params=pltpu.CompilerParams(vmem_limit_bytes=48 * 2**20),
        cost_estimate=pl.CostEstimate(
            flops=20 * ROWS * ROWS * D, bytes_accessed=ROWS * D * 16, transcendentals=0
        ),
    )(home, deal)


def weight_grad_kernel(core_ref, *refs, parts, count, switch, steps):
    given = switch is None
    lefts, others, rights = refs[:parts], refs[parts : parts + count], refs[parts + count : -3]
    keep_ref, send_ref, turned_ref = refs[-3:]
    low = core_ref[0] == 0
    step = pl.program_id(0)

    def load(sides):
        at = 0
        for side in sides:
            rows = side.shape[0]
            turned_ref[:, at : at + rows] = side[...].T
            at += rows

    @pl.when(step == 0)
    def _():
        load(lefts)

    if not given:

        @pl.when(step == switch * steps)
        def _():
            load(others)

    def emit(total):
        depth = total.shape[0] // 16
        width = keep_ref.shape[-1]
        for z in range(total.shape[1] // width):
            cols = slice(z * width, (z + 1) * width)
            for p in range(8):
                at = 2 * p * depth
                even, odd = total[at : at + depth, cols], total[at + depth : at + 2 * depth, cols]
                keep_ref[p, z, 0] = jnp.where(low, even, odd)
                send_ref[p, z, 0] = jnp.where(low, odd, even)

    def product():
        right = jnp.concatenate([ref[0] for ref in rights], 0)
        emit(mm(turned_ref[...], right).astype(BF16))

    if given:
        pl.when(step < pl.num_programs(0) - 1)(product)

        @pl.when(step == pl.num_programs(0) - 1)
        def _():
            emit(others[0][...].T)
    else:
        product()


def weight_grads(core, lefts, others, rights, switch, steps):
    parts = len(lefts)
    made, _, width = rights[0].shape
    kinds = made + 1 if switch is None else made
    block, half = width // steps, width // 2
    sides = [pl.BlockSpec((v.shape[0], D), lambda s: (0, 0)) for v in list(lefts) + list(others)]
    moving = [
        pl.BlockSpec(
            (1, v.shape[1], block), lambda s: (jnp.minimum(s // steps, made - 1), 0, s % steps)
        )
        for v in rights
    ]
    rows = sum(v.shape[1] for v in rights)
    out = pl.pallas_call(
        functools.partial(
            weight_grad_kernel, parts=parts, count=len(others), switch=switch, steps=steps
        ),
        grid=(kinds * steps,),
        in_specs=[pl.BlockSpec(memory_space=pltpu.SMEM)] + sides + moving,
        out_specs=[
            pl.BlockSpec((8, 2 // steps, 1, 64, half), lambda s: (0, s % steps, s // steps, 0, 0))
        ]
        * 2,
        out_shape=[jax.ShapeDtypeStruct((8, 2, kinds, 64, half), BF16)] * 2,
        scratch_shapes=[pltpu.VMEM((D, rows), BF16)],
        compiler_params=pltpu.CompilerParams(vmem_limit_bytes=48 * 2**20),
        cost_estimate=pl.CostEstimate(
            flops=2 * kinds * rows * D * width,
            bytes_accessed=2 * kinds * D * width + 4 * rows * D + 2 * kinds * rows * width,
            transcendentals=0,
        ),
    )(core, *lefts, *others, *rights)
    return [v.reshape(16, kinds, 64, half) for v in out]


def head_sums(values):
    wide = values.shape[1]
    row = lax.broadcasted_iota(jnp.int32, (wide, wide), 0) // HEAD_DIM
    same = (row == lanes_of((wide, wide)) // HEAD_DIM).astype(BF16)
    high = values.astype(BF16)
    low = (values - high.astype(F32)).astype(BF16)
    return mm(high, same) + mm(low, same)


def partner(values):
    wide = values.shape[1]
    first = lanes_of(values.shape) % HEAD_DIM < HALF
    return jnp.where(first, pltpu.roll(values, wide - HALF, 1), pltpu.roll(values, HALF, 1))


def angles_of(facts, freq_ref):
    facts = facts.astype(F32)
    times = facts[:, 3:4] * 32.0 + facts[:, 4:5]
    angle = times * freq_ref[0:1, :WIDE]
    first = lanes_of(angle.shape) % HEAD_DIM < HALF
    cosine = jnp.cos(angle)
    sine = jnp.sin(angle)
    sine = jnp.where(first, -sine, sine)
    return jnp.concatenate([cosine, cosine], 1), jnp.concatenate([sine, sine], 1)


def project_kernel(core_ref, *refs):
    pieces_in = refs[:RING]
    w_ref, freq_ref, mine_ref, send_ref, raw_ref, facts_ref = refs[RING:]
    low = core_ref[0] == 0
    for r in range(RING):
        block = slice(r * ROWS, (r + 1) * ROWS)
        rows = pieces_in[r][:, :D]
        facts = pieces_in[r][:, D:]
        facts_ref[block] = facts
        cosine, sine = angles_of(facts, freq_ref)
        for kind in range(3):
            value = mm(rows, w_ref[kind])
            if kind < 2:
                raw_ref[kind, block] = value
                unit = value * lax.rsqrt(head_sums(value * value) * (1.0 / HEAD_DIM) + EPS)
                value = unit * freq_ref[1 + kind : 2 + kind, :]
                value = value * cosine + partner(value) * sine
            if kind == 0:
                value = value * (HEAD_DIM ** (-0.5) * LOG2E)
            left, right = value[:, :WIDE], value[:, WIDE:]
            mine_ref[kind, block] = jnp.where(low, left, right).astype(BF16)
            send_ref[kind, block] = jnp.where(low, right, left).astype(BF16)


def project(core, rows, attn_w, freq):
    low = jax.ShapeDtypeStruct((3, PLANE, WIDE), BF16)

    def whole(v):
        return pl.BlockSpec(v.shape, lambda i: (0,) * v.ndim)

    shapes = [
        low,
        low,
        jax.ShapeDtypeStruct((2, PLANE, 2 * WIDE), F32),
        jax.ShapeDtypeStruct((PLANE, WIDE), BF16),
    ]
    return pl.pallas_call(
        project_kernel,
        grid=(1,),
        in_specs=[pl.BlockSpec(memory_space=pltpu.SMEM)]
        + [whole(v) for v in rows]
        + [pl.BlockSpec((3, D, 2 * WIDE), lambda i: (0, 0, 0)), whole(freq)],
        out_specs=[whole(v) for v in shapes],
        out_shape=shapes,
        compiler_params=pltpu.CompilerParams(vmem_limit_bytes=48 * 2**20),
        cost_estimate=pl.CostEstimate(
            flops=8 * PLANE * D * 2 * WIDE, bytes_accessed=PLANE * D * 8, transcendentals=PLANE * 1024
        ),
    )(core, *rows, attn_w, freq)


def unproject_kernel(core_ref, mine_ref, got_ref, raw_ref, facts_ref, w_ref, freq_ref, dp_ref, gain_ref, *part_refs):
    low = core_ref[0] == 0
    gains = [0.0, 0.0]
    for r in range(RING):
        block = slice(r * ROWS, (r + 1) * ROWS)
        cosine, sine = angles_of(facts_ref[block], freq_ref)
        total = None
        for kind in range(3):
            mine, got = mine_ref[kind, block], got_ref[kind, block]
            grad = jnp.concatenate([jnp.where(low, mine, got), jnp.where(low, got, mine)], 1)
            if kind < 2:
                grad = grad.astype(F32)
                if kind == 0:
                    grad = grad * (HEAD_DIM ** (-0.5))
                raw = raw_ref[kind, block]
                inv = lax.rsqrt(head_sums(raw * raw) * (1.0 / HEAD_DIM) + EPS)
                unit = raw * inv
                grad = grad * cosine - partner(grad) * sine
                gains[kind] += jnp.sum(grad * unit, axis=0, keepdims=True)
                scaled = grad * freq_ref[1 + kind : 2 + kind, :]
                mean = head_sums(scaled * unit) * (1.0 / HEAD_DIM)
                grad = (inv * (scaled - unit * mean)).astype(BF16)
            dp_ref[kind, block] = grad
            part = mm(grad, w_ref[kind], NT)
            total = part if total is None else total + part
        part_refs[r][...] = total.astype(BF16)
    gain_ref[...] = jnp.zeros_like(gain_ref)
    gain_ref[0:1, :] = gains[0]
    gain_ref[1:2, :] = gains[1]


def unproject(core, mine, got, raw, facts, attn_w, freq):
    three = pl.BlockSpec((3, D, 2 * WIDE), lambda i: (0, 0, 0))

    def whole(v):
        return pl.BlockSpec(v.shape, lambda i: (0,) * v.ndim)

    shapes = [
        jax.ShapeDtypeStruct((3, PLANE, 2 * WIDE), BF16),
        jax.ShapeDtypeStruct((8, 2 * WIDE), F32),
    ] + [jax.ShapeDtypeStruct((ROWS, D), BF16)] * RING
    return pl.pallas_call(
        unproject_kernel,
        grid=(1,),
        in_specs=[pl.BlockSpec(memory_space=pltpu.SMEM)]
        + [whole(v) for v in (mine, got, raw, facts)]
        + [three, whole(freq)],
        out_specs=[whole(v) for v in shapes],
        out_shape=shapes,
        compiler_params=pltpu.CompilerParams(vmem_limit_bytes=48 * 2**20),
        cost_estimate=pl.CostEstimate(
            flops=8 * PLANE * D * 2 * WIDE, bytes_accessed=PLANE * D * 8, transcendentals=PLANE * 1024
        ),
    )(core, mine, got, raw, facts, attn_w, freq)


LOG_LANE = 3 * VARIATES + SEQS


def with_pieces(base, values, first_lane, lanes):
    for i in range(3):
        part = values.astype(BF16).astype(F32)
        base = jnp.where(lanes == first_lane + i, part, base)
        values = values - part
    return base


def key_rows(mine_ref, got_ref, start, size):
    if start < PLANE:
        return mine_ref, slice(start, start + size)
    return got_ref, slice(start - PLANE, start - PLANE + size)


def value_lanes(rows):
    return (lanes_of((rows, WIDE)) < 3).astype(BF16)


def attend_kernel(
    at_ref, mine_ref, got_ref, own_ref, other_ref, bias_ref,
    att_ref, near_ref, send_ref, tail_ref, kt_ref, q_scr, qt_scr, *, chunks,
):
    step = pl.program_id(0)
    block = att_ref.shape[0]
    size = GROUP // chunks

    @pl.when(step == 0)
    def _():
        q_scr[:PLANE] = mine_ref[0]
        q_scr[PLANE:] = got_ref[0]
        lane = lanes_of((ROWS, WIDE))
        tail_lane = lane % HEAD_DIM
        bias_lane = tail_lane < 3 * VARIATES
        seg_lane = (tail_lane >= 3 * VARIATES) & (tail_lane < LOG_LANE)
        one_lane = (tail_lane >= LOG_LANE) & (tail_lane < LOG_LANE + 3)
        row = lax.broadcasted_iota(jnp.int32, (ROWS, WIDE), 0)
        for b in range(2 * RING):
            source = own_ref if b < RING else other_ref
            facts = source[(b % RING) * ROWS : (b % RING + 1) * ROWS, :].astype(F32)
            variate = facts[:, 2:3]
            equal = bias_lane & ((tail_lane % VARIATES).astype(F32) == variate)
            position = at_ref[b] + row
            segment = jnp.zeros_like(row)
            for j in range(SEQS):
                segment += (position >= at_ref[2 * RING + j]).astype(jnp.int32)
            inside = seg_lane & (tail_lane - 3 * VARIATES == segment)
            rows = slice(b * ROWS, (b + 1) * ROWS)
            qt_scr[rows] = (equal | inside).astype(BF16)
            tail = jnp.where(equal, bias_ref[0:1, :], bias_ref[1:2, :])
            tail = jnp.where(bias_lane, tail, jnp.where(one_lane, 1.0, 0.0))
            tail = jnp.where(seg_lane & ~inside, FAR, tail)
            kt_ref[rows] = tail.astype(BF16)

    here = pl.ds(pl.multiple_of(step * block, block), block)
    query_tail = qt_scr[here, :]
    query = jnp.concatenate([q_scr[here, :], query_tail], 1)
    zero = jnp.zeros_like(query)
    head_of = (lanes_of(query.shape) // HEAD_DIM) % 2
    lanes = lanes_of((block, WIDE))
    ones = value_lanes(size)
    out = None
    tail = query_tail.astype(F32)
    for head in range(2):
        masked = jnp.where(head_of == head, query, zero)
        total = None
        for c in range(chunks):
            rows = slice(c * size, (c + 1) * size)
            ref, at = key_rows(mine_ref, got_ref, c * size, size)
            keys = jnp.concatenate([ref[1, at, :], kt_ref[rows, :]], 1)
            values = jnp.concatenate([ref[2, at, :], ones], 1)
            prob = jnp.exp2(mm(masked, keys, NT)).astype(BF16)
            part = mm(prob, values)
            total = part if total is None else total + part
        row_sum = total[:, WIDE : WIDE + 1]
        now = total[:, :WIDE] / row_sum
        out = now if head == 0 else jnp.where(lanes < HEAD_DIM, out, now)
        tail = with_pieces(tail, -jnp.log2(row_sum), head * HEAD_DIM + LOG_LANE, lanes)
    att_ref[...] = out
    tail_ref[...] = tail.astype(BF16)
    low = out.astype(BF16)
    half = pl.num_programs(0) // 2

    @pl.when(step < half)
    def _():
        near_ref[here, :] = low

    @pl.when(step >= half)
    def _():
        send_ref[pl.ds(pl.multiple_of((step - half) * block, block), block), :] = low


def attend(at, mine, got, facts, facts_other, bias_rows):
    block = 512
    moving = pl.BlockSpec((block, WIDE), lambda i: (i, 0))
    plane = pl.BlockSpec((PLANE, WIDE), lambda i: (0, 0))
    three = pl.BlockSpec((3, PLANE, WIDE), lambda i: (0, 0, 0))
    low = jax.ShapeDtypeStruct((GROUP, WIDE), BF16)
    low_plane = jax.ShapeDtypeStruct((PLANE, WIDE), BF16)
    return pl.pallas_call(
        functools.partial(attend_kernel, chunks=8),
        grid=(GROUP // block,),
        in_specs=[
            pl.BlockSpec(memory_space=pltpu.SMEM),
            three,
            three,
            plane,
            plane,
            pl.BlockSpec((8, WIDE), lambda i: (0, 0)),
        ],
        out_specs=[moving, plane, plane, moving, pl.BlockSpec((GROUP, WIDE), lambda i: (0, 0))],
        out_shape=[jax.ShapeDtypeStruct((GROUP, WIDE), F32), low_plane, low_plane, low, low],
        scratch_shapes=[pltpu.VMEM((GROUP, WIDE), BF16)] * 2,
        compiler_params=pltpu.CompilerParams(vmem_limit_bytes=48 * 2**20),
        cost_estimate=pl.CostEstimate(
            flops=16 * GROUP * GROUP * WIDE, bytes_accessed=GROUP * WIDE * 24,
            transcendentals=2 * GROUP * GROUP,
        ),
    )(at, mine, got, facts, facts_other, bias_rows)


def attend_back_kernel(
    mine_ref, got_ref, qt_ref, kt_ref, hot_ref, near_ref, other_ref, att_ref,
    keep_ref, send_ref, bias_ref, q_scr, grad_scr, dk_sum, dv_sum, *, chunks,
):
    size = GROUP // chunks
    step = pl.program_id(0)
    block = qt_ref.shape[0]

    @pl.when(step == 0)
    def _():
        q_scr[:PLANE] = mine_ref[0]
        q_scr[PLANE:] = got_ref[0]
        grad_scr[:PLANE] = near_ref[...]
        grad_scr[PLANE:] = other_ref[...]
        dk_sum[...] = jnp.zeros_like(dk_sum)
        dv_sum[...] = jnp.zeros_like(dv_sum)

    here = pl.ds(pl.multiple_of(step * block, block), block)
    query = jnp.concatenate([q_scr[here, :], qt_ref[...]], 1)
    grad = grad_scr[here, :]
    zero = jnp.zeros_like(query)
    head_of = (lanes_of(query.shape) // HEAD_DIM) % 2
    lanes = lanes_of((block, WIDE))
    overlap = grad.astype(F32) * att_ref[...]
    ones = value_lanes(size)
    out = None
    for head in range(2):
        mine = head_of[:, :WIDE] == head
        masked = jnp.where(head_of == head, query, zero)
        grad_here = jnp.where(mine, grad, zero[:, :WIDE])
        dots = jnp.sum(jnp.where(mine, overlap, 0.0), axis=1, keepdims=True)
        extra = with_pieces(jnp.zeros(lanes.shape, F32), -dots, 0, lanes).astype(BF16)
        grad_wide = jnp.concatenate([grad_here, extra], 1)
        total = None
        for c in range(chunks):
            rows = slice(c * size, (c + 1) * size)
            ref, at = key_rows(mine_ref, got_ref, c * size, size)
            keys = ref[1, at, :]
            prob = jnp.exp2(mm(jnp.concatenate([keys, kt_ref[rows, :]], 1), masked, NT))
            slope = mm(jnp.concatenate([ref[2, at, :], ones], 1), grad_wide, NT)
            d_score = (prob * slope).astype(BF16)
            dv_sum[rows, :] += mm(prob.astype(BF16), grad_here)
            dk_sum[rows, :] += mm(d_score, masked)
            part = mm(d_score, keys, TN)
            total = part if total is None else total + part
        out = total if head == 0 else jnp.where(lanes < HEAD_DIM, out, total)
    low = out.astype(BF16)
    half = pl.num_programs(0) // 2

    @pl.when(step < half)
    def _():
        keep_ref[0, here, :] = low

    @pl.when(step >= half)
    def _():
        send_ref[0, pl.ds(pl.multiple_of((step - half) * block, block), block), :] = low

    @pl.when(step == pl.num_programs(0) - 1)
    def _():
        for ref, rows in ((keep_ref, slice(0, PLANE)), (send_ref, slice(PLANE, GROUP))):
            ref[1] = (dk_sum[rows, :WIDE] * (1.0 / LOG2E)).astype(BF16)
            ref[2] = dv_sum[rows, :].astype(BF16)
        counts = dk_sum[:, WIDE:]
        bias_ref[...] = jnp.zeros_like(bias_ref)
        bias_ref[0:1, :] = jnp.sum(counts * hot_ref[...].astype(F32), axis=0, keepdims=True)
        bias_ref[1:2, :] = jnp.sum(counts, axis=0, keepdims=True)


def attend_back(mine, got, query_tail, key_tail, near, other, attended):
    block = 512
    moving = pl.BlockSpec((block, WIDE), lambda i: (i, 0))
    fixed = pl.BlockSpec((GROUP, WIDE), lambda i: (0, 0))
    plane = pl.BlockSpec((PLANE, WIDE), lambda i: (0, 0))
    three = pl.BlockSpec((3, PLANE, WIDE), lambda i: (0, 0, 0))
    low = jax.ShapeDtypeStruct((3, PLANE, WIDE), BF16)
    return pl.pallas_call(
        functools.partial(attend_back_kernel, chunks=4),
        grid=(GROUP // block,),
        in_specs=[three, three, moving, fixed, fixed, plane, plane, moving],
        out_specs=[three, three, pl.BlockSpec((8, WIDE), lambda i: (0, 0))],
        out_shape=[low, low, jax.ShapeDtypeStruct((8, WIDE), F32)],
        scratch_shapes=[
            pltpu.VMEM((GROUP, WIDE), BF16),
            pltpu.VMEM((GROUP, WIDE), BF16),
            pltpu.VMEM((GROUP, 2 * WIDE), F32),
            pltpu.VMEM((GROUP, WIDE), F32),
        ],
        compiler_params=pltpu.CompilerParams(vmem_limit_bytes=48 * 2**20),
        cost_estimate=pl.CostEstimate(
            flops=40 * GROUP * GROUP * WIDE, bytes_accessed=GROUP * WIDE * 24,
            transcendentals=2 * GROUP * GROUP,
        ),
    )(mine, got, query_tail, key_tail, query_tail, near, other, attended)


def feed_kernel(b_ref, g_ref, w_ref, y_ref, db_ref, act_ref, *, cuts):
    rows, grads = b_ref[...], g_ref[...]
    size = w_ref.shape[2] // cuts

    def products(j):
        cols = slice(j * size, (j + 1) * size)
        return mm(rows, w_ref[0, :, cols]), mm(rows, w_ref[1, :, cols]), mm(grads, w_ref[2, :, cols])

    y_sum, db_sum = None, None
    ready = products(0)
    for j in range(cuts):
        gate, up, d_hidden = ready
        if j + 1 < cuts:
            ready = products(j + 1)
        cols = slice(j * size, (j + 1) * size)
        sig = 0.5 + 0.5 * jnp.tanh(0.5 * gate)
        silu = gate * sig
        hidden = (silu * up).astype(BF16)
        d_gate = (d_hidden * up * (sig + silu * (1.0 - sig))).astype(BF16)
        d_up = (d_hidden * silu).astype(BF16)
        act_ref[0, :, cols] = d_gate
        act_ref[1, :, cols] = d_up
        act_ref[2, :, cols] = hidden
        y_part = mm(hidden, w_ref[2, :, cols], NT)
        db_part = mm(d_gate, w_ref[0, :, cols], NT) + mm(d_up, w_ref[1, :, cols], NT)
        y_sum = y_part if y_sum is None else y_sum + y_part
        db_sum = db_part if db_sum is None else db_sum + db_part
    y_ref[...] = y_sum.astype(BF16)
    db_ref[...] = db_sum.astype(BF16)


def feed(rows_b, rows_g, weights):
    rows = rows_b.shape[0]
    width = weights.shape[2]
    low_d = jax.ShapeDtypeStruct((rows, D), BF16)
    low_f = jax.ShapeDtypeStruct((3, rows, width), BF16)
    return pl.pallas_call(
        functools.partial(feed_kernel, cuts=2),
        out_shape=[low_d, low_d, low_f],
        compiler_params=pltpu.CompilerParams(vmem_limit_bytes=26 * 2**20),
        cost_estimate=pl.CostEstimate(
            flops=12 * rows * D * width, bytes_accessed=6 * D * width + rows * D * 8 + rows * width * 6,
            transcendentals=rows * width,
        ),
    )(rows_b, rows_g, weights)


def body(
    tokens,
    cotangent,
    destination,
    variate_ids,
    time_ids,
    seq_lengths,
    qkv_weight,
    out_weight,
    gate_up_weight,
    down_weight,
    norm_gains,
    qk_gains,
    variate_bias,
):
    core = lax.axis_index("core")
    low_core = core == 0
    y_at = lax.axis_index("y")
    zl_at = lax.axis_index("zl")

    core_scalar = core.reshape(1).astype(jnp.int32)

    def side_by_side(mine, other):
        return jnp.concatenate(
            [jnp.where(low_core, mine, other), jnp.where(low_core, other, mine)], axis=-1
        )

    feed_shard = jnp.concatenate([gate_up_weight, down_weight.T[None]], 0)

    slot = destination % ROWS
    group_at = destination // GROUP
    block_at = (destination % GROUP) // ROWS
    device_at = ((group_at // 2) * 2 + block_at // 4) * 8 + (block_at % 4) * 2 + group_at % 2
    key = device_at * ROWS + slot
    zero = jnp.zeros_like(slot)
    facts = jnp.stack([key, slot, variate_ids, time_ids // 32, time_ids % 32, zero, zero, zero])
    gains_row = jnp.pad(
        norm_gains.reshape(8, 16), ((0, 0), (GAIN_LANE, WIDE - GAIN_LANE - 16))
    ).astype(F32)
    outgoing, deal = deal_rows(tokens, cotangent, facts.astype(F32), gains_row)
    arrived = lax.all_to_all(outgoing.reshape(DEVICES, 8, SPAN), ALL, 0, 0, tiled=True)
    out_shard, outgoing = lax.optimization_barrier((out_weight.T, outgoing))
    attn_shard = jnp.concatenate([qkv_weight, jnp.stack(gather_direct(out_shard))], 0)
    attn_mine = gather_round(attn_shard, ("zh", "zl"), lax.axis_index("zh") * 2 + zl_at)
    attn_mine, arrived = lax.optimization_barrier((attn_mine, arrived))
    attn_mine = jnp.stack(gather_ahead(attn_mine, "x")).reshape((16,) + attn_shard.shape)

    lengths_other = swap_core(seq_lengths)
    lengths = jnp.where(zl_at == core, seq_lengths, lengths_other)[0]
    bias_other = lax.ppermute(variate_bias, "zl", [(0, 1), (1, 0)])
    bias_pair = jnp.where(zl_at == core, variate_bias, bias_other)

    arrived, lengths, bias_pair = lax.optimization_barrier((arrived, lengths, bias_pair))
    all_gains = arrived.reshape(16, 8, 8, SPAN)[:, 0, :, PAIR + GAIN_LANE : PAIR + GAIN_LANE + 16]
    inputs, grad_rows, attn_in, place, gains = receive(
        arrived.reshape(4 * ROWS, SPAN), all_gains.reshape(16, WIDE)
    )
    feed_shard, attn_in = lax.optimization_barrier((feed_shard, attn_in))
    feed_many = jnp.broadcast_to(feed_shard[None], (16,) + feed_shard.shape)
    zero_at = jnp.zeros((1,), jnp.int32)
    x_at = lax.axis_index("x").reshape(1).astype(jnp.int32)
    ahead, behind = ring(attn_in, -1), ring(attn_in, 1)
    ahead, feed_many = lax.optimization_barrier((ahead, feed_many))
    far_top, far_low = ring(ahead[: ROWS // 2], -1), ring(behind[ROWS // 2 :], 1)
    far_top, far_low, attn_mine, feed_many = lax.optimization_barrier(
        (far_top, far_low, attn_mine, feed_many)
    )
    feed_mine = lax.all_to_all(feed_many, FLAT, 0, 0, tiled=True)
    attn_w = assemble(core_scalar, x_at, attn_mine, swap_core(attn_mine))
    attn_all = [attn_in, ahead, jnp.concatenate([far_top, far_low], 0), behind]
    grad_rows, attn_all = lax.optimization_barrier((grad_rows, attn_all))
    grad_all = gather_direct(grad_rows)

    blocks_y = (y_at + jnp.arange(RING)) % RING
    blocks = jnp.concatenate([core * RING + blocks_y, (1 - core) * RING + blocks_y])
    at = jnp.concatenate([blocks * ROWS, jnp.cumsum(lengths)]).astype(jnp.int32)

    inverse = THETA ** (-2.0 * jnp.arange(HALF).astype(F32) / HEAD_DIM)
    freq = jnp.concatenate(
        [
            jnp.tile(inverse, 8)[None],
            jnp.tile(qk_gains, (1, 4)),
            jnp.zeros((5, 2 * WIDE), F32),
        ]
    )
    qkv_mine, qkv_send, raw, facts_all = project(core_scalar, attn_all, attn_w, freq)
    facts_other = swap_core(facts_all)
    qkv_got = swap_core(qkv_send)

    bias_parts = jnp.stack(pieces(bias_pair * LOG2E, 3)).astype(F32)
    bias_rows = jnp.repeat(bias_parts, VARIATES, axis=0).transpose(1, 2, 0)
    bias_rows = jnp.pad(bias_rows, ((0, 0), (0, 0), (0, HEAD_DIM - 3 * VARIATES))).reshape(2, WIDE)
    bias_rows = jnp.pad(bias_rows, ((0, 6), (0, 0)))
    attended, att_near, att_send, query_back, key_tail = attend(
        at, qkv_mine, qkv_got, facts_all, facts_other, bias_rows
    )
    att_send, feed_mine = lax.optimization_barrier((att_send, feed_mine))
    att_other = swap_core(att_send)
    att_other, grad_all = lax.optimization_barrier((att_other, grad_all))
    att_plane = side_by_side(att_near, att_other).reshape(RING, ROWS, 2 * WIDE)
    att_rows = trade_ring([att_plane[r] for r in range(RING)])
    att_rows, feed_mine = lax.optimization_barrier((att_rows, feed_mine))
    feed_w = assemble(core_scalar, zero_at, feed_mine, swap_core(feed_mine))
    hidden_one, feed_in = out_project(att_rows, attn_w, inputs, gains)

    ahead, behind = ring(feed_in, -1), ring(feed_in, 1)
    fed_own = feed(feed_in, grad_all[0], feed_w)
    ahead, behind, fed_own = lax.optimization_barrier((ahead, behind, fed_own))
    far_top, far_low = ring(ahead[: ROWS // 2], -1), ring(behind[ROWS // 2 :], 1)
    fed_ahead = feed(ahead, grad_all[1], feed_w)
    fed_behind = feed(behind, grad_all[3], feed_w)
    far_top, far_low, fed_ahead, fed_behind = lax.optimization_barrier(
        (far_top, far_low, fed_ahead, fed_behind)
    )
    far = jnp.concatenate([far_top, far_low], 0)
    fed_far = feed(far, grad_all[2], feed_w)
    feed_all = [feed_in, ahead, far, behind]
    fed = [fed_own, fed_ahead, fed_far, fed_behind]
    feed_split = weight_grads(core_scalar, feed_all, grad_all, [f[2] for f in fed], 2, 2)
    db_got = send_ring([f[1] for f in fed], True)
    db_got, feed_split = lax.optimization_barrier((db_got, feed_split))
    grad_one, gain_two_grad, d_att, *both = middle(
        att_rows, attn_w, [f[0] for f in fed], fed_own[1], db_got, hidden_one, grad_rows, gains
    )
    feed_total = chip_total(feed_split)
    feed_got = trade(feed_total, "x")

    grad_att = trade_ring([d_att[r] for r in range(RING)])
    grad_att[1], feed_total = lax.optimization_barrier((grad_att[1], feed_total))
    grad_att = jnp.concatenate(grad_att, 0)
    both, grad_att = lax.optimization_barrier((both, grad_att))
    both_got = send_ring(both)
    grad_left, grad_right = grad_att[:, :WIDE], grad_att[:, WIDE:]
    grad_other = swap_core(jnp.where(low_core, grad_right, grad_left))
    grad_near = jnp.where(low_core, grad_left, grad_right)
    d_keep, d_send, bias_sums = attend_back(
        qkv_mine, qkv_got, query_back, key_tail, grad_near, grad_other, attended
    )
    first_part = (jnp.arange(HEAD_DIM) < VARIATES)[None, None]
    bias_sums = jnp.where(first_part, bias_sums[:2].reshape(2, 2, HEAD_DIM), 0.0)
    bias_sums = jnp.sum(bias_sums, axis=2)
    bias_part = jnp.stack([bias_sums[0], bias_sums[1] - bias_sums[0]])
    d_got = swap_core(d_send)
    grad_proj, qk_sums, *in_part = unproject(
        core_scalar, d_keep, d_got, raw, facts_all, attn_w, freq
    )
    in_got = send_ring(in_part)
    feed_half = added(feed_got).astype(BF16)
    in_got[0], feed_half = lax.optimization_barrier((in_got[0], feed_half))
    grad_proj, both_got = lax.optimization_barrier((grad_proj, both_got))
    both_sum = add_ring(both[0], both_got)
    mixed = (hidden_one + both_sum[:ROWS]).astype(BF16)
    out_full = both_sum[ROWS:].astype(BF16)
    attn_split = weight_grads(core_scalar, attn_all, [out_full], [grad_proj], None, 1)
    attn_total = chip_total(attn_split)
    in_got, _ = lax.optimization_barrier((in_got, attn_split))
    mixed, _ = lax.optimization_barrier((mixed, attn_total))
    feed_got = trade(feed_half, ("zh", "zl"))
    attn_own, attn_got = send_round(attn_total.reshape((RING, RING) + attn_total.shape[1:]), "x")
    qk_sums = jnp.sum(qk_sums[:2].reshape(2, 4, HEAD_DIM), axis=1)

    small = jnp.zeros((8, WIDE), F32).at[0].set(qk_sums.reshape(WIDE))
    small = small.at[1, :4].set(bias_part.reshape(4))
    tensor_at = (y_at * 2 + core).reshape(1).astype(jnp.int32)
    last = finish(
        in_part[0], in_got, inputs, grad_one, mixed, place, gains, gain_two_grad, small, tensor_at
    )
    last = last.reshape(DEVICES, 8, 2 * QUARTER + WIDE)
    last, attn_got, feed_got = lax.optimization_barrier((last, attn_got, feed_got))
    home = lax.all_to_all(last, ALL, 0, 0, tiled=True)
    own, got = send_round(add_round(attn_own, attn_got).astype(BF16), ("zh", "zl"))
    home, got = lax.optimization_barrier((home, got))
    attn_grad = add_round(own, got)
    feed_grad = added(feed_got).reshape(3, 64, 512)
    new_tokens, token_grads, sums = settle(home.reshape(4 * ROWS, 2 * QUARTER + WIDE), deal)
    gains_grad = sums[0].reshape(2, 64)
    qk_grad = sums[1].reshape(2, 64)
    bias_grad = sums[2, :4].reshape(2, 2)

    return (
        new_tokens,
        token_grads,
        attn_grad[:3],
        attn_grad[3].T,
        feed_grad[:2],
        feed_grad[2].T,
        gains_grad,
        qk_grad,
        bias_grad,
    )


def solution(mesh):
    fine = Mesh(mesh.devices.reshape(4, 2, 2, 4, 2), ALL)
    dp = ("x", "zh", "core")
    tensor = ("y", "zl")
    in_specs = (
        P(ALL, None),
        P(ALL, None),
        P(ALL),
        P(ALL),
        P(ALL),
        P(dp, None),
        P(None, dp, tensor),
        P(tensor, dp),
        P(None, dp, tensor),
        P(tensor, dp),
        P(None, dp),
        P(),
        P(None, tensor),
    )
    out_specs = (
        P(ALL, None),
        P(ALL, None),
        P(None, dp, tensor),
        P(tensor, dp),
        P(None, dp, tensor),
        P(tensor, dp),
        P(None, dp),
        P(),
        P(None, tensor),
    )
    return jax.shard_map(body, mesh=fine, in_specs=in_specs, out_specs=out_specs, check_vma=False)
```
